32 devices in a mesh: lon: 8 (over y, x, core), lat: 4 (over z).
Axes of the slice: x: 2, y: 2, z: 4, core: 2. Of those that a mesh axis runs over, the one named last changes fastest.
Arguments:
- record_values: bfloat16 [64, 16, 2, 128], P('lon', 'lat'), may hold values from -6 to 6
- record_cell: int32 [64, 16, 2], P('lon', 'lat'), may hold values from 0 to 287
- record_instrument: int32 [64, 16, 2], P('lon', 'lat'), may hold values from 0 to 7
- block_counts: int32 [64, 16], P('lon', 'lat'), may hold values from 0 to 2, as said below
- background: bfloat16 [48, 192, 2, 192], P('lat', 'lon'), may hold values from -6 to 6
- input_weight: bfloat16 [128, 192], replicated, may hold values from -0.5 to 0.5
- instrument_table: bfloat16 [8, 192], replicated, may hold values from -4 to 4
- lift_weight: bfloat16 [192, 384], replicated, may hold values from -0.4375 to 0.4375
- first_gain: bfloat16 [192], replicated, may hold values from 0.5 to 1.5
- attn_weight: bfloat16 [192, 576], replicated
- mix_weight: bfloat16 [192, 192], replicated, may hold values from -0.4375 to 0.4375
- second_gain: bfloat16 [192], replicated, may hold values from 0.5 to 1.5
- up_weight: bfloat16 [192, 768], replicated, may hold values from -0.4375 to 0.4375
- down_weight: bfloat16 [768, 192], replicated, may hold values from -0.21875 to 0.21875
Outputs:
- result: bfloat16 [48, 192, 2, 192], P('lat', 'lon')
The draws below stay inside these ranges and needn't reach their ends.
Inputs may be any that keep to these rules, and one draw needn't show every extreme that they name: `block_counts`: each block's count is at most 2; for some tiles every source fills all 2 slots.
All inputs are finite; a program needn't handle non-finite values.
Results may differ from the reference program's by a relative error of at most 0.017.
Values may be sent and summed in bfloat16 or wider, within the bound.
No kernel may reach another device: no remote copies, remote signals or barrier semaphores. Data moves between devices by JAX's collectives and lax.ppermute only.
A program may use at most 64 MiB of HBM per device.

```python
import jax
import jax.numpy as jnp
from jax import lax

C = 192
HEADS = 6
MLPW = 768
F = 128
INSTR = 8
LEV = 2
WLAT = 6
WLON = 12
CLAT = 12
CLON = 24
CAP = 2
HD = 32
NLAT = 48
NLON = 192
N_LON = 8
N_LAT = 4


def draw_block_counts(key, part):
    first, second, third, fourth = jax.random.split(key, 4)
    base = jax.random.randint(first, (N_LON * N_LON, N_LAT * N_LAT), 0, CAP + 1)
    dense = jax.random.randint(second, (N_LON, N_LAT), 0, 8) == 0
    pick_lon = jax.random.randint(third, (), 0, N_LON)
    pick_lat = jax.random.randint(fourth, (), 0, N_LAT)
    forced = (jnp.arange(N_LON)[:, None] == pick_lon) & (jnp.arange(N_LAT)[None, :] == pick_lat)
    dense_all = jnp.tile(dense | forced, (N_LON, N_LAT))
    return jnp.where(dense_all, CAP, base).astype(jnp.int32)


def draw_attn_weight(key, part):
    spread = C ** (-0.5)
    base = jax.random.normal(key, (C, 3 * C), jnp.float32) * spread
    return base.astype(jnp.bfloat16)


def place_ends(drawn, rng, smallest, high):
    place = [jax.random.randint(jax.random.fold_in(rng, axis), (), 0, length) for axis, length in enumerate(drawn.shape)]
    widest = drawn.shape.index(max(drawn.shape))
    neighbour = place[:widest] + [(place[widest] + 1) % drawn.shape[widest]] + place[widest + 1:]
    return drawn.at[tuple(place)].set(smallest).at[tuple(neighbour)].set(high)


def block_levels(own_key, shape, cuts, smallest, high):
    factor_of, own = 1.0, jax.random.fold_in(own_key, 6)
    for axis_at, blocks in cuts:
        steps = jnp.exp(jax.random.uniform(jax.random.fold_in(own, axis_at), (blocks,), jnp.float32, smallest / len(cuts), high / len(cuts)))
        factor_of = factor_of * jnp.repeat(steps, shape[axis_at] // blocks).reshape([-1 if axis == axis_at else 1 for axis in range(len(shape))])
    return factor_of


def normal_values(key, extent, deviation, reach, shards=(), held_as=jnp.bfloat16):
    level = block_levels(key, extent, shards, -0.22, 0.18) if shards else 1.0
    values = jax.random.normal(key, extent, jnp.float32) * deviation * level
    return jnp.minimum(jnp.maximum(values, -reach), reach).astype(held_as)


def setup_inputs(seed: int = 0) -> dict:
    streams_of = jax.random.split(jax.random.key(seed), 15)
    record_values = normal_values(streams_of[0], (N_LON * N_LON, N_LAT * N_LAT, CAP, F), 1.0, 6.0, ((0, 8), (1, 4)))
    record_cell = place_ends(jax.random.randint(streams_of[1], (N_LON * N_LON, N_LAT * N_LAT, CAP), 0, CLAT * CLON), jax.random.fold_in(streams_of[1], 1), 0, (CLAT * CLON) - 1).astype(jnp.int32)
    record_instrument = place_ends(jax.random.randint(streams_of[2], (N_LON * N_LON, N_LAT * N_LAT, CAP), 0, INSTR), jax.random.fold_in(streams_of[2], 1), 0, INSTR - 1).astype(jnp.int32)
    block_counts = draw_block_counts(jax.random.fold_in(streams_of[14], 71), 0)
    background = normal_values(streams_of[4], (NLAT, NLON, LEV, C), 1.0, 6.0, ((0, 4), (1, 8)))
    input_weight = normal_values(streams_of[5], (F, C), F ** -0.5, 0.5)
    instrument_table = normal_values(streams_of[6], (INSTR, C), 1.0, 4.0)
    lift_weight = normal_values(streams_of[7], (C, LEV * C), C ** -0.5, 0.4375)
    first_gain = jnp.clip(1.0 + 0.1 * jax.random.normal(streams_of[8], (C,), jnp.float32), 0.5, 1.5).astype(jnp.bfloat16)
    attn_weight = draw_attn_weight(jax.random.fold_in(streams_of[14], 71), 0)
    mix_weight = normal_values(streams_of[10], (C, C), C ** -0.5, 0.4375)
    second_gain = jnp.clip(1.0 + 0.1 * jax.random.normal(streams_of[11], (C,), jnp.float32), 0.5, 1.5).astype(jnp.bfloat16)
    up_weight = normal_values(streams_of[12], (C, MLPW), C ** -0.5, 0.4375)
    down_weight = normal_values(streams_of[13], (MLPW, C), MLPW ** -0.5, 0.21875)
    return {"record_values": record_values, "record_cell": record_cell, "record_instrument": record_instrument, "block_counts": block_counts, "background": background, "input_weight": input_weight, "instrument_table": instrument_table, "lift_weight": lift_weight, "first_gain": first_gain, "attn_weight": attn_weight, "mix_weight": mix_weight, "second_gain": second_gain, "up_weight": up_weight, "down_weight": down_weight}


def layer_norm(tensor, norm_gain):
    wide = tensor.astype(jnp.float32)
    average = lax.optimization_barrier(jnp.mean(wide, axis=-1, keepdims=True))
    centred = wide - average
    spread = lax.optimization_barrier(jnp.mean(centred * centred, axis=-1, keepdims=True))
    return (centred * lax.rsqrt(spread + 1e-05) * norm_gain.astype(jnp.float32)).astype(jnp.bfloat16)

def to_windows(tensor):
    height, breadth, levels, width = tensor.shape
    shaped = tensor.reshape(height // WLAT, WLAT, breadth // WLON, WLON, levels, width)
    shaped = shaped.transpose(0, 2, 1, 3, 4, 5)
    return shaped.reshape(height // WLAT * (breadth // WLON), WLAT * WLON * levels, width)

def from_windows(tensor, height, breadth):
    width = tensor.shape[-1]
    shaped = tensor.reshape(height // WLAT, breadth // WLON, WLAT, WLON, LEV, width)
    return shaped.transpose(0, 2, 1, 3, 4, 5).reshape(height, breadth, LEV, width)

def reference(record_values, record_cell, record_instrument, block_counts, background, input_weight, instrument_table, lift_weight, first_gain, attn_weight, mix_weight, second_gain, up_weight, down_weight):
    blocks = record_values.reshape(N_LON, N_LON, N_LAT, N_LAT, CAP, F)
    cell_blocks = record_cell.reshape(N_LON, N_LON, N_LAT, N_LAT, CAP)
    instr_blocks = record_instrument.reshape(N_LON, N_LON, N_LAT, N_LAT, CAP)
    count_blocks = block_counts.reshape(N_LON, N_LON, N_LAT, N_LAT)
    back_tiles = background.reshape(N_LAT, CLAT, N_LON, CLON, LEV, C)

    def tile_latent(tile_id):
        dest_lon = tile_id // N_LAT
        dest_lat = tile_id % N_LAT
        values = jnp.take(jnp.take(blocks, dest_lon, axis=1), dest_lat, axis=2).reshape(-1, F)
        cells = jnp.take(jnp.take(cell_blocks, dest_lon, axis=1), dest_lat, axis=2)
        instruments = jnp.take(jnp.take(instr_blocks, dest_lon, axis=1), dest_lat, axis=2).reshape(-1)
        counts = jnp.take(jnp.take(count_blocks, dest_lon, axis=1), dest_lat, axis=2)
        is_live = jnp.arange(CAP, dtype=jnp.int32)[None, None, :] < counts[:, :, None]
        before = jnp.dot(values, input_weight, preferred_element_type=jnp.float32)
        before = before + jnp.take(instrument_table, instruments, axis=0).astype(jnp.float32)
        encoded = jax.nn.gelu(before).astype(jnp.bfloat16)
        lifted = jax.nn.gelu(jnp.dot(encoded, lift_weight, preferred_element_type=jnp.float32)).astype(jnp.bfloat16)
        cell_flat = jnp.where(is_live, cells, -1).reshape(-1).astype(jnp.int32)
        onehot = (jnp.arange(CLAT * CLON, dtype=jnp.int32)[:, None] == cell_flat[None, :]).astype(jnp.bfloat16)
        summed = jnp.dot(onehot, lifted, preferred_element_type=jnp.float32)
        tallies = lax.optimization_barrier(jnp.sum(onehot.astype(jnp.float32), axis=1))
        prior = jnp.take(jnp.take(back_tiles, dest_lat, axis=0), dest_lon, axis=1).astype(jnp.float32)
        latent_tile = (prior + summed.reshape(CLAT, CLON, LEV, C)) / (1.0 + tallies).reshape(CLAT, CLON, 1, 1)
        return latent_tile.astype(jnp.bfloat16)
    tiles = lax.map(tile_latent, jnp.arange(N_LON * N_LAT, dtype=jnp.int32))
    latent = tiles.reshape(N_LON, N_LAT, CLAT, CLON, LEV, C).transpose(1, 2, 0, 3, 4, 5).reshape(NLAT, NLON, LEV, C)
    normed = layer_norm(latent, first_gain)
    rolled = jnp.roll(normed, (-(WLAT // 2), -(WLON // 2)), axis=(0, 1))
    projected = jnp.dot(rolled.reshape(-1, C), attn_weight, preferred_element_type=jnp.float32).reshape(NLAT, NLON, LEV, 3 * C)
    query = (projected[..., :C] * HD ** (-0.5)).astype(jnp.bfloat16)
    keys = projected[..., C:2 * C].astype(jnp.bfloat16)
    value_rows = projected[..., 2 * C:].astype(jnp.bfloat16)
    initial = (jnp.arange(NLAT, dtype=jnp.int32) + WLAT // 2) % NLAT
    region = (initial >= NLAT - WLAT // 2).astype(jnp.float32)
    region = jnp.broadcast_to(region[:, None, None, None], (NLAT, NLON, LEV, 1))
    row_windows = NLAT // WLAT
    col_windows = NLON // WLON
    tokens = WLAT * WLON * LEV
    query_w = to_windows(query).reshape(row_windows, col_windows, tokens, HEADS, HD)
    keys_w = to_windows(keys).reshape(row_windows, col_windows, tokens, HEADS, HD)
    values_w = to_windows(value_rows).reshape(row_windows, col_windows, tokens, HEADS, HD)
    region_w = to_windows(region).reshape(row_windows, col_windows, tokens)

    def window_row(pieces):
        query_p, keys_p, values_p, region_p = pieces
        scores = jnp.einsum('wqhd,wkhd->whqk', query_p.astype(jnp.float32), keys_p.astype(jnp.float32))
        allowed = region_p[:, None, :, None] == region_p[:, None, None, :]
        scores = jnp.where(allowed, scores, jnp.float32(-1e+30))
        largest = lax.optimization_barrier(jnp.max(scores, axis=-1, keepdims=True))
        raised = jnp.exp(scores - largest)
        attn_weights = (raised / lax.optimization_barrier(jnp.sum(raised, axis=-1, keepdims=True))).astype(jnp.bfloat16)
        out = jnp.einsum('whqk,wkhd->wqhd', attn_weights.astype(jnp.float32), values_p.astype(jnp.float32))
        return out.astype(jnp.bfloat16)
    mixed_w = lax.map(window_row, (query_w, keys_w, values_w, region_w))
    mixed_rolled = from_windows(mixed_w.reshape(row_windows * col_windows, tokens, C), NLAT, NLON)
    mixed = jnp.roll(mixed_rolled, (WLAT // 2, WLON // 2), axis=(0, 1))
    after_attn = latent.astype(jnp.float32) + jnp.dot(mixed.reshape(-1, C), mix_weight, preferred_element_type=jnp.float32).reshape(NLAT, NLON, LEV, C)
    after_attn = after_attn.astype(jnp.bfloat16)
    normed_two = layer_norm(after_attn, second_gain)
    hidden = jax.nn.gelu(jnp.dot(normed_two.reshape(-1, C), up_weight, preferred_element_type=jnp.float32)).astype(jnp.bfloat16)
    result = after_attn.astype(jnp.float32) + jnp.dot(hidden, down_weight, preferred_element_type=jnp.float32).reshape(NLAT, NLON, LEV, C)
    return result.astype(jnp.bfloat16)
```

```python
import functools

import jax
import jax.numpy as jnp
import ml_dtypes
import numpy as np
from jax import lax
from jax.experimental import pallas as pl
from jax.experimental.pallas import tpu as pltpu
from jax.sharding import PartitionSpec as P

HEADS = 6
INSTR = 8
LEV = 2
WLAT = 6
WLON = 12
HLAT = WLAT // 2
HLON = WLON // 2
PAD = 256
FIELDS = 4
GROUP = 8
CHUNK = 32
BF16 = jnp.bfloat16
F32 = jnp.float32

AROUND = [(dy, dx) for dy in (-1, 0, 1) for dx in (-1, 0, 1)]


def shifted(value, axis, steps):
    count = lax.axis_size(axis)
    pairs = [(source, (source + steps) % count) for source in range(count)]
    return lax.ppermute(value, axis, pairs)


def window_cells(lat_cells, lon_cells):
    high, wide = lat_cells + WLAT, lon_cells + WLON
    windows = []
    for top in range(0, high, WLAT):
        for left in range(0, wide, WLON):
            cells = [(r, c) for r in range(top, top + WLAT) for c in range(left, left + WLON)]
            own = [
                (r, c)
                for r, c in cells
                if HLAT <= r < HLAT + lat_cells and HLON <= c < HLON + lon_cells
            ]
            rest = [cell for cell in cells if cell not in own]
            windows.append((own, rest))
    return windows


def gelu(x):
    return jax.nn.gelu(x)


def normalise(wide, gain):
    average = jnp.mean(wide, axis=-1, keepdims=True)
    centred = wide - average
    spread = jnp.mean(centred * centred, axis=-1, keepdims=True)
    return centred * lax.rsqrt(spread + 1e-05) * gain


def dot(a, b):
    return jnp.dot(a, b, preferred_element_type=F32)


def dot_nt(a, b):
    return lax.dot_general(a, b, (((1,), (1,)), ((), ())), preferred_element_type=F32)


def block_kernel(
    plan,
    pole_ref,
    recv_ref,
    bg_ref,
    find_ref,
    pick_ref,
    coef_ref,
    place_ref,
    code_ref,
    keep_ref,
    sel_ref,
    win_ref,
    tab_ref,
    lift_ref,
    g1_ref,
    wq_ref,
    wk_ref,
    wv_ref,
    wm_ref,
    g2_ref,
    wu_ref,
    wd_ref,
    out_ref,
    lifted_ref,
    hot_ref,
    sum_ref,
):
    width = win_ref.shape[0]
    stride = find_ref.shape[0]
    per_chunk = lifted_ref.shape[0]
    chunks = recv_ref.shape[0] // per_chunk
    cells = bg_ref.shape[0]
    in_window = WLAT * WLON

    def scatter(base):
        for group in range(per_chunk // stride):
            at = group * stride
            recs = recv_ref[pl.ds(base + at, stride), :]
            meta = (dot(find_ref[...], recs) * pick_ref[...].astype(F32)).astype(BF16)
            lane = lax.broadcasted_iota(jnp.int32, (stride, 128), 1).astype(F32)
            tag = dot(meta, coef_ref[8:, :])
            chooser = jnp.where(tag == lane, 1.0, 0.0).astype(BF16)
            before = dot_nt(recs, win_ref[...]) + dot(chooser[:, :INSTR], tab_ref[...])
            encoded = gelu(before).astype(BF16)
            lifted = gelu(dot(encoded, lift_ref[...]))
            lanes = lax.broadcasted_iota(jnp.int32, lifted.shape, 1) % PAD
            lifted_ref[at : at + stride, :] = jnp.where(lanes >= width, 1.0, lifted).astype(BF16)
            code = dot_nt(coef_ref[:8, :], meta)[:1, :] + place_ref[:, at : at + stride]
            hot_ref[:, at : at + stride] = jnp.where(code_ref[...] == code, 1.0, 0.0).astype(BF16)
        return dot(hot_ref[...], lifted_ref[...])

    if chunks == 1:
        sum_ref[...] = scatter(0)
    else:
        sum_ref[...] = jnp.zeros_like(sum_ref)

        @pl.loop(0, chunks)
        def _(step):
            sum_ref[...] += scatter(pl.multiple_of(step * per_chunk, per_chunk))

    gain_one = g1_ref[...].astype(F32)
    latents, normeds = [], []
    for level in range(LEV):
        piece = sum_ref[:, level * PAD : (level + 1) * PAD]
        share = 1.0 / (1.0 + piece[:, width : width + 1])
        back = bg_ref[:, level * PAD : level * PAD + width].astype(F32)
        latent = ((back + piece[:, :width]) * share).astype(BF16).astype(F32)
        latents.append(latent)
        normeds.append(normalise(latent, gain_one))

    def gathered(tensors, counts):
        return jnp.concatenate(
            [t[w * in_window : w * in_window + n] for w, n in enumerate(counts) for t in tensors],
            axis=0,
        )

    all_n = gathered(normeds, [in_window] * len(plan)).astype(BF16)
    own_n = gathered(normeds, plan).astype(BF16)
    own_latent = gathered(latents, plan)
    keys = dot(all_n, wk_ref[...]).astype(BF16)
    values = dot(all_n, wv_ref[...])
    lanes = lax.broadcasted_iota(jnp.int32, values.shape, 1)
    values = jnp.where(lanes >= width, 1.0, values).astype(BF16)
    head = width // HEADS
    query = (dot(own_n, wq_ref[...]) * head ** (-0.5)).astype(BF16)

    head_of = lax.broadcasted_iota(jnp.int32, (1, width), 1) // head
    tokens = LEV * in_window
    mixed, start = [], 0
    for w, count in enumerate(plan):
        rows = LEV * count
        part = query[start : start + rows]
        start += rows
        stacked = jnp.concatenate(
            [jnp.where(head_of == h, part, jnp.zeros_like(part)) for h in range(HEADS)], axis=0
        )
        scores = dot_nt(stacked, keys[w * tokens : (w + 1) * tokens])
        side = w // 3
        if side != 1:
            kept = keep_ref[w : w + 1, :] > pole_ref[side // 2].astype(F32)
            scores = jnp.where(kept, scores, -1e30)
        largest = jnp.max(scores, axis=-1, keepdims=True)
        raised = jnp.exp(scores - largest).astype(BF16)
        product = dot(raised, values[w * tokens : (w + 1) * tokens])
        product = product[:, :width] * (1.0 / product[:, width : width + 1])
        total = jnp.zeros((rows, width), F32)
        for h in range(HEADS):
            total = jnp.where(head_of == h, product[h * rows : (h + 1) * rows], total)
        mixed.append(total.astype(BF16))
    mixed = jnp.concatenate(mixed, axis=0)

    after = (own_latent + dot(mixed, wm_ref[...])).astype(BF16).astype(F32)
    normed_two = normalise(after, g2_ref[...].astype(F32)).astype(BF16)
    hidden = gelu(dot(normed_two, wu_ref[...])).astype(BF16)
    result = (after + dot_nt(hidden, wd_ref[...])).astype(BF16)
    out_ref[...] = dot(sel_ref[...], result).astype(BF16)


def constants(lat_cells, lon_cells, capacity, sources):
    windows = window_cells(lat_cells, lon_cells)
    order = [cell for own, rest in windows for cell in own + rest]
    plan = [-(-len(own) // 8) * 8 for own, _ in windows]
    code = np.array([[r * 64 + c] for r, c in order], np.float32)
    wide = lon_cells + WLON
    perm = np.zeros((len(order), len(order)), ml_dtypes.bfloat16)
    for place, (r, c) in enumerate(order):
        perm[place, r * wide + c] = 1
    keep = np.zeros((16, LEV * WLAT * WLON), np.float32)
    for w, (own, rest) in enumerate(windows):
        for k, (r, c) in enumerate(own + rest):
            inside = HLAT <= r < HLAT + lat_cells
            keep[w, [k, k + WLAT * WLON]] = 1.0 if inside else 0.0
    sel = np.zeros((lat_cells * lon_cells * LEV, LEV * sum(plan)), ml_dtypes.bfloat16)
    start = 0
    for (own, _), count in zip(windows, plan):
        for level in range(LEV):
            for k, (r, c) in enumerate(own):
                row = ((r - HLAT) * lon_cells + c - HLON) * LEV + level
                sel[row, start + level * count + k] = 1
        start += LEV * count
    per_source = (len(AROUND) + 1) * capacity
    stride = GROUP * per_source
    find = np.zeros((stride, stride), ml_dtypes.bfloat16)
    pick = np.zeros((stride, 128), ml_dtypes.bfloat16)
    for row in range(stride):
        source, tile, slot = row // per_source, row % per_source // capacity, row % capacity
        find[row, source * per_source + len(AROUND) * capacity + slot] = 1
        if tile < len(AROUND):
            pick[row, tile * FIELDS : (tile + 1) * FIELDS] = 1
    place = np.full((1, sources * per_source), 1e6, np.float32)
    for row in range(place.shape[1]):
        tile = row % per_source // capacity
        if tile < len(AROUND):
            dy, dx = AROUND[tile]
            place[0, row] = (dy * lat_cells + HLAT) * 64 + dx * lon_cells + HLON
    coef = np.zeros((8 + 128, 128), ml_dtypes.bfloat16)
    coef[0, 0::FIELDS] = 64
    coef[0, 1::FIELDS] = 1
    coef[8 + 2 :: FIELDS, :] = 1
    return plan, code, perm, keep, sel, find, pick, coef, place


def packed(record_values, record_cell, record_instrument, block_counts, lon_cells):
    capacity = record_values.shape[2]
    is_live = jnp.arange(capacity, dtype=jnp.int32)[None, None, :] < block_counts[:, :, None]
    row = jnp.where(is_live, record_cell // lon_cells, 255)[..., None]
    col = (record_cell % lon_cells)[..., None]
    lane = jnp.arange(128, dtype=jnp.int32)
    field = lane % FIELDS
    tags = jnp.where(
        field == 0, row, jnp.where(field == 1, col, record_instrument[..., None])
    ).astype(BF16)
    pieces, meta = [], jnp.zeros(record_values.shape, BF16)
    for n, (dy, dx) in enumerate(AROUND):
        pieces.append(jnp.roll(record_values, (-dx, -dy), (0, 1)))
        meta = jnp.where(lane // FIELDS == n, jnp.roll(tags, (-dx, -dy), (0, 1)), meta)
    stacked = jnp.stack(pieces + [meta], axis=2)
    return stacked.reshape((-1,) + stacked.shape[2:])


def local(
    record_values,
    record_cell,
    record_instrument,
    block_counts,
    background,
    input_weight,
    instrument_table,
    lift_weight,
    first_gain,
    attn_weight,
    mix_weight,
    second_gain,
    up_weight,
    down_weight,
):
    lat_cells, lon_cells, _, width = background.shape
    capacity = record_values.shape[2]
    sources = record_values.shape[0] * record_values.shape[1]
    chunk = min(CHUNK, sources)
    plan, code, perm, keep, sel, find, pick, coef, place = constants(
        lat_cells, lon_cells, capacity, chunk
    )

    west = shifted(background[:, lon_cells - HLON :], "lon", 1)
    east = shifted(background[:, :HLON], "lon", -1)
    bordered = jnp.concatenate([west, background, east], axis=1)
    north = shifted(bordered[lat_cells - HLAT :], "lat", 1)
    south = shifted(bordered[:HLAT], "lat", -1)
    bordered = jnp.concatenate([north, bordered, south], axis=0)
    bordered = jnp.pad(bordered, ((0, 0), (0, 0), (0, 0), (0, PAD - width)))
    prior = dot(jnp.asarray(perm), bordered.reshape(len(code), LEV * PAD)).astype(BF16)

    sent = packed(record_values, record_cell, record_instrument, block_counts, lon_cells)
    received = lax.all_to_all(sent, ("lon", "lat"), split_axis=0, concat_axis=0, tiled=True)
    received = received.reshape(-1, received.shape[-1])

    lift = jnp.pad(
        lift_weight.reshape(width, LEV, width), ((0, 0), (0, 0), (0, PAD - width))
    ).reshape(width, LEV * PAD)
    values_weight = jnp.pad(attn_weight[:, 2 * width :], ((0, 0), (0, PAD - width)))
    where = lax.axis_index("lat")
    last = lax.axis_size("lat") - 1
    pole = jnp.stack([where == 0, where == last]).astype(jnp.int32)
    pole = pole - 1

    cells = len(code)
    rows = chunk * (len(AROUND) + 1) * capacity
    vmem = pl.BlockSpec(memory_space=pltpu.VMEM)
    out = pl.pallas_call(
        functools.partial(block_kernel, plan),
        out_shape=jax.ShapeDtypeStruct((lat_cells * lon_cells * LEV, width), BF16),
        in_specs=[pl.BlockSpec(memory_space=pltpu.SMEM)] + [vmem] * 20,
        out_specs=vmem,
        scratch_shapes=[
            pltpu.VMEM((rows, LEV * PAD), BF16),
            pltpu.VMEM((cells, rows), BF16),
            pltpu.VMEM((cells, LEV * PAD), F32),
        ],
        compiler_params=pltpu.CompilerParams(vmem_limit_bytes=40 * 2**20),
        cost_estimate=pl.CostEstimate(
            flops=4 * 10**9, bytes_accessed=6 * 10**6, transcendentals=2 * 10**6
        ),
    )(
        pole,
        received,
        prior,
        jnp.asarray(find),
        jnp.asarray(pick),
        jnp.asarray(coef),
        jnp.asarray(place),
        jnp.asarray(code),
        jnp.asarray(keep),
        jnp.asarray(sel),
        input_weight.T,
        instrument_table,
        lift,
        first_gain.reshape(1, width),
        attn_weight[:, :width],
        attn_weight[:, width : 2 * width],
        values_weight,
        mix_weight,
        second_gain.reshape(1, width),
        up_weight,
        down_weight.T,
    )
    return out.reshape(lat_cells, lon_cells, LEV, width)


def solution(mesh):
    placed = (
        P("lon", "lat", None, None),
        P("lon", "lat", None),
        P("lon", "lat", None),
        P("lon", "lat"),
        P("lat", "lon", None, None),
        P(),
        P(),
        P(),
        P(),
        P(),
        P(),
        P(),
        P(),
        P(),
    )
    return jax.shard_map(
        local, mesh=mesh, in_specs=placed, out_specs=P("lat", "lon", None, None), check_vma=False
    )
```

```python
import functools

import jax
import jax.numpy as jnp
import ml_dtypes
import numpy as np
from jax import lax
from jax.experimental import pallas as pl
from jax.experimental.pallas import tpu as pltpu
from jax.sharding import PartitionSpec as P

HEADS = 6
INSTR = 8
LEV = 2
WLAT = 6
WLON = 12
HLAT = WLAT // 2
HLON = WLON // 2
PAD = 256
FIELDS = 4
GROUP = 8
CHUNK = 32
BF16 = jnp.bfloat16
F32 = jnp.float32

AROUND = [(dy, dx) for dy in (-1, 0, 1) for dx in (-1, 0, 1)]


def shifted(value, axis, steps):
    count = lax.axis_size(axis)
    pairs = [(source, (source + steps) % count) for source in range(count)]
    return lax.ppermute(value, axis, pairs)


def window_cells(lat_cells, lon_cells):
    high, wide = lat_cells + WLAT, lon_cells + WLON
    windows = []
    for top in range(0, high, WLAT):
        for left in range(0, wide, WLON):
            cells = [(r, c) for r in range(top, top + WLAT) for c in range(left, left + WLON)]
            own = [
                (r, c)
                for r, c in cells
                if HLAT <= r < HLAT + lat_cells and HLON <= c < HLON + lon_cells
            ]
            rest = [cell for cell in cells if cell not in own]
            windows.append((own, rest))
    return windows


def gelu(x):
    return jax.nn.gelu(x)


def normalise(wide, gain):
    average = jnp.mean(wide, axis=-1, keepdims=True)
    centred = wide - average
    spread = jnp.mean(centred * centred, axis=-1, keepdims=True)
    return centred * lax.rsqrt(spread + 1e-05) * gain


def dot(a, b):
    return jnp.dot(a, b, preferred_element_type=F32)


def dot_nt(a, b):
    return lax.dot_general(a, b, (((1,), (1,)), ((), ())), preferred_element_type=F32)


def block_kernel(
    plan,
    pole_ref,
    recv_ref,
    own_ref,
    north_ref,
    south_ref,
    west_ref,
    east_ref,
    perm_ref,
    find_ref,
    pick_ref,
    coef_ref,
    place_ref,
    code_ref,
    keep_ref,
    sel_ref,
    win_ref,
    tab_ref,
    lift_ref,
    g1_ref,
    wq_ref,
    wk_ref,
    wv_ref,
    wm_ref,
    g2_ref,
    wu_ref,
    wd_ref,
    out_ref,
    lifted_ref,
    hot_ref,
    prior_ref,
    sum_ref,
):
    width = win_ref.shape[0]
    stride = find_ref.shape[0]
    per_chunk = lifted_ref.shape[0]
    chunks = recv_ref.shape[0] // per_chunk
    in_window = WLAT * WLON

    start = 0
    for strip in (own_ref, north_ref, south_ref, west_ref, east_ref):
        count = strip.shape[0]
        held = -(-count // 16) * 16
        value = strip[...].astype(F32)
        if held > count:
            value = jnp.concatenate([value, jnp.zeros((held - count, value.shape[1]), F32)], axis=0)
        prior_ref[start : start + held, :] = value.astype(BF16)
        start += held
    prior = dot(perm_ref[...], prior_ref[...])

    def scatter(base):
        for group in range(per_chunk // stride):
            at = group * stride
            recs = recv_ref[pl.ds(base + at, stride), :]
            meta = (dot(find_ref[...], recs) * pick_ref[...].astype(F32)).astype(BF16)
            lane = lax.broadcasted_iota(jnp.int32, (stride, 128), 1).astype(F32)
            tag = dot(meta, coef_ref[8:, :])
            chooser = jnp.where(tag == lane, 1.0, 0.0).astype(BF16)
            before = dot_nt(recs, win_ref[...]) + dot(chooser[:, :INSTR], tab_ref[...])
            encoded = gelu(before).astype(BF16)
            lifted = gelu(dot(encoded, lift_ref[...]))
            lanes = lax.broadcasted_iota(jnp.int32, lifted.shape, 1) % PAD
            lifted_ref[at : at + stride, :] = jnp.where(lanes >= width, 1.0, lifted).astype(BF16)
            code = dot_nt(coef_ref[:8, :], meta)[:1, :] + place_ref[:, at : at + stride]
            hot_ref[:, at : at + stride] = jnp.where(code_ref[...] == code, 1.0, 0.0).astype(BF16)
        return dot(hot_ref[...], lifted_ref[...])

    if chunks == 1:
        sum_ref[...] = prior + scatter(0)
    else:
        sum_ref[...] = prior

        @pl.loop(0, chunks)
        def _(step):
            sum_ref[...] += scatter(pl.multiple_of(step * per_chunk, per_chunk))

    gain_one = g1_ref[...].astype(F32)
    latents, normeds = [], []
    for level in range(LEV):
        piece = sum_ref[:, level * PAD : (level + 1) * PAD]
        share = 1.0 / (1.0 + piece[:, width : width + 1])
        latent = (piece[:, :width] * share).astype(BF16).astype(F32)
        latents.append(latent)
        normeds.append(normalise(latent, gain_one))

    def gathered(tensors, counts):
        return jnp.concatenate(
            [t[w * in_window : w * in_window + n] for w, n in enumerate(counts) for t in tensors],
            axis=0,
        )

    all_n = gathered(normeds, [in_window] * len(plan)).astype(BF16)
    own_n = gathered(normeds, plan).astype(BF16)
    own_latent = gathered(latents, plan)
    keys = dot(all_n, wk_ref[...]).astype(BF16)
    values = dot(all_n, wv_ref[...])
    lanes = lax.broadcasted_iota(jnp.int32, values.shape, 1)
    values = jnp.where(lanes >= width, 1.0, values).astype(BF16)
    head = width // HEADS
    query = (dot(own_n, wq_ref[...]) * head ** (-0.5)).astype(BF16)

    head_of = lax.broadcasted_iota(jnp.int32, (1, width), 1) // head
    tokens = LEV * in_window
    mixed, start = [], 0
    for w, count in enumerate(plan):
        rows = LEV * count
        part = query[start : start + rows]
        start += rows
        stacked = jnp.concatenate(
            [jnp.where(head_of == h, part, jnp.zeros_like(part)) for h in range(HEADS)], axis=0
        )
        scores = dot_nt(stacked, keys[w * tokens : (w + 1) * tokens])
        side = w // 3
        if side != 1:
            kept = keep_ref[w : w + 1, :] > pole_ref[side // 2].astype(F32)
            scores = jnp.where(kept, scores, -1e30)
        largest = jnp.max(scores, axis=-1, keepdims=True)
        raised = jnp.exp(scores - largest).astype(BF16)
        product = dot(raised, values[w * tokens : (w + 1) * tokens])
        product = product[:, :width] * (1.0 / product[:, width : width + 1])
        total = jnp.zeros((rows, width), F32)
        for h in range(HEADS):
            total = jnp.where(head_of == h, product[h * rows : (h + 1) * rows], total)
        mixed.append(total.astype(BF16))
    mixed = jnp.concatenate(mixed, axis=0)

    after = (own_latent + dot(mixed, wm_ref[...])).astype(BF16).astype(F32)
    normed_two = normalise(after, g2_ref[...].astype(F32)).astype(BF16)
    hidden = gelu(dot(normed_two, wu_ref[...])).astype(BF16)
    result = (after + dot_nt(hidden, wd_ref[...])).astype(BF16)
    out_ref[...] = dot(sel_ref[...], result).astype(BF16)


def constants(lat_cells, lon_cells, capacity, sources):
    windows = window_cells(lat_cells, lon_cells)
    order = [cell for own, rest in windows for cell in own + rest]
    plan = [-(-len(own) // 8) * 8 for own, _ in windows]
    code = np.array([[r * 64 + c] for r, c in order], np.float32)
    up16 = lambda count: -(-count // 16) * 16
    high = lat_cells + WLAT
    strips = [lat_cells * lon_cells, HLAT * lon_cells, HLAT * lon_cells, high * HLON, high * HLON]
    begins = np.cumsum([0] + [up16(count) for count in strips])
    perm = np.zeros((len(order), begins[-1]), ml_dtypes.bfloat16)
    for place, (r, c) in enumerate(order):
        row, col = r - HLAT, c - HLON
        if col < 0:
            at = begins[3] + r * HLON + c
        elif col >= lon_cells:
            at = begins[4] + r * HLON + col - lon_cells
        elif row < 0:
            at = begins[1] + r * lon_cells + col
        elif row >= lat_cells:
            at = begins[2] + (row - lat_cells) * lon_cells + col
        else:
            at = begins[0] + row * lon_cells + col
        perm[place, at] = 1
    keep = np.zeros((16, LEV * WLAT * WLON), np.float32)
    for w, (own, rest) in enumerate(windows):
        for k, (r, c) in enumerate(own + rest):
            inside = HLAT <= r < HLAT + lat_cells
            keep[w, [k, k + WLAT * WLON]] = 1.0 if inside else 0.0
    sel = np.zeros((lat_cells * lon_cells * LEV, LEV * sum(plan)), ml_dtypes.bfloat16)
    start = 0
    for (own, _), count in zip(windows, plan):
        for level in range(LEV):
            for k, (r, c) in enumerate(own):
                row = ((r - HLAT) * lon_cells + c - HLON) * LEV + level
                sel[row, start + level * count + k] = 1
        start += LEV * count
    per_source = (len(AROUND) + 1) * capacity
    stride = GROUP * per_source
    find = np.zeros((stride, stride), ml_dtypes.bfloat16)
    pick = np.zeros((stride, 128), ml_dtypes.bfloat16)
    for row in range(stride):
        source, tile, slot = row // per_source, row % per_source // capacity, row % capacity
        find[row, source * per_source + len(AROUND) * capacity + slot] = 1
        if tile < len(AROUND):
            pick[row, tile * FIELDS : (tile + 1) * FIELDS] = 1
    place = np.full((1, sources * per_source), 1e6, np.float32)
    for row in range(place.shape[1]):
        tile = row % per_source // capacity
        if tile < len(AROUND):
            dy, dx = AROUND[tile]
            place[0, row] = (dy * lat_cells + HLAT) * 64 + dx * lon_cells + HLON
    coef = np.zeros((8 + 128, 128), ml_dtypes.bfloat16)
    coef[0, 0::FIELDS] = 64
    coef[0, 1::FIELDS] = 1
    coef[8 + 2 :: FIELDS, :] = 1
    return plan, code, perm, keep, sel, find, pick, coef, place


def pack_kernel(values_ref, cell_ref, tag_ref, count_ref, spread_ref, out_ref, *, lon_cells):
    tiles_lon, tiles_lat, capacity, _ = values_ref.shape
    for n, (dy, dx) in enumerate(AROUND):
        lat_parts = [(0, tiles_lat)] if dy == 0 else [(0, tiles_lat - 1), (tiles_lat - 1, tiles_lat)]
        if dy < 0:
            lat_parts = [(0, 1), (1, tiles_lat)]

        def copy_tiles(lon, n=n, dx=dx, dy=dy, lat_parts=lat_parts):
            source = lax.rem(lon + dx + tiles_lon, tiles_lon)
            for low, end in lat_parts:
                first = (low + dy) % tiles_lat
                out_ref[lon, low:end, n] = values_ref[source, first : first + end - low]

        if tiles_lon <= 8:
            for lon in range(tiles_lon):
                copy_tiles(lon)
        else:
            pl.loop(0, tiles_lon)(copy_tiles)

    cell = cell_ref[...]
    counts = count_ref[...]
    counts = jnp.concatenate(
        [counts[tile : tile + 1] for tile in range(tiles_lat) for _ in range(capacity)], axis=0
    )
    slot = lax.broadcasted_iota(jnp.int32, cell.shape, 0) % capacity
    row = cell // lon_cells
    fields = [jnp.where(slot < counts, row, 255), cell - row * lon_cells, tag_ref[...]]
    fields = [field.astype(F32) for field in fields]
    block = 8
    for begin in range(0, tiles_lon, block):
        parts = []
        for field in fields:
            around = jnp.concatenate([field[:, -1:], field, field[:, :1]], axis=1)
            around = around[:, begin : begin + block + 2]
            for dy in (-1, 0, 1):
                by = dy * capacity % field.shape[0]
                parts.append(
                    jnp.concatenate([around[by:], around[:by]], axis=0) if by else around
                )
        meta = dot(jnp.concatenate(parts, axis=1).astype(BF16), spread_ref[...])
        for lon in range(block):
            piece = meta[:, lon * 128 : (lon + 1) * 128].astype(BF16)
            for lat in range(tiles_lat):
                out_ref[begin + lon, lat, len(AROUND)] = piece[lat * capacity : (lat + 1) * capacity]


def packed(record_values, record_cell, record_instrument, block_counts, lon_cells):
    tiles_lon, tiles_lat, capacity, wide = record_values.shape
    block = 8
    spread = np.zeros((9 * (block + 2), block * 128), ml_dtypes.bfloat16)
    for lon in range(block):
        for n, (dy, dx) in enumerate(AROUND):
            for field in range(3):
                spread[(field * 3 + dy + 1) * (block + 2) + lon + 1 + dx, lon * 128 + n * FIELDS + field] = 1
    vmem = pl.BlockSpec(memory_space=pltpu.VMEM)
    shape = (tiles_lon, tiles_lat, len(AROUND) + 1, capacity, wide)
    out = pl.pallas_call(
        functools.partial(pack_kernel, lon_cells=lon_cells),
        out_shape=jax.ShapeDtypeStruct(shape, BF16),
        in_specs=[vmem] * 5,
        out_specs=vmem,
        compiler_params=pltpu.CompilerParams(vmem_limit_bytes=32 * 2**20),
    )(
        record_values,
        record_cell.transpose(1, 2, 0).reshape(-1, tiles_lon),
        record_instrument.transpose(1, 2, 0).reshape(-1, tiles_lon),
        block_counts.T,
        jnp.asarray(spread),
    )
    return out.reshape((-1,) + shape[2:])


def local(
    record_values,
    record_cell,
    record_instrument,
    block_counts,
    background,
    input_weight,
    instrument_table,
    lift_weight,
    first_gain,
    attn_weight,
    mix_weight,
    second_gain,
    up_weight,
    down_weight,
):
    lat_cells, lon_cells, _, width = background.shape
    capacity = record_values.shape[2]
    sources = record_values.shape[0] * record_values.shape[1]
    chunk = min(CHUNK, sources)
    plan, code, perm, keep, sel, find, pick, coef, place = constants(
        lat_cells, lon_cells, capacity, chunk
    )

    laid = jnp.pad(background, ((0, 0), (0, 0), (0, 0), (0, PAD - width)))
    laid = lax.optimization_barrier(laid.reshape(lat_cells, lon_cells, LEV * PAD))
    north = shifted(laid[lat_cells - HLAT :], "lat", 1)
    south = shifted(laid[:HLAT], "lat", -1)

    def columns(low, end):
        return jnp.concatenate([north[:, low:end], laid[:, low:end], south[:, low:end]], axis=0)

    west = shifted(columns(lon_cells - HLON, lon_cells), "lon", 1)
    east = shifted(columns(0, HLON), "lon", -1)
    strips = [strip.reshape(-1, LEV * PAD) for strip in (laid, north, south, west, east)]

    sent = packed(record_values, record_cell, record_instrument, block_counts, lon_cells)
    received = lax.all_to_all(sent, ("lon", "lat"), split_axis=0, concat_axis=0, tiled=True)
    received = received.reshape(-1, received.shape[-1])

    lift = jnp.pad(
        lift_weight.reshape(width, LEV, width), ((0, 0), (0, 0), (0, PAD - width))
    ).reshape(width, LEV * PAD)
    values_weight = jnp.pad(attn_weight[:, 2 * width :], ((0, 0), (0, PAD - width)))
    where = lax.axis_index("lat")
    last = lax.axis_size("lat") - 1
    pole = jnp.stack([where == 0, where == last]).astype(jnp.int32)
    pole = pole - 1

    cells = len(code)
    rows = chunk * (len(AROUND) + 1) * capacity
    vmem = pl.BlockSpec(memory_space=pltpu.VMEM)
    out = pl.pallas_call(
        functools.partial(block_kernel, plan),
        out_shape=jax.ShapeDtypeStruct((lat_cells * lon_cells * LEV, width), BF16),
        in_specs=[pl.BlockSpec(memory_space=pltpu.SMEM)] + [vmem] * 25,
        out_specs=vmem,
        scratch_shapes=[
            pltpu.VMEM((rows, LEV * PAD), BF16),
            pltpu.VMEM((cells, rows), BF16),
            pltpu.VMEM((perm.shape[1], LEV * PAD), BF16),
            pltpu.VMEM((cells, LEV * PAD), F32),
        ],
        compiler_params=pltpu.CompilerParams(vmem_limit_bytes=40 * 2**20),
        cost_estimate=pl.CostEstimate(
            flops=4 * 10**9, bytes_accessed=6 * 10**6, transcendentals=2 * 10**6
        ),
    )(
        pole,
        received,
        *strips,
        jnp.asarray(perm),
        jnp.asarray(find),
        jnp.asarray(pick),
        jnp.asarray(coef),
        jnp.asarray(place),
        jnp.asarray(code),
        jnp.asarray(keep),
        jnp.asarray(sel),
        input_weight.T,
        instrument_table,
        lift,
        first_gain.reshape(1, width),
        attn_weight[:, :width],
        attn_weight[:, width : 2 * width],
        values_weight,
        mix_weight,
        second_gain.reshape(1, width),
        up_weight,
        down_weight.T,
    )
    return out.reshape(lat_cells, lon_cells, LEV, width)


def solution(mesh):
    placed = (
        P("lon", "lat", None, None),
        P("lon", "lat", None),
        P("lon", "lat", None),
        P("lon", "lat"),
        P("lat", "lon", None, None),
        P(),
        P(),
        P(),
        P(),
        P(),
        P(),
        P(),
        P(),
        P(),
    )
    return jax.shard_map(
        local, mesh=mesh, in_specs=placed, out_specs=P("lat", "lon", None, None), check_vma=False
    )
```

```python
import functools

import jax
import jax.numpy as jnp
import ml_dtypes
import numpy as np
from jax import lax
from jax.experimental import pallas as pl
from jax.experimental.pallas import tpu as pltpu
from jax.sharding import PartitionSpec as P

HEADS = 6
INSTR = 8
LEV = 2
WLAT = 6
WLON = 12
HLAT = WLAT // 2
HLON = WLON // 2
PAD = 256
FIELDS = 4
GROUP = 8
CHUNK = 32
LIMIT = 56 * 2**20
FEW = 32
BF16 = jnp.bfloat16
F32 = jnp.float32

AROUND = [(dy, dx) for dy in (-1, 0, 1) for dx in (-1, 0, 1)]


def shifted(value, axis, steps, wraps=True):
    count = lax.axis_size(axis)
    pairs = [(source, (source + steps) % count) for source in range(count)]
    if not wraps:
        pairs = [pair for pair in pairs if pair[1] == pair[0] + steps]
    return lax.ppermute(value, axis, pairs)


def window_cells(lat_cells, lon_cells):
    high, wide = lat_cells + WLAT, lon_cells + WLON
    windows = []
    for top in range(0, high, WLAT):
        for left in range(0, wide, WLON):
            cells = [(r, c) for r in range(top, top + WLAT) for c in range(left, left + WLON)]
            own = [
                (r, c)
                for r, c in cells
                if HLAT <= r < HLAT + lat_cells and HLON <= c < HLON + lon_cells
            ]
            rest = [cell for cell in cells if cell not in own]
            windows.append((own, rest))
    return windows


def gelu(x):
    return jax.nn.gelu(x)


def normalise(wide, gain):
    average = jnp.mean(wide, axis=-1, keepdims=True)
    centred = wide - average
    spread = jnp.mean(centred * centred, axis=-1, keepdims=True)
    return centred * lax.rsqrt(spread + 1e-05) * gain


def dot(a, b):
    return jnp.dot(a, b, preferred_element_type=F32)


def dot_nt(a, b):
    return lax.dot_general(a, b, (((1,), (1,)), ((), ())), preferred_element_type=F32)


def put_ones(lifted, width):
    lanes = lax.broadcasted_iota(jnp.int32, lifted.shape, 1) % PAD
    return jnp.where(lanes >= width, 1.0, lifted).astype(BF16)


def sums_gathered(scalars_ref, all_ref, take, work):
    tiles_ref, meta_ref, hot_ref, lifted_ref, sem = work
    sources, tiles = all_ref.shape[0], all_ref.shape[1] - 1
    per_tile = sources * all_ref.shape[2]
    copies = [pltpu.make_async_copy(all_ref.at[:, tiles], meta_ref, sem.at[0])]
    for n in range(len(AROUND)):
        source = all_ref.at[:, scalars_ref[2 + n]]
        copies.append(pltpu.make_async_copy(source, tiles_ref.at[n], sem.at[1 + n]))
    for copy in copies:
        copy.start()

    def finish(place):
        copies[0].wait()
        meta = meta_ref.reshape(per_tile, 128)[...]
        lane = lax.broadcasted_iota(jnp.int32, (16, 128), 1)
        sub = lax.broadcasted_iota(jnp.int32, (16, 128), 0)
        wanted = jnp.zeros((16, 128), F32)
        lane_two = lax.broadcasted_iota(jnp.int32, (128, 128), 1)
        sub_two = lax.broadcasted_iota(jnp.int32, (128, 128), 0)
        tag_at = jnp.full((128, 128), -1, jnp.int32)
        for n in range(len(AROUND)):
            at = scalars_ref[2 + len(AROUND) + n]
            wanted = jnp.where((sub == n) & (lane == at), 64.0, wanted)
            wanted = jnp.where((sub == n) & (lane == tiles + at), 1.0, wanted)
            tag_at = jnp.where(lane_two // INSTR == n, 2 * tiles + at, tag_at)
        codes = dot_nt(wanted.astype(BF16), meta)
        code_row = jnp.concatenate([codes[n : n + 1] + place[n] for n in range(len(AROUND))], axis=1)
        tag = dot(meta, jnp.where(tag_at == sub_two, 1.0, 0.0).astype(BF16))
        lane = lax.broadcasted_iota(jnp.int32, tag.shape, 1)
        chosen = jnp.where(tag == (lane % INSTR).astype(F32), 1.0, 0.0)
        hot_ref[...] = jnp.where(take("code")[...] == code_row, 1.0, 0.0).astype(BF16)
        weight, lift = take("first")[...], take("lift")[...]
        width = weight.shape[1]
        for group in range(0, len(AROUND), 3):
            rows = []
            for n in range(group, group + 3):
                copies[1 + n].wait()
                records = tiles_ref.at[n].reshape(per_tile, 128)[...]
                own = jnp.where(lane // INSTR == n, chosen, 0.0).astype(BF16)
                rows.append(jnp.concatenate([records, own], axis=1))
            encoded = gelu(dot(jnp.concatenate(rows, axis=0), weight)).astype(BF16)
            lifted = put_ones(gelu(dot(encoded, lift)), width)
            lifted_ref[group * per_tile : (group + 3) * per_tile, :] = lifted
        return dot(hot_ref[...], lifted_ref[...])

    return finish


def sums_exchanged(recv_ref, take, work):
    hot_ref, lifted_ref, total_ref = work
    per_chunk = lifted_ref.shape[0]
    chunks = recv_ref.shape[0] // per_chunk

    def finish(_):
        find, pick, coef = take("find")[...], take("pick")[...], take("coef")
        win, tab, lift, place = take("win")[...], take("tab")[...], take("lift")[...], take("place")
        code_column = take("code")[...]
        stride = find.shape[0]

        def scatter(base):
            for at in range(0, per_chunk, stride):
                recs = recv_ref[pl.ds(base + at, stride), :]
                meta = (dot(find, recs) * pick.astype(F32)).astype(BF16)
                lane = lax.broadcasted_iota(jnp.int32, (stride, 128), 1).astype(F32)
                tag = dot(meta, coef[8:, :])
                chooser = jnp.where(tag == lane, 1.0, 0.0).astype(BF16)
                before = dot_nt(recs, win) + dot(chooser[:, :INSTR], tab)
                encoded = gelu(before).astype(BF16)
                lifted_ref[at : at + stride, :] = put_ones(gelu(dot(encoded, lift)), win.shape[0])
                code = dot_nt(coef[:8, :], meta)[:1, :] + place[:, at : at + stride]
                hot_ref[:, at : at + stride] = jnp.where(code_column == code, 1.0, 0.0).astype(BF16)
            return dot(hot_ref[...], lifted_ref[...])

        total_ref[...] = scatter(0)

        @pl.loop(1, chunks)
        def _(step):
            total_ref[...] += scatter(pl.multiple_of(step * per_chunk, per_chunk))

        return total_ref[...]

    return finish


def block_kernel(plan, names, gathers, place, *refs):
    refs = list(refs)
    scalars_ref, records_ref, *strips = refs[:7]
    kept = dict(zip(names, refs[7 : 7 + len(names)]))
    out_ref, prior_ref, load_sem = refs[7 + len(names) : 10 + len(names)]
    held = dict(zip(names, refs[10 + len(names) : 10 + 2 * len(names)]))
    work = refs[10 + 2 * len(names) :]
    loads = {
        name: pltpu.make_async_copy(kept[name], held[name], load_sem.at[n])
        for n, name in enumerate(names)
    }
    waiting = set(names)

    def take(name):
        if name in waiting:
            loads[name].wait()
            waiting.remove(name)
        return held[name]

    if gathers:
        finish = sums_gathered(scalars_ref, records_ref, take, work)
    else:
        finish = sums_exchanged(records_ref, take, work)
    for name in names:
        loads[name].start()

    in_window = WLAT * WLON
    start = 0
    for strip in strips:
        count = strip.shape[0]
        full = -(-count // 16) * 16
        value = strip[...].astype(F32)
        if full > count:
            value = jnp.concatenate([value, jnp.zeros((full - count, value.shape[1]), F32)], axis=0)
        prior_ref[start : start + full, :] = value.astype(BF16)
        start += full
    sums = finish(place)
    prior = dot(take("perm")[...], prior_ref[...])

    width = held["wm"].shape[0]
    gains = take("gains")[...]
    latents, normeds = [], []
    for level in range(LEV):
        piece = sums[:, level * PAD : (level + 1) * PAD]
        share = 1.0 / (1.0 + piece[:, width : width + 1])
        latent = (prior[:, level * PAD : (level + 1) * PAD] + piece)[:, :width] * share
        latent = latent.astype(BF16).astype(F32)
        latents.append(latent)
        normeds.append(normalise(latent, gains[:1]))

    def gathered(tensors, counts):
        return jnp.concatenate(
            [t[w * in_window : w * in_window + n] for w, n in enumerate(counts) for t in tensors],
            axis=0,
        )

    all_n = gathered(normeds, [in_window] * len(plan)).astype(BF16)
    own_n = gathered(normeds, plan).astype(BF16)
    own_latent = gathered(latents, plan)
    keys = dot(all_n, take("wk")[...]).astype(BF16)
    values = put_ones(dot(all_n, take("wv")[...]), width)
    head = width // HEADS
    query = (dot(own_n, take("wq")[...]) * head ** (-0.5)).astype(BF16)

    head_of = lax.broadcasted_iota(jnp.int32, (1, width), 1) // head
    tokens = LEV * in_window
    keep = take("keep")[...]
    mixed, start = [], 0
    for w, count in enumerate(plan):
        rows = LEV * count
        part = query[start : start + rows]
        start += rows
        stacked = jnp.concatenate(
            [jnp.where(head_of == h, part, jnp.zeros_like(part)) for h in range(HEADS)], axis=0
        )
        scores = dot_nt(stacked, keys[w * tokens : (w + 1) * tokens])
        side = w // 3
        if side != 1:
            allowed = keep[w : w + 1, :] > scalars_ref[side // 2].astype(F32)
            scores = jnp.where(allowed, scores, -1e30)
        largest = jnp.max(scores, axis=-1, keepdims=True)
        raised = jnp.exp(scores - largest).astype(BF16)
        product = dot(raised, values[w * tokens : (w + 1) * tokens])
        product = product[:, :width] * (1.0 / product[:, width : width + 1])
        total = jnp.zeros((rows, width), F32)
        for h in range(HEADS):
            total = jnp.where(head_of == h, product[h * rows : (h + 1) * rows], total)
        mixed.append(total.astype(BF16))
    mixed = jnp.concatenate(mixed, axis=0)

    after = (own_latent + dot(mixed, take("wm")[...])).astype(BF16).astype(F32)
    normed_two = normalise(after, gains[1:2]).astype(BF16)
    hidden = gelu(dot(normed_two, take("wu")[...])).astype(BF16)
    result = (after + dot_nt(hidden, take("wd")[...])).astype(BF16)
    out_ref[...] = dot(take("sel")[...], result).astype(BF16)


def constants(lat_cells, lon_cells, capacity, sources):
    windows = window_cells(lat_cells, lon_cells)
    order = [cell for own, rest in windows for cell in own + rest]
    plan = [-(-len(own) // 8) * 8 for own, _ in windows]
    code = np.array([[r * 64 + c] for r, c in order], np.float32)
    up16 = lambda count: -(-count // 16) * 16
    high = lat_cells + WLAT
    strips = [lat_cells * lon_cells, HLAT * lon_cells, HLAT * lon_cells, high * HLON, high * HLON]
    begins = np.cumsum([0] + [up16(count) for count in strips])
    perm = np.zeros((len(order), begins[-1]), ml_dtypes.bfloat16)
    for place, (r, c) in enumerate(order):
        row, col = r - HLAT, c - HLON
        if col < 0:
            at = begins[3] + r * HLON + c
        elif col >= lon_cells:
            at = begins[4] + r * HLON + col - lon_cells
        elif row < 0:
            at = begins[1] + r * lon_cells + col
        elif row >= lat_cells:
            at = begins[2] + (row - lat_cells) * lon_cells + col
        else:
            at = begins[0] + row * lon_cells + col
        perm[place, at] = 1
    keep = np.zeros((16, LEV * WLAT * WLON), np.float32)
    for w, (own, rest) in enumerate(windows):
        for k, (r, c) in enumerate(own + rest):
            inside = HLAT <= r < HLAT + lat_cells
            keep[w, [k, k + WLAT * WLON]] = 1.0 if inside else 0.0
    sel = np.zeros((lat_cells * lon_cells * LEV, LEV * sum(plan)), ml_dtypes.bfloat16)
    start = 0
    for (own, _), count in zip(windows, plan):
        for level in range(LEV):
            for k, (r, c) in enumerate(own):
                row = ((r - HLAT) * lon_cells + c - HLON) * LEV + level
                sel[row, start + level * count + k] = 1
        start += LEV * count
    per_source = (len(AROUND) + 1) * capacity
    stride = GROUP * per_source
    find = np.zeros((stride, stride), ml_dtypes.bfloat16)
    pick = np.zeros((stride, 128), ml_dtypes.bfloat16)
    for row in range(stride):
        source, tile, slot = row // per_source, row % per_source // capacity, row % capacity
        find[row, source * per_source + len(AROUND) * capacity + slot] = 1
        if tile < len(AROUND):
            pick[row, tile * FIELDS : (tile + 1) * FIELDS] = 1
    place = np.full((1, sources * per_source), 1e6, np.float32)
    for row in range(place.shape[1]):
        tile = row % per_source // capacity
        if tile < len(AROUND):
            dy, dx = AROUND[tile]
            place[0, row] = (dy * lat_cells + HLAT) * 64 + dx * lon_cells + HLON
    coef = np.zeros((8 + 128, 128), ml_dtypes.bfloat16)
    coef[0, 0::FIELDS] = 64
    coef[0, 1::FIELDS] = 1
    coef[8 + 2 :: FIELDS, :] = 1
    return plan, code, perm, keep, sel, find, pick, coef, place


def pack_kernel(values_ref, cell_ref, tag_ref, count_ref, spread_ref, out_ref, *, lon_cells):
    tiles_lon, tiles_lat, capacity, _ = values_ref.shape
    for n, (dy, dx) in enumerate(AROUND):
        lat_parts = [(0, tiles_lat)] if dy == 0 else [(0, tiles_lat - 1), (tiles_lat - 1, tiles_lat)]
        if dy < 0:
            lat_parts = [(0, 1), (1, tiles_lat)]

        def copy_tiles(lon, n=n, dx=dx, dy=dy, lat_parts=lat_parts):
            source = lax.rem(lon + dx + tiles_lon, tiles_lon)
            for low, end in lat_parts:
                first = (low + dy) % tiles_lat
                out_ref[lon, low:end, n] = values_ref[source, first : first + end - low]

        if tiles_lon <= 8:
            for lon in range(tiles_lon):
                copy_tiles(lon)
        else:
            pl.loop(0, tiles_lon)(copy_tiles)

    cell = cell_ref[...]
    counts = count_ref[...]
    counts = jnp.concatenate(
        [counts[tile : tile + 1] for tile in range(tiles_lat) for _ in range(capacity)], axis=0
    )
    slot = lax.broadcasted_iota(jnp.int32, cell.shape, 0) % capacity
    row = cell // lon_cells
    fields = [jnp.where(slot < counts, row, 255), cell - row * lon_cells, tag_ref[...]]
    fields = [field.astype(F32) for field in fields]
    block = 8
    for begin in range(0, tiles_lon, block):
        parts = []
        for field in fields:
            around = jnp.concatenate([field[:, -1:], field, field[:, :1]], axis=1)
            around = around[:, begin : begin + block + 2]
            for dy in (-1, 0, 1):
                by = dy * capacity % field.shape[0]
                parts.append(
                    jnp.concatenate([around[by:], around[:by]], axis=0) if by else around
                )
        meta = dot(jnp.concatenate(parts, axis=1).astype(BF16), spread_ref[...])
        for lon in range(block):
            piece = meta[:, lon * 128 : (lon + 1) * 128].astype(BF16)
            for lat in range(tiles_lat):
                out_ref[begin + lon, lat, len(AROUND)] = piece[lat * capacity : (lat + 1) * capacity]


def shard_kernel(values_ref, cell_ref, tag_ref, count_ref, out_ref, cells, tags, held, sem, *, lon_cells):
    tiles, capacity, _ = values_ref.shape
    copies = [
        pltpu.make_async_copy(values_ref, out_ref.at[pl.ds(0, tiles)], sem.at[0]),
        pltpu.make_async_copy(cell_ref, cells, sem.at[1]),
        pltpu.make_async_copy(tag_ref, tags, sem.at[2]),
        pltpu.make_async_copy(count_ref, held, sem.at[3]),
    ]
    for copy in copies:
        copy.start()
    for copy in copies[1:]:
        copy.wait()
    tiles_lat = held.shape[0]
    counts = jnp.concatenate(
        [held[tile : tile + 1, :] for tile in range(tiles_lat) for _ in range(capacity)], axis=0
    )
    cell = cells[...]
    slot = lax.broadcasted_iota(jnp.int32, cell.shape, 0) % capacity
    row = cell // lon_cells
    fields = [jnp.where(slot < counts, row, 255), cell - row * lon_cells, tags[...]]
    parts = [
        field[tile * capacity : (tile + 1) * capacity].astype(F32)
        for field in fields
        for tile in range(tiles_lat)
    ]
    used = len(fields) * tiles
    if used < 128:
        parts.append(jnp.zeros((capacity, 128 - used), F32))
    out_ref[tiles] = jnp.concatenate(parts, axis=1).astype(BF16)
    copies[0].wait()


def shard(record_values, record_cell, record_instrument, block_counts, lon_cells):
    tiles_lon, tiles_lat, capacity, wide = record_values.shape
    tiles = tiles_lon * tiles_lat
    anywhere = pl.BlockSpec(memory_space=pl.ANY)
    ints = pltpu.VMEM((tiles_lat * capacity, tiles_lon), jnp.int32)
    return pl.pallas_call(
        functools.partial(shard_kernel, lon_cells=lon_cells),
        out_shape=jax.ShapeDtypeStruct((tiles + 1, capacity, wide), BF16),
        in_specs=[anywhere] * 4,
        out_specs=pl.BlockSpec(memory_space=pltpu.VMEM),
        scratch_shapes=[
            ints,
            ints,
            pltpu.VMEM((tiles_lat, tiles_lon), jnp.int32),
            pltpu.SemaphoreType.DMA((4,)),
        ],
        compiler_params=pltpu.CompilerParams(vmem_limit_bytes=LIMIT),
    )(
        record_values.reshape(tiles, capacity, wide),
        record_cell.transpose(1, 2, 0).reshape(-1, tiles_lon),
        record_instrument.transpose(1, 2, 0).reshape(-1, tiles_lon),
        block_counts.T,
    )


def packed(record_values, record_cell, record_instrument, block_counts, lon_cells):
    tiles_lon, tiles_lat, capacity, wide = record_values.shape
    block = 8
    spread = np.zeros((9 * (block + 2), block * 128), ml_dtypes.bfloat16)
    for lon in range(block):
        for n, (dy, dx) in enumerate(AROUND):
            for field in range(3):
                spread[(field * 3 + dy + 1) * (block + 2) + lon + 1 + dx, lon * 128 + n * FIELDS + field] = 1
    vmem = pl.BlockSpec(memory_space=pltpu.VMEM)
    shape = (tiles_lon, tiles_lat, len(AROUND) + 1, capacity, wide)
    out = pl.pallas_call(
        functools.partial(pack_kernel, lon_cells=lon_cells),
        out_shape=jax.ShapeDtypeStruct(shape, BF16),
        in_specs=[vmem] * 5,
        out_specs=vmem,
        compiler_params=pltpu.CompilerParams(vmem_limit_bytes=32 * 2**20),
    )(
        record_values,
        record_cell.transpose(1, 2, 0).reshape(-1, tiles_lon),
        record_instrument.transpose(1, 2, 0).reshape(-1, tiles_lon),
        block_counts.T,
        jnp.asarray(spread),
    )
    return out.reshape((-1,) + shape[2:])


def local(
    record_values,
    record_cell,
    record_instrument,
    block_counts,
    background,
    input_weight,
    instrument_table,
    lift_weight,
    first_gain,
    attn_weight,
    mix_weight,
    second_gain,
    up_weight,
    down_weight,
):
    lat_cells, lon_cells, _, width = background.shape
    capacity = record_values.shape[2]
    sources = record_values.shape[0] * record_values.shape[1]
    tiles_lon, tiles_lat = record_values.shape[:2]
    gathers = sources <= FEW
    chunk = min(CHUNK, sources)
    plan, code, perm, keep, sel, find, pick, coef, place = constants(
        lat_cells, lon_cells, capacity, chunk
    )

    if gathers:
        mine = shard(record_values, record_cell, record_instrument, block_counts, lon_cells)
        records = lax.all_gather(mine, ("lon", "lat"), axis=0, tiled=True)
        records = records.reshape((sources,) + mine.shape)
        grown = jnp.tile(instrument_table, (128 // INSTR, 1))
        special = {"code": code, "first": jnp.concatenate([input_weight, grown], axis=0)}
    else:
        sent = packed(record_values, record_cell, record_instrument, block_counts, lon_cells)
        records = lax.all_to_all(sent, ("lon", "lat"), split_axis=0, concat_axis=0, tiled=True)
        records = records.reshape(-1, records.shape[-1])
        special = {"find": find, "pick": pick, "coef": coef, "place": place, "code": code}
        special.update(win=input_weight.T, tab=instrument_table)

    laid = jnp.pad(background, ((0, 0), (0, 0), (0, 0), (0, PAD - width)))
    laid = lax.optimization_barrier(laid.reshape(lat_cells, lon_cells, LEV * PAD))
    north = shifted(laid[lat_cells - HLAT :], "lat", 1, wraps=False)
    south = shifted(laid[:HLAT], "lat", -1, wraps=False)

    def columns(low, end):
        return jnp.concatenate([north[:, low:end], laid[:, low:end], south[:, low:end]], axis=0)

    west = shifted(columns(lon_cells - HLON, lon_cells), "lon", 1)
    east = shifted(columns(0, HLON), "lon", -1)
    strips = [strip.reshape(-1, LEV * PAD) for strip in (laid, north, south, west, east)]

    lift = jnp.pad(
        lift_weight.reshape(width, LEV, width), ((0, 0), (0, 0), (0, PAD - width))
    ).reshape(width, LEV * PAD)
    gains = jnp.pad(jnp.stack([first_gain, second_gain]).astype(F32), ((0, 6), (0, 0)))
    loaded = special | {
        "lift": lift,
        "perm": perm,
        "gains": gains,
        "wk": attn_weight[:, width : 2 * width],
        "wv": jnp.pad(attn_weight[:, 2 * width :], ((0, 0), (0, PAD - width))),
        "wq": attn_weight[:, :width],
        "keep": keep,
        "wm": mix_weight,
        "wu": up_weight,
        "wd": down_weight.T,
        "sel": sel,
    }
    loaded = {name: jnp.asarray(value) for name, value in loaded.items()}

    lon, lat = lax.axis_index("lon"), lax.axis_index("lat")
    scalars = [(lat == 0).astype(jnp.int32) - 1, (lat == tiles_lat - 1).astype(jnp.int32) - 1]
    near = [((lon + dx) % tiles_lon, (lat + dy) % tiles_lat) for dy, dx in AROUND]
    scalars += [x * tiles_lat + y for x, y in near] + [y * tiles_lon + x for x, y in near]

    cells = len(code)
    vmem = pl.BlockSpec(memory_space=pltpu.VMEM)
    anywhere = pl.BlockSpec(memory_space=pl.ANY)
    if gathers:
        rows = sources * len(AROUND) * capacity
        work = [
            pltpu.VMEM((len(AROUND), sources, capacity, 128), BF16),
            pltpu.VMEM((sources, capacity, 128), BF16),
            pltpu.VMEM((cells, rows), BF16),
            pltpu.VMEM((rows, LEV * PAD), BF16),
            pltpu.SemaphoreType.DMA((1 + len(AROUND),)),
        ]
    else:
        rows = chunk * (len(AROUND) + 1) * capacity
        work = [
            pltpu.VMEM((cells, rows), BF16),
            pltpu.VMEM((rows, LEV * PAD), BF16),
            pltpu.VMEM((cells, LEV * PAD), F32),
        ]
    starts = [
        float((dy * lat_cells + HLAT) * 64 + dx * lon_cells + HLON) for dy, dx in AROUND
    ]
    out = pl.pallas_call(
        functools.partial(block_kernel, plan, list(loaded), gathers, starts),
        out_shape=jax.ShapeDtypeStruct((lat_cells * lon_cells * LEV, width), BF16),
        in_specs=[pl.BlockSpec(memory_space=pltpu.SMEM)]
        + [anywhere if gathers else vmem]
        + [vmem] * len(strips)
        + [anywhere] * len(loaded),
        out_specs=vmem,
        scratch_shapes=[
            pltpu.VMEM((perm.shape[1], LEV * PAD), BF16),
            pltpu.SemaphoreType.DMA((len(loaded),)),
            *[pltpu.VMEM(value.shape, value.dtype) for value in loaded.values()],
            *work,
        ],
        compiler_params=pltpu.CompilerParams(vmem_limit_bytes=LIMIT),
        cost_estimate=pl.CostEstimate(
            flops=4 * 10**9, bytes_accessed=6 * 10**6, transcendentals=2 * 10**6
        ),
    )(jnp.stack(scalars), records, *strips, *loaded.values())
    return out.reshape(lat_cells, lon_cells, LEV, width)


def solution(mesh):
    placed = (
        P("lon", "lat", None, None),
        P("lon", "lat", None),
        P("lon", "lat", None),
        P("lon", "lat"),
        P("lat", "lon", None, None),
        P(),
        P(),
        P(),
        P(),
        P(),
        P(),
        P(),
        P(),
        P(),
    )
    return jax.shard_map(
        local, mesh=mesh, in_specs=placed, out_specs=P("lat", "lon", None, None), check_vma=False
    )
```

```python
import functools

import jax
import jax.numpy as jnp
import numpy as np
from jax import lax
from jax.experimental import pallas as pl
from jax.experimental.pallas import tpu as pltpu
from jax.sharding import PartitionSpec as P

HEADS = 6
INSTR = 8
LEV = 2
WLAT = 6
WLON = 12
HLAT = WLAT // 2
HLON = WLON // 2
LANES = 128
PAD = 256
CHUNK = 32
BF16 = jnp.bfloat16
F32 = jnp.float32


def shifted(value, axis, steps, wraps=True):
    count = lax.axis_size(axis)
    pairs = [(source, (source + steps) % count) for source in range(count)]
    if not wraps:
        pairs = [pair for pair in pairs if pair[1] == pair[0] + steps]
    return lax.ppermute(value, axis, pairs)


def rectangles(lat_cells, lon_cells):
    parts = []
    for top, high in ((0, HLAT), (HLAT, lat_cells - WLAT), (lat_cells - HLAT, HLAT)):
        for left, wide in ((0, HLON), (HLON, lon_cells - WLON), (lon_cells - HLON, HLON)):
            tokens = high * wide * LEV
            parts.append((top, high, left, wide, -(-tokens // 16) * 16))
    return parts


def gelu(x):
    return jax.nn.gelu(x)


def normalise(wide, gain):
    average = jnp.mean(wide, axis=-1, keepdims=True)
    centred = wide - average
    spread = jnp.mean(centred * centred, axis=-1, keepdims=True)
    return centred * lax.rsqrt(spread + 1e-05) * gain


def dot(a, b):
    return jnp.dot(a, b, preferred_element_type=F32)


def dot_nt(a, b):
    return lax.dot_general(a, b, (((1,), (1,)), ((), ())), preferred_element_type=F32)


def put_ones(tensor, width):
    lanes = lax.broadcasted_iota(jnp.int32, tensor.shape, 1) % PAD
    return jnp.where(lanes >= width, 1.0, tensor).astype(BF16)


def pack_kernel(values_ref, cell_ref, tag_ref, count_ref, out_ref, cells, tags, held, sem, *, lon_cells):
    tiles_lon, tiles_lat, capacity, _ = values_ref.shape
    copies = [
        pltpu.make_async_copy(values_ref, out_ref.at[:, :, 0], sem.at[0]),
        pltpu.make_async_copy(cell_ref, cells, sem.at[1]),
        pltpu.make_async_copy(tag_ref, tags, sem.at[2]),
        pltpu.make_async_copy(count_ref, held, sem.at[3]),
    ]
    for copy in copies:
        copy.start()
    for copy in copies[1:]:
        copy.wait()
    counts = jnp.concatenate(
        [held[tile : tile + 1, :] for tile in range(tiles_lat) for _ in range(capacity)], axis=0
    )
    cell = cells[...]
    slot = lax.broadcasted_iota(jnp.int32, cell.shape, 0) % capacity
    row = cell // lon_cells
    fields = [jnp.where(slot < counts, row, 255), cell - row * lon_cells, tags[...]]
    rows, columns, kinds = (field.astype(F32) for field in fields)
    lane = lax.broadcasted_iota(jnp.int32, (cell.shape[0], LANES), 1)
    for lon in range(tiles_lon):
        kind = jnp.where(lane.astype(F32) == kinds[:, lon : lon + 1], 1.0, 0.0)
        meta = jnp.where(lane == INSTR, rows[:, lon : lon + 1], kind)
        meta = jnp.where(lane == INSTR + 1, columns[:, lon : lon + 1], meta).astype(BF16)
        out_ref[lon, :, 1] = meta.reshape(tiles_lat, capacity, LANES)
    copies[0].wait()


def packed(record_values, record_cell, record_instrument, block_counts, lon_cells):
    tiles_lon, tiles_lat, capacity, wide = record_values.shape
    anywhere = pl.BlockSpec(memory_space=pl.ANY)
    ints = pltpu.VMEM((tiles_lat * capacity, tiles_lon), jnp.int32)
    shape = (tiles_lon, tiles_lat, 2, capacity, wide)
    out = pl.pallas_call(
        functools.partial(pack_kernel, lon_cells=lon_cells),
        out_shape=jax.ShapeDtypeStruct(shape, BF16),
        in_specs=[anywhere] * 4,
        out_specs=pl.BlockSpec(memory_space=pltpu.VMEM),
        scratch_shapes=[
            ints,
            ints,
            pltpu.VMEM((tiles_lat, tiles_lon), jnp.int32),
            pltpu.SemaphoreType.DMA((4,)),
        ],
        compiler_params=pltpu.CompilerParams(vmem_limit_bytes=56 * 2**20),
    )(
        record_values,
        record_cell.transpose(1, 2, 0).reshape(-1, tiles_lon),
        record_instrument.transpose(1, 2, 0).reshape(-1, tiles_lon),
        block_counts.T,
    )
    return out.reshape((-1,) + shape[2:])


def latent_kernel(
    parts, recv_ref, back_ref, code_ref, first_ref, lift_ref, gain_ref, latent_ref, normed_ref, lifted_ref
):
    sources, _, capacity, _ = recv_ref.shape
    width = first_ref.shape[1]
    lon_cells = back_ref.shape[1]
    chunk = min(CHUNK, sources)
    slots = chunk * capacity

    def scatter(begin):
        records = recv_ref[pl.ds(begin, chunk), 0].reshape(slots, LANES)
        meta = recv_ref[pl.ds(begin, chunk), 1].reshape(slots, LANES)
        encoded = dot(jnp.concatenate([records, meta], axis=1), first_ref[...])
        lifted = put_ones(gelu(dot(gelu(encoded).astype(BF16), lift_ref[...])), width)
        for level in range(LEV):
            lifted_ref[level * slots : (level + 1) * slots, :] = lifted[:, level * PAD : (level + 1) * PAD]
        lane = lax.broadcasted_iota(jnp.int32, (16, LANES), 1)
        weigh = jnp.where(lane == INSTR, float(lon_cells * LEV), 0.0)
        weigh = jnp.where(lane == INSTR + 1, float(LEV), weigh).astype(BF16)
        token = dot_nt(weigh, meta)[:1]
        token = jnp.concatenate([token + float(level) for level in range(LEV)], axis=1)
        hot = jnp.where(code_ref[...] == token, 1.0, 0.0).astype(BF16)
        return dot(hot, lifted_ref[...])

    sums = scatter(0)
    if sources > chunk:
        sums = lax.fori_loop(
            1, sources // chunk, lambda step, total: total + scatter(step * chunk), sums
        )
    back = []
    for top, high, left, wide, padded in parts:
        tokens = high * wide * LEV
        part = back_ref[top : top + high, left : left + wide].reshape(tokens, width).astype(F32)
        if padded > tokens:
            part = jnp.concatenate([part, jnp.zeros((padded - tokens, width), F32)], axis=0)
        back.append(part)
    latent = jnp.concatenate(back, axis=0) + sums[:, :width]
    latent = (latent * (1.0 / (1.0 + sums[:, width : width + 1]))).astype(BF16)
    latent_ref[...] = latent
    normed_ref[...] = normalise(latent.astype(F32), gain_ref[...].astype(F32)).astype(BF16)


def window_pieces(parts):
    own = np.cumsum([0] + [part[4] for part in parts])
    edge = [np.cumsum([0] + [parts[n][4] for n in group]) for group in ((0, 1, 2), (0, 0, 3, 6, 6))]

    def piece(array, first, part):
        return array, int(first), parts[part][4], parts[part][1] * parts[part][3] * LEV

    windows = []
    for i in range(3):
        for j in range(3):
            pieces = [piece("own", own[3 * i + j], 3 * i + j)]
            if i != 1:
                pieces.append(piece("north" if i == 0 else "south", edge[0][j], j))
            if j != 1:
                side = "west" if j == 0 else "east"
                pieces.append(piece(side, edge[1][i + 1], 3 * i))
                if i != 1:
                    pieces.append(piece(side, edge[1][0 if i == 0 else 4], 0))
            windows.append(pieces)
    return windows


def block_kernel(
    parts,
    scalars_ref,
    latent_ref,
    own_ref,
    north_ref,
    south_ref,
    west_ref,
    east_ref,
    keep_ref,
    wk_ref,
    wv_ref,
    wq_ref,
    wm_ref,
    gain_ref,
    wu_ref,
    wd_ref,
    out_ref,
):
    width = wm_ref.shape[0]
    head = width // HEADS
    arrays = dict(own=own_ref, north=north_ref, south=south_ref, west=west_ref, east=east_ref)
    windows = window_pieces(parts)
    tokens = [
        arrays[array][first : first + rows] for pieces in windows for array, first, rows, _ in pieces
    ]
    tokens = jnp.concatenate(tokens, axis=0)
    keys = dot(tokens, wk_ref[...]).astype(BF16)
    values = put_ones(dot(tokens, wv_ref[...]), width)
    query = (dot(own_ref[...], wq_ref[...]) * head ** (-0.5)).astype(BF16)

    head_of = lax.broadcasted_iota(jnp.int32, (1, width), 1) // head
    mixed, start, begin = [], 0, 0
    for w, pieces in enumerate(windows):
        rows = parts[w][4]
        held = sum(piece[2] for piece in pieces)
        part = query[start : start + rows]
        stacked = jnp.concatenate(
            [jnp.where(head_of == h, part, jnp.zeros_like(part)) for h in range(HEADS)], axis=0
        )
        scores = dot_nt(stacked, keys[begin : begin + held])
        if len(pieces) > 1:
            floor = scalars_ref[w // 3].astype(F32)
            scores = jnp.where(keep_ref[w : w + 1, :held] > floor, scores, -1e30)
        largest = jnp.max(scores, axis=-1, keepdims=True)
        raised = jnp.exp(scores - largest).astype(BF16)
        product = dot(raised, values[begin : begin + held])
        product = product[:, :width] * (1.0 / product[:, width : width + 1])
        total = jnp.zeros((rows, width), F32)
        for h in range(HEADS):
            total = jnp.where(head_of == h, product[h * rows : (h + 1) * rows], total)
        mixed.append(total.astype(BF16))
        start += rows
        begin += held
    mixed = jnp.concatenate(mixed, axis=0)

    after = (latent_ref[...].astype(F32) + dot(mixed, wm_ref[...])).astype(BF16).astype(F32)
    normed_two = normalise(after, gain_ref[...].astype(F32)).astype(BF16)
    hidden = gelu(dot(normed_two, wu_ref[...])).astype(BF16)
    result = (after + dot_nt(hidden, wd_ref[...])).astype(BF16)
    start = 0
    for top, high, left, wide, padded in parts:
        part = result[start : start + padded][: high * wide * LEV]
        out_ref[top : top + high, left : left + wide] = part.reshape(high, wide, LEV, width)
        start += padded


def local(
    record_values,
    record_cell,
    record_instrument,
    block_counts,
    background,
    input_weight,
    instrument_table,
    lift_weight,
    first_gain,
    attn_weight,
    mix_weight,
    second_gain,
    up_weight,
    down_weight,
):
    lat_cells, lon_cells, _, width = background.shape
    capacity = record_values.shape[2]
    tiles_lat = record_values.shape[1]
    parts = rectangles(lat_cells, lon_cells)
    starts = np.cumsum([0] + [part[4] for part in parts])
    padded = int(starts[-1])
    code = np.full((padded, 1), -8, np.float32)
    for start, (top, high, left, wide, _) in zip(starts, parts):
        for n in range(high * wide * LEV):
            cell, level = divmod(n, LEV)
            code[start + n] = ((top + cell // wide) * lon_cells + left + cell % wide) * LEV + level
    windows = window_pieces(parts)
    keep = np.zeros((16, max(sum(piece[2] for piece in pieces) for pieces in windows)), np.float32)
    for w, pieces in enumerate(windows):
        at = 0
        for n, (array, _, rows, tokens) in enumerate(pieces):
            beyond = array in ("north", "south") or n == 3
            keep[w, at : at + tokens] = 1 if beyond else 2
            at += rows

    sent = packed(record_values, record_cell, record_instrument, block_counts, lon_cells)
    received = lax.all_to_all(sent, ("lon", "lat"), split_axis=0, concat_axis=0, tiled=True)

    first = jnp.concatenate(
        [input_weight, instrument_table, jnp.zeros((LANES - INSTR, width), BF16)], axis=0
    )
    lift = jnp.pad(
        lift_weight.reshape(width, LEV, width), ((0, 0), (0, 0), (0, PAD - width))
    ).reshape(width, LEV * PAD)
    vmem = pl.BlockSpec(memory_space=pltpu.VMEM)
    latent, normed = pl.pallas_call(
        functools.partial(latent_kernel, parts),
        out_shape=[jax.ShapeDtypeStruct((padded, width), BF16)] * 2,
        in_specs=[vmem] * 6,
        out_specs=[vmem] * 2,
        scratch_shapes=[pltpu.VMEM((min(CHUNK, sent.shape[0]) * capacity * LEV, PAD), BF16)],
        compiler_params=pltpu.CompilerParams(vmem_limit_bytes=24 * 2**20),
    )(received, background, jnp.asarray(code), first, lift, first_gain.reshape(1, width))

    north = shifted(normed[starts[6] :], "lat", 1, wraps=False)
    south = shifted(normed[: starts[3]], "lat", -1, wraps=False)

    def side(j):
        low, end = starts[j] , starts[j + 1]
        own = [normed[starts[3 * i + j] : starts[3 * i + j + 1]] for i in range(3)]
        return jnp.concatenate([north[low:end], *own, south[low:end]], axis=0)

    west = shifted(side(2), "lon", 1)
    east = shifted(side(0), "lon", -1)

    lat = lax.axis_index("lat")
    scalars = jnp.stack([lat == 0, lat < 0, lat == tiles_lat - 1]).astype(jnp.int32)
    return pl.pallas_call(
        functools.partial(block_kernel, parts),
        out_shape=jax.ShapeDtypeStruct(background.shape, BF16),
        in_specs=[pl.BlockSpec(memory_space=pltpu.SMEM)] + [vmem] * 14,
        out_specs=vmem,
        compiler_params=pltpu.CompilerParams(vmem_limit_bytes=40 * 2**20),
    )(
        scalars,
        latent,
        normed,
        north,
        south,
        west,
        east,
        jnp.asarray(keep),
        attn_weight[:, width : 2 * width],
        jnp.pad(attn_weight[:, 2 * width :], ((0, 0), (0, PAD - width))),
        attn_weight[:, :width],
        mix_weight,
        second_gain.reshape(1, width),
        up_weight,
        down_weight.T,
    )


def solution(mesh):
    placed = (
        P("lon", "lat", None, None),
        P("lon", "lat", None),
        P("lon", "lat", None),
        P("lon", "lat"),
        P("lat", "lon", None, None),
        P(),
        P(),
        P(),
        P(),
        P(),
        P(),
        P(),
        P(),
        P(),
    )
    return jax.shard_map(
        local, mesh=mesh, in_specs=placed, out_specs=P("lat", "lon", None, None), check_vma=False
    )
```

```python
import functools

import jax
import jax.numpy as jnp
import numpy as np
from jax import lax
from jax.experimental import pallas as pl
from jax.experimental.pallas import tpu as pltpu
from jax.sharding import PartitionSpec as P

HEADS = 6
INSTR = 8
LEV = 2
WLAT = 6
WLON = 12
HLAT = WLAT // 2
HLON = WLON // 2
LANES = 128
PAD = 256
CHUNK = 32
BF16 = jnp.bfloat16
F32 = jnp.float32


def shifted(value, axis, steps, wraps=True):
    count = lax.axis_size(axis)
    pairs = [(source, (source + steps) % count) for source in range(count)]
    if not wraps:
        pairs = [pair for pair in pairs if pair[1] == pair[0] + steps]
    return lax.ppermute(value, axis, pairs)


def rectangles(lat_cells, lon_cells):
    parts = []
    for top, high in ((0, HLAT), (HLAT, lat_cells - WLAT), (lat_cells - HLAT, HLAT)):
        for left, wide in ((0, HLON), (HLON, lon_cells - WLON), (lon_cells - HLON, HLON)):
            tokens = high * wide * LEV
            parts.append((top, high, left, wide, -(-tokens // 16) * 16))
    return parts


def gelu(x):
    return jax.nn.gelu(x)


def normalise(wide, gain):
    average = jnp.mean(wide, axis=-1, keepdims=True)
    centred = wide - average
    spread = jnp.mean(centred * centred, axis=-1, keepdims=True)
    return centred * lax.rsqrt(spread + 1e-05) * gain


def dot(a, b):
    return jnp.dot(a, b, preferred_element_type=F32)


def dot_nt(a, b):
    return lax.dot_general(a, b, (((1,), (1,)), ((), ())), preferred_element_type=F32)


def with_ones(tensor):
    ones = jnp.ones((tensor.shape[0], PAD - tensor.shape[1]), F32)
    return jnp.concatenate([tensor, ones], axis=1).astype(BF16)


def beside(left, right):
    return jnp.concatenate([left, right], axis=1)


def below(*pieces):
    return jnp.concatenate(pieces, axis=0)


def pack_kernel(values_ref, cell_ref, tag_ref, count_ref, out_ref, cells, tags, held, sem, *, lon_cells):
    tiles_lon, tiles_lat, capacity, _ = values_ref.shape
    copies = [
        pltpu.make_async_copy(values_ref, out_ref.at[:, :, 0], sem.at[0]),
        pltpu.make_async_copy(cell_ref, cells, sem.at[1]),
        pltpu.make_async_copy(tag_ref, tags, sem.at[2]),
        pltpu.make_async_copy(count_ref, held, sem.at[3]),
    ]
    for copy in copies:
        copy.start()
    for copy in copies[1:]:
        copy.wait()
    counts = jnp.concatenate(
        [held[tile : tile + 1, :] for tile in range(tiles_lat) for _ in range(capacity)], axis=0
    )
    cell = cells[...]
    slot = lax.broadcasted_iota(jnp.int32, cell.shape, 0) % capacity
    row = cell // lon_cells
    fields = [jnp.where(slot < counts, row, 255), cell - row * lon_cells, tags[...]]
    rows, columns, kinds = (field.astype(F32) for field in fields)
    lane = lax.broadcasted_iota(jnp.int32, (cell.shape[0], LANES), 1)
    for lon in range(tiles_lon):
        kind = jnp.where(lane.astype(F32) == kinds[:, lon : lon + 1], 1.0, 0.0)
        meta = jnp.where(lane == INSTR, rows[:, lon : lon + 1], kind)
        meta = jnp.where(lane == INSTR + 1, columns[:, lon : lon + 1], meta).astype(BF16)
        out_ref[lon, :, 1] = meta.reshape(tiles_lat, capacity, LANES)
    copies[0].wait()


def packed(record_values, record_cell, record_instrument, block_counts, lon_cells):
    tiles_lon, tiles_lat, capacity, wide = record_values.shape
    anywhere = pl.BlockSpec(memory_space=pl.ANY)
    ints = pltpu.VMEM((tiles_lat * capacity, tiles_lon), jnp.int32)
    shape = (tiles_lon, tiles_lat, 2, capacity, wide)
    out = pl.pallas_call(
        functools.partial(pack_kernel, lon_cells=lon_cells),
        out_shape=jax.ShapeDtypeStruct(shape, BF16),
        in_specs=[anywhere] * 4,
        out_specs=pl.BlockSpec(memory_space=pltpu.VMEM),
        scratch_shapes=[
            ints,
            ints,
            pltpu.VMEM((tiles_lat, tiles_lon), jnp.int32),
            pltpu.SemaphoreType.DMA((4,)),
        ],
        compiler_params=pltpu.CompilerParams(vmem_limit_bytes=56 * 2**20),
    )(
        record_values,
        record_cell.transpose(1, 2, 0).reshape(-1, tiles_lon),
        record_instrument.transpose(1, 2, 0).reshape(-1, tiles_lon),
        block_counts.T,
    )
    return out.reshape((-1,) + shape[2:])


def latent_kernel(
    parts,
    recv_ref,
    back_ref,
    code_ref,
    first_ref,
    table_ref,
    lift_ref,
    gain_ref,
    latent_ref,
    normed_ref,
    up_ref,
    down_ref,
    left_ref,
    right_ref,
):
    sources, _, capacity, _ = recv_ref.shape
    width = table_ref.shape[1]
    lon_cells = back_ref.shape[1]
    chunk = min(CHUNK, sources)
    slots = chunk * capacity

    def scatter(begin):
        records = recv_ref[pl.ds(begin, chunk), 0].reshape(slots, LANES)
        meta = recv_ref[pl.ds(begin, chunk), 1].reshape(slots, LANES)
        encoded = dot_nt(records, first_ref[...]) + dot(meta[:, :INSTR], table_ref[...])
        lifted = gelu(dot(gelu(encoded).astype(BF16), lift_ref[...]))
        lifted = with_ones(
            below(*[lifted[:, level * width : (level + 1) * width] for level in range(LEV)])
        )
        lane = lax.broadcasted_iota(jnp.int32, (16, LANES), 1)
        weigh = jnp.where(lane == INSTR, float(lon_cells * LEV), 0.0)
        weigh = jnp.where(lane == INSTR + 1, float(LEV), weigh).astype(BF16)
        token = dot_nt(weigh, meta)[:1]
        token = jnp.concatenate([token + float(level) for level in range(LEV)], axis=1)
        hot = jnp.where(code_ref[...] == token, 1.0, 0.0).astype(BF16)
        return dot(hot, lifted)

    sums = scatter(0)
    if sources > chunk:
        sums = lax.fori_loop(
            1, sources // chunk, lambda step, total: total + scatter(step * chunk), sums
        )
    back = []
    for top, high, left, wide, padded in parts:
        tokens = high * wide * LEV
        part = back_ref[top : top + high, left : left + wide].reshape(tokens, width).astype(F32)
        if padded > tokens:
            part = jnp.concatenate([part, jnp.zeros((padded - tokens, width), F32)], axis=0)
        back.append(part)
    latent = jnp.concatenate(back, axis=0) + sums[:, :width]
    latent = (latent * (1.0 / (1.0 + sums[:, width : width + 1]))).astype(BF16)
    latent_ref[...] = latent
    normed = normalise(latent.astype(F32), gain_ref[...].astype(F32))
    normed_ref[...] = normed.astype(BF16)

    own, start = [], 0
    for top, high, left, wide, padded in parts:
        own.append(normed[start : start + high * wide * LEV])
        start += padded
    half = own[0].shape[0]

    def halves(n):
        return beside(own[n][:half], own[n][half:])

    down_ref[...] = below(beside(own[6], own[8]), halves(7)).astype(BF16)
    up_ref[...] = below(beside(own[2], own[0]), halves(1)).astype(BF16)
    left_ref[...] = below(beside(own[0], own[3][:half]), beside(own[6], own[3][half:])).astype(BF16)
    right_ref[...] = below(beside(own[2], own[5][:half]), beside(own[8], own[5][half:])).astype(BF16)


def block_kernel(
    parts,
    scalars_ref,
    latent_ref,
    own_ref,
    north_ref,
    south_ref,
    west_ref,
    east_ref,
    keep_ref,
    attn_ref,
    wm_ref,
    gain_ref,
    wu_ref,
    wd_ref,
    out_ref,
):
    width = wm_ref.shape[0]
    head = width // HEADS
    half = parts[0][1] * parts[0][3] * LEV
    own, start = [], 0
    for top, high, left, wide, padded in parts:
        own.append(own_ref[start : start + padded, :].astype(F32)[: high * wide * LEV])
        start += padded

    def pieces(ref):
        value = ref[...].astype(F32)
        rows = [value[at : at + half] for at in range(0, value.shape[0], half)]
        return [part[:, at : at + width] for part in rows for at in (0, width)]

    north_w, north_e, north_1, north_2 = pieces(north_ref)
    south_e, south_w, south_1, south_2 = pieces(south_ref)
    west_n, west_1, west_s, west_2, west_far_s, west_far_n = pieces(west_ref)
    east_n, east_1, east_s, east_2, east_far_n, east_far_s = pieces(east_ref)
    windows = [
        (own[0], north_w, west_n, west_far_n),
        (own[1], north_1, north_2),
        (own[2], north_e, east_n, east_far_n),
        (own[3], west_1, west_2),
        (own[4],),
        (own[5], east_1, east_2),
        (own[6], south_w, west_s, west_far_s),
        (own[7], south_1, south_2),
        (own[8], south_e, east_s, east_far_s),
    ]
    tokens = below(*[piece for window in windows for piece in window]).astype(BF16)
    weight = attn_ref[...]
    keys = dot(tokens, weight[:, width : 2 * width]).astype(BF16)
    values = with_ones(dot(tokens, weight[:, 2 * width :]))
    query = (dot(own_ref[...], weight[:, :width]) * head ** (-0.5)).astype(BF16)

    head_of = lax.broadcasted_iota(jnp.int32, (1, width), 1) // head
    held = WLAT * WLON * LEV
    mixed, start = [], 0
    for w in range(len(parts)):
        rows = parts[w][4]
        part = query[start : start + rows]
        stacked = below(
            *[jnp.where(head_of == h, part, jnp.zeros_like(part)) for h in range(HEADS)]
        )
        scores = dot_nt(stacked, keys[w * held : (w + 1) * held])
        if w // 3 != 1:
            floor = scalars_ref[w // 3].astype(F32)
            scores = jnp.where(keep_ref[w : w + 1, :] > floor, scores, -1e30)
        largest = jnp.max(scores, axis=-1, keepdims=True)
        raised = jnp.exp(scores - largest).astype(BF16)
        product = dot(raised, values[w * held : (w + 1) * held])
        product = product[:, :width] * (1.0 / product[:, width : width + 1])
        total = jnp.zeros((rows, width), F32)
        for h in range(HEADS):
            total = jnp.where(head_of == h, product[h * rows : (h + 1) * rows], total)
        mixed.append(total.astype(BF16))
        start += rows
    mixed = below(*mixed)

    after = (latent_ref[...].astype(F32) + dot(mixed, wm_ref[...])).astype(BF16).astype(F32)
    normed_two = normalise(after, gain_ref[...].astype(F32)).astype(BF16)
    hidden = gelu(dot(normed_two, wu_ref[...])).astype(BF16)
    result = (after + dot_nt(hidden, wd_ref[...])).astype(BF16)
    start = 0
    for top, high, left, wide, padded in parts:
        part = result[start : start + padded][: high * wide * LEV]
        out_ref[top : top + high, left : left + wide] = part.reshape(high, wide, LEV, width)
        start += padded


def local(
    record_values,
    record_cell,
    record_instrument,
    block_counts,
    background,
    input_weight,
    instrument_table,
    lift_weight,
    first_gain,
    attn_weight,
    mix_weight,
    second_gain,
    up_weight,
    down_weight,
):
    lat_cells, lon_cells, _, width = background.shape
    capacity = record_values.shape[2]
    tiles_lat = record_values.shape[1]
    parts = rectangles(lat_cells, lon_cells)
    starts = np.cumsum([0] + [part[4] for part in parts])
    padded = int(starts[-1])
    code = np.full((padded, 1), -8, np.float32)
    for start, (top, high, left, wide, _) in zip(starts, parts):
        for n in range(high * wide * LEV):
            cell, level = divmod(n, LEV)
            code[start + n] = ((top + cell // wide) * lon_cells + left + cell % wide) * LEV + level
    half = HLAT * HLON * LEV
    keep = np.zeros((16, WLAT * WLON * LEV), np.float32)
    keep[:, :half] = 1
    keep[[1, 7], : 2 * half] = 1
    keep[[0, 2, 6, 8], 2 * half : 3 * half] = 1

    sent = packed(record_values, record_cell, record_instrument, block_counts, lon_cells)
    received = lax.all_to_all(sent, ("lon", "lat"), split_axis=0, concat_axis=0, tiled=True)

    vmem = pl.BlockSpec(memory_space=pltpu.VMEM)
    whole = jax.ShapeDtypeStruct((padded, width), BF16)
    strip = jax.ShapeDtypeStruct((2 * half, 2 * width), BF16)
    latent, normed, up, down, left, right = pl.pallas_call(
        functools.partial(latent_kernel, parts),
        out_shape=[whole, whole, strip, strip, strip, strip],
        in_specs=[vmem] * 7,
        out_specs=[vmem] * 6,
        compiler_params=pltpu.CompilerParams(vmem_limit_bytes=24 * 2**20),
    )(
        received,
        background,
        jnp.asarray(code),
        input_weight.T,
        instrument_table,
        lift_weight,
        first_gain.reshape(1, width),
    )

    north = shifted(down, "lat", 1, wraps=False)
    south = shifted(up, "lat", -1, wraps=False)
    right = below(right, beside(south[:half, :width], north[:half, width:]))
    left = below(left, beside(north[:half, :width], south[:half, width:]))
    west = shifted(right, "lon", 1)
    east = shifted(left, "lon", -1)

    lat = lax.axis_index("lat")
    scalars = jnp.stack([lat == 0, lat < 0, lat == tiles_lat - 1]).astype(jnp.int32) - 1
    return pl.pallas_call(
        functools.partial(block_kernel, parts),
        out_shape=jax.ShapeDtypeStruct(background.shape, BF16),
        in_specs=[pl.BlockSpec(memory_space=pltpu.SMEM)] + [vmem] * 12,
        out_specs=vmem,
        compiler_params=pltpu.CompilerParams(vmem_limit_bytes=40 * 2**20),
    )(
        scalars,
        latent,
        normed,
        north,
        south,
        west,
        east,
        jnp.asarray(keep),
        attn_weight,
        mix_weight,
        second_gain.reshape(1, width),
        up_weight,
        down_weight.T,
    )


def solution(mesh):
    placed = (
        P("lon", "lat", None, None),
        P("lon", "lat", None),
        P("lon", "lat", None),
        P("lon", "lat"),
        P("lat", "lon", None, None),
        P(),
        P(),
        P(),
        P(),
        P(),
        P(),
        P(),
        P(),
        P(),
    )
    return jax.shard_map(
        local, mesh=mesh, in_specs=placed, out_specs=P("lat", "lon", None, None), check_vma=False
    )
```

```python
import functools

import jax
import jax.numpy as jnp
from jax import lax
from jax.experimental import pallas as pl
from jax.experimental.pallas import tpu as pltpu
from jax.sharding import PartitionSpec as P

HEADS = 6
INSTR = 8
LEV = 2
WLAT = 6
WLON = 12
HLAT = WLAT // 2
HLON = WLON // 2
LANES = 128
PAD = 256
CHUNK = 32
LIMIT = 40 * 2**20
BF16 = jnp.bfloat16
F32 = jnp.float32

AROUND = [(dy, dx) for dy in (-1, 0, 1) for dx in (-1, 0, 1)]
ROWS = INSTR * len(AROUND)
COLS = ROWS + len(AROUND)


def shifted(value, axis, steps, wraps=True):
    count = lax.axis_size(axis)
    pairs = [(source, (source + steps) % count) for source in range(count)]
    if not wraps:
        pairs = [pair for pair in pairs if pair[1] == pair[0] + steps]
    return lax.ppermute(value, axis, pairs)


def rectangles(lat_cells, lon_cells):
    lat = {-1: [(lat_cells - HLAT, HLAT)], 1: [(0, HLAT)]}
    lat[0] = [(0, HLAT), (HLAT, lat_cells - WLAT), (lat_cells - HLAT, HLAT)]
    lon = {-1: [(lon_cells - HLON, HLON)], 1: [(0, HLON)]}
    lon[0] = [(0, HLON), (HLON, lon_cells - WLON), (lon_cells - HLON, HLON)]
    return [
        [(top, high, left, wide) for top, high in lat[dy] for left, wide in lon[dx]]
        for dy, dx in AROUND
    ]


def tokens_of(part):
    return part[1] * part[3] * LEV


def padded(count):
    return -(-count // 8) * 8


def gelu(x):
    return jax.nn.gelu(x)


def normalise(wide, gain):
    average = jnp.mean(wide, axis=-1, keepdims=True)
    centred = wide - average
    spread = jnp.mean(centred * centred, axis=-1, keepdims=True)
    return centred * lax.rsqrt(spread + 1e-05) * gain


def dot(a, b):
    return jnp.dot(a, b, preferred_element_type=F32)


def dot_nt(a, b):
    return lax.dot_general(a, b, (((1,), (1,)), ((), ())), preferred_element_type=F32)


def with_ones(tensor):
    ones = jnp.ones((tensor.shape[0], PAD - tensor.shape[1]), F32)
    return jnp.concatenate([tensor, ones], axis=1).astype(BF16)


def below(*pieces):
    return jnp.concatenate(pieces, axis=0) if len(pieces) > 1 else pieces[0]


def pack_kernel(
    values_ref, cell_ref, tag_ref, count_ref, out_ref, values, cells, tags, held, sem, *, lon_cells
):
    tiles_lon, tiles_lat, capacity, _ = values_ref.shape
    copies = [
        pltpu.make_async_copy(cell_ref, cells, sem.at[0]),
        pltpu.make_async_copy(tag_ref, tags, sem.at[1]),
        pltpu.make_async_copy(count_ref, held, sem.at[2]),
        pltpu.make_async_copy(values_ref, values, sem.at[3]),
    ]
    for copy in copies:
        copy.start()
    for copy in copies[:3]:
        copy.wait()
    counts = below(*[held[tile : tile + 1, :] for tile in range(tiles_lat) for _ in range(capacity)])
    cell = cells[...]
    slot = lax.broadcasted_iota(jnp.int32, cell.shape, 0) % capacity
    row = cell // lon_cells
    fields = [jnp.where(slot < counts, row, 255), cell - row * lon_cells, tags[...]]
    rows, columns, kinds = (field.astype(F32) for field in fields)
    lane = lax.broadcasted_iota(jnp.int32, (cell.shape[0], LANES), 1)
    kind_of = (lane % INSTR).astype(F32)
    marks = [
        ((lane < ROWS) & (lane // INSTR == n)) | (lane == ROWS + n) | (lane == COLS + n)
        for n in range(len(AROUND))
    ]
    turned = []
    for lon in range(tiles_lon):
        meta = jnp.where(kind_of == kinds[:, lon : lon + 1], 1.0, 0.0)
        meta = jnp.where(lane >= ROWS, rows[:, lon : lon + 1], meta)
        meta = jnp.where(lane >= COLS, columns[:, lon : lon + 1], meta)
        turns = {0: meta}
        for dy in (-1, 1):
            by = dy * capacity % meta.shape[0]
            turns[dy] = below(meta[by:], meta[:by])
        turned.append(turns)
    for lon in range(tiles_lon):
        meta = jnp.zeros(lane.shape, F32)
        for mark, (dy, dx) in zip(marks, AROUND):
            meta = jnp.where(mark, turned[(lon + dx) % tiles_lon][dy], meta)
        out_ref[lon, :, len(AROUND)] = meta.astype(BF16).reshape(tiles_lat, capacity, LANES)
    copies[3].wait()
    for n, (dy, dx) in enumerate(AROUND):
        spans = {0: [(0, tiles_lat)], 1: [(0, tiles_lat - 1), (tiles_lat - 1, tiles_lat)]}
        spans[-1] = [(0, 1), (1, tiles_lat)]

        def copy_tiles(lon, n=n, dx=dx, dy=dy, spans=spans[dy]):
            source = lax.rem(lon + dx + tiles_lon, tiles_lon)
            for low, end in spans:
                first = (low + dy) % tiles_lat
                out_ref[lon, low:end, n] = values[source, first : first + end - low]

        if tiles_lon <= 8:
            for lon in range(tiles_lon):
                copy_tiles(lon)
        else:
            pl.loop(0, tiles_lon)(copy_tiles)


def packed(record_values, record_cell, record_instrument, block_counts, lon_cells):
    tiles_lon, tiles_lat, capacity, wide = record_values.shape
    anywhere = pl.BlockSpec(memory_space=pltpu.HBM)
    ints = pltpu.VMEM((tiles_lat * capacity, tiles_lon), jnp.int32)
    shape = (tiles_lon, tiles_lat, len(AROUND) + 1, capacity, wide)
    out = pl.pallas_call(
        functools.partial(pack_kernel, lon_cells=lon_cells),
        out_shape=jax.ShapeDtypeStruct(shape, BF16),
        in_specs=[anywhere] * 4,
        out_specs=pl.BlockSpec(memory_space=pltpu.VMEM),
        scratch_shapes=[
            pltpu.VMEM(record_values.shape, BF16),
            ints,
            ints,
            pltpu.VMEM((tiles_lat, tiles_lon), jnp.int32),
            pltpu.SemaphoreType.DMA((4,)),
        ],
        compiler_params=pltpu.CompilerParams(vmem_limit_bytes=56 * 2**20),
    )(
        record_values,
        record_cell.transpose(1, 2, 0).reshape(-1, tiles_lon),
        record_instrument.transpose(1, 2, 0).reshape(-1, tiles_lon),
        block_counts.T,
    )
    return out.reshape((-1,) + shape[2:])


def token_codes(part, lon_cells):
    top, high, left, wide = part
    count = tokens_of(part)
    place = lax.broadcasted_iota(jnp.int32, (padded(count), LANES), 0)
    code = place + (top * lon_cells + left) * LEV
    for row in range(1, high):
        step = (lon_cells - wide) * LEV
        code = code + jnp.where(place >= row * wide * LEV, step, 0)
    return jnp.where(place < count, code, -8).astype(F32)


def block_kernel(
    plan,
    scalars_ref,
    recv_ref,
    north_ref,
    south_ref,
    west_ref,
    east_ref,
    back_ref,
    first_ref,
    table_ref,
    lift_ref,
    gain_one_ref,
    attn_ref,
    mix_ref,
    gain_two_ref,
    up_ref,
    down_ref,
    out_ref,
):
    sources, _, capacity, _ = recv_ref.shape
    lat_cells, lon_cells, _, width = back_ref.shape
    chunk = min(CHUNK, sources)
    slots = chunk * capacity

    first, table, lift = first_ref[...], table_ref[...].astype(F32), lift_ref[...]
    table = below(*[table] * (LANES // INSTR)).astype(BF16)
    lane = lax.broadcasted_iota(jnp.int32, (16, LANES), 1)
    sub = lax.broadcasted_iota(jnp.int32, (16, LANES), 0)
    weigh = jnp.where(lane == ROWS + sub, float(lon_cells * LEV), 0.0)
    weigh = jnp.where(lane == COLS + sub, float(LEV), weigh).astype(BF16)
    codes = [below(*[token_codes(part, lon_cells) for part in parts]) for parts in plan]

    def scatter(begin):
        meta = recv_ref[pl.ds(begin, chunk), len(AROUND)].reshape(slots, LANES)
        records = below(
            *[
                recv_ref[pl.ds(begin, chunk), n].reshape(slots, LANES)
                for n in range(len(AROUND))
            ]
        )
        lane = lax.broadcasted_iota(jnp.int32, meta.shape, 1) // INSTR
        wide = meta.astype(F32)
        chosen = below(*[jnp.where(lane == n, wide, 0.0) for n in range(len(AROUND))]).astype(BF16)
        encoded = gelu(dot_nt(records, first) + dot(chosen, table)).astype(BF16)
        lifted = gelu(dot(encoded, lift))
        tokens = dot_nt(weigh, meta)
        sums = []
        for n in range(len(AROUND)):
            part = lifted[n * slots : (n + 1) * slots]
            part = with_ones(
                below(*[part[:, level * width : (level + 1) * width] for level in range(LEV)])
            )
            token = tokens[n : n + 1]
            token = jnp.concatenate([token + float(level) for level in range(LEV)], axis=1)
            if token.shape[1] == LANES:
                hot = codes[n] == token
            else:
                hot = codes[n][:, :1] == token
            sums.append(dot(jnp.where(hot, 1.0, 0.0).astype(BF16), part))
        return below(*sums)

    sums = scatter(0)
    if sources > chunk:
        sums = lax.fori_loop(
            1, sources // chunk, lambda step, total: total + scatter(step * chunk), sums
        )

    pieces, spans, start = [], [], 0
    for (dy, dx), parts in zip(AROUND, plan):
        for part in parts:
            top, high, left, wide = part
            count = tokens_of(part)
            if dx:
                ref = west_ref if dx < 0 else east_ref
                top = {-1: 0, 0: top + HLAT, 1: lat_cells + HLAT}[dy]
                left = 0
            elif dy:
                ref, top = (north_ref, 0) if dy < 0 else (south_ref, 0)
            else:
                ref = back_ref
            piece = ref[top : top + high, left : left + wide].reshape(count, width).astype(F32)
            full = padded(count)
            if full > count:
                piece = below(piece, jnp.zeros((full - count, width), F32))
            pieces.append(piece)
            spans.append((start, count, full))
            start += full
    share = 1.0 / (1.0 + sums[:, width : width + 1])
    latent = ((below(*pieces) + sums[:, :width]) * share).astype(BF16).astype(F32)
    normed = normalise(latent, gain_one_ref[...].astype(F32))

    def piece_of(tile, number):
        at = sum(len(parts) for parts in plan[:tile]) + number
        start, count, _ = spans[at]
        return normed[start : start + count]

    own = 4
    begin = spans[sum(len(parts) for parts in plan[:own])][0]
    groups = [padded(tokens_of(part)) for part in plan[own]]
    end = begin + sum(groups)
    windows = []
    for i, dy in enumerate((-1, 0, 1)):
        for j, dx in enumerate((-1, 0, 1)):
            window = [piece_of(own, 3 * i + j)]
            if dy:
                window.append(piece_of(3 * (dy + 1) + 1, j))
            if dx:
                window.append(piece_of(3 + dx + 1, i))
            if dy and dx:
                window.append(piece_of(3 * (dy + 1) + dx + 1, 0))
            windows.append(window)
    tokens = below(*[piece for window in windows for piece in window]).astype(BF16)
    weight = attn_ref[...]
    head = width // HEADS
    keys = dot(tokens, weight[:, width : 2 * width]).astype(BF16)
    values = with_ones(dot(tokens, weight[:, 2 * width :]))
    query = dot(normed[begin:end].astype(BF16), weight[:, :width]) * head ** (-0.5)

    head_of = lax.broadcasted_iota(jnp.int32, (1, width), 1) // head
    many = WLAT * WLON * LEV
    corner = HLAT * HLON * LEV
    key = lax.broadcasted_iota(jnp.int32, (1, many), 1)
    mixed, start = [], 0
    for w, rows in enumerate(groups):
        part = query[start : start + rows]
        stacked = below(*[jnp.where(head_of == h, part, 0.0) for h in range(HEADS)]).astype(BF16)
        scores = dot_nt(stacked, keys[w * many : (w + 1) * many])
        if w // 3 != 1:
            if w % 3 == 1:
                inside = key < 2 * corner
            else:
                inside = (key < corner) | ((key >= 2 * corner) & (key < 3 * corner))
            scores = jnp.where(inside | (scalars_ref[w // 3] == 0), scores, -1e30)
        largest = jnp.max(scores, axis=-1, keepdims=True)
        raised = jnp.exp(scores - largest).astype(BF16)
        product = dot(raised, values[w * many : (w + 1) * many])
        product = product[:, :width] * (1.0 / product[:, width : width + 1])
        total = jnp.zeros((rows, width), F32)
        for h in range(HEADS):
            total = jnp.where(head_of == h, product[h * rows : (h + 1) * rows], total)
        mixed.append(total)
        start += rows
    mixed = below(*mixed).astype(BF16)

    after = (latent[begin:end] + dot(mixed, mix_ref[...])).astype(BF16).astype(F32)
    normed_two = normalise(after, gain_two_ref[...].astype(F32)).astype(BF16)
    hidden = gelu(dot(normed_two, up_ref[...])).astype(BF16)
    result = after + dot_nt(hidden, down_ref[...])
    start = 0
    for part, rows in zip(plan[own], groups):
        top, high, left, wide = part
        piece = result[start : start + tokens_of(part)].astype(BF16)
        out_ref[top : top + high, left : left + wide] = piece.reshape(high, wide, LEV, width)
        start += rows


def local(
    record_values,
    record_cell,
    record_instrument,
    block_counts,
    background,
    input_weight,
    instrument_table,
    lift_weight,
    first_gain,
    attn_weight,
    mix_weight,
    second_gain,
    up_weight,
    down_weight,
):
    lat_cells, lon_cells, _, width = background.shape
    tiles_lat = record_values.shape[1]

    north = shifted(background[lat_cells - HLAT :], "lat", 1, wraps=False)
    south = shifted(background[:HLAT], "lat", -1, wraps=False)
    sent = packed(record_values, record_cell, record_instrument, block_counts, lon_cells)
    sent, north, south = lax.optimization_barrier((sent, north, south))
    received = lax.all_to_all(sent, ("lon", "lat"), split_axis=0, concat_axis=0, tiled=True)

    def columns(low, end):
        return jnp.concatenate(
            [north[:, low:end], background[:, low:end], south[:, low:end]], axis=0
        )

    west = shifted(columns(lon_cells - HLON, lon_cells), "lon", 1)
    east = shifted(columns(0, HLON), "lon", -1)

    lat = lax.axis_index("lat")
    scalars = jnp.stack([lat == 0, lat < 0, lat == tiles_lat - 1]).astype(jnp.int32)
    vmem = pl.BlockSpec(memory_space=pltpu.VMEM)
    return pl.pallas_call(
        functools.partial(block_kernel, rectangles(lat_cells, lon_cells)),
        out_shape=jax.ShapeDtypeStruct(background.shape, BF16),
        in_specs=[pl.BlockSpec(memory_space=pltpu.SMEM)] + [vmem] * 15,
        out_specs=vmem,
        compiler_params=pltpu.CompilerParams(vmem_limit_bytes=LIMIT),
    )(
        scalars,
        received,
        north,
        south,
        west,
        east,
        background,
        input_weight.T,
        instrument_table,
        lift_weight,
        first_gain.reshape(1, width),
        attn_weight,
        mix_weight,
        second_gain.reshape(1, width),
        up_weight,
        down_weight.T,
    )


def solution(mesh):
    placed = (
        P("lon", "lat", None, None),
        P("lon", "lat", None),
        P("lon", "lat", None),
        P("lon", "lat"),
        P("lat", "lon", None, None),
        P(),
        P(),
        P(),
        P(),
        P(),
        P(),
        P(),
        P(),
        P(),
    )
    return jax.shard_map(
        local, mesh=mesh, in_specs=placed, out_specs=P("lat", "lon", None, None), check_vma=False
    )
```

```python
import functools

import jax
import jax.numpy as jnp
from jax import lax
from jax.experimental import pallas as pl
from jax.experimental.pallas import tpu as pltpu
from jax.sharding import PartitionSpec as P

HEADS = 6
INSTR = 8
LEV = 2
WLAT = 6
WLON = 12
HLAT = WLAT // 2
HLON = WLON // 2
LANES = 128
PAD = 256
CHUNK = 32
LIMIT = 40 * 2**20
BF16 = jnp.bfloat16
F32 = jnp.float32

AROUND = [(dy, dx) for dy in (-1, 0, 1) for dx in (-1, 0, 1)]
ROWS = INSTR * len(AROUND)
COLS = ROWS + len(AROUND)


def shifted(value, axis, steps, wraps=True):
    count = lax.axis_size(axis)
    pairs = [(source, (source + steps) % count) for source in range(count)]
    if not wraps:
        pairs = [pair for pair in pairs if pair[1] == pair[0] + steps]
    return lax.ppermute(value, axis, pairs)


def rectangles(lat_cells, lon_cells):
    lat = {-1: [(lat_cells - HLAT, HLAT)], 1: [(0, HLAT)]}
    lat[0] = [(0, HLAT), (HLAT, lat_cells - WLAT), (lat_cells - HLAT, HLAT)]
    lon = {-1: [(lon_cells - HLON, HLON)], 1: [(0, HLON)]}
    lon[0] = [(0, HLON), (HLON, lon_cells - WLON), (lon_cells - HLON, HLON)]
    return [
        [(top, high, left, wide) for top, high in lat[dy] for left, wide in lon[dx]]
        for dy, dx in AROUND
    ]


def tokens_of(part):
    return part[1] * part[3] * LEV


def padded(count):
    return -(-count // 8) * 8


def gelu(x):
    return jax.nn.gelu(x)


def normalise(wide, gain):
    average = jnp.mean(wide, axis=-1, keepdims=True)
    centred = wide - average
    spread = jnp.mean(centred * centred, axis=-1, keepdims=True)
    return centred * lax.rsqrt(spread + 1e-05) * gain


def dot(a, b):
    return jnp.dot(a, b, preferred_element_type=F32)


def dot_nt(a, b):
    return lax.dot_general(a, b, (((1,), (1,)), ((), ())), preferred_element_type=F32)


def with_ones(tensor):
    ones = jnp.ones((tensor.shape[0], PAD - tensor.shape[1]), F32)
    return jnp.concatenate([tensor, ones], axis=1).astype(BF16)


def below(*pieces):
    return jnp.concatenate(pieces, axis=0) if len(pieces) > 1 else pieces[0]


def pack_kernel(
    values_ref,
    cell_ref,
    tag_ref,
    count_ref,
    back_ref,
    out_ref,
    up_ref,
    down_ref,
    left_ref,
    right_ref,
    values,
    cells,
    tags,
    held,
    sem,
):
    tiles_lon, tiles_lat, capacity, _ = values_ref.shape
    lat_cells, lon_cells = back_ref.shape[:2]
    strips = [
        (back_ref.at[:HLAT], up_ref),
        (back_ref.at[lat_cells - HLAT :], down_ref),
        (back_ref.at[:, :HLON], left_ref),
        (back_ref.at[:, lon_cells - HLON :], right_ref),
    ]
    copies = [
        pltpu.make_async_copy(cell_ref, cells, sem.at[0]),
        pltpu.make_async_copy(tag_ref, tags, sem.at[1]),
        pltpu.make_async_copy(count_ref, held, sem.at[2]),
        pltpu.make_async_copy(values_ref, values, sem.at[3]),
    ]
    copies += [
        pltpu.make_async_copy(source, strip, sem.at[4 + n])
        for n, (source, strip) in enumerate(strips)
    ]
    for copy in copies:
        copy.start()
    for copy in copies[:3]:
        copy.wait()
    counts = below(*[held[tile : tile + 1, :] for tile in range(tiles_lat) for _ in range(capacity)])
    cell = cells[...]
    slot = lax.broadcasted_iota(jnp.int32, cell.shape, 0) % capacity
    row = cell // lon_cells
    fields = [jnp.where(slot < counts, row, 255), cell - row * lon_cells, tags[...]]
    rows, columns, kinds = (field.astype(F32) for field in fields)
    lane = lax.broadcasted_iota(jnp.int32, (cell.shape[0], LANES), 1)
    kind_of = (lane % INSTR).astype(F32)
    marks = [
        ((lane < ROWS) & (lane // INSTR == n)) | (lane == ROWS + n) | (lane == COLS + n)
        for n in range(len(AROUND))
    ]
    turned = []
    for lon in range(tiles_lon):
        meta = jnp.where(kind_of == kinds[:, lon : lon + 1], 1.0, 0.0)
        meta = jnp.where(lane >= ROWS, rows[:, lon : lon + 1], meta)
        meta = jnp.where(lane >= COLS, columns[:, lon : lon + 1], meta)
        turns = {0: meta}
        for dy in (-1, 1):
            by = dy * capacity % meta.shape[0]
            turns[dy] = below(meta[by:], meta[:by])
        turned.append(turns)
    for lon in range(tiles_lon):
        meta = jnp.zeros(lane.shape, F32)
        for mark, (dy, dx) in zip(marks, AROUND):
            meta = jnp.where(mark, turned[(lon + dx) % tiles_lon][dy], meta)
        out_ref[lon, :, len(AROUND)] = meta.astype(BF16).reshape(tiles_lat, capacity, LANES)
    copies[3].wait()
    for n, (dy, dx) in enumerate(AROUND):
        spans = {0: [(0, tiles_lat)], 1: [(0, tiles_lat - 1), (tiles_lat - 1, tiles_lat)]}
        spans[-1] = [(0, 1), (1, tiles_lat)]

        def copy_tiles(lon, n=n, dx=dx, dy=dy, spans=spans[dy]):
            source = lax.rem(lon + dx + tiles_lon, tiles_lon)
            for low, end in spans:
                first = (low + dy) % tiles_lat
                out_ref[lon, low:end, n] = values[source, first : first + end - low]

        if tiles_lon <= 8:
            for lon in range(tiles_lon):
                copy_tiles(lon)
        else:
            pl.loop(0, tiles_lon)(copy_tiles)
    for copy in copies[4:]:
        copy.wait()


def packed(record_values, record_cell, record_instrument, block_counts, background):
    tiles_lon, tiles_lat, capacity, wide = record_values.shape
    anywhere = pl.BlockSpec(memory_space=pltpu.HBM)
    ints = pltpu.VMEM((tiles_lat * capacity, tiles_lon), jnp.int32)
    shape = (tiles_lon, tiles_lat, len(AROUND) + 1, capacity, wide)
    lat_cells, lon_cells, levels, width = background.shape
    across = jax.ShapeDtypeStruct((HLAT, lon_cells, levels, width), BF16)
    along = jax.ShapeDtypeStruct((lat_cells, HLON, levels, width), BF16)
    out, *strips = pl.pallas_call(
        pack_kernel,
        out_shape=[jax.ShapeDtypeStruct(shape, BF16), across, across, along, along],
        in_specs=[anywhere] * 5,
        out_specs=[pl.BlockSpec(memory_space=pltpu.VMEM)] * 5,
        scratch_shapes=[
            pltpu.VMEM(record_values.shape, BF16),
            ints,
            ints,
            pltpu.VMEM((tiles_lat, tiles_lon), jnp.int32),
            pltpu.SemaphoreType.DMA((8,)),
        ],
        compiler_params=pltpu.CompilerParams(vmem_limit_bytes=56 * 2**20),
    )(
        record_values,
        record_cell.transpose(1, 2, 0).reshape(-1, tiles_lon),
        record_instrument.transpose(1, 2, 0).reshape(-1, tiles_lon),
        block_counts.T,
        background,
    )
    return out.reshape((-1,) + shape[2:]), *strips


def token_codes(part, lon_cells):
    top, high, left, wide = part
    count = tokens_of(part)
    place = lax.broadcasted_iota(jnp.int32, (padded(count), LANES), 0)
    code = place + (top * lon_cells + left) * LEV
    for row in range(1, high):
        step = (lon_cells - wide) * LEV
        code = code + jnp.where(place >= row * wide * LEV, step, 0)
    return jnp.where(place < count, code, -8).astype(F32)


def column_entries(plan, columns):
    own = [(4, 3 * i + j) for i in range(3) for j in columns]
    around = [(tile, j) for tile in (1, 7) for j in columns]
    for j in columns:
        if j != 1:
            around += [(3 + j, i) for i in range(3)] + [(j, 0), (6 + j, 0)]
    return own + around


def scattered(recv_ref, first_ref, table_ref, lift_ref, plan, lon_cells):
    sources, _, capacity, _ = recv_ref.shape
    width = table_ref.shape[1]
    chunk = min(CHUNK, sources)
    slots = chunk * capacity
    first, lift = first_ref[...], lift_ref[...]
    table = below(*[table_ref[...].astype(F32)] * (LANES // INSTR)).astype(BF16)
    lane = lax.broadcasted_iota(jnp.int32, (16, LANES), 1)
    sub = lax.broadcasted_iota(jnp.int32, (16, LANES), 0)
    weigh = jnp.where(lane == ROWS + sub, float(lon_cells * LEV), 0.0)
    weigh = jnp.where(lane == COLS + sub, float(LEV), weigh).astype(BF16)
    codes = [below(*[token_codes(part, lon_cells) for part in parts]) for parts in plan]

    def scatter(begin):
        meta = recv_ref[pl.ds(begin, chunk), len(AROUND)].reshape(slots, LANES)
        records = below(
            *[
                recv_ref[pl.ds(begin, chunk), n].reshape(slots, LANES)
                for n in range(len(AROUND))
            ]
        )
        lane = lax.broadcasted_iota(jnp.int32, meta.shape, 1) // INSTR
        wide = meta.astype(F32)
        chosen = below(*[jnp.where(lane == n, wide, 0.0) for n in range(len(AROUND))]).astype(BF16)
        encoded = gelu(dot_nt(records, first) + dot(chosen, table)).astype(BF16)
        lifted = gelu(dot(encoded, lift))
        tokens = dot_nt(weigh, meta)
        sums = []
        for n in range(len(AROUND)):
            part = lifted[n * slots : (n + 1) * slots]
            part = with_ones(
                below(*[part[:, level * width : (level + 1) * width] for level in range(LEV)])
            )
            token = tokens[n : n + 1]
            token = jnp.concatenate([token + float(level) for level in range(LEV)], axis=1)
            if token.shape[1] == LANES:
                hot = codes[n] == token
            else:
                hot = codes[n][:, :1] == token
            sums.append(dot(jnp.where(hot, 1.0, 0.0).astype(BF16), part))
        return tuple(sums)

    sums = scatter(0)
    if sources > chunk:
        sums = lax.fori_loop(
            1,
            sources // chunk,
            lambda step, total: tuple(a + b for a, b in zip(total, scatter(step * chunk))),
            sums,
        )
    return sums


def worked(plan, columns, sums, borders, weights, scalars_ref, put):
    back_ref, north_ref, south_ref, west_ref, east_ref = borders
    gain_one_ref, attn_ref, mix_ref, gain_two_ref, up_ref, down_ref = weights
    lat_cells, width = back_ref.shape[0], back_ref.shape[3]
    pieces, spans, start = [], {}, 0
    for tile, number in column_entries(plan, columns):
        dy, dx = AROUND[tile]
        part = plan[tile][number]
        top, high, left, wide = part
        count = tokens_of(part)
        if dx:
            ref = west_ref if dx < 0 else east_ref
            top, left = {-1: 0, 0: top + HLAT, 1: lat_cells + HLAT}[dy], 0
        elif dy:
            ref, top = (north_ref, 0) if dy < 0 else (south_ref, 0)
        else:
            ref = back_ref
        piece = ref[top : top + high, left : left + wide].reshape(count, width).astype(F32)
        full = padded(count)
        if full > count:
            piece = below(piece, jnp.zeros((full - count, width), F32))
        pieces.append(piece)
        spans[tile, number] = (start, count)
        start += full
    share = 1.0 / (1.0 + sums[:, width : width + 1])
    latent = ((below(*pieces) + sums[:, :width]) * share).astype(BF16).astype(F32)
    normed = normalise(latent, gain_one_ref[...].astype(F32))

    def piece_of(tile, number):
        start, count = spans[tile, number]
        return normed[start : start + count]

    places = [(i, j) for i in range(3) for j in columns]
    groups = [padded(tokens_of(plan[4][3 * i + j])) for i, j in places]
    end = sum(groups)
    windows = []
    for i, j in places:
        window = [piece_of(4, 3 * i + j)]
        if i != 1:
            window.append(piece_of(3 * i + 1, j))
        if j != 1:
            window.append(piece_of(3 + j, i))
        if i != 1 and j != 1:
            window.append(piece_of(3 * i + j, 0))
        windows.append(window)
    tokens = below(*[piece for window in windows for piece in window]).astype(BF16)
    weight = attn_ref[...]
    head = width // HEADS
    keys = dot(tokens, weight[:, width : 2 * width]).astype(BF16)
    values = with_ones(dot(tokens, weight[:, 2 * width :]))
    query = dot(normed[:end].astype(BF16), weight[:, :width]) * head ** (-0.5)

    head_of = lax.broadcasted_iota(jnp.int32, (1, width), 1) // head
    many = WLAT * WLON * LEV
    corner = HLAT * HLON * LEV
    key = lax.broadcasted_iota(jnp.int32, (1, many), 1)
    mixed, start = [], 0
    for w, ((i, j), rows) in enumerate(zip(places, groups)):
        part = query[start : start + rows]
        stacked = below(*[jnp.where(head_of == h, part, 0.0) for h in range(HEADS)]).astype(BF16)
        scores = dot_nt(stacked, keys[w * many : (w + 1) * many])
        if i != 1:
            if j == 1:
                inside = key < 2 * corner
            else:
                inside = (key < corner) | ((key >= 2 * corner) & (key < 3 * corner))
            scores = jnp.where(inside | (scalars_ref[i] == 0), scores, -1e30)
        largest = jnp.max(scores, axis=-1, keepdims=True)
        raised = jnp.exp(scores - largest).astype(BF16)
        product = dot(raised, values[w * many : (w + 1) * many])
        product = product[:, :width] * (1.0 / product[:, width : width + 1])
        total = jnp.zeros((rows, width), F32)
        for h in range(HEADS):
            total = jnp.where(head_of == h, product[h * rows : (h + 1) * rows], total)
        mixed.append(total)
        start += rows
    mixed = below(*mixed).astype(BF16)

    after = (latent[:end] + dot(mixed, mix_ref[...])).astype(BF16).astype(F32)
    normed_two = normalise(after, gain_two_ref[...].astype(F32)).astype(BF16)
    hidden = gelu(dot(normed_two, up_ref[...])).astype(BF16)
    result = after + dot_nt(hidden, down_ref[...])
    start = 0
    for (i, j), rows in zip(places, groups):
        part = plan[4][3 * i + j]
        piece = result[start : start + tokens_of(part)].astype(BF16)
        put(part, j, piece.reshape(part[1], part[3], LEV, width))
        start += rows


def middle_kernel(
    plan,
    scalars_ref,
    recv_ref,
    north_ref,
    south_ref,
    back_ref,
    first_ref,
    table_ref,
    lift_ref,
    *refs,
):
    *weights, out_ref, rest_ref, held_ref, sem = refs
    sums = scattered(recv_ref, first_ref, table_ref, lift_ref, plan, back_ref.shape[1])

    def sum_of(tile, number):
        start = sum(padded(tokens_of(part)) for part in plan[tile][:number])
        return sums[tile][start : start + padded(tokens_of(plan[tile][number]))]

    rest_ref[...] = below(*[sum_of(*entry) for entry in column_entries(plan, (0, 2))])
    mine = below(*[sum_of(*entry) for entry in column_entries(plan, (1,))])
    left, wide = plan[4][4][2:]

    def put(part, _, piece):
        held_ref[part[0] : part[0] + part[1]] = piece

    borders = (back_ref, north_ref, south_ref, None, None)
    worked(plan, (1,), mine, borders, weights, scalars_ref, put)
    copy = pltpu.make_async_copy(held_ref, out_ref.at[:, left : left + wide], sem.at[0])
    copy.start()
    copy.wait()


def side_kernel(
    plan,
    scalars_ref,
    rest_ref,
    north_ref,
    south_ref,
    west_ref,
    east_ref,
    back_ref,
    *refs,
):
    *weights, _, out_ref, held_ref, sem = refs

    def put(part, j, piece):
        held_ref[j // 2, part[0] : part[0] + part[1]] = piece

    borders = (back_ref, north_ref, south_ref, west_ref, east_ref)
    worked(plan, (0, 2), rest_ref[...], borders, weights, scalars_ref, put)
    copies = []
    for n, number in enumerate((0, 2)):
        left, wide = plan[4][number][2:]
        copies.append(
            pltpu.make_async_copy(held_ref.at[n], out_ref.at[:, left : left + wide], sem.at[n])
        )
        copies[n].start()
    for copy in copies:
        copy.wait()


def local(
    record_values,
    record_cell,
    record_instrument,
    block_counts,
    background,
    input_weight,
    instrument_table,
    lift_weight,
    first_gain,
    attn_weight,
    mix_weight,
    second_gain,
    up_weight,
    down_weight,
):
    lat_cells, lon_cells, _, width = background.shape
    tiles_lat = record_values.shape[1]

    sent, up, down, left, right = packed(
        record_values, record_cell, record_instrument, block_counts, background
    )
    received = lax.all_to_all(sent, ("lon", "lat"), split_axis=0, concat_axis=0, tiled=True)
    north = shifted(down, "lat", 1, wraps=False)
    south = shifted(up, "lat", -1, wraps=False)
    right = jnp.concatenate([north[:, lon_cells - HLON :], right, south[:, lon_cells - HLON :]], axis=0)
    left = jnp.concatenate([north[:, :HLON], left, south[:, :HLON]], axis=0)
    west = shifted(right, "lon", 1)
    east = shifted(left, "lon", -1)

    lat = lax.axis_index("lat")
    scalars = jnp.stack([lat == 0, lat < 0, lat == tiles_lat - 1]).astype(jnp.int32)
    plan = rectangles(lat_cells, lon_cells)
    rest = sum(
        padded(tokens_of(plan[tile][number])) for tile, number in column_entries(plan, (0, 2))
    )
    weights = [
        first_gain.reshape(1, width),
        attn_weight,
        mix_weight,
        second_gain.reshape(1, width),
        up_weight,
        down_weight.T,
    ]
    smem = pl.BlockSpec(memory_space=pltpu.SMEM)
    vmem = pl.BlockSpec(memory_space=pltpu.VMEM)
    anywhere = pl.BlockSpec(memory_space=pl.ANY)
    params = pltpu.CompilerParams(vmem_limit_bytes=LIMIT)
    result = jax.ShapeDtypeStruct(background.shape, BF16)
    middle, rest = pl.pallas_call(
        functools.partial(middle_kernel, plan),
        out_shape=[result, jax.ShapeDtypeStruct((rest, PAD), F32)],
        in_specs=[smem] + [vmem] * (7 + len(weights)),
        out_specs=[anywhere, vmem],
        scratch_shapes=[
            pltpu.VMEM((lat_cells, lon_cells - WLON, LEV, width), BF16),
            pltpu.SemaphoreType.DMA((1,)),
        ],
        compiler_params=params,
        cost_estimate=pl.CostEstimate(
            flops=4 * 10**9, bytes_accessed=4 * 10**6, transcendentals=10**6
        ),
    )(
        scalars,
        received,
        north,
        south,
        background,
        input_weight.T,
        instrument_table,
        lift_weight,
        *weights,
    )
    return pl.pallas_call(
        functools.partial(side_kernel, plan),
        out_shape=result,
        in_specs=[smem] + [vmem] * (6 + len(weights)) + [anywhere],
        out_specs=anywhere,
        scratch_shapes=[
            pltpu.VMEM((2, lat_cells, HLON, LEV, width), BF16),
            pltpu.SemaphoreType.DMA((2,)),
        ],
        input_output_aliases={7 + len(weights): 0},
        compiler_params=params,
        cost_estimate=pl.CostEstimate(
            flops=3 * 10**9, bytes_accessed=4 * 10**6, transcendentals=10**6
        ),
    )(scalars, rest, north, south, west, east, background, *weights, middle)


def solution(mesh):
    placed = (
        P("lon", "lat", None, None),
        P("lon", "lat", None),
        P("lon", "lat", None),
        P("lon", "lat"),
        P("lat", "lon", None, None),
        P(),
        P(),
        P(),
        P(),
        P(),
        P(),
        P(),
        P(),
        P(),
    )
    return jax.shard_map(
        local, mesh=mesh, in_specs=placed, out_specs=P("lat", "lon", None, None), check_vma=False
    )
```

```python
import functools

import jax
import jax.numpy as jnp
from jax import lax
from jax.experimental import pallas as pl
from jax.experimental.pallas import tpu as pltpu
from jax.sharding import PartitionSpec as P

HEADS = 6
INSTR = 8
LEV = 2
WLAT = 6
WLON = 12
HLAT = WLAT // 2
HLON = WLON // 2
LANES = 128
PAD = 256
CHUNK = 32
LIMIT = 40 * 2**20
BF16 = jnp.bfloat16
F32 = jnp.float32

AROUND = [(dy, dx) for dy in (-1, 0, 1) for dx in (-1, 0, 1)]
ROWS = INSTR * len(AROUND)
COLS = ROWS + len(AROUND)


def shifted(value, axis, steps, wraps=True):
    count = lax.axis_size(axis)
    pairs = [(source, (source + steps) % count) for source in range(count)]
    if not wraps:
        pairs = [pair for pair in pairs if pair[1] == pair[0] + steps]
    return lax.ppermute(value, axis, pairs)


def rectangles(lat_cells, lon_cells):
    lat = {-1: [(lat_cells - HLAT, HLAT)], 1: [(0, HLAT)]}
    lat[0] = [(0, HLAT), (HLAT, lat_cells - WLAT), (lat_cells - HLAT, HLAT)]
    lon = {-1: [(lon_cells - HLON, HLON)], 1: [(0, HLON)]}
    lon[0] = [(0, HLON), (HLON, lon_cells - WLON), (lon_cells - HLON, HLON)]
    return [
        [(top, high, left, wide) for top, high in lat[dy] for left, wide in lon[dx]]
        for dy, dx in AROUND
    ]


def tokens_of(part):
    return part[1] * part[3] * LEV


def padded(count):
    return -(-count // 8) * 8


def gelu(x):
    half = 0.5 * x
    inner = x * (0.7978845608028654 + 0.035677408136300125 * (x * x))
    return half + half * jnp.tanh(inner)


def normalise(wide, gain):
    average = jnp.mean(wide, axis=-1, keepdims=True)
    centred = wide - average
    spread = jnp.mean(centred * centred, axis=-1, keepdims=True)
    return centred * lax.rsqrt(spread + 1e-05) * gain


def dot(a, b):
    return jnp.dot(a, b, preferred_element_type=F32)


def dot_nt(a, b):
    return lax.dot_general(a, b, (((1,), (1,)), ((), ())), preferred_element_type=F32)


def with_ones(tensor):
    ones = jnp.ones((tensor.shape[0], PAD - tensor.shape[1]), F32)
    return jnp.concatenate([tensor, ones], axis=1).astype(BF16)


def below(*pieces):
    return jnp.concatenate(pieces, axis=0) if len(pieces) > 1 else pieces[0]


def pack_kernel(
    values_ref,
    cell_ref,
    tag_ref,
    count_ref,
    back_ref,
    *refs,
):
    out_ref, up_ref, down_ref, left_ref, right_ref, values, cells, tags, held, sem = refs
    tiles_lon, tiles_lat, capacity, _ = values_ref.shape
    lat_cells, lon_cells = back_ref.shape[:2]
    strips = [
        (back_ref.at[:HLAT], up_ref),
        (back_ref.at[lat_cells - HLAT :], down_ref),
        (back_ref.at[:, :HLON], left_ref.at[HLAT : HLAT + lat_cells]),
        (back_ref.at[:, lon_cells - HLON :], right_ref.at[HLAT : HLAT + lat_cells]),
    ]
    copies = [
        pltpu.make_async_copy(cell_ref, cells, sem.at[0]),
        pltpu.make_async_copy(tag_ref, tags, sem.at[1]),
        pltpu.make_async_copy(count_ref, held, sem.at[2]),
        pltpu.make_async_copy(values_ref, values, sem.at[3]),
    ]
    copies += [
        pltpu.make_async_copy(source, strip, sem.at[4 + n])
        for n, (source, strip) in enumerate(strips)
    ]
    for copy in copies:
        copy.start()
    for copy in copies[:3]:
        copy.wait()
    counts = below(*[held[tile : tile + 1, :] for tile in range(tiles_lat) for _ in range(capacity)])
    cell = cells[...]
    slot = lax.broadcasted_iota(jnp.int32, cell.shape, 0) % capacity
    row = cell // lon_cells
    fields = [jnp.where(slot < counts, row, 255), cell - row * lon_cells, tags[...]]
    rows, columns, kinds = (field.astype(F32) for field in fields)
    lane = lax.broadcasted_iota(jnp.int32, (cell.shape[0], LANES), 1)
    kind_of = (lane % INSTR).astype(F32)
    marks = [
        ((lane < ROWS) & (lane // INSTR == n)) | (lane == ROWS + n) | (lane == COLS + n)
        for n in range(len(AROUND))
    ]
    turned = []
    for lon in range(tiles_lon):
        meta = jnp.where(kind_of == kinds[:, lon : lon + 1], 1.0, 0.0)
        meta = jnp.where(lane >= ROWS, rows[:, lon : lon + 1], meta)
        meta = jnp.where(lane >= COLS, columns[:, lon : lon + 1], meta)
        turns = {0: meta}
        for dy in (-1, 1):
            by = dy * capacity % meta.shape[0]
            turns[dy] = below(meta[by:], meta[:by])
        turned.append(turns)
    for lon in range(tiles_lon):
        meta = jnp.zeros(lane.shape, F32)
        for mark, (dy, dx) in zip(marks, AROUND):
            meta = jnp.where(mark, turned[(lon + dx) % tiles_lon][dy], meta)
        out_ref[lon, :, len(AROUND)] = meta.astype(BF16).reshape(tiles_lat, capacity, LANES)
    copies[3].wait()
    for n, (dy, dx) in enumerate(AROUND):
        spans = {0: [(0, tiles_lat)], 1: [(0, tiles_lat - 1), (tiles_lat - 1, tiles_lat)]}
        spans[-1] = [(0, 1), (1, tiles_lat)]

        def copy_tiles(lon, n=n, dx=dx, dy=dy, spans=spans[dy]):
            source = lax.rem(lon + dx + tiles_lon, tiles_lon)
            for low, end in spans:
                first = (low + dy) % tiles_lat
                out_ref[lon, low:end, n] = values[source, first : first + end - low]

        if tiles_lon <= 8:
            for lon in range(tiles_lon):
                copy_tiles(lon)
        else:
            pl.loop(0, tiles_lon)(copy_tiles)
    for copy in copies[4:]:
        copy.wait()


def packed(record_values, record_cell, record_instrument, block_counts, background):
    tiles_lon, tiles_lat, capacity, wide = record_values.shape
    anywhere = pl.BlockSpec(memory_space=pltpu.HBM)
    ints = pltpu.VMEM((tiles_lat * capacity, tiles_lon), jnp.int32)
    shape = (tiles_lon, tiles_lat, len(AROUND) + 1, capacity, wide)
    lat_cells, lon_cells, levels, width = background.shape
    across = jax.ShapeDtypeStruct((HLAT, lon_cells, levels, width), BF16)
    along = jax.ShapeDtypeStruct((lat_cells + WLAT, HLON, levels, width), BF16)
    out, *strips = pl.pallas_call(
        pack_kernel,
        out_shape=[jax.ShapeDtypeStruct(shape, BF16), across, across, along, along],
        in_specs=[anywhere] * 5,
        out_specs=[pl.BlockSpec(memory_space=pltpu.VMEM)] * 5,
        scratch_shapes=[
            pltpu.VMEM(record_values.shape, BF16),
            ints,
            ints,
            pltpu.VMEM((tiles_lat, tiles_lon), jnp.int32),
            pltpu.SemaphoreType.DMA((8,)),
        ],
        compiler_params=pltpu.CompilerParams(vmem_limit_bytes=56 * 2**20),
        cost_estimate=pl.CostEstimate(
            flops=20 * 10**9, bytes_accessed=10**6, transcendentals=0
        ),
    )(
        record_values,
        record_cell.transpose(1, 2, 0).reshape(-1, tiles_lon),
        record_instrument.transpose(1, 2, 0).reshape(-1, tiles_lon),
        block_counts.T,
        background,
    )
    return out.reshape((-1,) + shape[2:]), *strips


def token_codes(part, lon_cells):
    top, high, left, wide = part
    count = tokens_of(part)
    place = lax.broadcasted_iota(jnp.int32, (padded(count), LANES), 0)
    code = place + (top * lon_cells + left) * LEV
    for row in range(1, high):
        step = (lon_cells - wide) * LEV
        code = code + jnp.where(place >= row * wide * LEV, step, 0)
    return jnp.where(place < count, code, -8).astype(F32)


def entries_of(windows):
    entries = [(4, 3 * i + j) for i, j in windows]
    for i, j in windows:
        if i != 1:
            entries.append((3 * i + 1, j))
        if j != 1:
            entries.append((3 + j, i))
        if i != 1 and j != 1:
            entries.append((3 * i + j, 0))
    return entries


def alternate(*chains):
    chains, begun = list(chains), 1
    while chains:
        for chain in chains[:begun]:
            if next(chain, None) is None:
                chains.remove(chain)
                begun -= 1
        begun += 1


def scattered(recv_ref, first_ref, table_ref, lift_ref, plan, lon_cells):
    sources, _, capacity, _ = recv_ref.shape
    width = table_ref.shape[1]
    chunk = min(CHUNK, sources)
    slots = chunk * capacity
    first, lift = first_ref[...], lift_ref[...]
    table = below(*[table_ref[...].astype(F32)] * (LANES // INSTR)).astype(BF16)
    lane = lax.broadcasted_iota(jnp.int32, (16, LANES), 1)
    sub = lax.broadcasted_iota(jnp.int32, (16, LANES), 0)
    weigh = jnp.where(lane == ROWS + sub, float(lon_cells * LEV), 0.0)
    weigh = jnp.where(lane == COLS + sub, float(LEV), weigh).astype(BF16)
    codes = [below(*[token_codes(part, lon_cells) for part in parts]) for parts in plan]

    def scatter(begin):
        meta = recv_ref[pl.ds(begin, chunk), len(AROUND)].reshape(slots, LANES)
        records = below(
            *[
                recv_ref[pl.ds(begin, chunk), n].reshape(slots, LANES)
                for n in range(len(AROUND))
            ]
        )
        lane = lax.broadcasted_iota(jnp.int32, meta.shape, 1) // INSTR
        wide = meta.astype(F32)
        chosen = below(*[jnp.where(lane == n, wide, 0.0) for n in range(len(AROUND))]).astype(BF16)
        encoded = gelu(dot_nt(records, first) + dot(chosen, table)).astype(BF16)
        lifted = gelu(dot(encoded, lift))
        tokens = dot_nt(weigh, meta)
        sums = []
        for n in range(len(AROUND)):
            part = lifted[n * slots : (n + 1) * slots]
            part = with_ones(
                below(*[part[:, level * width : (level + 1) * width] for level in range(LEV)])
            )
            token = tokens[n : n + 1]
            token = jnp.concatenate([token + float(level) for level in range(LEV)], axis=1)
            if token.shape[1] == LANES:
                hot = codes[n] == token
            else:
                hot = codes[n][:, :1] == token
            sums.append(dot(jnp.where(hot, 1.0, 0.0).astype(BF16), part))
        return tuple(sums)

    sums = scatter(0)
    if sources > chunk:
        sums = lax.fori_loop(
            1,
            sources // chunk,
            lambda step, total: tuple(a + b for a, b in zip(total, scatter(step * chunk))),
            sums,
        )
    return sums


def worked(plan, places, sum_of, borders, weights, scalars_ref, put):
    back_ref, north_ref, south_ref, west_ref, east_ref = borders
    gain_one_ref, attn_ref, mix_ref, gain_two_ref, up_ref, down_ref = weights
    lat_cells, width = back_ref.shape[0], back_ref.shape[3]
    pieces, spans, start = [], {}, 0
    for tile, number in entries_of(places):
        dy, dx = AROUND[tile]
        part = plan[tile][number]
        top, high, left, wide = part
        count = tokens_of(part)
        if dx:
            ref = west_ref if dx < 0 else east_ref
            top, left = {-1: 0, 0: top + HLAT, 1: lat_cells + HLAT}[dy], 0
        elif dy:
            ref, top = (north_ref, 0) if dy < 0 else (south_ref, 0)
        else:
            ref = back_ref
        piece = ref[top : top + high, left : left + wide].reshape(count, width).astype(F32)
        full = padded(count)
        if full > count:
            piece = below(piece, jnp.zeros((full - count, width), F32))
        pieces.append(piece)
        spans[tile, number] = (start, count)
        start += full
    sums = below(*[sum_of(*entry) for entry in entries_of(places)])
    share = 1.0 / (1.0 + sums[:, width : width + 1])
    latent = ((below(*pieces) + sums[:, :width]) * share).astype(BF16).astype(F32)
    normed = normalise(latent, gain_one_ref[...].astype(F32))
    yield True

    def piece_of(tile, number):
        start, count = spans[tile, number]
        return normed[start : start + count]

    groups = [padded(tokens_of(plan[4][3 * i + j])) for i, j in places]
    end = sum(groups)
    windows = []
    for i, j in places:
        window = [piece_of(4, 3 * i + j)]
        if i != 1:
            window.append(piece_of(3 * i + 1, j))
        if j != 1:
            window.append(piece_of(3 + j, i))
        if i != 1 and j != 1:
            window.append(piece_of(3 * i + j, 0))
        windows.append(window)
    tokens = below(*[piece for window in windows for piece in window]).astype(BF16)
    weight = attn_ref[...]
    head = width // HEADS
    keys = dot(tokens, weight[:, width : 2 * width]).astype(BF16)
    query = dot(normed[:end].astype(BF16), weight[:, :width]) * head ** (-0.5)
    values = with_ones(dot(tokens, weight[:, 2 * width :]))
    yield True

    head_of = lax.broadcasted_iota(jnp.int32, (1, width), 1) // head
    many = WLAT * WLON * LEV
    corner = HLAT * HLON * LEV
    key = lax.broadcasted_iota(jnp.int32, (1, many), 1)
    mixed, start = [], 0
    for w, ((i, j), rows) in enumerate(zip(places, groups)):
        part = query[start : start + rows]
        stacked = below(*[jnp.where(head_of == h, part, 0.0) for h in range(HEADS)]).astype(BF16)
        scores = dot_nt(stacked, keys[w * many : (w + 1) * many])
        yield True
        if i != 1:
            if j == 1:
                inside = key < 2 * corner
            else:
                inside = (key < corner) | ((key >= 2 * corner) & (key < 3 * corner))
            scores = jnp.where(inside | (scalars_ref[i] == 0), scores, -1e30)
        largest = jnp.max(scores, axis=-1, keepdims=True)
        raised = jnp.exp(scores - largest).astype(BF16)
        product = dot(raised, values[w * many : (w + 1) * many])
        yield True
        product = product[:, :width] * (1.0 / product[:, width : width + 1])
        total = jnp.zeros((rows, width), F32)
        for h in range(HEADS):
            total = jnp.where(head_of == h, product[h * rows : (h + 1) * rows], total)
        mixed.append(total)
        start += rows
    mixed = below(*mixed).astype(BF16)

    after = (latent[:end] + dot(mixed, mix_ref[...])).astype(BF16).astype(F32)
    yield True
    normed_two = normalise(after, gain_two_ref[...].astype(F32)).astype(BF16)
    hidden = dot(normed_two, up_ref[...])
    yield True
    result = after + dot_nt(gelu(hidden).astype(BF16), down_ref[...])
    yield True
    start = 0
    for (i, j), rows in zip(places, groups):
        part = plan[4][3 * i + j]
        piece = result[start : start + tokens_of(part)].astype(BF16)
        put(part, j, piece.reshape(part[1], part[3], LEV, width))
        start += rows


MIDDLE = [[(0, 1), (2, 1)], [(1, 1)]]
SIDES = [[(0, 0), (1, 0), (2, 0)], [(0, 2), (1, 2), (2, 2)]]


def side_entries():
    return [entry for places in SIDES for entry in entries_of(places)]


def middle_kernel(
    plan,
    scalars_ref,
    recv_ref,
    north_ref,
    south_ref,
    back_ref,
    first_ref,
    table_ref,
    lift_ref,
    *refs,
):
    *weights, out_ref, rest_ref, held_ref, sem = refs
    sums = scattered(recv_ref, first_ref, table_ref, lift_ref, plan, back_ref.shape[1])

    def sum_of(tile, number):
        start = sum(padded(tokens_of(part)) for part in plan[tile][:number])
        return sums[tile][start : start + padded(tokens_of(plan[tile][number]))]

    rest_ref[...] = below(*[sum_of(*entry) for entry in side_entries()])
    left, wide = plan[4][4][2:]

    def put(part, _, piece):
        held_ref[part[0] : part[0] + part[1]] = piece

    borders = (back_ref, north_ref, south_ref, None, None)
    alternate(
        *[worked(plan, places, sum_of, borders, weights, scalars_ref, put) for places in MIDDLE]
    )
    copy = pltpu.make_async_copy(held_ref, out_ref.at[:, left : left + wide], sem.at[0])
    copy.start()
    copy.wait()


def side_kernel(
    plan,
    scalars_ref,
    rest_ref,
    north_ref,
    south_ref,
    west_ref,
    east_ref,
    back_ref,
    *refs,
):
    *weights, _, out_ref, held_ref, sem = refs
    spans, start = {}, 0
    for tile, number in side_entries():
        rows = padded(tokens_of(plan[tile][number]))
        spans[tile, number] = (start, start + rows)
        start += rows

    def sum_of(tile, number):
        start, end = spans[tile, number]
        return rest_ref[start:end, :]

    def put(part, j, piece):
        held_ref[j // 2, part[0] : part[0] + part[1]] = piece

    borders = (back_ref, north_ref, south_ref, west_ref, east_ref)
    alternate(
        *[worked(plan, places, sum_of, borders, weights, scalars_ref, put) for places in SIDES]
    )
    copies = []
    for n, number in enumerate((0, 2)):
        left, wide = plan[4][number][2:]
        copies.append(
            pltpu.make_async_copy(held_ref.at[n], out_ref.at[:, left : left + wide], sem.at[n])
        )
        copies[n].start()
    for copy in copies:
        copy.wait()


def local(
    record_values,
    record_cell,
    record_instrument,
    block_counts,
    background,
    input_weight,
    instrument_table,
    lift_weight,
    first_gain,
    attn_weight,
    mix_weight,
    second_gain,
    up_weight,
    down_weight,
):
    lat_cells, lon_cells, _, width = background.shape
    tiles_lat = record_values.shape[1]

    sent, up, down, left, right = packed(
        record_values, record_cell, record_instrument, block_counts, background
    )
    received = lax.all_to_all(sent, ("lon", "lat"), split_axis=0, concat_axis=0, tiled=True)
    north = shifted(down, "lat", 1, wraps=False)
    south = shifted(up, "lat", -1, wraps=False)
    right = right.at[:HLAT].set(north[:, lon_cells - HLON :])
    right = right.at[HLAT + lat_cells :].set(south[:, lon_cells - HLON :])
    left = left.at[:HLAT].set(north[:, :HLON])
    left = left.at[HLAT + lat_cells :].set(south[:, :HLON])
    west = shifted(right, "lon", 1)
    east = shifted(left, "lon", -1)

    lat = lax.axis_index("lat")
    scalars = jnp.stack([lat == 0, lat < 0, lat == tiles_lat - 1]).astype(jnp.int32)
    plan = rectangles(lat_cells, lon_cells)
    rest = sum(padded(tokens_of(plan[tile][number])) for tile, number in side_entries())
    weights = [
        first_gain.reshape(1, width),
        attn_weight,
        mix_weight,
        second_gain.reshape(1, width),
        up_weight,
        down_weight.T,
    ]
    smem = pl.BlockSpec(memory_space=pltpu.SMEM)
    vmem = pl.BlockSpec(memory_space=pltpu.VMEM)
    anywhere = pl.BlockSpec(memory_space=pl.ANY)
    params = pltpu.CompilerParams(vmem_limit_bytes=LIMIT)
    result = jax.ShapeDtypeStruct(background.shape, BF16)
    middle, rest = pl.pallas_call(
        functools.partial(middle_kernel, plan),
        out_shape=[result, jax.ShapeDtypeStruct((rest, PAD), F32)],
        in_specs=[smem] + [vmem] * (7 + len(weights)),
        out_specs=[anywhere, vmem],
        scratch_shapes=[
            pltpu.VMEM((lat_cells, lon_cells - WLON, LEV, width), BF16),
            pltpu.SemaphoreType.DMA((1,)),
        ],
        compiler_params=params,
        cost_estimate=pl.CostEstimate(
            flops=4 * 10**9, bytes_accessed=4 * 10**6, transcendentals=10**6
        ),
    )(
        scalars,
        received,
        north,
        south,
        background,
        input_weight.T,
        instrument_table,
        lift_weight,
        *weights,
    )
    return pl.pallas_call(
        functools.partial(side_kernel, plan),
        out_shape=result,
        in_specs=[smem] + [vmem] * (6 + len(weights)) + [anywhere],
        out_specs=anywhere,
        scratch_shapes=[
            pltpu.VMEM((2, lat_cells, HLON, LEV, width), BF16),
            pltpu.SemaphoreType.DMA((2,)),
        ],
        input_output_aliases={7 + len(weights): 0},
        compiler_params=params,
        cost_estimate=pl.CostEstimate(
            flops=3 * 10**9, bytes_accessed=4 * 10**6, transcendentals=10**6
        ),
    )(scalars, rest, north, south, west, east, background, *weights, middle)


def solution(mesh):
    placed = (
        P("lon", "lat", None, None),
        P("lon", "lat", None),
        P("lon", "lat", None),
        P("lon", "lat"),
        P("lat", "lon", None, None),
        P(),
        P(),
        P(),
        P(),
        P(),
        P(),
        P(),
        P(),
        P(),
    )
    return jax.shard_map(
        local, mesh=mesh, in_specs=placed, out_specs=P("lat", "lon", None, None), check_vma=False
    )
```

```python
import functools

import jax
import jax.numpy as jnp
from jax import lax
from jax.experimental import pallas as pl
from jax.experimental.pallas import tpu as pltpu
from jax.sharding import PartitionSpec as P

HEADS = 6
INSTR = 8
LEV = 2
WLAT = 6
WLON = 12
HLAT = WLAT // 2
HLON = WLON // 2
LANES = 128
PAD = 256
CHUNK = 32
LIMIT = 40 * 2**20
BF16 = jnp.bfloat16
F32 = jnp.float32

AROUND = [(dy, dx) for dy in (-1, 0, 1) for dx in (-1, 0, 1)]
ROWS = INSTR * len(AROUND)
COLS = ROWS + len(AROUND)


def swapped(up, down, axis, wraps):
    count = lax.axis_size(axis)
    even = lax.axis_index(axis) % 2 == 0
    got = []
    for first, mine in ((0, jnp.where(even, down, up)), (1, jnp.where(even, up, down))):
        pairs = []
        for low in range(first, count, 2):
            high = (low + 1) % count
            if high > low or wraps:
                pairs += [(low, high), (high, low)]
        got.append(lax.ppermute(mine, axis, pairs))
    return jnp.where(even, got[1], got[0]), jnp.where(even, got[0], got[1])


def rectangles(lat_cells, lon_cells):
    lat = {-1: [(lat_cells - HLAT, HLAT)], 1: [(0, HLAT)]}
    lat[0] = [(0, HLAT), (HLAT, lat_cells - WLAT), (lat_cells - HLAT, HLAT)]
    lon = {-1: [(lon_cells - HLON, HLON)], 1: [(0, HLON)]}
    lon[0] = [(0, HLON), (HLON, lon_cells - WLON), (lon_cells - HLON, HLON)]
    return [
        [(top, high, left, wide) for top, high in lat[dy] for left, wide in lon[dx]]
        for dy, dx in AROUND
    ]


def tokens_of(part):
    return part[1] * part[3] * LEV


def padded(count):
    return -(-count // 8) * 8


def gelu(x):
    half = 0.5 * x
    inner = x * (0.7978845608028654 + 0.035677408136300125 * (x * x))
    return half + half * jnp.tanh(inner)


def normalise(wide, gain):
    average = jnp.mean(wide, axis=-1, keepdims=True)
    centred = wide - average
    spread = jnp.mean(centred * centred, axis=-1, keepdims=True)
    return centred * lax.rsqrt(spread + 1e-05) * gain


def dot(a, b):
    return jnp.dot(a, b, preferred_element_type=F32)


def dot_nt(a, b):
    return lax.dot_general(a, b, (((1,), (1,)), ((), ())), preferred_element_type=F32)


def with_ones(tensor):
    ones = jnp.ones((tensor.shape[0], PAD - tensor.shape[1]), F32)
    return jnp.concatenate([tensor, ones], axis=1).astype(BF16)


def below(*pieces):
    return jnp.concatenate(pieces, axis=0) if len(pieces) > 1 else pieces[0]


def pack_kernel(
    values_ref,
    cell_ref,
    tag_ref,
    count_ref,
    back_ref,
    *refs,
):
    out_ref, up_ref, down_ref, values, cells, tags, held, sem = refs
    tiles_lon, tiles_lat, capacity, _ = values_ref.shape
    lat_cells, lon_cells = back_ref.shape[:2]
    strips = [
        (back_ref.at[:HLAT], up_ref),
        (back_ref.at[lat_cells - HLAT :], down_ref),
    ]
    copies = [
        pltpu.make_async_copy(cell_ref, cells, sem.at[0]),
        pltpu.make_async_copy(tag_ref, tags, sem.at[1]),
        pltpu.make_async_copy(count_ref, held, sem.at[2]),
        pltpu.make_async_copy(values_ref, values, sem.at[3]),
    ]
    copies += [
        pltpu.make_async_copy(source, strip, sem.at[4 + n])
        for n, (source, strip) in enumerate(strips)
    ]
    for copy in copies:
        copy.start()
    for copy in copies[:3]:
        copy.wait()
    counts = below(*[held[tile : tile + 1, :] for tile in range(tiles_lat) for _ in range(capacity)])
    cell = cells[...]
    slot = lax.broadcasted_iota(jnp.int32, cell.shape, 0) % capacity
    row = cell // lon_cells
    fields = [jnp.where(slot < counts, row, 255), cell - row * lon_cells, tags[...]]
    rows, columns, kinds = (field.astype(F32) for field in fields)
    lane = lax.broadcasted_iota(jnp.int32, (cell.shape[0], LANES), 1)
    kind_of = (lane % INSTR).astype(F32)
    marks = [
        ((lane < ROWS) & (lane // INSTR == n)) | (lane == ROWS + n) | (lane == COLS + n)
        for n in range(len(AROUND))
    ]
    turned = []
    for lon in range(tiles_lon):
        meta = jnp.where(kind_of == kinds[:, lon : lon + 1], 1.0, 0.0)
        meta = jnp.where(lane >= ROWS, rows[:, lon : lon + 1], meta)
        meta = jnp.where(lane >= COLS, columns[:, lon : lon + 1], meta)
        turns = {0: meta}
        for dy in (-1, 1):
            by = dy * capacity % meta.shape[0]
            turns[dy] = below(meta[by:], meta[:by])
        turned.append(turns)
    for lon in range(tiles_lon):
        meta = jnp.zeros(lane.shape, F32)
        for mark, (dy, dx) in zip(marks, AROUND):
            meta = jnp.where(mark, turned[(lon + dx) % tiles_lon][dy], meta)
        out_ref[lon, :, len(AROUND)] = meta.astype(BF16).reshape(tiles_lat, capacity, LANES)
    copies[3].wait()
    for n, (dy, dx) in enumerate(AROUND):
        spans = {0: [(0, tiles_lat)], 1: [(0, tiles_lat - 1), (tiles_lat - 1, tiles_lat)]}
        spans[-1] = [(0, 1), (1, tiles_lat)]

        def copy_tiles(lon, n=n, dx=dx, dy=dy, spans=spans[dy]):
            source = lax.rem(lon + dx + tiles_lon, tiles_lon)
            for low, end in spans:
                first = (low + dy) % tiles_lat
                out_ref[lon, low:end, n] = values[source, first : first + end - low]

        if tiles_lon <= 8:
            for lon in range(tiles_lon):
                copy_tiles(lon)
        else:
            pl.loop(0, tiles_lon)(copy_tiles)
    for copy in copies[4:]:
        copy.wait()


def packed(record_values, record_cell, record_instrument, block_counts, background):
    tiles_lon, tiles_lat, capacity, wide = record_values.shape
    anywhere = pl.BlockSpec(memory_space=pltpu.HBM)
    ints = pltpu.VMEM((tiles_lat * capacity, tiles_lon), jnp.int32)
    shape = (tiles_lon, tiles_lat, len(AROUND) + 1, capacity, wide)
    lat_cells, lon_cells, levels, width = background.shape
    across = jax.ShapeDtypeStruct((HLAT, lon_cells, levels, width), BF16)
    out, *strips = pl.pallas_call(
        pack_kernel,
        out_shape=[jax.ShapeDtypeStruct(shape, BF16), across, across],
        in_specs=[anywhere] * 5,
        out_specs=[pl.BlockSpec(memory_space=pltpu.VMEM)] * 3,
        scratch_shapes=[
            pltpu.VMEM(record_values.shape, BF16),
            ints,
            ints,
            pltpu.VMEM((tiles_lat, tiles_lon), jnp.int32),
            pltpu.SemaphoreType.DMA((6,)),
        ],
        compiler_params=pltpu.CompilerParams(vmem_limit_bytes=56 * 2**20),
        cost_estimate=pl.CostEstimate(
            flops=20 * 10**9, bytes_accessed=10**6, transcendentals=0
        ),
    )(
        record_values,
        record_cell.transpose(1, 2, 0).reshape(-1, tiles_lon),
        record_instrument.transpose(1, 2, 0).reshape(-1, tiles_lon),
        block_counts.T,
        background,
    )
    return out.reshape((-1,) + shape[2:]), *strips


def token_codes(part, lon_cells):
    top, high, left, wide = part
    count = tokens_of(part)
    place = lax.broadcasted_iota(jnp.int32, (padded(count), LANES), 0)
    code = place + (top * lon_cells + left) * LEV
    for row in range(1, high):
        step = (lon_cells - wide) * LEV
        code = code + jnp.where(place >= row * wide * LEV, step, 0)
    return jnp.where(place < count, code, -8).astype(F32)


def entries_of(windows):
    entries = [(4, 3 * i + j) for i, j in windows]
    for i, j in windows:
        if i != 1:
            entries.append((3 * i + 1, j))
        if j != 1:
            entries.append((3 + j, i))
        if i != 1 and j != 1:
            entries.append((3 * i + j, 0))
    return entries


def alternate(*chains):
    chains, begun = list(chains), 1
    while chains:
        for chain in chains[:begun]:
            if next(chain, None) is None:
                chains.remove(chain)
                begun -= 1
        begun += 1


def scattered(recv_ref, first_ref, table_ref, lift_ref, plan, lon_cells):
    sources, _, capacity, _ = recv_ref.shape
    width = table_ref.shape[1]
    chunk = min(CHUNK, sources)
    slots = chunk * capacity
    first, lift = first_ref[...], lift_ref[...]
    table = below(*[table_ref[...].astype(F32)] * (LANES // INSTR)).astype(BF16)
    lane = lax.broadcasted_iota(jnp.int32, (16, LANES), 1)
    sub = lax.broadcasted_iota(jnp.int32, (16, LANES), 0)
    weigh = jnp.where(lane == ROWS + sub, float(lon_cells * LEV), 0.0)
    weigh = jnp.where(lane == COLS + sub, float(LEV), weigh).astype(BF16)
    codes = [below(*[token_codes(part, lon_cells) for part in parts]) for parts in plan]

    def scatter(begin):
        meta = recv_ref[pl.ds(begin, chunk), len(AROUND)].reshape(slots, LANES)
        records = below(
            *[
                recv_ref[pl.ds(begin, chunk), n].reshape(slots, LANES)
                for n in range(len(AROUND))
            ]
        )
        lane = lax.broadcasted_iota(jnp.int32, meta.shape, 1) // INSTR
        wide = meta.astype(F32)
        chosen = below(*[jnp.where(lane == n, wide, 0.0) for n in range(len(AROUND))]).astype(BF16)
        encoded = gelu(dot_nt(records, first) + dot(chosen, table)).astype(BF16)
        lifted = gelu(dot(encoded, lift))
        tokens = dot_nt(weigh, meta)
        sums = []
        for n in range(len(AROUND)):
            part = lifted[n * slots : (n + 1) * slots]
            part = with_ones(
                below(*[part[:, level * width : (level + 1) * width] for level in range(LEV)])
            )
            token = tokens[n : n + 1]
            token = jnp.concatenate([token + float(level) for level in range(LEV)], axis=1)
            if token.shape[1] == LANES:
                hot = codes[n] == token
            else:
                hot = codes[n][:, :1] == token
            sums.append(dot(jnp.where(hot, 1.0, 0.0).astype(BF16), part))
        return tuple(sums)

    sums = scatter(0)
    if sources > chunk:
        sums = lax.fori_loop(
            1,
            sources // chunk,
            lambda step, total: tuple(a + b for a, b in zip(total, scatter(step * chunk))),
            sums,
        )
    return sums


def worked(plan, places, sum_of, borders, weights, scalars_ref, put):
    back_ref, north_ref, south_ref, west_ref, east_ref = borders
    gain_one_ref, attn_ref, mix_ref, gain_two_ref, up_ref, down_ref = weights
    lat_cells, width = back_ref.shape[0], back_ref.shape[3]
    pieces, spans, start = [], {}, 0
    for tile, number in entries_of(places):
        dy, dx = AROUND[tile]
        part = plan[tile][number]
        top, high, left, wide = part
        count = tokens_of(part)
        if dx:
            ref = west_ref if dx < 0 else east_ref
            top, left = {-1: 0, 0: top + HLAT, 1: lat_cells + HLAT}[dy], 0
        elif dy:
            ref, top = (north_ref, 0) if dy < 0 else (south_ref, 0)
        else:
            ref = back_ref
        piece = ref[top : top + high, left : left + wide].reshape(count, width).astype(F32)
        full = padded(count)
        if full > count:
            piece = below(piece, jnp.zeros((full - count, width), F32))
        pieces.append(piece)
        spans[tile, number] = (start, count)
        start += full
    sums = below(*[sum_of(*entry) for entry in entries_of(places)])
    share = 1.0 / (1.0 + sums[:, width : width + 1])
    latent = ((below(*pieces) + sums[:, :width]) * share).astype(BF16).astype(F32)
    normed = normalise(latent, gain_one_ref[...].astype(F32))
    yield True

    def piece_of(tile, number):
        start, count = spans[tile, number]
        return normed[start : start + count]

    groups = [padded(tokens_of(plan[4][3 * i + j])) for i, j in places]
    end = sum(groups)
    windows = []
    for i, j in places:
        window = [piece_of(4, 3 * i + j)]
        if i != 1:
            window.append(piece_of(3 * i + 1, j))
        if j != 1:
            window.append(piece_of(3 + j, i))
        if i != 1 and j != 1:
            window.append(piece_of(3 * i + j, 0))
        windows.append(window)
    tokens = below(*[piece for window in windows for piece in window]).astype(BF16)
    weight = attn_ref[...]
    head = width // HEADS
    keys = dot(tokens, weight[:, width : 2 * width]).astype(BF16)
    query = dot(normed[:end].astype(BF16), weight[:, :width]) * head ** (-0.5)
    values = with_ones(dot(tokens, weight[:, 2 * width :]))
    yield True

    head_of = lax.broadcasted_iota(jnp.int32, (1, width), 1) // head
    many = WLAT * WLON * LEV
    corner = HLAT * HLON * LEV
    key = lax.broadcasted_iota(jnp.int32, (1, many), 1)
    mixed, start = [], 0
    for w, ((i, j), rows) in enumerate(zip(places, groups)):
        part = query[start : start + rows]
        stacked = below(*[jnp.where(head_of == h, part, 0.0) for h in range(HEADS)]).astype(BF16)
        scores = dot_nt(stacked, keys[w * many : (w + 1) * many])
        yield True
        if i != 1:
            if j == 1:
                inside = key < 2 * corner
            else:
                inside = (key < corner) | ((key >= 2 * corner) & (key < 3 * corner))
            scores = jnp.where(inside | (scalars_ref[i] == 0), scores, -1e30)
        largest = jnp.max(scores, axis=-1, keepdims=True)
        raised = jnp.exp(scores - largest).astype(BF16)
        product = dot(raised, values[w * many : (w + 1) * many])
        yield True
        product = product[:, :width] * (1.0 / product[:, width : width + 1])
        total = jnp.zeros((rows, width), F32)
        for h in range(HEADS):
            total = jnp.where(head_of == h, product[h * rows : (h + 1) * rows], total)
        mixed.append(total)
        start += rows
    mixed = below(*mixed).astype(BF16)

    after = (latent[:end] + dot(mixed, mix_ref[...])).astype(BF16).astype(F32)
    yield True
    normed_two = normalise(after, gain_two_ref[...].astype(F32)).astype(BF16)
    hidden = dot(normed_two, up_ref[...])
    yield True
    result = after + dot_nt(gelu(hidden).astype(BF16), down_ref[...])
    yield True
    start = 0
    for (i, j), rows in zip(places, groups):
        part = plan[4][3 * i + j]
        piece = result[start : start + tokens_of(part)].astype(BF16)
        put(part, j, piece.reshape(part[1], part[3], LEV, width))
        start += rows


MIDDLE = [[(0, 1), (2, 1)], [(1, 1)]]
SIDES = [[(0, 0), (1, 0), (2, 0)], [(0, 2), (1, 2), (2, 2)]]


def side_entries():
    return [entry for places in SIDES for entry in entries_of(places)]


def middle_kernel(
    plan,
    scalars_ref,
    recv_ref,
    north_ref,
    south_ref,
    back_ref,
    first_ref,
    table_ref,
    lift_ref,
    *refs,
):
    *weights, out_ref, rest_ref, held_ref, sem = refs
    sums = scattered(recv_ref, first_ref, table_ref, lift_ref, plan, back_ref.shape[1])

    def sum_of(tile, number):
        start = sum(padded(tokens_of(part)) for part in plan[tile][:number])
        return sums[tile][start : start + padded(tokens_of(plan[tile][number]))]

    rest_ref[...] = below(*[sum_of(*entry) for entry in side_entries()])
    left, wide = plan[4][4][2:]

    def put(part, _, piece):
        held_ref[part[0] : part[0] + part[1]] = piece

    borders = (back_ref, north_ref, south_ref, None, None)
    alternate(
        *[worked(plan, places, sum_of, borders, weights, scalars_ref, put) for places in MIDDLE]
    )
    copy = pltpu.make_async_copy(held_ref, out_ref.at[:, left : left + wide], sem.at[0])
    copy.start()
    copy.wait()


def side_kernel(
    plan,
    scalars_ref,
    rest_ref,
    north_ref,
    south_ref,
    west_ref,
    east_ref,
    back_ref,
    *refs,
):
    *weights, _, out_ref, held_ref, sem = refs
    spans, start = {}, 0
    for tile, number in side_entries():
        rows = padded(tokens_of(plan[tile][number]))
        spans[tile, number] = (start, start + rows)
        start += rows

    def sum_of(tile, number):
        start, end = spans[tile, number]
        return rest_ref[start:end, :]

    def put(part, j, piece):
        held_ref[j // 2, part[0] : part[0] + part[1]] = piece

    borders = (back_ref, north_ref, south_ref, west_ref, east_ref)
    alternate(
        *[worked(plan, places, sum_of, borders, weights, scalars_ref, put) for places in SIDES]
    )
    copies = []
    for n, number in enumerate((0, 2)):
        left, wide = plan[4][number][2:]
        copies.append(
            pltpu.make_async_copy(held_ref.at[n], out_ref.at[:, left : left + wide], sem.at[n])
        )
        copies[n].start()
    for copy in copies:
        copy.wait()


def local(
    record_values,
    record_cell,
    record_instrument,
    block_counts,
    background,
    input_weight,
    instrument_table,
    lift_weight,
    first_gain,
    attn_weight,
    mix_weight,
    second_gain,
    up_weight,
    down_weight,
):
    lat_cells, lon_cells, _, width = background.shape
    tiles_lat = record_values.shape[1]

    sent, up, down = packed(
        record_values, record_cell, record_instrument, block_counts, background
    )
    received = lax.all_to_all(sent, ("lon", "lat"), split_axis=0, concat_axis=0, tiled=True)
    north, south = swapped(up, down, "lat", wraps=False)

    later, _ = lax.optimization_barrier((background, up))

    def columns(low, end):
        return jnp.concatenate([north[:, low:end], later[:, low:end], south[:, low:end]], axis=0)

    west, east = swapped(columns(0, HLON), columns(lon_cells - HLON, lon_cells), "lon", wraps=True)

    lat = lax.axis_index("lat")
    scalars = jnp.stack([lat == 0, lat < 0, lat == tiles_lat - 1]).astype(jnp.int32)
    plan = rectangles(lat_cells, lon_cells)
    rest = sum(padded(tokens_of(plan[tile][number])) for tile, number in side_entries())
    weights = [
        first_gain.reshape(1, width),
        attn_weight,
        mix_weight,
        second_gain.reshape(1, width),
        up_weight,
        down_weight.T,
    ]
    smem = pl.BlockSpec(memory_space=pltpu.SMEM)
    vmem = pl.BlockSpec(memory_space=pltpu.VMEM)
    anywhere = pl.BlockSpec(memory_space=pl.ANY)
    params = pltpu.CompilerParams(vmem_limit_bytes=LIMIT)
    result = jax.ShapeDtypeStruct(background.shape, BF16)
    middle, rest = pl.pallas_call(
        functools.partial(middle_kernel, plan),
        out_shape=[result, jax.ShapeDtypeStruct((rest, PAD), F32)],
        in_specs=[smem] + [vmem] * (7 + len(weights)),
        out_specs=[anywhere, vmem],
        scratch_shapes=[
            pltpu.VMEM((lat_cells, lon_cells - WLON, LEV, width), BF16),
            pltpu.SemaphoreType.DMA((1,)),
        ],
        compiler_params=params,
        cost_estimate=pl.CostEstimate(
            flops=4 * 10**9, bytes_accessed=4 * 10**6, transcendentals=10**6
        ),
    )(
        scalars,
        received,
        north,
        south,
        background,
        input_weight.T,
        instrument_table,
        lift_weight,
        *weights,
    )
    return pl.pallas_call(
        functools.partial(side_kernel, plan),
        out_shape=result,
        in_specs=[smem] + [vmem] * (6 + len(weights)) + [anywhere],
        out_specs=anywhere,
        scratch_shapes=[
            pltpu.VMEM((2, lat_cells, HLON, LEV, width), BF16),
            pltpu.SemaphoreType.DMA((2,)),
        ],
        input_output_aliases={7 + len(weights): 0},
        compiler_params=params,
        cost_estimate=pl.CostEstimate(
            flops=3 * 10**9, bytes_accessed=4 * 10**6, transcendentals=10**6
        ),
    )(scalars, rest, north, south, west, east, background, *weights, middle)


def solution(mesh):
    placed = (
        P("lon", "lat", None, None),
        P("lon", "lat", None),
        P("lon", "lat", None),
        P("lon", "lat"),
        P("lat", "lon", None, None),
        P(),
        P(),
        P(),
        P(),
        P(),
        P(),
        P(),
        P(),
        P(),
    )
    return jax.shard_map(
        local, mesh=mesh, in_specs=placed, out_specs=P("lat", "lon", None, None), check_vma=False
    )
```

```python
import functools

import jax
import jax.numpy as jnp
from jax import lax
from jax.experimental import pallas as pl
from jax.experimental.pallas import tpu as pltpu
from jax.sharding import PartitionSpec as P

HEADS = 6
INSTR = 8
LEV = 2
WLAT = 6
WLON = 12
HLAT = WLAT // 2
HLON = WLON // 2
LANES = 128
PAD = 256
CHUNK = 32
LIMIT = 40 * 2**20
BF16 = jnp.bfloat16
F32 = jnp.float32

AROUND = [(dy, dx) for dy in (-1, 0, 1) for dx in (-1, 0, 1)]
ROWS = INSTR * len(AROUND)
COLS = ROWS + len(AROUND)


def swapped(up, down, axis, wraps):
    count = lax.axis_size(axis)
    even = lax.axis_index(axis) % 2 == 0
    got = []
    for first, mine in ((0, jnp.where(even, down, up)), (1, jnp.where(even, up, down))):
        pairs = []
        for low in range(first, count, 2):
            high = (low + 1) % count
            if high > low or wraps:
                pairs += [(low, high), (high, low)]
        got.append(lax.ppermute(mine, axis, pairs))
    return got


def before_and_after(got, axis):
    even = lax.axis_index(axis) % 2 == 0
    return jnp.where(even, got[1], got[0]), jnp.where(even, got[0], got[1])


def rectangles(lat_cells, lon_cells):
    lat = {-1: [(lat_cells - HLAT, HLAT)], 1: [(0, HLAT)]}
    lat[0] = [(0, HLAT), (HLAT, lat_cells - WLAT), (lat_cells - HLAT, HLAT)]
    lon = {-1: [(lon_cells - HLON, HLON)], 1: [(0, HLON)]}
    lon[0] = [(0, HLON), (HLON, lon_cells - WLON), (lon_cells - HLON, HLON)]
    return [
        [(top, high, left, wide) for top, high in lat[dy] for left, wide in lon[dx]]
        for dy, dx in AROUND
    ]


def tokens_of(part):
    return part[1] * part[3] * LEV


def padded(count):
    return -(-count // 8) * 8


def gelu(x):
    half = 0.5 * x
    inner = x * (0.7978845608028654 + 0.035677408136300125 * (x * x))
    return half + half * jnp.tanh(inner)


def normalise(wide, gain):
    average = jnp.mean(wide, axis=-1, keepdims=True)
    centred = wide - average
    spread = jnp.mean(centred * centred, axis=-1, keepdims=True)
    return centred * lax.rsqrt(spread + 1e-05) * gain


def dot(a, b):
    return jnp.dot(a, b, preferred_element_type=F32)


def dot_nt(a, b):
    return lax.dot_general(a, b, (((1,), (1,)), ((), ())), preferred_element_type=F32)


def with_ones(tensor):
    ones = jnp.ones((tensor.shape[0], PAD - tensor.shape[1]), F32)
    return jnp.concatenate([tensor, ones], axis=1).astype(BF16)


def below(*pieces):
    return jnp.concatenate(pieces, axis=0) if len(pieces) > 1 else pieces[0]


def pack_kernel(
    values_ref,
    cell_ref,
    tag_ref,
    count_ref,
    back_ref,
    *refs,
):
    out_ref, up_ref, down_ref, values, cells, tags, held, sem = refs
    tiles_lon, tiles_lat, capacity, _ = values_ref.shape
    lat_cells, lon_cells = back_ref.shape[:2]
    strips = [
        (back_ref.at[:HLAT], up_ref),
        (back_ref.at[lat_cells - HLAT :], down_ref),
    ]
    copies = [
        pltpu.make_async_copy(cell_ref, cells, sem.at[0]),
        pltpu.make_async_copy(tag_ref, tags, sem.at[1]),
        pltpu.make_async_copy(count_ref, held, sem.at[2]),
        pltpu.make_async_copy(values_ref, values, sem.at[3]),
    ]
    copies += [
        pltpu.make_async_copy(source, strip, sem.at[4 + n])
        for n, (source, strip) in enumerate(strips)
    ]
    for copy in copies:
        copy.start()
    for copy in copies[:3]:
        copy.wait()
    counts = below(*[held[tile : tile + 1, :] for tile in range(tiles_lat) for _ in range(capacity)])
    cell = cells[...]
    slot = lax.broadcasted_iota(jnp.int32, cell.shape, 0) % capacity
    row = cell // lon_cells
    fields = [jnp.where(slot < counts, row, 255), cell - row * lon_cells, tags[...]]
    rows, columns, kinds = (field.astype(F32) for field in fields)
    lane = lax.broadcasted_iota(jnp.int32, (cell.shape[0], LANES), 1)
    kind_of = (lane % INSTR).astype(F32)
    marks = [
        ((lane < ROWS) & (lane // INSTR == n)) | (lane == ROWS + n) | (lane == COLS + n)
        for n in range(len(AROUND))
    ]
    turned = []
    for lon in range(tiles_lon):
        meta = jnp.where(kind_of == kinds[:, lon : lon + 1], 1.0, 0.0)
        meta = jnp.where(lane >= ROWS, rows[:, lon : lon + 1], meta)
        meta = jnp.where(lane >= COLS, columns[:, lon : lon + 1], meta)
        turns = {0: meta}
        for dy in (-1, 1):
            by = dy * capacity % meta.shape[0]
            turns[dy] = below(meta[by:], meta[:by])
        turned.append(turns)
    for lon in range(tiles_lon):
        meta = jnp.zeros(lane.shape, F32)
        for mark, (dy, dx) in zip(marks, AROUND):
            meta = jnp.where(mark, turned[(lon + dx) % tiles_lon][dy], meta)
        out_ref[lon, :, len(AROUND)] = meta.astype(BF16).reshape(tiles_lat, capacity, LANES)
    copies[3].wait()
    for n, (dy, dx) in enumerate(AROUND):
        spans = {0: [(0, tiles_lat)], 1: [(0, tiles_lat - 1), (tiles_lat - 1, tiles_lat)]}
        spans[-1] = [(0, 1), (1, tiles_lat)]

        def copy_tiles(lon, n=n, dx=dx, dy=dy, spans=spans[dy]):
            source = lax.rem(lon + dx + tiles_lon, tiles_lon)
            for low, end in spans:
                first = (low + dy) % tiles_lat
                out_ref[lon, low:end, n] = values[source, first : first + end - low]

        if tiles_lon <= 8:
            for lon in range(tiles_lon):
                copy_tiles(lon)
        else:
            pl.loop(0, tiles_lon)(copy_tiles)
    for copy in copies[4:]:
        copy.wait()


def packed(record_values, record_cell, record_instrument, block_counts, background):
    tiles_lon, tiles_lat, capacity, wide = record_values.shape
    anywhere = pl.BlockSpec(memory_space=pltpu.HBM)
    ints = pltpu.VMEM((tiles_lat * capacity, tiles_lon), jnp.int32)
    shape = (tiles_lon, tiles_lat, len(AROUND) + 1, capacity, wide)
    lat_cells, lon_cells, levels, width = background.shape
    across = jax.ShapeDtypeStruct((HLAT, lon_cells, levels, width), BF16)
    out, *strips = pl.pallas_call(
        pack_kernel,
        out_shape=[jax.ShapeDtypeStruct(shape, BF16), across, across],
        in_specs=[anywhere] * 5,
        out_specs=[pl.BlockSpec(memory_space=pltpu.VMEM)] * 3,
        scratch_shapes=[
            pltpu.VMEM(record_values.shape, BF16),
            ints,
            ints,
            pltpu.VMEM((tiles_lat, tiles_lon), jnp.int32),
            pltpu.SemaphoreType.DMA((6,)),
        ],
        compiler_params=pltpu.CompilerParams(vmem_limit_bytes=56 * 2**20),
        cost_estimate=pl.CostEstimate(
            flops=20 * 10**9, bytes_accessed=10**6, transcendentals=0
        ),
    )(
        record_values,
        record_cell.transpose(1, 2, 0).reshape(-1, tiles_lon),
        record_instrument.transpose(1, 2, 0).reshape(-1, tiles_lon),
        block_counts.T,
        background,
    )
    return out.reshape((-1,) + shape[2:]), *strips


def token_codes(part, lon_cells):
    top, high, left, wide = part
    count = tokens_of(part)
    place = lax.broadcasted_iota(jnp.int32, (padded(count), LANES), 0)
    code = place + (top * lon_cells + left) * LEV
    for row in range(1, high):
        step = (lon_cells - wide) * LEV
        code = code + jnp.where(place >= row * wide * LEV, step, 0)
    return jnp.where(place < count, code, -8).astype(F32)


def entries_of(windows):
    entries = [(4, 3 * i + j) for i, j in windows]
    for i, j in windows:
        if i != 1:
            entries.append((3 * i + 1, j))
        if j != 1:
            entries.append((3 + j, i))
        if i != 1 and j != 1:
            entries.append((3 * i + j, 0))
    return entries


def alternate(*chains):
    chains, begun = list(chains), 1
    while chains:
        for chain in chains[:begun]:
            if next(chain, None) is None:
                chains.remove(chain)
                begun -= 1
        begun += 1


def scattered(recv_ref, first_ref, table_ref, lift_ref, plan, lon_cells):
    sources, _, capacity, _ = recv_ref.shape
    width = table_ref.shape[1]
    chunk = min(CHUNK, sources)
    slots = chunk * capacity
    first, lift = first_ref[...], lift_ref[...]
    table = below(*[table_ref[...].astype(F32)] * (LANES // INSTR)).astype(BF16)
    lane = lax.broadcasted_iota(jnp.int32, (16, LANES), 1)
    sub = lax.broadcasted_iota(jnp.int32, (16, LANES), 0)
    weigh = jnp.where(lane == ROWS + sub, float(lon_cells * LEV), 0.0)
    weigh = jnp.where(lane == COLS + sub, float(LEV), weigh).astype(BF16)
    codes = [below(*[token_codes(part, lon_cells) for part in parts]) for parts in plan]

    def scatter(begin):
        meta = recv_ref[pl.ds(begin, chunk), len(AROUND)].reshape(slots, LANES)
        records = below(
            *[
                recv_ref[pl.ds(begin, chunk), n].reshape(slots, LANES)
                for n in range(len(AROUND))
            ]
        )
        lane = lax.broadcasted_iota(jnp.int32, meta.shape, 1) // INSTR
        wide = meta.astype(F32)
        chosen = below(*[jnp.where(lane == n, wide, 0.0) for n in range(len(AROUND))]).astype(BF16)
        encoded = gelu(dot_nt(records, first) + dot(chosen, table)).astype(BF16)
        lifted = gelu(dot(encoded, lift))
        tokens = dot_nt(weigh, meta)
        sums = []
        for n in range(len(AROUND)):
            part = lifted[n * slots : (n + 1) * slots]
            part = with_ones(
                below(*[part[:, level * width : (level + 1) * width] for level in range(LEV)])
            )
            token = tokens[n : n + 1]
            token = jnp.concatenate([token + float(level) for level in range(LEV)], axis=1)
            if token.shape[1] == LANES:
                hot = codes[n] == token
            else:
                hot = codes[n][:, :1] == token
            sums.append(dot(jnp.where(hot, 1.0, 0.0).astype(BF16), part))
        return tuple(sums)

    sums = scatter(0)
    if sources > chunk:
        sums = lax.fori_loop(
            1,
            sources // chunk,
            lambda step, total: tuple(a + b for a, b in zip(total, scatter(step * chunk))),
            sums,
        )
    return sums


def worked(plan, places, sum_of, borders, weights, scalars_ref, put):
    back_ref, north_ref, south_ref, west_ref, east_ref = borders
    gain_one_ref, attn_ref, mix_ref, gain_two_ref, up_ref, down_ref = weights
    lat_cells, width = back_ref.shape[0], back_ref.shape[3]
    pieces, spans, start = [], {}, 0
    for tile, number in entries_of(places):
        dy, dx = AROUND[tile]
        part = plan[tile][number]
        top, high, left, wide = part
        count = tokens_of(part)
        if dx:
            ref = west_ref if dx < 0 else east_ref
            top, left = {-1: 0, 0: top + HLAT, 1: lat_cells + HLAT}[dy], 0
        elif dy:
            ref, top = (north_ref, 0) if dy < 0 else (south_ref, 0)
        else:
            ref = back_ref
        piece = ref[top : top + high, left : left + wide].reshape(count, width).astype(F32)
        full = padded(count)
        if full > count:
            piece = below(piece, jnp.zeros((full - count, width), F32))
        pieces.append(piece)
        spans[tile, number] = (start, count)
        start += full
    sums = below(*[sum_of(*entry) for entry in entries_of(places)])
    share = 1.0 / (1.0 + sums[:, width : width + 1])
    latent = ((below(*pieces) + sums[:, :width]) * share).astype(BF16).astype(F32)
    normed = normalise(latent, gain_one_ref[...].astype(F32))
    yield True

    def piece_of(tile, number):
        start, count = spans[tile, number]
        return normed[start : start + count]

    groups = [padded(tokens_of(plan[4][3 * i + j])) for i, j in places]
    end = sum(groups)
    windows = []
    for i, j in places:
        window = [piece_of(4, 3 * i + j)]
        if i != 1:
            window.append(piece_of(3 * i + 1, j))
        if j != 1:
            window.append(piece_of(3 + j, i))
        if i != 1 and j != 1:
            window.append(piece_of(3 * i + j, 0))
        windows.append(window)
    tokens = below(*[piece for window in windows for piece in window]).astype(BF16)
    weight = attn_ref[...]
    head = width // HEADS
    keys = dot(tokens, weight[:, width : 2 * width]).astype(BF16)
    query = dot(normed[:end].astype(BF16), weight[:, :width]) * head ** (-0.5)
    values = with_ones(dot(tokens, weight[:, 2 * width :]))
    yield True

    head_of = lax.broadcasted_iota(jnp.int32, (1, width), 1) // head
    many = WLAT * WLON * LEV
    corner = HLAT * HLON * LEV
    key = lax.broadcasted_iota(jnp.int32, (1, many), 1)
    mixed, start = [], 0
    for w, ((i, j), rows) in enumerate(zip(places, groups)):
        part = query[start : start + rows]
        stacked = below(*[jnp.where(head_of == h, part, 0.0) for h in range(HEADS)]).astype(BF16)
        scores = dot_nt(stacked, keys[w * many : (w + 1) * many])
        yield True
        if i != 1:
            if j == 1:
                inside = key < 2 * corner
            else:
                inside = (key < corner) | ((key >= 2 * corner) & (key < 3 * corner))
            scores = jnp.where(inside | (scalars_ref[i] == 0), scores, -1e30)
        largest = jnp.max(scores, axis=-1, keepdims=True)
        raised = jnp.exp(scores - largest).astype(BF16)
        product = dot(raised, values[w * many : (w + 1) * many])
        yield True
        product = product[:, :width] * (1.0 / product[:, width : width + 1])
        total = jnp.zeros((rows, width), F32)
        for h in range(HEADS):
            total = jnp.where(head_of == h, product[h * rows : (h + 1) * rows], total)
        mixed.append(total)
        start += rows
    mixed = below(*mixed).astype(BF16)

    after = (latent[:end] + dot(mixed, mix_ref[...])).astype(BF16).astype(F32)
    yield True
    normed_two = normalise(after, gain_two_ref[...].astype(F32)).astype(BF16)
    hidden = dot(normed_two, up_ref[...])
    yield True
    result = after + dot_nt(gelu(hidden).astype(BF16), down_ref[...])
    yield True
    start = 0
    for (i, j), rows in zip(places, groups):
        part = plan[4][3 * i + j]
        piece = result[start : start + tokens_of(part)].astype(BF16)
        put(part, j, piece.reshape(part[1], part[3], LEV, width))
        start += rows


MIDDLE = [[(0, 1), (2, 1)], [(1, 1)]]
SIDES = [[(0, 0), (1, 0), (2, 0)], [(0, 2), (1, 2), (2, 2)]]


def side_entries():
    return [entry for places in SIDES for entry in entries_of(places)]


def middle_kernel(
    plan,
    scalars_ref,
    recv_ref,
    north_ref,
    south_ref,
    back_ref,
    first_ref,
    table_ref,
    lift_ref,
    *refs,
):
    *weights, out_ref, rest_ref, held_ref, sem = refs
    sums = scattered(recv_ref, first_ref, table_ref, lift_ref, plan, back_ref.shape[1])

    def sum_of(tile, number):
        start = sum(padded(tokens_of(part)) for part in plan[tile][:number])
        return sums[tile][start : start + padded(tokens_of(plan[tile][number]))]

    rest_ref[...] = below(*[sum_of(*entry) for entry in side_entries()])
    left, wide = plan[4][4][2:]

    def put(part, _, piece):
        held_ref[part[0] : part[0] + part[1]] = piece

    borders = (back_ref, north_ref, south_ref, None, None)
    alternate(
        *[worked(plan, places, sum_of, borders, weights, scalars_ref, put) for places in MIDDLE]
    )
    copy = pltpu.make_async_copy(held_ref, out_ref.at[:, left : left + wide], sem.at[0])
    copy.start()
    copy.wait()


def side_kernel(
    plan,
    scalars_ref,
    rest_ref,
    north_ref,
    south_ref,
    west_ref,
    east_ref,
    back_ref,
    *refs,
):
    *weights, _, out_ref, held_ref, sem = refs
    spans, start = {}, 0
    for tile, number in side_entries():
        rows = padded(tokens_of(plan[tile][number]))
        spans[tile, number] = (start, start + rows)
        start += rows

    def sum_of(tile, number):
        start, end = spans[tile, number]
        return rest_ref[start:end, :]

    def put(part, j, piece):
        held_ref[j // 2, part[0] : part[0] + part[1]] = piece

    borders = (back_ref, north_ref, south_ref, west_ref, east_ref)
    alternate(
        *[worked(plan, places, sum_of, borders, weights, scalars_ref, put) for places in SIDES]
    )
    copies = []
    for n, number in enumerate((0, 2)):
        left, wide = plan[4][number][2:]
        copies.append(
            pltpu.make_async_copy(held_ref.at[n], out_ref.at[:, left : left + wide], sem.at[n])
        )
        copies[n].start()
    for copy in copies:
        copy.wait()


def local(
    record_values,
    record_cell,
    record_instrument,
    block_counts,
    background,
    input_weight,
    instrument_table,
    lift_weight,
    first_gain,
    attn_weight,
    mix_weight,
    second_gain,
    up_weight,
    down_weight,
):
    lat_cells, lon_cells, _, width = background.shape
    tiles_lat = record_values.shape[1]

    sent, up, down = packed(
        record_values, record_cell, record_instrument, block_counts, background
    )
    received = lax.all_to_all(sent, ("lon", "lat"), split_axis=0, concat_axis=0, tiled=True)
    north, south = before_and_after(swapped(up, down, "lat", wraps=False), "lat")

    later, _ = lax.optimization_barrier((background, up))

    def columns(low, end):
        return jnp.concatenate([north[:, low:end], later[:, low:end], south[:, low:end]], axis=0)

    got = swapped(columns(0, HLON), columns(lon_cells - HLON, lon_cells), "lon", wraps=True)

    lat = lax.axis_index("lat")
    scalars = jnp.stack([lat == 0, lat < 0, lat == tiles_lat - 1]).astype(jnp.int32)
    plan = rectangles(lat_cells, lon_cells)
    rest = sum(padded(tokens_of(plan[tile][number])) for tile, number in side_entries())
    weights = [
        first_gain.reshape(1, width),
        attn_weight,
        mix_weight,
        second_gain.reshape(1, width),
        up_weight,
        down_weight.T,
    ]
    smem = pl.BlockSpec(memory_space=pltpu.SMEM)
    vmem = pl.BlockSpec(memory_space=pltpu.VMEM)
    anywhere = pl.BlockSpec(memory_space=pl.ANY)
    params = pltpu.CompilerParams(vmem_limit_bytes=LIMIT)
    result = jax.ShapeDtypeStruct(background.shape, BF16)
    middle, rest = pl.pallas_call(
        functools.partial(middle_kernel, plan),
        out_shape=[result, jax.ShapeDtypeStruct((rest, PAD), F32)],
        in_specs=[smem] + [vmem] * (7 + len(weights)),
        out_specs=[anywhere, vmem],
        scratch_shapes=[
            pltpu.VMEM((lat_cells, lon_cells - WLON, LEV, width), BF16),
            pltpu.SemaphoreType.DMA((1,)),
        ],
        compiler_params=params,
        cost_estimate=pl.CostEstimate(
            flops=4 * 10**9, bytes_accessed=4 * 10**6, transcendentals=10**6
        ),
    )(
        scalars,
        received,
        north,
        south,
        background,
        input_weight.T,
        instrument_table,
        lift_weight,
        *weights,
    )
    rest, *got = lax.optimization_barrier((rest, *got))
    west, east = before_and_after(got, "lon")
    return pl.pallas_call(
        functools.partial(side_kernel, plan),
        out_shape=result,
        in_specs=[smem] + [vmem] * (6 + len(weights)) + [anywhere],
        out_specs=anywhere,
        scratch_shapes=[
            pltpu.VMEM((2, lat_cells, HLON, LEV, width), BF16),
            pltpu.SemaphoreType.DMA((2,)),
        ],
        input_output_aliases={7 + len(weights): 0},
        compiler_params=params,
        cost_estimate=pl.CostEstimate(
            flops=3 * 10**9, bytes_accessed=4 * 10**6, transcendentals=10**6
        ),
    )(scalars, rest, north, south, west, east, background, *weights, middle)


def solution(mesh):
    placed = (
        P("lon", "lat", None, None),
        P("lon", "lat", None),
        P("lon", "lat", None),
        P("lon", "lat"),
        P("lat", "lon", None, None),
        P(),
        P(),
        P(),
        P(),
        P(),
        P(),
        P(),
        P(),
        P(),
    )
    return jax.shard_map(
        local, mesh=mesh, in_specs=placed, out_specs=P("lat", "lon", None, None), check_vma=False
    )
```

```python
import functools

import jax
import jax.numpy as jnp
from jax import lax
from jax.experimental import pallas as pl
from jax.experimental.pallas import tpu as pltpu
from jax.sharding import PartitionSpec as P

HEADS = 6
INSTR = 8
LEV = 2
WLAT = 6
WLON = 12
HLAT = WLAT // 2
HLON = WLON // 2
LANES = 128
PAD = 256
CHUNK = 32
LIMIT = 40 * 2**20
BF16 = jnp.bfloat16
F32 = jnp.float32

AROUND = [(dy, dx) for dy in (-1, 0, 1) for dx in (-1, 0, 1)]
ROWS = INSTR * len(AROUND)
COLS = ROWS + len(AROUND)


def swap_pairs(axis, first, wraps):
    count = lax.axis_size(axis)
    pairs = []
    for low in range(first, count, 2):
        high = (low + 1) % count
        if high > low or wraps:
            pairs += [(low, high), (high, low)]
    return pairs


def swapped(mine, axis, wraps):
    return [lax.ppermute(one, axis, swap_pairs(axis, n, wraps)) for n, one in enumerate(mine)]


def in_order(got, axis):
    even = lax.axis_index(axis) % 2 == 0
    return jnp.where(even, got[1], got[0]), jnp.where(even, got[0], got[1])


def rectangles(lat_cells, lon_cells):
    lat = {-1: [(lat_cells - HLAT, HLAT)], 1: [(0, HLAT)]}
    lat[0] = [(0, HLAT), (HLAT, lat_cells - WLAT), (lat_cells - HLAT, HLAT)]
    lon = {-1: [(lon_cells - HLON, HLON)], 1: [(0, HLON)]}
    lon[0] = [(0, HLON), (HLON, lon_cells - WLON), (lon_cells - HLON, HLON)]
    return [
        [(top, high, left, wide) for top, high in lat[dy] for left, wide in lon[dx]]
        for dy, dx in AROUND
    ]


def tokens_of(part):
    return part[1] * part[3] * LEV


def padded(count):
    return -(-count // 8) * 8


def gelu(x):
    half = 0.5 * x
    inner = x * (0.7978845608028654 + 0.035677408136300125 * (x * x))
    return half + half * jnp.tanh(inner)


def normalise(wide, gain):
    average = jnp.mean(wide, axis=-1, keepdims=True)
    centred = wide - average
    spread = jnp.mean(centred * centred, axis=-1, keepdims=True)
    return centred * lax.rsqrt(spread + 1e-05) * gain


def dot(a, b):
    return jnp.dot(a, b, preferred_element_type=F32)


def dot_nt(a, b):
    return lax.dot_general(a, b, (((1,), (1,)), ((), ())), preferred_element_type=F32)


def with_ones(tensor):
    ones = jnp.ones((tensor.shape[0], PAD - tensor.shape[1]), F32)
    return jnp.concatenate([tensor, ones], axis=1).astype(BF16)


def below(*pieces):
    return jnp.concatenate(pieces, axis=0) if len(pieces) > 1 else pieces[0]


def pack_kernel(
    values_ref,
    cell_ref,
    tag_ref,
    count_ref,
    back_ref,
    *refs,
):
    out_ref, up_ref, down_ref, values, cells, tags, held, sem = refs
    tiles_lon, tiles_lat, capacity, _ = values_ref.shape
    lat_cells, lon_cells = back_ref.shape[:2]
    strips = [
        (back_ref.at[:HLAT], up_ref),
        (back_ref.at[lat_cells - HLAT :], down_ref),
    ]
    copies = [
        pltpu.make_async_copy(cell_ref, cells, sem.at[0]),
        pltpu.make_async_copy(tag_ref, tags, sem.at[1]),
        pltpu.make_async_copy(count_ref, held, sem.at[2]),
        pltpu.make_async_copy(values_ref, values, sem.at[3]),
    ]
    copies += [
        pltpu.make_async_copy(source, strip, sem.at[4 + n])
        for n, (source, strip) in enumerate(strips)
    ]
    for copy in copies:
        copy.start()
    for copy in copies[:3]:
        copy.wait()
    counts = below(*[held[tile : tile + 1, :] for tile in range(tiles_lat) for _ in range(capacity)])
    cell = cells[...]
    slot = lax.broadcasted_iota(jnp.int32, cell.shape, 0) % capacity
    row = cell // lon_cells
    fields = [jnp.where(slot < counts, row, 255), cell - row * lon_cells, tags[...]]
    rows, columns, kinds = (field.astype(F32) for field in fields)
    lane = lax.broadcasted_iota(jnp.int32, (cell.shape[0], LANES), 1)
    kind_of = (lane % INSTR).astype(F32)
    marks = [
        ((lane < ROWS) & (lane // INSTR == n)) | (lane == ROWS + n) | (lane == COLS + n)
        for n in range(len(AROUND))
    ]
    turned = []
    for lon in range(tiles_lon):
        meta = jnp.where(kind_of == kinds[:, lon : lon + 1], 1.0, 0.0)
        meta = jnp.where(lane >= ROWS, rows[:, lon : lon + 1], meta)
        meta = jnp.where(lane >= COLS, columns[:, lon : lon + 1], meta)
        turns = {0: meta}
        for dy in (-1, 1):
            by = dy * capacity % meta.shape[0]
            turns[dy] = below(meta[by:], meta[:by])
        turned.append(turns)
    for lon in range(tiles_lon):
        meta = jnp.zeros(lane.shape, F32)
        for mark, (dy, dx) in zip(marks, AROUND):
            meta = jnp.where(mark, turned[(lon + dx) % tiles_lon][dy], meta)
        out_ref[lon, :, len(AROUND)] = meta.astype(BF16).reshape(tiles_lat, capacity, LANES)
    copies[3].wait()
    for n, (dy, dx) in enumerate(AROUND):
        spans = {0: [(0, tiles_lat)], 1: [(0, tiles_lat - 1), (tiles_lat - 1, tiles_lat)]}
        spans[-1] = [(0, 1), (1, tiles_lat)]

        def copy_tiles(lon, n=n, dx=dx, dy=dy, spans=spans[dy]):
            source = lax.rem(lon + dx + tiles_lon, tiles_lon)
            for low, end in spans:
                first = (low + dy) % tiles_lat
                out_ref[lon, low:end, n] = values[source, first : first + end - low]

        if tiles_lon <= 8:
            for lon in range(tiles_lon):
                copy_tiles(lon)
        else:
            pl.loop(0, tiles_lon)(copy_tiles)
    for copy in copies[4:]:
        copy.wait()


def packed(record_values, record_cell, record_instrument, block_counts, background):
    tiles_lon, tiles_lat, capacity, wide = record_values.shape
    anywhere = pl.BlockSpec(memory_space=pltpu.HBM)
    ints = pltpu.VMEM((tiles_lat * capacity, tiles_lon), jnp.int32)
    shape = (tiles_lon, tiles_lat, len(AROUND) + 1, capacity, wide)
    lat_cells, lon_cells, levels, width = background.shape
    across = jax.ShapeDtypeStruct((HLAT, lon_cells, levels, width), BF16)
    out, *strips = pl.pallas_call(
        pack_kernel,
        out_shape=[jax.ShapeDtypeStruct(shape, BF16), across, across],
        in_specs=[anywhere] * 5,
        out_specs=[pl.BlockSpec(memory_space=pltpu.VMEM)] * 3,
        scratch_shapes=[
            pltpu.VMEM(record_values.shape, BF16),
            ints,
            ints,
            pltpu.VMEM((tiles_lat, tiles_lon), jnp.int32),
            pltpu.SemaphoreType.DMA((6,)),
        ],
        compiler_params=pltpu.CompilerParams(vmem_limit_bytes=56 * 2**20),
        cost_estimate=pl.CostEstimate(
            flops=20 * 10**9, bytes_accessed=10**6, transcendentals=0
        ),
    )(
        record_values,
        record_cell.transpose(1, 2, 0).reshape(-1, tiles_lon),
        record_instrument.transpose(1, 2, 0).reshape(-1, tiles_lon),
        block_counts.T,
        background,
    )
    return out.reshape((-1,) + shape[2:]), *strips


def token_codes(part, lon_cells):
    top, high, left, wide = part
    count = tokens_of(part)
    place = lax.broadcasted_iota(jnp.int32, (padded(count), LANES), 0)
    code = place + (top * lon_cells + left) * LEV
    for row in range(1, high):
        step = (lon_cells - wide) * LEV
        code = code + jnp.where(place >= row * wide * LEV, step, 0)
    return jnp.where(place < count, code, -8).astype(F32)


def entries_of(windows):
    entries = [(4, 3 * i + j) for i, j in windows]
    for i, j in windows:
        if i != 1:
            entries.append((3 * i + 1, j))
        if j != 1:
            entries.append((3 + j, i))
        if i != 1 and j != 1:
            entries.append((3 * i + j, 0))
    return entries


def alternate(*chains):
    chains, begun = list(chains), 1
    while chains:
        for chain in chains[:begun]:
            if next(chain, None) is None:
                chains.remove(chain)
                begun -= 1
        begun += 1


def scattered(recv_ref, first_ref, table_ref, lift_ref, plan, lon_cells):
    sources, _, capacity, _ = recv_ref.shape
    width = table_ref.shape[1]
    chunk = min(CHUNK, sources)
    slots = chunk * capacity
    first, lift = first_ref[...], lift_ref[...]
    table = below(*[table_ref[...].astype(F32)] * (LANES // INSTR)).astype(BF16)
    lane = lax.broadcasted_iota(jnp.int32, (16, LANES), 1)
    sub = lax.broadcasted_iota(jnp.int32, (16, LANES), 0)
    weigh = jnp.where(lane == ROWS + sub, float(lon_cells * LEV), 0.0)
    weigh = jnp.where(lane == COLS + sub, float(LEV), weigh).astype(BF16)
    codes = [below(*[token_codes(part, lon_cells) for part in parts]) for parts in plan]

    def scatter(begin):
        meta = recv_ref[pl.ds(begin, chunk), len(AROUND)].reshape(slots, LANES)
        records = below(
            *[
                recv_ref[pl.ds(begin, chunk), n].reshape(slots, LANES)
                for n in range(len(AROUND))
            ]
        )
        lane = lax.broadcasted_iota(jnp.int32, meta.shape, 1) // INSTR
        wide = meta.astype(F32)
        chosen = below(*[jnp.where(lane == n, wide, 0.0) for n in range(len(AROUND))]).astype(BF16)
        encoded = gelu(dot_nt(records, first) + dot(chosen, table)).astype(BF16)
        lifted = gelu(dot(encoded, lift))
        tokens = dot_nt(weigh, meta)
        sums = []
        for n in range(len(AROUND)):
            part = lifted[n * slots : (n + 1) * slots]
            part = with_ones(
                below(*[part[:, level * width : (level + 1) * width] for level in range(LEV)])
            )
            token = tokens[n : n + 1]
            token = jnp.concatenate([token + float(level) for level in range(LEV)], axis=1)
            if token.shape[1] == LANES:
                hot = codes[n] == token
            else:
                hot = codes[n][:, :1] == token
            sums.append(dot(jnp.where(hot, 1.0, 0.0).astype(BF16), part))
        return tuple(sums)

    sums = scatter(0)
    if sources > chunk:
        sums = lax.fori_loop(
            1,
            sources // chunk,
            lambda step, total: tuple(a + b for a, b in zip(total, scatter(step * chunk))),
            sums,
        )
    return sums


def worked(plan, places, sum_of, borders, weights, scalars_ref, put):
    back_ref, north_ref, south_ref, west_ref, east_ref = borders
    gain_one_ref, attn_ref, mix_ref, gain_two_ref, up_ref, down_ref = weights
    lat_cells, width = back_ref.shape[0], back_ref.shape[3]
    pieces, spans, start = [], {}, 0
    for tile, number in entries_of(places):
        dy, dx = AROUND[tile]
        part = plan[tile][number]
        top, high, left, wide = part
        count = tokens_of(part)
        if dx:
            ref = west_ref if dx < 0 else east_ref
            top, left = {-1: 0, 0: top + HLAT, 1: lat_cells + HLAT}[dy], 0
        elif dy:
            ref, top = (north_ref, 0) if dy < 0 else (south_ref, 0)
        else:
            ref = back_ref
        piece = ref[top : top + high, left : left + wide].reshape(count, width).astype(F32)
        full = padded(count)
        if full > count:
            piece = below(piece, jnp.zeros((full - count, width), F32))
        pieces.append(piece)
        spans[tile, number] = (start, count)
        start += full
    sums = below(*[sum_of(*entry) for entry in entries_of(places)])
    share = 1.0 / (1.0 + sums[:, width : width + 1])
    latent = ((below(*pieces) + sums[:, :width]) * share).astype(BF16).astype(F32)
    normed = normalise(latent, gain_one_ref[...].astype(F32))
    yield True

    def piece_of(tile, number):
        start, count = spans[tile, number]
        return normed[start : start + count]

    groups = [padded(tokens_of(plan[4][3 * i + j])) for i, j in places]
    end = sum(groups)
    windows = []
    for i, j in places:
        window = [piece_of(4, 3 * i + j)]
        if i != 1:
            window.append(piece_of(3 * i + 1, j))
        if j != 1:
            window.append(piece_of(3 + j, i))
        if i != 1 and j != 1:
            window.append(piece_of(3 * i + j, 0))
        windows.append(window)
    tokens = below(*[piece for window in windows for piece in window]).astype(BF16)
    weight = attn_ref[...]
    head = width // HEADS
    keys = dot(tokens, weight[:, width : 2 * width]).astype(BF16)
    query = dot(normed[:end].astype(BF16), weight[:, :width]) * head ** (-0.5)
    values = with_ones(dot(tokens, weight[:, 2 * width :]))
    yield True

    head_of = lax.broadcasted_iota(jnp.int32, (1, width), 1) // head
    many = WLAT * WLON * LEV
    corner = HLAT * HLON * LEV
    key = lax.broadcasted_iota(jnp.int32, (1, many), 1)
    mixed, start = [], 0
    for w, ((i, j), rows) in enumerate(zip(places, groups)):
        part = query[start : start + rows]
        stacked = below(*[jnp.where(head_of == h, part, 0.0) for h in range(HEADS)]).astype(BF16)
        scores = dot_nt(stacked, keys[w * many : (w + 1) * many])
        yield True
        if i != 1:
            if j == 1:
                inside = key < 2 * corner
            else:
                inside = (key < corner) | ((key >= 2 * corner) & (key < 3 * corner))
            scores = jnp.where(inside | (scalars_ref[i] == 0), scores, -1e30)
        largest = jnp.max(scores, axis=-1, keepdims=True)
        raised = jnp.exp(scores - largest).astype(BF16)
        product = dot(raised, values[w * many : (w + 1) * many])
        yield True
        product = product[:, :width] * (1.0 / product[:, width : width + 1])
        total = jnp.zeros((rows, width), F32)
        for h in range(HEADS):
            total = jnp.where(head_of == h, product[h * rows : (h + 1) * rows], total)
        mixed.append(total)
        start += rows
    mixed = below(*mixed).astype(BF16)

    after = (latent[:end] + dot(mixed, mix_ref[...])).astype(BF16).astype(F32)
    yield True
    normed_two = normalise(after, gain_two_ref[...].astype(F32)).astype(BF16)
    hidden = dot(normed_two, up_ref[...])
    yield True
    result = after + dot_nt(gelu(hidden).astype(BF16), down_ref[...])
    yield True
    start = 0
    for (i, j), rows in zip(places, groups):
        part = plan[4][3 * i + j]
        piece = result[start : start + tokens_of(part)].astype(BF16)
        put(part, j, piece.reshape(part[1], part[3], LEV, width))
        start += rows


MIDDLE = [[(0, 1), (2, 1)], [(1, 1)]]
SIDES = [[(0, 0), (1, 0), (2, 0)], [(0, 2), (1, 2), (2, 2)]]


def side_entries():
    return [entry for places in SIDES for entry in entries_of(places)]


def middle_kernel(
    plan,
    scalars_ref,
    recv_ref,
    north_ref,
    south_ref,
    back_ref,
    first_ref,
    table_ref,
    lift_ref,
    *refs,
):
    *weights, out_ref, rest_ref, held_ref, sem = refs
    sums = scattered(recv_ref, first_ref, table_ref, lift_ref, plan, back_ref.shape[1])

    def sum_of(tile, number):
        start = sum(padded(tokens_of(part)) for part in plan[tile][:number])
        return sums[tile][start : start + padded(tokens_of(plan[tile][number]))]

    rest_ref[...] = below(*[sum_of(*entry) for entry in side_entries()])
    left, wide = plan[4][4][2:]

    def put(part, _, piece):
        held_ref[part[0] : part[0] + part[1]] = piece

    borders = (back_ref, north_ref, south_ref, None, None)
    alternate(
        *[worked(plan, places, sum_of, borders, weights, scalars_ref, put) for places in MIDDLE]
    )
    copy = pltpu.make_async_copy(held_ref, out_ref.at[:, left : left + wide], sem.at[0])
    copy.start()
    copy.wait()


def side_kernel(
    plan,
    scalars_ref,
    rest_ref,
    north_ref,
    south_ref,
    west_ref,
    east_ref,
    back_ref,
    *refs,
):
    *weights, _, out_ref, held_ref, sem = refs
    spans, start = {}, 0
    for tile, number in side_entries():
        rows = padded(tokens_of(plan[tile][number]))
        spans[tile, number] = (start, start + rows)
        start += rows

    def sum_of(tile, number):
        start, end = spans[tile, number]
        return rest_ref[start:end, :]

    def put(part, j, piece):
        held_ref[j // 2, part[0] : part[0] + part[1]] = piece

    borders = (back_ref, north_ref, south_ref, west_ref, east_ref)
    alternate(
        *[worked(plan, places, sum_of, borders, weights, scalars_ref, put) for places in SIDES]
    )
    copies = []
    for n, number in enumerate((0, 2)):
        left, wide = plan[4][number][2:]
        copies.append(
            pltpu.make_async_copy(held_ref.at[n], out_ref.at[:, left : left + wide], sem.at[n])
        )
        copies[n].start()
    for copy in copies:
        copy.wait()


def join_kernel(even_ref, one_ref, two_ref, back_ref, north_ref, south_ref, first_ref, second_ref):
    lat_cells, lon_cells = back_ref.shape[:2]

    def strips(before, after):
        north_ref[...] = before[...]
        south_ref[...] = after[...]

    def sides(left, right):
        for ref, low in ((left, 0), (right, lon_cells - HLON)):
            ref[:HLAT] = north_ref[:, low : low + HLON]
            ref[HLAT : HLAT + lat_cells] = back_ref[:, low : low + HLON]
            ref[HLAT + lat_cells :] = south_ref[:, low : low + HLON]

    pl.when(even_ref[0] == 1)(lambda: strips(two_ref, one_ref))
    pl.when(even_ref[0] == 0)(lambda: strips(one_ref, two_ref))
    pl.when(even_ref[1] == 1)(lambda: sides(second_ref, first_ref))
    pl.when(even_ref[1] == 0)(lambda: sides(first_ref, second_ref))


def joined(even, got, background):
    lat_cells, lon_cells, levels, width = background.shape
    across = jax.ShapeDtypeStruct((HLAT, lon_cells, levels, width), BF16)
    along = jax.ShapeDtypeStruct((lat_cells + WLAT, HLON, levels, width), BF16)
    vmem = pl.BlockSpec(memory_space=pltpu.VMEM)
    return pl.pallas_call(
        join_kernel,
        out_shape=[across, across, along, along],
        in_specs=[pl.BlockSpec(memory_space=pltpu.SMEM), vmem, vmem, vmem],
        out_specs=[vmem] * 4,
        compiler_params=pltpu.CompilerParams(vmem_limit_bytes=LIMIT),
        cost_estimate=pl.CostEstimate(
            flops=20 * 10**9, bytes_accessed=10**6, transcendentals=0
        ),
    )(even, *got, background)


def local(
    record_values,
    record_cell,
    record_instrument,
    block_counts,
    background,
    input_weight,
    instrument_table,
    lift_weight,
    first_gain,
    attn_weight,
    mix_weight,
    second_gain,
    up_weight,
    down_weight,
):
    lat_cells, lon_cells, _, width = background.shape
    tiles_lat = record_values.shape[1]

    sent, up, down = packed(
        record_values, record_cell, record_instrument, block_counts, background
    )
    received = lax.all_to_all(sent, ("lon", "lat"), split_axis=0, concat_axis=0, tiled=True)
    even = [lax.axis_index(axis) % 2 == 0 for axis in ("lat", "lon")]
    mine = (jnp.where(even[0], down, up), jnp.where(even[0], up, down))
    got = swapped(mine, "lat", wraps=False)
    later, _ = lax.optimization_barrier((background, up))
    north, south, *mine = joined(jnp.stack(even).astype(jnp.int32), got, later)
    got = swapped(mine, "lon", wraps=True)

    lat = lax.axis_index("lat")
    scalars = jnp.stack([lat == 0, lat < 0, lat == tiles_lat - 1]).astype(jnp.int32)
    plan = rectangles(lat_cells, lon_cells)
    rest = sum(padded(tokens_of(plan[tile][number])) for tile, number in side_entries())
    weights = [
        first_gain.reshape(1, width),
        attn_weight,
        mix_weight,
        second_gain.reshape(1, width),
        up_weight,
        down_weight.T,
    ]
    smem = pl.BlockSpec(memory_space=pltpu.SMEM)
    vmem = pl.BlockSpec(memory_space=pltpu.VMEM)
    anywhere = pl.BlockSpec(memory_space=pl.ANY)
    params = pltpu.CompilerParams(vmem_limit_bytes=LIMIT)
    result = jax.ShapeDtypeStruct(background.shape, BF16)
    middle, rest = pl.pallas_call(
        functools.partial(middle_kernel, plan),
        out_shape=[result, jax.ShapeDtypeStruct((rest, PAD), F32)],
        in_specs=[smem] + [vmem] * (7 + len(weights)),
        out_specs=[anywhere, vmem],
        scratch_shapes=[
            pltpu.VMEM((lat_cells, lon_cells - WLON, LEV, width), BF16),
            pltpu.SemaphoreType.DMA((1,)),
        ],
        compiler_params=params,
        cost_estimate=pl.CostEstimate(
            flops=4 * 10**9, bytes_accessed=4 * 10**6, transcendentals=10**6
        ),
    )(
        scalars,
        received,
        north,
        south,
        background,
        input_weight.T,
        instrument_table,
        lift_weight,
        *weights,
    )
    rest, *got = lax.optimization_barrier((rest, *got))
    west, east = in_order(got, "lon")
    return pl.pallas_call(
        functools.partial(side_kernel, plan),
        out_shape=result,
        in_specs=[smem] + [vmem] * (6 + len(weights)) + [anywhere],
        out_specs=anywhere,
        scratch_shapes=[
            pltpu.VMEM((2, lat_cells, HLON, LEV, width), BF16),
            pltpu.SemaphoreType.DMA((2,)),
        ],
        input_output_aliases={7 + len(weights): 0},
        compiler_params=params,
        cost_estimate=pl.CostEstimate(
            flops=3 * 10**9, bytes_accessed=4 * 10**6, transcendentals=10**6
        ),
    )(scalars, rest, north, south, west, east, background, *weights, middle)


def solution(mesh):
    placed = (
        P("lon", "lat", None, None),
        P("lon", "lat", None),
        P("lon", "lat", None),
        P("lon", "lat"),
        P("lat", "lon", None, None),
        P(),
        P(),
        P(),
        P(),
        P(),
        P(),
        P(),
        P(),
        P(),
    )
    return jax.shard_map(
        local, mesh=mesh, in_specs=placed, out_specs=P("lat", "lon", None, None), check_vma=False
    )
```

```python
import functools

import jax
import jax.numpy as jnp
from jax import lax
from jax.experimental import pallas as pl
from jax.experimental.pallas import tpu as pltpu
from jax.sharding import PartitionSpec as P

HEADS = 6
INSTR = 8
LEV = 2
WLAT = 6
WLON = 12
HLAT = WLAT // 2
HLON = WLON // 2
LANES = 128
PAD = 256
CHUNK = 32
LIMIT = 40 * 2**20
BF16 = jnp.bfloat16
F32 = jnp.float32

AROUND = [(dy, dx) for dy in (-1, 0, 1) for dx in (-1, 0, 1)]
ROWS = INSTR * len(AROUND)
COLS = ROWS + len(AROUND)


def swapped(up, down, axis, wraps):
    count = lax.axis_size(axis)
    even = lax.axis_index(axis) % 2 == 0
    got = []
    for first, mine in ((0, jnp.where(even, down, up)), (1, jnp.where(even, up, down))):
        pairs = []
        for low in range(first, count, 2):
            high = (low + 1) % count
            if high > low or wraps:
                pairs += [(low, high), (high, low)]
        got.append(lax.ppermute(mine, axis, pairs))
    return got


def before_and_after(got, axis):
    even = lax.axis_index(axis) % 2 == 0
    return jnp.where(even, got[1], got[0]), jnp.where(even, got[0], got[1])


def rectangles(lat_cells, lon_cells):
    lat = {-1: [(lat_cells - HLAT, HLAT)], 1: [(0, HLAT)]}
    lat[0] = [(0, HLAT), (HLAT, lat_cells - WLAT), (lat_cells - HLAT, HLAT)]
    lon = {-1: [(lon_cells - HLON, HLON)], 1: [(0, HLON)]}
    lon[0] = [(0, HLON), (HLON, lon_cells - WLON), (lon_cells - HLON, HLON)]
    return [
        [(top, high, left, wide) for top, high in lat[dy] for left, wide in lon[dx]]
        for dy, dx in AROUND
    ]


def tokens_of(part):
    return part[1] * part[3] * LEV


def padded(count):
    return -(-count // 8) * 8


def gelu(x):
    half = 0.5 * x
    inner = x * (0.7978845608028654 + 0.035677408136300125 * (x * x))
    return half + half * jnp.tanh(inner)


def normalise(wide, gain):
    average = jnp.mean(wide, axis=-1, keepdims=True)
    centred = wide - average
    spread = jnp.mean(centred * centred, axis=-1, keepdims=True)
    return centred * lax.rsqrt(spread + 1e-05) * gain


def dot(a, b):
    return jnp.dot(a, b, preferred_element_type=F32)


def dot_nt(a, b):
    return lax.dot_general(a, b, (((1,), (1,)), ((), ())), preferred_element_type=F32)


def about_one_over(x):
    return pl.reciprocal(x, approx=True)


def with_ones(tensor):
    ones = jnp.ones((tensor.shape[0], PAD - tensor.shape[1]), F32)
    return jnp.concatenate([tensor, ones], axis=1).astype(BF16)


def below(*pieces):
    return jnp.concatenate(pieces, axis=0) if len(pieces) > 1 else pieces[0]


def pack_kernel(
    values_ref,
    cell_ref,
    tag_ref,
    count_ref,
    back_ref,
    *refs,
):
    out_ref, up_ref, down_ref, values, cells, tags, held, sem = refs
    tiles_lon, tiles_lat, capacity, _ = values_ref.shape
    lat_cells, lon_cells = back_ref.shape[:2]
    strips = [
        (back_ref.at[:HLAT], up_ref),
        (back_ref.at[lat_cells - HLAT :], down_ref),
    ]
    copies = [
        pltpu.make_async_copy(cell_ref, cells, sem.at[0]),
        pltpu.make_async_copy(tag_ref, tags, sem.at[1]),
        pltpu.make_async_copy(count_ref, held, sem.at[2]),
        pltpu.make_async_copy(values_ref, values, sem.at[3]),
    ]
    copies += [
        pltpu.make_async_copy(source, strip, sem.at[4 + n])
        for n, (source, strip) in enumerate(strips)
    ]
    for copy in copies:
        copy.start()
    for copy in copies[:3]:
        copy.wait()
    counts = below(*[held[tile : tile + 1, :] for tile in range(tiles_lat) for _ in range(capacity)])
    cell = cells[...]
    slot = lax.broadcasted_iota(jnp.int32, cell.shape, 0) % capacity
    row = cell // lon_cells
    fields = [jnp.where(slot < counts, row, 255), cell - row * lon_cells, tags[...]]
    rows, columns, kinds = (field.astype(F32) for field in fields)
    lane = lax.broadcasted_iota(jnp.int32, (cell.shape[0], LANES), 1)
    kind_of = (lane % INSTR).astype(F32)
    marks = [
        ((lane < ROWS) & (lane // INSTR == n)) | (lane == ROWS + n) | (lane == COLS + n)
        for n in range(len(AROUND))
    ]
    turned = []
    for lon in range(tiles_lon):
        meta = jnp.where(kind_of == kinds[:, lon : lon + 1], 1.0, 0.0)
        meta = jnp.where(lane >= ROWS, rows[:, lon : lon + 1], meta)
        meta = jnp.where(lane >= COLS, columns[:, lon : lon + 1], meta)
        turns = {0: meta}
        for dy in (-1, 1):
            by = dy * capacity % meta.shape[0]
            turns[dy] = below(meta[by:], meta[:by])
        turned.append(turns)
    for lon in range(tiles_lon):
        meta = jnp.zeros(lane.shape, F32)
        for mark, (dy, dx) in zip(marks, AROUND):
            meta = jnp.where(mark, turned[(lon + dx) % tiles_lon][dy], meta)
        out_ref[lon, :, len(AROUND)] = meta.astype(BF16).reshape(tiles_lat, capacity, LANES)
    copies[3].wait()
    for n, (dy, dx) in enumerate(AROUND):
        spans = {0: [(0, tiles_lat)], 1: [(0, tiles_lat - 1), (tiles_lat - 1, tiles_lat)]}
        spans[-1] = [(0, 1), (1, tiles_lat)]

        def copy_tiles(lon, n=n, dx=dx, dy=dy, spans=spans[dy]):
            source = lax.rem(lon + dx + tiles_lon, tiles_lon)
            for low, end in spans:
                first = (low + dy) % tiles_lat
                out_ref[lon, low:end, n] = values[source, first : first + end - low]

        if tiles_lon <= 8:
            for lon in range(tiles_lon):
                copy_tiles(lon)
        else:
            pl.loop(0, tiles_lon)(copy_tiles)
    for copy in copies[4:]:
        copy.wait()


def packed(record_values, record_cell, record_instrument, block_counts, background):
    tiles_lon, tiles_lat, capacity, wide = record_values.shape
    anywhere = pl.BlockSpec(memory_space=pltpu.HBM)
    ints = pltpu.VMEM((tiles_lat * capacity, tiles_lon), jnp.int32)
    shape = (tiles_lon, tiles_lat, len(AROUND) + 1, capacity, wide)
    lat_cells, lon_cells, levels, width = background.shape
    across = jax.ShapeDtypeStruct((HLAT, lon_cells, levels, width), BF16)
    out, *strips = pl.pallas_call(
        pack_kernel,
        out_shape=[jax.ShapeDtypeStruct(shape, BF16), across, across],
        in_specs=[anywhere] * 5,
        out_specs=[pl.BlockSpec(memory_space=pltpu.VMEM)] * 3,
        scratch_shapes=[
            pltpu.VMEM(record_values.shape, BF16),
            ints,
            ints,
            pltpu.VMEM((tiles_lat, tiles_lon), jnp.int32),
            pltpu.SemaphoreType.DMA((6,)),
        ],
        compiler_params=pltpu.CompilerParams(vmem_limit_bytes=56 * 2**20),
        cost_estimate=pl.CostEstimate(
            flops=20 * 10**9, bytes_accessed=10**6, transcendentals=0
        ),
    )(
        record_values,
        record_cell.transpose(1, 2, 0).reshape(-1, tiles_lon),
        record_instrument.transpose(1, 2, 0).reshape(-1, tiles_lon),
        block_counts.T,
        background,
    )
    return out.reshape((-1,) + shape[2:]), *strips


def token_codes(part, lon_cells):
    top, high, left, wide = part
    count = tokens_of(part)
    place = lax.broadcasted_iota(jnp.int32, (padded(count), LANES), 0)
    code = place + (top * lon_cells + left) * LEV
    for row in range(1, high):
        step = (lon_cells - wide) * LEV
        code = code + jnp.where(place >= row * wide * LEV, step, 0)
    return jnp.where(place < count, code, -8).astype(F32)


def entries_of(windows):
    entries = [(4, 3 * i + j) for i, j in windows]
    for i, j in windows:
        if i != 1:
            entries.append((3 * i + 1, j))
        if j != 1:
            entries.append((3 + j, i))
        if i != 1 and j != 1:
            entries.append((3 * i + j, 0))
    return entries


def alternate(*chains):
    chains, begun = list(chains), 1
    while chains:
        for chain in chains[:begun]:
            if next(chain, None) is None:
                chains.remove(chain)
                begun -= 1
        begun += 1


def scattered(recv_ref, first_ref, table_ref, lift_ref, plan, lon_cells):
    sources, _, capacity, _ = recv_ref.shape
    width = table_ref.shape[1]
    chunk = min(CHUNK, sources)
    slots = chunk * capacity
    first, lift = first_ref[...], lift_ref[...]
    table = below(*[table_ref[...].astype(F32)] * (LANES // INSTR)).astype(BF16)
    lane = lax.broadcasted_iota(jnp.int32, (16, LANES), 1)
    sub = lax.broadcasted_iota(jnp.int32, (16, LANES), 0)
    weigh = jnp.where(lane == ROWS + sub, float(lon_cells * LEV), 0.0)
    weigh = jnp.where(lane == COLS + sub, float(LEV), weigh).astype(BF16)
    codes = [below(*[token_codes(part, lon_cells) for part in parts]) for parts in plan]

    def scatter(begin):
        meta = recv_ref[pl.ds(begin, chunk), len(AROUND)].reshape(slots, LANES)
        records = below(
            *[
                recv_ref[pl.ds(begin, chunk), n].reshape(slots, LANES)
                for n in range(len(AROUND))
            ]
        )
        lane = lax.broadcasted_iota(jnp.int32, meta.shape, 1) // INSTR
        wide = meta.astype(F32)
        chosen = below(*[jnp.where(lane == n, wide, 0.0) for n in range(len(AROUND))]).astype(BF16)
        encoded = gelu(dot(records, first) + dot(chosen, table)).astype(BF16)
        lifted = gelu(dot(encoded, lift))
        tokens = dot_nt(weigh, meta)
        sums = []
        for n in range(len(AROUND)):
            part = lifted[n * slots : (n + 1) * slots]
            part = with_ones(
                below(*[part[:, level * width : (level + 1) * width] for level in range(LEV)])
            )
            token = tokens[n : n + 1]
            token = jnp.concatenate([token + float(level) for level in range(LEV)], axis=1)
            if token.shape[1] == LANES:
                hot = codes[n] == token
            else:
                hot = codes[n][:, :1] == token
            sums.append(dot(jnp.where(hot, 1.0, 0.0).astype(BF16), part))
        return tuple(sums)

    sums = scatter(0)
    if sources > chunk:
        sums = lax.fori_loop(
            1,
            sources // chunk,
            lambda step, total: tuple(a + b for a, b in zip(total, scatter(step * chunk))),
            sums,
        )
    return sums


def worked(plan, places, sum_of, borders, weights, scalars_ref, put, done):
    back_ref, north_ref, south_ref, west_ref, east_ref = borders
    gain_one_ref, attn_ref, mix_ref, gain_two_ref, up_ref, down_ref = weights
    lat_cells, width = back_ref.shape[0], back_ref.shape[3]
    pieces, spans, start = [], {}, 0
    for tile, number in entries_of(places):
        dy, dx = AROUND[tile]
        part = plan[tile][number]
        top, high, left, wide = part
        count = tokens_of(part)
        if dx:
            ref = west_ref if dx < 0 else east_ref
            top, left = {-1: 0, 0: top + HLAT, 1: lat_cells + HLAT}[dy], 0
        elif dy:
            ref, top = (north_ref, 0) if dy < 0 else (south_ref, 0)
        else:
            ref = back_ref
        piece = ref[top : top + high, left : left + wide].reshape(count, width).astype(F32)
        full = padded(count)
        if full > count:
            piece = below(piece, jnp.zeros((full - count, width), F32))
        pieces.append(piece)
        spans[tile, number] = (start, count)
        start += full
    sums = below(*[sum_of(*entry) for entry in entries_of(places)])
    tally = 1.0 + sums[:, width : width + 1]
    share = about_one_over(tally)
    share = share * (2.0 - tally * share)
    latent = ((below(*pieces) + sums[:, :width]) * share).astype(BF16).astype(F32)
    normed = normalise(latent, gain_one_ref[...].astype(F32))
    yield True

    def piece_of(tile, number):
        start, count = spans[tile, number]
        return normed[start : start + count]

    groups = [padded(tokens_of(plan[4][3 * i + j])) for i, j in places]
    end = sum(groups)
    windows = []
    for i, j in places:
        window = [piece_of(4, 3 * i + j)]
        if i != 1:
            window.append(piece_of(3 * i + 1, j))
        if j != 1:
            window.append(piece_of(3 + j, i))
        if i != 1 and j != 1:
            window.append(piece_of(3 * i + j, 0))
        windows.append(window)
    tokens = below(*[piece for window in windows for piece in window]).astype(BF16)
    weight = attn_ref[...]
    head = width // HEADS
    keys = dot(tokens, weight[:, width : 2 * width]).astype(BF16)
    query = dot(normed[:end].astype(BF16), weight[:, :width]) * head ** (-0.5)
    values = with_ones(dot(tokens, weight[:, 2 * width :]))
    yield True

    head_of = lax.broadcasted_iota(jnp.int32, (1, width), 1) // head
    many = WLAT * WLON * LEV
    corner = HLAT * HLON * LEV
    key = lax.broadcasted_iota(jnp.int32, (1, many), 1)
    mixed, start = [], 0
    for w, ((i, j), rows) in enumerate(zip(places, groups)):
        part = query[start : start + rows]
        stacked = below(*[jnp.where(head_of == h, part, 0.0) for h in range(HEADS)]).astype(BF16)
        scores = dot_nt(stacked, keys[w * many : (w + 1) * many])
        yield True
        if i != 1:
            if j == 1:
                inside = key < 2 * corner
            else:
                inside = (key < corner) | ((key >= 2 * corner) & (key < 3 * corner))
            scores = jnp.where(inside | (scalars_ref[i] == 0), scores, -1e30)
        largest = jnp.max(scores, axis=-1, keepdims=True)
        raised = jnp.exp(scores - largest).astype(BF16)
        product = dot(raised, values[w * many : (w + 1) * many])
        yield True
        product = product[:, :width] * about_one_over(product[:, width : width + 1])
        total = jnp.zeros((rows, width), F32)
        for h in range(HEADS):
            total = jnp.where(head_of == h, product[h * rows : (h + 1) * rows], total)
        mixed.append(total)
        start += rows
    mixed = below(*mixed).astype(BF16)

    after = (latent[:end] + dot(mixed, mix_ref[...])).astype(BF16).astype(F32)
    yield True
    normed_two = normalise(after, gain_two_ref[...].astype(F32)).astype(BF16)
    hidden = dot(normed_two, up_ref[...])
    yield True
    result = after + dot(gelu(hidden).astype(BF16), down_ref[...])
    yield True
    start = 0
    for (i, j), rows in zip(places, groups):
        part = plan[4][3 * i + j]
        piece = result[start : start + tokens_of(part)].astype(BF16)
        put(part, j, piece.reshape(part[1], part[3], LEV, width))
        start += rows
    done(places)


MIDDLE = [[(0, 1), (2, 1)], [(1, 1)]]
SIDES = [[(0, 0), (1, 0), (2, 0)], [(0, 2), (1, 2), (2, 2)]]


def side_entries():
    return [entry for places in SIDES for entry in entries_of(places)]


def middle_kernel(
    plan,
    scalars_ref,
    recv_ref,
    north_ref,
    south_ref,
    back_ref,
    first_ref,
    table_ref,
    lift_ref,
    *refs,
):
    *weights, out_ref, rest_ref, held_ref, sem = refs
    sums = scattered(recv_ref, first_ref, table_ref, lift_ref, plan, back_ref.shape[1])

    def sum_of(tile, number):
        start = sum(padded(tokens_of(part)) for part in plan[tile][:number])
        return sums[tile][start : start + padded(tokens_of(plan[tile][number]))]

    rest_ref[...] = below(*[sum_of(*entry) for entry in side_entries()])
    left, wide = plan[4][4][2:]

    def put(part, _, piece):
        held_ref[part[0] : part[0] + part[1]] = piece

    copies = []

    def done(places):
        for i, _ in places:
            top, high = plan[4][3 * i + 1][:2]
            copies.append(
                pltpu.make_async_copy(
                    held_ref.at[top : top + high],
                    out_ref.at[top : top + high, left : left + wide],
                    sem.at[i],
                )
            )
            copies[-1].start()

    borders = (back_ref, north_ref, south_ref, None, None)
    alternate(
        *[
            worked(plan, places, sum_of, borders, weights, scalars_ref, put, done)
            for places in MIDDLE
        ]
    )
    for copy in copies:
        copy.wait()


def side_kernel(
    plan,
    scalars_ref,
    rest_ref,
    north_ref,
    south_ref,
    west_ref,
    east_ref,
    back_ref,
    *refs,
):
    *weights, _, out_ref, held_ref, sem = refs
    spans, start = {}, 0
    for tile, number in side_entries():
        rows = padded(tokens_of(plan[tile][number]))
        spans[tile, number] = (start, start + rows)
        start += rows

    def sum_of(tile, number):
        start, end = spans[tile, number]
        return rest_ref[start:end, :]

    def put(part, j, piece):
        held_ref[j // 2, part[0] : part[0] + part[1]] = piece

    copies = []

    def done(places):
        j = places[0][1]
        left, wide = plan[4][j][2:]
        copies.append(
            pltpu.make_async_copy(
                held_ref.at[j // 2], out_ref.at[:, left : left + wide], sem.at[j // 2]
            )
        )
        copies[-1].start()

    borders = (back_ref, north_ref, south_ref, west_ref, east_ref)
    alternate(
        *[
            worked(plan, places, sum_of, borders, weights, scalars_ref, put, done)
            for places in SIDES
        ]
    )
    for copy in copies:
        copy.wait()


def local(
    record_values,
    record_cell,
    record_instrument,
    block_counts,
    background,
    input_weight,
    instrument_table,
    lift_weight,
    first_gain,
    attn_weight,
    mix_weight,
    second_gain,
    up_weight,
    down_weight,
):
    lat_cells, lon_cells, _, width = background.shape
    tiles_lat = record_values.shape[1]

    sent, up, down = packed(
        record_values, record_cell, record_instrument, block_counts, background
    )
    received = lax.all_to_all(sent, ("lon", "lat"), split_axis=0, concat_axis=0, tiled=True)
    north, south = before_and_after(swapped(up, down, "lat", wraps=False), "lat")

    later, input_weight, down_weight, _ = lax.optimization_barrier(
        (background, input_weight, down_weight, up)
    )

    def columns(low, end):
        return jnp.concatenate([north[:, low:end], later[:, low:end], south[:, low:end]], axis=0)

    got = swapped(columns(0, HLON), columns(lon_cells - HLON, lon_cells), "lon", wraps=True)

    lat = lax.axis_index("lat")
    scalars = jnp.stack([lat == 0, lat < 0, lat == tiles_lat - 1]).astype(jnp.int32)
    plan = rectangles(lat_cells, lon_cells)
    rest = sum(padded(tokens_of(plan[tile][number])) for tile, number in side_entries())
    weights = [
        first_gain.reshape(1, width),
        attn_weight,
        mix_weight,
        second_gain.reshape(1, width),
        up_weight,
        down_weight,
    ]
    smem = pl.BlockSpec(memory_space=pltpu.SMEM)
    vmem = pl.BlockSpec(memory_space=pltpu.VMEM)
    anywhere = pl.BlockSpec(memory_space=pl.ANY)
    params = pltpu.CompilerParams(vmem_limit_bytes=LIMIT)
    result = jax.ShapeDtypeStruct(background.shape, BF16)
    middle, rest = pl.pallas_call(
        functools.partial(middle_kernel, plan),
        out_shape=[result, jax.ShapeDtypeStruct((rest, PAD), F32)],
        in_specs=[smem] + [vmem] * (7 + len(weights)),
        out_specs=[anywhere, vmem],
        scratch_shapes=[
            pltpu.VMEM((lat_cells, lon_cells - WLON, LEV, width), BF16),
            pltpu.SemaphoreType.DMA((3,)),
        ],
        compiler_params=params,
        cost_estimate=pl.CostEstimate(
            flops=4 * 10**9, bytes_accessed=4 * 10**6, transcendentals=10**6
        ),
    )(
        scalars,
        received,
        north,
        south,
        background,
        input_weight,
        instrument_table,
        lift_weight,
        *weights,
    )
    rest, *got = lax.optimization_barrier((rest, *got))
    west, east = before_and_after(got, "lon")
    return pl.pallas_call(
        functools.partial(side_kernel, plan),
        out_shape=result,
        in_specs=[smem] + [vmem] * (6 + len(weights)) + [anywhere],
        out_specs=anywhere,
        scratch_shapes=[
            pltpu.VMEM((2, lat_cells, HLON, LEV, width), BF16),
            pltpu.SemaphoreType.DMA((2,)),
        ],
        input_output_aliases={7 + len(weights): 0},
        compiler_params=params,
        cost_estimate=pl.CostEstimate(
            flops=3 * 10**9, bytes_accessed=4 * 10**6, transcendentals=10**6
        ),
    )(scalars, rest, north, south, west, east, background, *weights, middle)


def solution(mesh):
    placed = (
        P("lon", "lat", None, None),
        P("lon", "lat", None),
        P("lon", "lat", None),
        P("lon", "lat"),
        P("lat", "lon", None, None),
        P(),
        P(),
        P(),
        P(),
        P(),
        P(),
        P(),
        P(),
        P(),
    )
    return jax.shard_map(
        local, mesh=mesh, in_specs=placed, out_specs=P("lat", "lon", None, None), check_vma=False
    )
```

```python
import functools

import jax
import jax.numpy as jnp
from jax import lax
from jax.experimental import pallas as pl
from jax.experimental.pallas import tpu as pltpu
from jax.sharding import PartitionSpec as P

HEADS = 6
INSTR = 8
LEV = 2
WLAT = 6
WLON = 12
HLAT = WLAT // 2
HLON = WLON // 2
LANES = 128
PAD = 256
CHUNK = 32
LIMIT = 40 * 2**20
BF16 = jnp.bfloat16
F32 = jnp.float32

AROUND = [(dy, dx) for dy in (-1, 0, 1) for dx in (-1, 0, 1)]
ROWS = INSTR * len(AROUND)
COLS = ROWS + len(AROUND)


def swapped(up, down, axis, wraps):
    count = lax.axis_size(axis)
    even = lax.axis_index(axis) % 2 == 0
    got = []
    for first, mine in ((0, jnp.where(even, down, up)), (1, jnp.where(even, up, down))):
        pairs = []
        for low in range(first, count, 2):
            high = (low + 1) % count
            if high > low or wraps:
                pairs += [(low, high), (high, low)]
        got.append(lax.ppermute(mine, axis, pairs))
    return got


def before_and_after(got, axis):
    even = lax.axis_index(axis) % 2 == 0
    return jnp.where(even, got[1], got[0]), jnp.where(even, got[0], got[1])


def rectangles(lat_cells, lon_cells):
    lat = {-1: [(lat_cells - HLAT, HLAT)], 1: [(0, HLAT)]}
    lat[0] = [(0, HLAT), (HLAT, lat_cells - WLAT), (lat_cells - HLAT, HLAT)]
    lon = {-1: [(lon_cells - HLON, HLON)], 1: [(0, HLON)]}
    lon[0] = [(0, HLON), (HLON, lon_cells - WLON), (lon_cells - HLON, HLON)]
    return [
        [(top, high, left, wide) for top, high in lat[dy] for left, wide in lon[dx]]
        for dy, dx in AROUND
    ]


def tokens_of(part):
    return part[1] * part[3] * LEV


def padded(count):
    return -(-count // 8) * 8


def gelu(x):
    half = 0.5 * x
    inner = x * (0.7978845608028654 + 0.035677408136300125 * (x * x))
    return half + half * jnp.tanh(inner)


def row_sums(tensor):
    width = tensor.shape[1]
    return dot(tensor, jnp.ones((width, PAD), BF16))[:, :width]


def normalise(tensor, gain):
    scale = 1.0 / tensor.shape[1]
    centred = tensor - row_sums(tensor.astype(BF16)) * scale
    square = centred * centred
    high = square.astype(BF16)
    low = (square - high.astype(F32)).astype(BF16)
    spread = (row_sums(high) + row_sums(low)) * scale
    return centred * lax.rsqrt(spread + 1e-05) * gain


def dot(a, b):
    return jnp.dot(a, b, preferred_element_type=F32)


def dot_nt(a, b):
    return lax.dot_general(a, b, (((1,), (1,)), ((), ())), preferred_element_type=F32)


def about_one_over(x):
    return pl.reciprocal(x, approx=True)


def with_ones(tensor):
    ones = jnp.ones((tensor.shape[0], PAD - tensor.shape[1]), F32)
    return jnp.concatenate([tensor, ones], axis=1).astype(BF16)


def below(*pieces):
    return jnp.concatenate(pieces, axis=0) if len(pieces) > 1 else pieces[0]


def pack_kernel(
    values_ref,
    cell_ref,
    tag_ref,
    count_ref,
    back_ref,
    *refs,
):
    out_ref, up_ref, down_ref, values, cells, tags, held, sem = refs
    tiles_lon, tiles_lat, capacity, _ = values_ref.shape
    lat_cells, lon_cells = back_ref.shape[:2]
    strips = [
        (back_ref.at[:HLAT], up_ref),
        (back_ref.at[lat_cells - HLAT :], down_ref),
    ]
    copies = [
        pltpu.make_async_copy(cell_ref, cells, sem.at[0]),
        pltpu.make_async_copy(tag_ref, tags, sem.at[1]),
        pltpu.make_async_copy(count_ref, held, sem.at[2]),
        pltpu.make_async_copy(values_ref, values, sem.at[3]),
    ]
    copies += [
        pltpu.make_async_copy(source, strip, sem.at[4 + n])
        for n, (source, strip) in enumerate(strips)
    ]
    for copy in copies:
        copy.start()
    for copy in copies[:3]:
        copy.wait()
    counts = below(*[held[tile : tile + 1, :] for tile in range(tiles_lat) for _ in range(capacity)])
    cell = cells[...]
    slot = lax.broadcasted_iota(jnp.int32, cell.shape, 0) % capacity
    row = cell // lon_cells
    fields = [jnp.where(slot < counts, row, 255), cell - row * lon_cells, tags[...]]
    rows, columns, kinds = (field.astype(F32) for field in fields)
    lane = lax.broadcasted_iota(jnp.int32, (cell.shape[0], LANES), 1)
    kind_of = (lane % INSTR).astype(F32)
    marks = [
        ((lane < ROWS) & (lane // INSTR == n)) | (lane == ROWS + n) | (lane == COLS + n)
        for n in range(len(AROUND))
    ]
    turned = []
    for lon in range(tiles_lon):
        meta = jnp.where(kind_of == kinds[:, lon : lon + 1], 1.0, 0.0)
        meta = jnp.where(lane >= ROWS, rows[:, lon : lon + 1], meta)
        meta = jnp.where(lane >= COLS, columns[:, lon : lon + 1], meta)
        turns = {0: meta}
        for dy in (-1, 1):
            by = dy * capacity % meta.shape[0]
            turns[dy] = below(meta[by:], meta[:by])
        turned.append(turns)
    for lon in range(tiles_lon):
        meta = jnp.zeros(lane.shape, F32)
        for mark, (dy, dx) in zip(marks, AROUND):
            meta = jnp.where(mark, turned[(lon + dx) % tiles_lon][dy], meta)
        out_ref[lon, :, len(AROUND)] = meta.astype(BF16).reshape(tiles_lat, capacity, LANES)
    copies[3].wait()
    for n, (dy, dx) in enumerate(AROUND):
        spans = {0: [(0, tiles_lat)], 1: [(0, tiles_lat - 1), (tiles_lat - 1, tiles_lat)]}
        spans[-1] = [(0, 1), (1, tiles_lat)]

        def copy_tiles(lon, n=n, dx=dx, dy=dy, spans=spans[dy]):
            source = lax.rem(lon + dx + tiles_lon, tiles_lon)
            for low, end in spans:
                first = (low + dy) % tiles_lat
                out_ref[lon, low:end, n] = values[source, first : first + end - low]

        if tiles_lon <= 8:
            for lon in range(tiles_lon):
                copy_tiles(lon)
        else:
            pl.loop(0, tiles_lon)(copy_tiles)
    for copy in copies[4:]:
        copy.wait()


def packed(record_values, record_cell, record_instrument, block_counts, background):
    tiles_lon, tiles_lat, capacity, wide = record_values.shape
    anywhere = pl.BlockSpec(memory_space=pltpu.HBM)
    ints = pltpu.VMEM((tiles_lat * capacity, tiles_lon), jnp.int32)
    shape = (tiles_lon, tiles_lat, len(AROUND) + 1, capacity, wide)
    lat_cells, lon_cells, levels, width = background.shape
    across = jax.ShapeDtypeStruct((HLAT, lon_cells, levels, width), BF16)
    out, *strips = pl.pallas_call(
        pack_kernel,
        out_shape=[jax.ShapeDtypeStruct(shape, BF16), across, across],
        in_specs=[anywhere] * 5,
        out_specs=[pl.BlockSpec(memory_space=pltpu.VMEM)] * 3,
        scratch_shapes=[
            pltpu.VMEM(record_values.shape, BF16),
            ints,
            ints,
            pltpu.VMEM((tiles_lat, tiles_lon), jnp.int32),
            pltpu.SemaphoreType.DMA((6,)),
        ],
        compiler_params=pltpu.CompilerParams(vmem_limit_bytes=56 * 2**20),
        cost_estimate=pl.CostEstimate(
            flops=20 * 10**9, bytes_accessed=10**6, transcendentals=0
        ),
    )(
        record_values,
        record_cell.transpose(1, 2, 0).reshape(-1, tiles_lon),
        record_instrument.transpose(1, 2, 0).reshape(-1, tiles_lon),
        block_counts.T,
        background,
    )
    return out.reshape((-1,) + shape[2:]), *strips


def token_codes(part, lon_cells):
    top, high, left, wide = part
    count = tokens_of(part)
    place = lax.broadcasted_iota(jnp.int32, (padded(count), LANES), 0)
    code = place + (top * lon_cells + left) * LEV
    for row in range(1, high):
        step = (lon_cells - wide) * LEV
        code = code + jnp.where(place >= row * wide * LEV, step, 0)
    return jnp.where(place < count, code, -8).astype(F32)


def entries_of(windows):
    entries = [(4, 3 * i + j) for i, j in windows]
    for i, j in windows:
        if i != 1:
            entries.append((3 * i + 1, j))
        if j != 1:
            entries.append((3 + j, i))
        if i != 1 and j != 1:
            entries.append((3 * i + j, 0))
    return entries


def alternate(*chains):
    chains, begun = list(chains), 1
    while chains:
        for chain in chains[:begun]:
            if next(chain, None) is None:
                chains.remove(chain)
                begun -= 1
        begun += 1


def scattered(recv_ref, first_ref, table_ref, lift_ref, plan, lon_cells):
    sources, _, capacity, _ = recv_ref.shape
    width = table_ref.shape[1]
    chunk = min(CHUNK, sources)
    slots = chunk * capacity
    first, lift = first_ref[...], lift_ref[...]
    table = below(*[table_ref[...].astype(F32)] * (LANES // INSTR)).astype(BF16)
    lane = lax.broadcasted_iota(jnp.int32, (16, LANES), 1)
    sub = lax.broadcasted_iota(jnp.int32, (16, LANES), 0)
    weigh = jnp.where(lane == ROWS + sub, float(lon_cells * LEV), 0.0)
    weigh = jnp.where(lane == COLS + sub, float(LEV), weigh).astype(BF16)
    codes = [below(*[token_codes(part, lon_cells) for part in parts]) for parts in plan]

    def scatter(begin):
        meta = recv_ref[pl.ds(begin, chunk), len(AROUND)].reshape(slots, LANES)
        records = below(
            *[
                recv_ref[pl.ds(begin, chunk), n].reshape(slots, LANES)
                for n in range(len(AROUND))
            ]
        )
        lane = lax.broadcasted_iota(jnp.int32, meta.shape, 1) // INSTR
        wide = meta.astype(F32)
        chosen = below(*[jnp.where(lane == n, wide, 0.0) for n in range(len(AROUND))]).astype(BF16)
        encoded = gelu(dot(records, first) + dot(chosen, table)).astype(BF16)
        lifted = gelu(dot(encoded, lift))
        tokens = dot_nt(weigh, meta)
        sums = []
        for n in range(len(AROUND)):
            part = lifted[n * slots : (n + 1) * slots]
            part = with_ones(
                below(*[part[:, level * width : (level + 1) * width] for level in range(LEV)])
            )
            token = tokens[n : n + 1]
            token = jnp.concatenate([token + float(level) for level in range(LEV)], axis=1)
            if token.shape[1] == LANES:
                hot = codes[n] == token
            else:
                hot = codes[n][:, :1] == token
            sums.append(dot(jnp.where(hot, 1.0, 0.0).astype(BF16), part))
        return tuple(sums)

    sums = scatter(0)
    if sources > chunk:
        sums = lax.fori_loop(
            1,
            sources // chunk,
            lambda step, total: tuple(a + b for a, b in zip(total, scatter(step * chunk))),
            sums,
        )
    return sums


def worked(plan, places, sum_of, borders, weights, scalars_ref, put, done):
    back_ref, north_ref, south_ref, west_ref, east_ref = borders
    gain_one_ref, attn_ref, mix_ref, gain_two_ref, up_ref, down_ref = weights
    lat_cells, width = back_ref.shape[0], back_ref.shape[3]
    pieces, spans, start = [], {}, 0
    for tile, number in entries_of(places):
        dy, dx = AROUND[tile]
        part = plan[tile][number]
        top, high, left, wide = part
        count = tokens_of(part)
        if dx:
            ref = west_ref if dx < 0 else east_ref
            top, left = {-1: 0, 0: top + HLAT, 1: lat_cells + HLAT}[dy], 0
        elif dy:
            ref, top = (north_ref, 0) if dy < 0 else (south_ref, 0)
        else:
            ref = back_ref
        piece = ref[top : top + high, left : left + wide].reshape(count, width).astype(F32)
        full = padded(count)
        if full > count:
            piece = below(piece, jnp.zeros((full - count, width), F32))
        pieces.append(piece)
        spans[tile, number] = (start, count)
        start += full
    sums = below(*[sum_of(*entry) for entry in entries_of(places)])
    tally = 1.0 + sums[:, width : width + 1]
    share = about_one_over(tally)
    share = share * (2.0 - tally * share)
    latent = ((below(*pieces) + sums[:, :width]) * share).astype(BF16).astype(F32)
    normed = normalise(latent, gain_one_ref[...].astype(F32))
    yield True

    def piece_of(tile, number):
        start, count = spans[tile, number]
        return normed[start : start + count]

    groups = [padded(tokens_of(plan[4][3 * i + j])) for i, j in places]
    end = sum(groups)
    windows = []
    for i, j in places:
        window = [piece_of(4, 3 * i + j)]
        if i != 1:
            window.append(piece_of(3 * i + 1, j))
        if j != 1:
            window.append(piece_of(3 + j, i))
        if i != 1 and j != 1:
            window.append(piece_of(3 * i + j, 0))
        windows.append(window)
    tokens = below(*[piece for window in windows for piece in window]).astype(BF16)
    weight = attn_ref[...]
    head = width // HEADS
    keys = dot(tokens, weight[:, width : 2 * width]).astype(BF16)
    query = dot(normed[:end].astype(BF16), weight[:, :width]) * head ** (-0.5)
    values = dot(tokens, weight[:, 2 * width :]).astype(BF16)
    yield True

    head_of = lax.broadcasted_iota(jnp.int32, (1, width), 1) // head
    many = WLAT * WLON * LEV
    corner = HLAT * HLON * LEV
    key = lax.broadcasted_iota(jnp.int32, (1, many), 1)
    ones = jnp.ones((many, width), BF16)
    mixed, start = [], 0
    for w, ((i, j), rows) in enumerate(zip(places, groups)):
        part = query[start : start + rows]
        stacked = below(*[jnp.where(head_of == h, part, 0.0) for h in range(HEADS)]).astype(BF16)
        scores = dot_nt(stacked, keys[w * many : (w + 1) * many])
        yield True
        if i != 1:
            if j == 1:
                inside = key < 2 * corner
            else:
                inside = (key < corner) | ((key >= 2 * corner) & (key < 3 * corner))
            scores = jnp.where(inside | (scalars_ref[i] == 0), scores, -1e30)
        largest = jnp.max(scores, axis=-1, keepdims=True)
        raised = jnp.exp(scores - largest).astype(BF16)
        product = dot(raised, values[w * many : (w + 1) * many])
        weight_sums = dot(raised, ones)
        yield True
        total, divisor = product[:rows], weight_sums[:rows]
        for h in range(1, HEADS):
            own = head_of == h
            total = jnp.where(own, product[h * rows : (h + 1) * rows], total)
            divisor = jnp.where(own, weight_sums[h * rows : (h + 1) * rows], divisor)
        total = total * about_one_over(divisor)
        mixed.append(total)
        start += rows
    mixed = below(*mixed).astype(BF16)

    after = (latent[:end] + dot(mixed, mix_ref[...])).astype(BF16).astype(F32)
    yield True
    normed_two = normalise(after, gain_two_ref[...].astype(F32)).astype(BF16)
    hidden = dot(normed_two, up_ref[...])
    yield True
    result = after + dot(gelu(hidden).astype(BF16), down_ref[...])
    yield True
    start = 0
    for (i, j), rows in zip(places, groups):
        part = plan[4][3 * i + j]
        piece = result[start : start + tokens_of(part)].astype(BF16)
        put(part, j, piece.reshape(part[1], part[3], LEV, width))
        start += rows
    done(places)


MIDDLE = [[(0, 1), (2, 1)], [(1, 1)]]
SIDES = [[(0, 0), (1, 0), (2, 0)], [(0, 2), (1, 2), (2, 2)]]


def side_entries():
    return [entry for places in SIDES for entry in entries_of(places)]


def middle_kernel(
    plan,
    scalars_ref,
    recv_ref,
    north_ref,
    south_ref,
    back_ref,
    first_ref,
    table_ref,
    lift_ref,
    *refs,
):
    *weights, out_ref, rest_ref, held_ref, sem = refs
    sums = scattered(recv_ref, first_ref, table_ref, lift_ref, plan, back_ref.shape[1])

    def sum_of(tile, number):
        start = sum(padded(tokens_of(part)) for part in plan[tile][:number])
        return sums[tile][start : start + padded(tokens_of(plan[tile][number]))]

    rest_ref[...] = below(*[sum_of(*entry) for entry in side_entries()])
    left, wide = plan[4][4][2:]

    def put(part, _, piece):
        held_ref[part[0] : part[0] + part[1]] = piece

    copies = []

    def done(places):
        for i, _ in places:
            top, high = plan[4][3 * i + 1][:2]
            copies.append(
                pltpu.make_async_copy(
                    held_ref.at[top : top + high],
                    out_ref.at[top : top + high, left : left + wide],
                    sem.at[i],
                )
            )
            copies[-1].start()

    borders = (back_ref, north_ref, south_ref, None, None)
    alternate(
        *[
            worked(plan, places, sum_of, borders, weights, scalars_ref, put, done)
            for places in MIDDLE
        ]
    )
    for copy in copies:
        copy.wait()


def side_kernel(
    plan,
    scalars_ref,
    rest_ref,
    north_ref,
    south_ref,
    west_ref,
    east_ref,
    back_ref,
    *refs,
):
    *weights, _, out_ref, held_ref, sem = refs
    spans, start = {}, 0
    for tile, number in side_entries():
        rows = padded(tokens_of(plan[tile][number]))
        spans[tile, number] = (start, start + rows)
        start += rows

    def sum_of(tile, number):
        start, end = spans[tile, number]
        return rest_ref[start:end, :]

    def put(part, j, piece):
        held_ref[j // 2, part[0] : part[0] + part[1]] = piece

    copies = []

    def done(places):
        j = places[0][1]
        left, wide = plan[4][j][2:]
        copies.append(
            pltpu.make_async_copy(
                held_ref.at[j // 2], out_ref.at[:, left : left + wide], sem.at[j // 2]
            )
        )
        copies[-1].start()

    borders = (back_ref, north_ref, south_ref, west_ref, east_ref)
    alternate(
        *[
            worked(plan, places, sum_of, borders, weights, scalars_ref, put, done)
            for places in SIDES
        ]
    )
    for copy in copies:
        copy.wait()


def local(
    record_values,
    record_cell,
    record_instrument,
    block_counts,
    background,
    input_weight,
    instrument_table,
    lift_weight,
    first_gain,
    attn_weight,
    mix_weight,
    second_gain,
    up_weight,
    down_weight,
):
    lat_cells, lon_cells, _, width = background.shape
    tiles_lat = record_values.shape[1]

    sent, up, down = packed(
        record_values, record_cell, record_instrument, block_counts, background
    )
    received = lax.all_to_all(sent, ("lon", "lat"), split_axis=0, concat_axis=0, tiled=True)
    north, south = before_and_after(swapped(up, down, "lat", wraps=False), "lat")

    later, input_weight, down_weight, _ = lax.optimization_barrier(
        (background, input_weight, down_weight, up)
    )

    def columns(low, end):
        return jnp.concatenate([north[:, low:end], later[:, low:end], south[:, low:end]], axis=0)

    got = swapped(columns(0, HLON), columns(lon_cells - HLON, lon_cells), "lon", wraps=True)

    lat = lax.axis_index("lat")
    scalars = jnp.stack([lat == 0, lat < 0, lat == tiles_lat - 1]).astype(jnp.int32)
    plan = rectangles(lat_cells, lon_cells)
    rest = sum(padded(tokens_of(plan[tile][number])) for tile, number in side_entries())
    weights = [
        first_gain.reshape(1, width),
        attn_weight,
        mix_weight,
        second_gain.reshape(1, width),
        up_weight,
        down_weight,
    ]
    smem = pl.BlockSpec(memory_space=pltpu.SMEM)
    vmem = pl.BlockSpec(memory_space=pltpu.VMEM)
    anywhere = pl.BlockSpec(memory_space=pl.ANY)
    params = pltpu.CompilerParams(vmem_limit_bytes=LIMIT)
    result = jax.ShapeDtypeStruct(background.shape, BF16)
    middle, rest = pl.pallas_call(
        functools.partial(middle_kernel, plan),
        out_shape=[result, jax.ShapeDtypeStruct((rest, PAD), F32)],
        in_specs=[smem] + [vmem] * (7 + len(weights)),
        out_specs=[anywhere, vmem],
        scratch_shapes=[
            pltpu.VMEM((lat_cells, lon_cells - WLON, LEV, width), BF16),
            pltpu.SemaphoreType.DMA((3,)),
        ],
        compiler_params=params,
        cost_estimate=pl.CostEstimate(
            flops=4 * 10**9, bytes_accessed=4 * 10**6, transcendentals=10**6
        ),
    )(
        scalars,
        received,
        north,
        south,
        background,
        input_weight,
        instrument_table,
        lift_weight,
        *weights,
    )
    rest, *got = lax.optimization_barrier((rest, *got))
    west, east = before_and_after(got, "lon")
    return pl.pallas_call(
        functools.partial(side_kernel, plan),
        out_shape=result,
        in_specs=[smem] + [vmem] * (6 + len(weights)) + [anywhere],
        out_specs=anywhere,
        scratch_shapes=[
            pltpu.VMEM((2, lat_cells, HLON, LEV, width), BF16),
            pltpu.SemaphoreType.DMA((2,)),
        ],
        input_output_aliases={7 + len(weights): 0},
        compiler_params=params,
        cost_estimate=pl.CostEstimate(
            flops=3 * 10**9, bytes_accessed=4 * 10**6, transcendentals=10**6
        ),
    )(scalars, rest, north, south, west, east, background, *weights, middle)


def solution(mesh):
    placed = (
        P("lon", "lat", None, None),
        P("lon", "lat", None),
        P("lon", "lat", None),
        P("lon", "lat"),
        P("lat", "lon", None, None),
        P(),
        P(),
        P(),
        P(),
        P(),
        P(),
        P(),
        P(),
        P(),
    )
    return jax.shard_map(
        local, mesh=mesh, in_specs=placed, out_specs=P("lat", "lon", None, None), check_vma=False
    )
```

```python
import functools

import jax
import jax.numpy as jnp
from jax import lax
from jax.experimental import pallas as pl
from jax.experimental.pallas import tpu as pltpu
from jax.sharding import PartitionSpec as P

HEADS = 6
INSTR = 8
LEV = 2
WLAT = 6
WLON = 12
HLAT = WLAT // 2
HLON = WLON // 2
LANES = 128
PAD = 256
CHUNK = 32
LIMIT = 40 * 2**20
BF16 = jnp.bfloat16
F32 = jnp.float32

AROUND = (-1, 0, 1)
ROWS = INSTR * len(AROUND)
COLS = ROWS + len(AROUND)


def swapped(first, second, axis, wraps):
    count = lax.axis_size(axis)
    got = []
    for begin, mine in enumerate((first, second)):
        pairs = []
        for low in range(begin, count, 2):
            high = (low + 1) % count
            if high > low or wraps:
                pairs += [(low, high), (high, low)]
        got.append(lax.ppermute(mine, axis, pairs))
    return got


def rectangles(lat_cells, lon_cells):
    lat = {-1: [(lat_cells - HLAT, HLAT)], 1: [(0, HLAT)]}
    lat[0] = [(0, HLAT), (HLAT, lat_cells - WLAT), (lat_cells - HLAT, HLAT)]
    lon = [(0, HLON), (HLON, lon_cells - WLON), (lon_cells - HLON, HLON)]
    return [[(top, high, left, wide) for top, high in lat[dy] for left, wide in lon] for dy in AROUND]


def tokens_of(part):
    return part[1] * part[3] * LEV


def padded(count):
    return -(-count // 8) * 8


def gelu(x):
    half = 0.5 * x
    inner = x * (0.7978845608028654 + 0.035677408136300125 * (x * x))
    return half + half * jnp.tanh(inner)


def normalise(wide, gain):
    average = jnp.mean(wide, axis=-1, keepdims=True)
    centred = wide - average
    spread = jnp.mean(centred * centred, axis=-1, keepdims=True)
    return centred * lax.rsqrt(spread + 1e-05) * gain


def dot(a, b):
    return jnp.dot(a, b, preferred_element_type=F32)


def dot_nt(a, b):
    return lax.dot_general(a, b, (((1,), (1,)), ((), ())), preferred_element_type=F32)


def about_one_over(x):
    return pl.reciprocal(x, approx=True)


def with_ones(tensor):
    ones = jnp.ones((tensor.shape[0], PAD - tensor.shape[1]), F32)
    return jnp.concatenate([tensor, ones], axis=1).astype(BF16)


def below(*pieces):
    return jnp.concatenate(pieces, axis=0) if len(pieces) > 1 else pieces[0]


def pack_kernel(
    values_ref,
    cell_ref,
    tag_ref,
    count_ref,
    back_ref,
    *refs,
):
    out_ref, up_ref, down_ref, values, cells, tags, held, sem = refs
    tiles_lon, tiles_lat, capacity, _ = values_ref.shape
    lat_cells, lon_cells = back_ref.shape[:2]
    strips = [
        (back_ref.at[:HLAT], up_ref),
        (back_ref.at[lat_cells - HLAT :], down_ref),
    ]
    copies = [
        pltpu.make_async_copy(cell_ref, cells, sem.at[0]),
        pltpu.make_async_copy(tag_ref, tags, sem.at[1]),
        pltpu.make_async_copy(count_ref, held, sem.at[2]),
        pltpu.make_async_copy(values_ref, values, sem.at[3]),
    ]
    copies += [
        pltpu.make_async_copy(source, strip, sem.at[4 + n])
        for n, (source, strip) in enumerate(strips)
    ]
    for copy in copies:
        copy.start()
    for copy in copies[:3]:
        copy.wait()
    counts = below(*[held[tile : tile + 1, :] for tile in range(tiles_lat) for _ in range(capacity)])
    cell = cells[...]
    slot = lax.broadcasted_iota(jnp.int32, cell.shape, 0) % capacity
    row = cell // lon_cells
    fields = [jnp.where(slot < counts, row, 255), cell - row * lon_cells, tags[...]]
    rows, columns, kinds = (field.astype(F32) for field in fields)
    lane = lax.broadcasted_iota(jnp.int32, (cell.shape[0], LANES), 1)
    kind_of = (lane % INSTR).astype(F32)
    marks = [
        ((lane < ROWS) & (lane // INSTR == n)) | (lane == ROWS + n) | (lane == COLS + n)
        for n in range(len(AROUND))
    ]
    turned = []
    for lon in range(tiles_lon):
        meta = jnp.where(kind_of == kinds[:, lon : lon + 1], 1.0, 0.0)
        meta = jnp.where(lane >= ROWS, rows[:, lon : lon + 1], meta)
        meta = jnp.where(lane >= COLS, columns[:, lon : lon + 1], meta)
        turns = {0: meta}
        for dy in (-1, 1):
            by = dy * capacity % meta.shape[0]
            turns[dy] = below(meta[by:], meta[:by])
        turned.append(turns)
    for lon in range(tiles_lon):
        meta = jnp.zeros(lane.shape, F32)
        for mark, dy in zip(marks, AROUND):
            meta = jnp.where(mark, turned[lon][dy], meta)
        out_ref[lon, :, len(AROUND)] = meta.astype(BF16).reshape(tiles_lat, capacity, LANES)
    copies[3].wait()
    for n, dy in enumerate(AROUND):
        spans = {0: [(0, tiles_lat)], 1: [(0, tiles_lat - 1), (tiles_lat - 1, tiles_lat)]}
        spans[-1] = [(0, 1), (1, tiles_lat)]

        for low, end in spans[dy]:
            first = (low + dy) % tiles_lat
            out_ref[:, low:end, n] = values[:, first : first + end - low]
    for copy in copies[4:]:
        copy.wait()


def packed(record_values, record_cell, record_instrument, block_counts, background):
    tiles_lon, tiles_lat, capacity, wide = record_values.shape
    anywhere = pl.BlockSpec(memory_space=pltpu.HBM)
    ints = pltpu.VMEM((tiles_lat * capacity, tiles_lon), jnp.int32)
    shape = (tiles_lon, tiles_lat, len(AROUND) + 1, capacity, wide)
    lat_cells, lon_cells, levels, width = background.shape
    across = jax.ShapeDtypeStruct((HLAT, lon_cells, levels, width), BF16)
    out, *strips = pl.pallas_call(
        pack_kernel,
        out_shape=[jax.ShapeDtypeStruct(shape, BF16), across, across],
        in_specs=[anywhere] * 5,
        out_specs=[pl.BlockSpec(memory_space=pltpu.VMEM)] * 3,
        scratch_shapes=[
            pltpu.VMEM(record_values.shape, BF16),
            ints,
            ints,
            pltpu.VMEM((tiles_lat, tiles_lon), jnp.int32),
            pltpu.SemaphoreType.DMA((6,)),
        ],
        compiler_params=pltpu.CompilerParams(vmem_limit_bytes=56 * 2**20),
        cost_estimate=pl.CostEstimate(
            flops=20 * 10**9, bytes_accessed=10**6, transcendentals=0
        ),
    )(
        record_values,
        record_cell.transpose(1, 2, 0).reshape(-1, tiles_lon),
        record_instrument.transpose(1, 2, 0).reshape(-1, tiles_lon),
        block_counts.T,
        background,
    )
    return out.reshape((-1,) + shape[2:]), *strips


def token_codes(part, lon_cells):
    top, high, left, wide = part
    count = tokens_of(part)
    place = lax.broadcasted_iota(jnp.int32, (padded(count), LANES), 0)
    code = place + (top * lon_cells + left) * LEV
    for row in range(1, high):
        step = (lon_cells - wide) * LEV
        code = code + jnp.where(place >= row * wide * LEV, step, 0)
    return jnp.where(place < count, code, -8).astype(F32)


def alternate(*chains):
    chains, begun = list(chains), 1
    while chains:
        for chain in chains[:begun]:
            if next(chain, None) is None:
                chains.remove(chain)
                begun -= 1
        begun += 1


def scattered(recv_ref, first_ref, table_ref, lift_ref, plan, lon_cells):
    sources, _, capacity, _ = recv_ref.shape
    width = table_ref.shape[1]
    chunk = min(CHUNK, sources)
    slots = chunk * capacity
    first, lift = first_ref[...], lift_ref[...]
    table = below(*[table_ref[...].astype(F32)] * (LANES // INSTR)).astype(BF16)
    lane = lax.broadcasted_iota(jnp.int32, (16, LANES), 1)
    sub = lax.broadcasted_iota(jnp.int32, (16, LANES), 0)
    weigh = jnp.where(lane == ROWS + sub, float(lon_cells * LEV), 0.0)
    weigh = jnp.where(lane == COLS + sub, float(LEV), weigh).astype(BF16)
    codes = [below(*[token_codes(part, lon_cells) for part in parts]) for parts in plan]

    def scatter(begin):
        meta = recv_ref[pl.ds(begin, chunk), len(AROUND)].reshape(slots, LANES)
        records = below(
            *[
                recv_ref[pl.ds(begin, chunk), n].reshape(slots, LANES)
                for n in range(len(AROUND))
            ]
        )
        lane = lax.broadcasted_iota(jnp.int32, meta.shape, 1) // INSTR
        wide = meta.astype(F32)
        chosen = below(*[jnp.where(lane == n, wide, 0.0) for n in range(len(AROUND))]).astype(BF16)
        encoded = gelu(dot(records, first) + dot(chosen, table)).astype(BF16)
        lifted = gelu(dot(encoded, lift))
        tokens = dot_nt(weigh, meta)
        sums = []
        for n in range(len(AROUND)):
            part = lifted[n * slots : (n + 1) * slots]
            part = with_ones(
                below(*[part[:, level * width : (level + 1) * width] for level in range(LEV)])
            )
            token = tokens[n : n + 1]
            token = jnp.concatenate([token + float(level) for level in range(LEV)], axis=1)
            if token.shape[1] == LANES:
                hot = codes[n] == token
            else:
                hot = codes[n][:, :1] == token
            sums.append(dot(jnp.where(hot, 1.0, 0.0).astype(BF16), part))
        return tuple(sums)

    sums = scatter(0)
    if sources > chunk:
        sums = lax.fori_loop(
            1,
            sources // chunk,
            lambda step, total: tuple(a + b for a, b in zip(total, scatter(step * chunk))),
            sums,
        )
    return sums


def spans_of(plan):
    spans, start = {}, 0
    for tile in (1, 0, 2):
        for number, part in enumerate(plan[tile]):
            spans[tile, number] = (start, tokens_of(part))
            start += padded(tokens_of(part))
    return spans, start


def norm_kernel(
    plan,
    even_ref,
    recv_ref,
    one_ref,
    two_ref,
    back_ref,
    first_ref,
    table_ref,
    lift_ref,
    gain_ref,
    latent_ref,
    normed_ref,
    mine_ref,
    other_ref,
    north_ref,
    south_ref,
):
    def sort(before, after):
        north_ref[...] = before[...]
        south_ref[...] = after[...]

    pl.when(even_ref[0] == 1)(lambda: sort(two_ref, one_ref))
    pl.when(even_ref[0] == 0)(lambda: sort(one_ref, two_ref))
    sums = scattered(recv_ref, first_ref, table_ref, lift_ref, plan, back_ref.shape[1])
    width = back_ref.shape[3]
    spans, _ = spans_of(plan)
    normed = {}
    for tile, ref in ((1, back_ref), (0, north_ref), (2, south_ref)):
        pieces = []
        for top, high, left, wide in plan[tile]:
            top = top if tile == 1 else 0
            count = high * wide * LEV
            piece = ref[top : top + high, left : left + wide].reshape(count, width).astype(F32)
            if padded(count) > count:
                piece = below(piece, jnp.zeros((padded(count) - count, width), F32))
            pieces.append(piece)
        total = sums[tile]
        tally = 1.0 + total[:, width : width + 1]
        share = about_one_over(tally)
        share = share * (2.0 - tally * share)
        latent = ((below(*pieces) + total[:, :width]) * share).astype(BF16)
        if tile == 1:
            latent_ref[...] = latent
        normed[tile] = normalise(latent.astype(F32), gain_ref[...].astype(F32))
    normed = below(*[normed[tile] for tile in (1, 0, 2)])
    normed_ref[...] = normed.astype(BF16)

    half = HLAT * HLON * LEV

    def piece_of(tile, number, at=0):
        start = spans[tile, number][0] + at
        return normed[start : start + half]

    def strip(j):
        pairs = [
            (piece_of(1, j), piece_of(1, 3 + j)),
            (piece_of(1, 6 + j), piece_of(1, 3 + j, half)),
            (piece_of(0, j), piece_of(2, j)),
        ]
        return below(*[jnp.concatenate(pair, axis=1) for pair in pairs]).astype(BF16)

    left, right = strip(0), strip(2)

    def store(first, second):
        mine_ref[...] = first
        other_ref[...] = second

    pl.when(even_ref[1] == 1)(lambda: store(right, left))
    pl.when(even_ref[1] == 0)(lambda: store(left, right))


def worked(plan, places, token_pieces, own_normed, latent, weights, scalars_ref, put, done):
    attn_ref, mix_ref, gain_ref, up_ref, down_ref = weights
    width = mix_ref.shape[0]
    head = width // HEADS
    many = WLAT * WLON * LEV
    corner = HLAT * HLON * LEV
    groups = [padded(tokens_of(plan[1][3 * i + j])) for i, j in places]
    tokens = below(*[piece for i, j in places for piece in token_pieces(i, j)]).astype(BF16)
    weight = attn_ref[...]
    keys = dot(tokens, weight[:, width : 2 * width])
    query = dot(own_normed.astype(BF16), weight[:, :width]) * head ** (-0.5)
    query = jnp.concatenate([query, jnp.ones((query.shape[0], PAD - width), F32)], axis=1)
    values = with_ones(dot(tokens, weight[:, 2 * width :]))
    yield True

    lane = lax.broadcasted_iota(jnp.int32, (1, PAD), 1)
    key = lax.broadcasted_iota(jnp.int32, (many, PAD - width), 0)
    spare = lax.broadcasted_iota(jnp.int32, (many, PAD - width), 1)
    mixed, start = [], 0
    for w, ((i, j), rows) in enumerate(zip(places, groups)):
        part = query[start : start + rows]
        stacked = below(
            *[jnp.where((lane // head == h) | (lane >= width), part, 0.0) for h in range(HEADS)]
        ).astype(BF16)
        bias = jnp.zeros((many, PAD - width), F32)
        if i != 1:
            if j == 1:
                inside = key < 2 * corner
            else:
                inside = (key < corner) | ((key >= 2 * corner) & (key < 3 * corner))
            bias = jnp.where(inside | (spare > 0), 0.0, -3e38) * scalars_ref[i].astype(F32)
        here = jnp.concatenate([keys[w * many : (w + 1) * many], bias], axis=1).astype(BF16)
        scores = dot_nt(stacked, here)
        yield True
        largest = jnp.max(scores, axis=-1, keepdims=True)
        raised = jnp.exp(scores - largest).astype(BF16)
        product = dot(raised, values[w * many : (w + 1) * many])
        yield True
        product = product[:, :width] * about_one_over(product[:, width : width + 1])
        total = product[:rows]
        for h in range(1, HEADS):
            own = lane[:, :width] // head == h
            total = jnp.where(own, product[h * rows : (h + 1) * rows], total)
        mixed.append(total)
        start += rows
    mixed = below(*mixed).astype(BF16)

    after = (latent + dot(mixed, mix_ref[...])).astype(BF16).astype(F32)
    yield True
    normed_two = normalise(after, gain_ref[...].astype(F32)).astype(BF16)
    hidden = dot(normed_two, up_ref[...])
    yield True
    result = after + dot(gelu(hidden).astype(BF16), down_ref[...])
    yield True
    start = 0
    for (i, j), rows in zip(places, groups):
        part = plan[1][3 * i + j]
        piece = result[start : start + tokens_of(part)].astype(BF16)
        put(part, j, piece.reshape(part[1], part[3], LEV, width))
        start += rows
    done(places)


MIDDLE = [[(0, 1), (2, 1)], [(1, 1)]]
SIDES = [[(0, 0), (1, 0), (2, 0)], [(0, 2), (1, 2), (2, 2)]]


def chains_of(plan, groups, latent_ref, normed_ref, far, weights, scalars_ref, put, done):
    spans, _ = spans_of(plan)

    def rows_of(ref, tile, number, full=False):
        start, count = spans[tile, number]
        stop = start + (padded(count) if full else count)
        low = start // 16 * 16
        high = min(-(-stop // 16) * 16, ref.shape[0])
        return ref[low:high, :].astype(F32)[start - low : stop - low]

    def token_pieces(i, j):
        pieces = [rows_of(normed_ref, 1, 3 * i + j)]
        if i != 1:
            pieces.append(rows_of(normed_ref, i, j))
        if j != 1:
            north, first, south, second, far_north, far_south = far[j]
            pieces += {0: [north, far_north], 1: [first, second], 2: [south, far_south]}[i]
        return pieces

    chains = []
    for places in groups:
        own = [(1, 3 * i + j) for i, j in places]
        own_normed = below(*[rows_of(normed_ref, *entry, True) for entry in own])
        latent = below(*[rows_of(latent_ref, *entry, True) for entry in own])
        chains.append(
            worked(
                plan, places, token_pieces, own_normed, latent, weights, scalars_ref, put, done
            )
        )
    return chains


def middle_kernel(plan, scalars_ref, latent_ref, normed_ref, *refs):
    *weights, out_ref, held_ref, sem = refs
    left, wide = plan[1][4][2:]

    def put(part, _, piece):
        held_ref[part[0] : part[0] + part[1]] = piece

    copies = []

    def done(places):
        for i, _ in places:
            top, high = plan[1][3 * i + 1][:2]
            copies.append(
                pltpu.make_async_copy(
                    held_ref.at[top : top + high],
                    out_ref.at[top : top + high, left : left + wide],
                    sem.at[i],
                )
            )
            copies[-1].start()

    alternate(
        *chains_of(plan, MIDDLE, latent_ref, normed_ref, {}, weights, scalars_ref, put, done)
    )
    for copy in copies:
        copy.wait()


def side_kernel(plan, scalars_ref, latent_ref, normed_ref, one_ref, two_ref, *refs):
    *weights, _, out_ref, held_ref, west_ref, east_ref, sem = refs

    def sort(before, after):
        west_ref[...] = before[...]
        east_ref[...] = after[...]

    pl.when(scalars_ref[3] == 1)(lambda: sort(two_ref, one_ref))
    pl.when(scalars_ref[3] == 0)(lambda: sort(one_ref, two_ref))
    far = {}
    width = normed_ref.shape[1]
    half = HLAT * HLON * LEV
    for j, ref in ((0, west_ref), (2, east_ref)):
        value = ref[...].astype(F32)
        rows = [value[at : at + half] for at in range(0, 3 * half, half)]
        far[j] = [part[:, at : at + width] for part in rows for at in (0, width)]

    def put(part, j, piece):
        held_ref[j // 2, part[0] : part[0] + part[1]] = piece

    copies = []

    def done(places):
        j = places[0][1]
        left, wide = plan[1][j][2:]
        copies.append(
            pltpu.make_async_copy(
                held_ref.at[j // 2], out_ref.at[:, left : left + wide], sem.at[j // 2]
            )
        )
        copies[-1].start()

    alternate(
        *chains_of(plan, SIDES, latent_ref, normed_ref, far, weights, scalars_ref, put, done)
    )
    for copy in copies:
        copy.wait()


def local(
    record_values,
    record_cell,
    record_instrument,
    block_counts,
    background,
    input_weight,
    instrument_table,
    lift_weight,
    first_gain,
    attn_weight,
    mix_weight,
    second_gain,
    up_weight,
    down_weight,
):
    lat_cells, lon_cells, _, width = background.shape
    tiles_lat = record_values.shape[1]

    sent, up, down = packed(
        record_values, record_cell, record_instrument, block_counts, background
    )
    received = lax.all_to_all(sent, ("lon", "lat"), split_axis=0, concat_axis=0, tiled=True)
    even = [lax.axis_index(axis) % 2 == 0 for axis in ("lat", "lon")]
    got = swapped(jnp.where(even[0], down, up), jnp.where(even[0], up, down), "lat", wraps=False)
    input_weight, down_weight, _ = lax.optimization_barrier((input_weight, down_weight, up))

    plan = rectangles(lat_cells, lon_cells)
    _, rows = spans_of(plan)
    own = sum(padded(tokens_of(part)) for part in plan[1])
    half = HLAT * HLON * LEV
    smem = pl.BlockSpec(memory_space=pltpu.SMEM)
    vmem = pl.BlockSpec(memory_space=pltpu.VMEM)
    anywhere = pl.BlockSpec(memory_space=pl.ANY)
    params = pltpu.CompilerParams(vmem_limit_bytes=LIMIT)
    border = pltpu.VMEM((HLAT, lon_cells, LEV, width), BF16)
    strip = jax.ShapeDtypeStruct((3 * half, 2 * width), BF16)
    latent, normed, first, second = pl.pallas_call(
        functools.partial(norm_kernel, plan),
        out_shape=[
            jax.ShapeDtypeStruct((own, width), BF16),
            jax.ShapeDtypeStruct((rows, width), BF16),
            strip,
            strip,
        ],
        in_specs=[smem] + [vmem] * 8,
        out_specs=[vmem] * 4,
        scratch_shapes=[border, border],
        compiler_params=params,
        cost_estimate=pl.CostEstimate(
            flops=10**9, bytes_accessed=2 * 10**6, transcendentals=10**6
        ),
    )(
        jnp.stack(even).astype(jnp.int32),
        received,
        *got,
        background,
        input_weight,
        instrument_table,
        lift_weight,
        first_gain.reshape(1, width),
    )
    got = swapped(first, second, "lon", wraps=True)

    lat = lax.axis_index("lat")
    scalars = jnp.stack([lat == 0, lat < 0, lat == tiles_lat - 1, even[1]]).astype(jnp.int32)
    weights = [attn_weight, mix_weight, second_gain.reshape(1, width), up_weight, down_weight]
    result = jax.ShapeDtypeStruct(background.shape, BF16)
    middle = pl.pallas_call(
        functools.partial(middle_kernel, plan),
        out_shape=result,
        in_specs=[smem] + [vmem] * (2 + len(weights)),
        out_specs=anywhere,
        scratch_shapes=[
            pltpu.VMEM((lat_cells, lon_cells - WLON, LEV, width), BF16),
            pltpu.SemaphoreType.DMA((3,)),
        ],
        compiler_params=params,
        cost_estimate=pl.CostEstimate(
            flops=4 * 10**9, bytes_accessed=4 * 10**6, transcendentals=10**6
        ),
    )(scalars, latent, normed, *weights)
    return pl.pallas_call(
        functools.partial(side_kernel, plan),
        out_shape=result,
        in_specs=[smem] + [vmem] * (4 + len(weights)) + [anywhere],
        out_specs=anywhere,
        scratch_shapes=[
            pltpu.VMEM((2, lat_cells, HLON, LEV, width), BF16),
            pltpu.VMEM(strip.shape, BF16),
            pltpu.VMEM(strip.shape, BF16),
            pltpu.SemaphoreType.DMA((2,)),
        ],
        input_output_aliases={5 + len(weights): 0},
        compiler_params=params,
        cost_estimate=pl.CostEstimate(
            flops=3 * 10**9, bytes_accessed=4 * 10**6, transcendentals=10**6
        ),
    )(scalars, latent, normed, *got, *weights, middle)


def solution(mesh):
    placed = (
        P("lon", "lat", None, None),
        P("lon", "lat", None),
        P("lon", "lat", None),
        P("lon", "lat"),
        P("lat", "lon", None, None),
        P(),
        P(),
        P(),
        P(),
        P(),
        P(),
        P(),
        P(),
        P(),
    )
    return jax.shard_map(
        local, mesh=mesh, in_specs=placed, out_specs=P("lat", "lon", None, None), check_vma=False
    )
```

```python
import functools

import jax
import jax.numpy as jnp
from jax import lax
from jax.experimental import pallas as pl
from jax.experimental.pallas import tpu as pltpu
from jax.sharding import PartitionSpec as P

HEADS = 6
INSTR = 8
LEV = 2
WLAT = 6
WLON = 12
HLAT = WLAT // 2
HLON = WLON // 2
LANES = 128
PAD = 256
CHUNK = 32
LIMIT = 40 * 2**20
BF16 = jnp.bfloat16
F32 = jnp.float32

AROUND = [(dy, dx) for dy in (-1, 0, 1) for dx in (-1, 0, 1)]
ROWS = INSTR * len(AROUND)
COLS = ROWS + len(AROUND)


def swapped(up, down, axis, wraps):
    count = lax.axis_size(axis)
    even = lax.axis_index(axis) % 2 == 0
    got = []
    for first, mine in ((0, jnp.where(even, down, up)), (1, jnp.where(even, up, down))):
        pairs = []
        for low in range(first, count, 2):
            high = (low + 1) % count
            if high > low or wraps:
                pairs += [(low, high), (high, low)]
        got.append(lax.ppermute(mine, axis, pairs))
    return got


def before_and_after(got, axis):
    even = lax.axis_index(axis) % 2 == 0
    return jnp.where(even, got[1], got[0]), jnp.where(even, got[0], got[1])


def rectangles(lat_cells, lon_cells):
    lat = {-1: [(lat_cells - HLAT, HLAT)], 1: [(0, HLAT)]}
    lat[0] = [(0, HLAT), (HLAT, lat_cells - WLAT), (lat_cells - HLAT, HLAT)]
    lon = {-1: [(lon_cells - HLON, HLON)], 1: [(0, HLON)]}
    lon[0] = [(0, HLON), (HLON, lon_cells - WLON), (lon_cells - HLON, HLON)]
    return [
        [(top, high, left, wide) for top, high in lat[dy] for left, wide in lon[dx]]
        for dy, dx in AROUND
    ]


def tokens_of(part):
    return part[1] * part[3] * LEV


def padded(count):
    return -(-count // 8) * 8


def gelu(x):
    half = 0.5 * x
    inner = x * (0.7978845608028654 + 0.035677408136300125 * (x * x))
    return half + half * jnp.tanh(inner)


def normalise(wide, gain):
    average = jnp.mean(wide, axis=-1, keepdims=True)
    centred = wide - average
    spread = jnp.mean(centred * centred, axis=-1, keepdims=True)
    return centred * lax.rsqrt(spread + 1e-05) * gain


def dot(a, b):
    return jnp.dot(a, b, preferred_element_type=F32)


def dot_nt(a, b):
    return lax.dot_general(a, b, (((1,), (1,)), ((), ())), preferred_element_type=F32)


def about_one_over(x):
    return pl.reciprocal(x, approx=True)


def with_ones(tensor):
    ones = jnp.ones((tensor.shape[0], PAD - tensor.shape[1]), F32)
    return jnp.concatenate([tensor, ones], axis=1).astype(BF16)


def below(*pieces):
    return jnp.concatenate(pieces, axis=0) if len(pieces) > 1 else pieces[0]


def pack_kernel(
    values_ref,
    cell_ref,
    tag_ref,
    count_ref,
    back_ref,
    *refs,
):
    out_ref, up_ref, down_ref, values, cells, tags, held, sem = refs
    tiles_lon, tiles_lat, capacity, _ = values_ref.shape
    lat_cells, lon_cells = back_ref.shape[:2]
    strips = [
        (back_ref.at[:HLAT], up_ref),
        (back_ref.at[lat_cells - HLAT :], down_ref),
    ]
    copies = [
        pltpu.make_async_copy(cell_ref, cells, sem.at[0]),
        pltpu.make_async_copy(tag_ref, tags, sem.at[1]),
        pltpu.make_async_copy(count_ref, held, sem.at[2]),
        pltpu.make_async_copy(values_ref, values, sem.at[3]),
    ]
    copies += [
        pltpu.make_async_copy(source, strip, sem.at[4 + n])
        for n, (source, strip) in enumerate(strips)
    ]
    for copy in copies:
        copy.start()
    for copy in copies[:3]:
        copy.wait()
    counts = below(*[held[tile : tile + 1, :] for tile in range(tiles_lat) for _ in range(capacity)])
    cell = cells[...]
    slot = lax.broadcasted_iota(jnp.int32, cell.shape, 0) % capacity
    row = cell // lon_cells
    fields = [jnp.where(slot < counts, row, 255), cell - row * lon_cells, tags[...]]
    rows, columns, kinds = (field.astype(F32) for field in fields)
    lane = lax.broadcasted_iota(jnp.int32, (cell.shape[0], LANES), 1)
    kind_of = (lane % INSTR).astype(F32)
    marks = [
        ((lane < ROWS) & (lane // INSTR == n)) | (lane == ROWS + n) | (lane == COLS + n)
        for n in range(len(AROUND))
    ]
    turned = []
    for lon in range(tiles_lon):
        meta = jnp.where(kind_of == kinds[:, lon : lon + 1], 1.0, 0.0)
        meta = jnp.where(lane >= ROWS, rows[:, lon : lon + 1], meta)
        meta = jnp.where(lane >= COLS, columns[:, lon : lon + 1], meta)
        turns = {0: meta}
        for dy in (-1, 1):
            by = dy * capacity % meta.shape[0]
            turns[dy] = below(meta[by:], meta[:by])
        turned.append(turns)
    for lon in range(tiles_lon):
        meta = jnp.zeros(lane.shape, F32)
        for mark, (dy, dx) in zip(marks, AROUND):
            meta = jnp.where(mark, turned[(lon + dx) % tiles_lon][dy], meta)
        out_ref[lon, :, len(AROUND)] = meta.astype(BF16).reshape(tiles_lat, capacity, LANES)
    copies[3].wait()
    for n, (dy, dx) in enumerate(AROUND):
        spans = {0: [(0, tiles_lat)], 1: [(0, tiles_lat - 1), (tiles_lat - 1, tiles_lat)]}
        spans[-1] = [(0, 1), (1, tiles_lat)]

        def copy_tiles(lon, n=n, dx=dx, dy=dy, spans=spans[dy]):
            source = lax.rem(lon + dx + tiles_lon, tiles_lon)
            for low, end in spans:
                first = (low + dy) % tiles_lat
                out_ref[lon, low:end, n] = values[source, first : first + end - low]

        if tiles_lon <= 8:
            for lon in range(tiles_lon):
                copy_tiles(lon)
        else:
            pl.loop(0, tiles_lon)(copy_tiles)
    for copy in copies[4:]:
        copy.wait()


def packed(record_values, record_cell, record_instrument, block_counts, background):
    tiles_lon, tiles_lat, capacity, wide = record_values.shape
    anywhere = pl.BlockSpec(memory_space=pltpu.HBM)
    ints = pltpu.VMEM((tiles_lat * capacity, tiles_lon), jnp.int32)
    shape = (tiles_lon, tiles_lat, len(AROUND) + 1, capacity, wide)
    lat_cells, lon_cells, levels, width = background.shape
    across = jax.ShapeDtypeStruct((HLAT, lon_cells, levels, width), BF16)
    out, *strips = pl.pallas_call(
        pack_kernel,
        out_shape=[jax.ShapeDtypeStruct(shape, BF16), across, across],
        in_specs=[anywhere] * 5,
        out_specs=[pl.BlockSpec(memory_space=pltpu.VMEM)] * 3,
        scratch_shapes=[
            pltpu.VMEM(record_values.shape, BF16),
            ints,
            ints,
            pltpu.VMEM((tiles_lat, tiles_lon), jnp.int32),
            pltpu.SemaphoreType.DMA((6,)),
        ],
        compiler_params=pltpu.CompilerParams(vmem_limit_bytes=56 * 2**20),
        cost_estimate=pl.CostEstimate(
            flops=20 * 10**9, bytes_accessed=10**6, transcendentals=0
        ),
    )(
        record_values,
        record_cell.transpose(1, 2, 0).reshape(-1, tiles_lon),
        record_instrument.transpose(1, 2, 0).reshape(-1, tiles_lon),
        block_counts.T,
        background,
    )
    return out.reshape((-1,) + shape[2:]), *strips


def token_codes(part, lon_cells):
    top, high, left, wide = part
    count = tokens_of(part)
    place = lax.broadcasted_iota(jnp.int32, (padded(count), LANES), 0)
    code = place + (top * lon_cells + left) * LEV
    for row in range(1, high):
        step = (lon_cells - wide) * LEV
        code = code + jnp.where(place >= row * wide * LEV, step, 0)
    return jnp.where(place < count, code, -8).astype(F32)


def entries_of(windows):
    entries = [(4, 3 * i + j) for i, j in windows]
    for i, j in windows:
        if i != 1:
            entries.append((3 * i + 1, j))
        if j != 1:
            entries.append((3 + j, i))
        if i != 1 and j != 1:
            entries.append((3 * i + j, 0))
    return entries


def alternate(*chains):
    chains, begun = list(chains), 1
    while chains:
        for chain in chains[:begun]:
            if next(chain, None) is None:
                chains.remove(chain)
                begun -= 1
        begun += 1


def scattered(recv_ref, first_ref, table_ref, lift_ref, plan, lon_cells):
    sources, _, capacity, _ = recv_ref.shape
    width = table_ref.shape[1]
    chunk = min(CHUNK, sources)
    slots = chunk * capacity
    first, lift = first_ref[...], lift_ref[...]
    table = below(*[table_ref[...].astype(F32)] * (LANES // INSTR)).astype(BF16)
    lane = lax.broadcasted_iota(jnp.int32, (16, LANES), 1)
    sub = lax.broadcasted_iota(jnp.int32, (16, LANES), 0)
    weigh = jnp.where(lane == ROWS + sub, float(lon_cells * LEV), 0.0)
    weigh = jnp.where(lane == COLS + sub, float(LEV), weigh).astype(BF16)
    codes = [below(*[token_codes(part, lon_cells) for part in parts]) for parts in plan]

    def scatter(begin):
        meta = recv_ref[pl.ds(begin, chunk), len(AROUND)].reshape(slots, LANES)
        records = below(
            *[
                recv_ref[pl.ds(begin, chunk), n].reshape(slots, LANES)
                for n in range(len(AROUND))
            ]
        )
        lane = lax.broadcasted_iota(jnp.int32, meta.shape, 1) // INSTR
        wide = meta.astype(F32)
        chosen = below(*[jnp.where(lane == n, wide, 0.0) for n in range(len(AROUND))]).astype(BF16)
        encoded = gelu(dot(records, first) + dot(chosen, table)).astype(BF16)
        lifted = gelu(dot(encoded, lift))
        tokens = dot_nt(weigh, meta)
        sums = []
        for n in range(len(AROUND)):
            part = lifted[n * slots : (n + 1) * slots]
            part = with_ones(
                below(*[part[:, level * width : (level + 1) * width] for level in range(LEV)])
            )
            token = tokens[n : n + 1]
            token = jnp.concatenate([token + float(level) for level in range(LEV)], axis=1)
            if token.shape[1] == LANES:
                hot = codes[n] == token
            else:
                hot = codes[n][:, :1] == token
            sums.append(dot(jnp.where(hot, 1.0, 0.0).astype(BF16), part))
        return tuple(sums)

    sums = scatter(0)
    if sources > chunk:
        sums = lax.fori_loop(
            1,
            sources // chunk,
            lambda step, total: tuple(a + b for a, b in zip(total, scatter(step * chunk))),
            sums,
        )
    return sums


def worked(plan, places, sum_of, borders, weights, scalars_ref, put, done):
    back_ref, north_ref, south_ref, west_ref, east_ref = borders
    gain_one_ref, attn_ref, mix_ref, gain_two_ref, up_ref, down_ref = weights
    lat_cells, width = back_ref.shape[0], back_ref.shape[3]
    pieces, spans, start = [], {}, 0
    for tile, number in entries_of(places):
        dy, dx = AROUND[tile]
        part = plan[tile][number]
        top, high, left, wide = part
        count = tokens_of(part)
        if dx:
            ref = west_ref if dx < 0 else east_ref
            top, left = {-1: 0, 0: top + HLAT, 1: lat_cells + HLAT}[dy], 0
        elif dy:
            ref, top = (north_ref, 0) if dy < 0 else (south_ref, 0)
        else:
            ref = back_ref
        piece = ref[top : top + high, left : left + wide].reshape(count, width).astype(F32)
        full = padded(count)
        if full > count:
            piece = below(piece, jnp.zeros((full - count, width), F32))
        pieces.append(piece)
        spans[tile, number] = (start, count)
        start += full
    sums = below(*[sum_of(*entry) for entry in entries_of(places)])
    tally = 1.0 + sums[:, width : width + 1]
    share = about_one_over(tally)
    share = share * (2.0 - tally * share)
    latent = ((below(*pieces) + sums[:, :width]) * share).astype(BF16).astype(F32)
    normed = normalise(latent, gain_one_ref[...].astype(F32))
    yield True

    def piece_of(tile, number):
        start, count = spans[tile, number]
        return normed[start : start + count]

    groups = [padded(tokens_of(plan[4][3 * i + j])) for i, j in places]
    end = sum(groups)
    windows = []
    for i, j in places:
        window = [piece_of(4, 3 * i + j)]
        if i != 1:
            window.append(piece_of(3 * i + 1, j))
        if j != 1:
            window.append(piece_of(3 + j, i))
        if i != 1 and j != 1:
            window.append(piece_of(3 * i + j, 0))
        windows.append(window)
    tokens = below(*[piece for window in windows for piece in window]).astype(BF16)
    weight = attn_ref[...]
    head = width // HEADS
    keys = dot(tokens, weight[:, width : 2 * width])
    query = dot(normed[:end].astype(BF16), weight[:, :width]) * head ** (-0.5)
    query = jnp.concatenate([query, jnp.ones((end, PAD - width), F32)], axis=1)
    values = with_ones(dot(tokens, weight[:, 2 * width :]))
    yield True

    lane = lax.broadcasted_iota(jnp.int32, (1, PAD), 1)
    many = WLAT * WLON * LEV
    corner = HLAT * HLON * LEV
    key = lax.broadcasted_iota(jnp.int32, (many, PAD - width), 0)
    spare = lax.broadcasted_iota(jnp.int32, (many, PAD - width), 1)
    unused = lax.broadcasted_iota(jnp.int32, (PAD - many, PAD), 1)
    unused = jnp.where(unused == width, -3e38, 0.0).astype(BF16)
    mixed, start = [], 0
    for w, ((i, j), rows) in enumerate(zip(places, groups)):
        part = query[start : start + rows]
        stacked = below(
            *[jnp.where((lane // head == h) | (lane >= width), part, 0.0) for h in range(HEADS)]
        ).astype(BF16)
        bias = jnp.zeros((many, PAD - width), F32)
        if i != 1:
            if j == 1:
                inside = key < 2 * corner
            else:
                inside = (key < corner) | ((key >= 2 * corner) & (key < 3 * corner))
            bias = jnp.where(inside | (spare > 0), 0.0, -3e38) * scalars_ref[i].astype(F32)
        here = jnp.concatenate([keys[w * many : (w + 1) * many], bias], axis=1).astype(BF16)
        scores = dot_nt(stacked, below(here, unused))
        yield True
        largest = jnp.max(scores, axis=-1, keepdims=True)
        raised = jnp.exp((scores - largest).astype(BF16))
        here = below(values[w * many : (w + 1) * many], jnp.zeros((PAD - many, PAD), BF16))
        product = dot(raised, here)
        yield True
        product = product[:, :width] * about_one_over(product[:, width : width + 1])
        total = product[:rows]
        for h in range(1, HEADS):
            own = lane[:, :width] // head == h
            total = jnp.where(own, product[h * rows : (h + 1) * rows], total)
        mixed.append(total)
        start += rows
    mixed = below(*mixed).astype(BF16)

    after = (latent[:end] + dot(mixed, mix_ref[...])).astype(BF16).astype(F32)
    yield True
    normed_two = normalise(after, gain_two_ref[...].astype(F32)).astype(BF16)
    hidden = dot(normed_two, up_ref[...])
    yield True
    result = after + dot(gelu(hidden.astype(BF16)), down_ref[...])
    yield True
    start = 0
    for (i, j), rows in zip(places, groups):
        part = plan[4][3 * i + j]
        piece = result[start : start + tokens_of(part)].astype(BF16)
        put(part, j, piece.reshape(part[1], part[3], LEV, width))
        start += rows
    done(places)


MIDDLE = [[(0, 1), (2, 1)], [(1, 1)]]
SIDES = [[(0, 0), (1, 0), (2, 0)], [(0, 2), (1, 2), (2, 2)]]


def side_entries():
    return [entry for places in SIDES for entry in entries_of(places)]


def middle_kernel(
    plan,
    scalars_ref,
    recv_ref,
    north_ref,
    south_ref,
    back_ref,
    first_ref,
    table_ref,
    lift_ref,
    *refs,
):
    *weights, out_ref, rest_ref, held_ref, sem = refs
    sums = scattered(recv_ref, first_ref, table_ref, lift_ref, plan, back_ref.shape[1])

    def sum_of(tile, number):
        start = sum(padded(tokens_of(part)) for part in plan[tile][:number])
        return sums[tile][start : start + padded(tokens_of(plan[tile][number]))]

    rest_ref[...] = below(*[sum_of(*entry) for entry in side_entries()])
    left, wide = plan[4][4][2:]

    def put(part, _, piece):
        held_ref[part[0] : part[0] + part[1]] = piece

    copies = []

    def done(places):
        for i, _ in places:
            top, high = plan[4][3 * i + 1][:2]
            copies.append(
                pltpu.make_async_copy(
                    held_ref.at[top : top + high],
                    out_ref.at[top : top + high, left : left + wide],
                    sem.at[i],
                )
            )
            copies[-1].start()

    borders = (back_ref, north_ref, south_ref, None, None)
    alternate(
        *[
            worked(plan, places, sum_of, borders, weights, scalars_ref, put, done)
            for places in MIDDLE
        ]
    )
    for copy in copies:
        copy.wait()


def side_kernel(
    plan,
    scalars_ref,
    rest_ref,
    north_ref,
    south_ref,
    west_ref,
    east_ref,
    back_ref,
    *refs,
):
    *weights, _, out_ref, held_ref, sem = refs
    spans, start = {}, 0
    for tile, number in side_entries():
        rows = padded(tokens_of(plan[tile][number]))
        spans[tile, number] = (start, start + rows)
        start += rows

    def sum_of(tile, number):
        start, end = spans[tile, number]
        return rest_ref[start:end, :]

    def put(part, j, piece):
        held_ref[j // 2, part[0] : part[0] + part[1]] = piece

    copies = []

    def done(places):
        j = places[0][1]
        left, wide = plan[4][j][2:]
        copies.append(
            pltpu.make_async_copy(
                held_ref.at[j // 2], out_ref.at[:, left : left + wide], sem.at[j // 2]
            )
        )
        copies[-1].start()

    borders = (back_ref, north_ref, south_ref, west_ref, east_ref)
    alternate(
        *[
            worked(plan, places, sum_of, borders, weights, scalars_ref, put, done)
            for places in SIDES
        ]
    )
    for copy in copies:
        copy.wait()


def local(
    record_values,
    record_cell,
    record_instrument,
    block_counts,
    background,
    input_weight,
    instrument_table,
    lift_weight,
    first_gain,
    attn_weight,
    mix_weight,
    second_gain,
    up_weight,
    down_weight,
):
    lat_cells, lon_cells, _, width = background.shape
    tiles_lat = record_values.shape[1]

    sent, up, down = packed(
        record_values, record_cell, record_instrument, block_counts, background
    )
    received = lax.all_to_all(sent, ("lon", "lat"), split_axis=0, concat_axis=0, tiled=True)
    north, south = before_and_after(swapped(up, down, "lat", wraps=False), "lat")

    later, input_weight, down_weight, _ = lax.optimization_barrier(
        (background, input_weight, down_weight, up)
    )

    def columns(low, end):
        return jnp.concatenate([north[:, low:end], later[:, low:end], south[:, low:end]], axis=0)

    got = swapped(columns(0, HLON), columns(lon_cells - HLON, lon_cells), "lon", wraps=True)

    lat = lax.axis_index("lat")
    scalars = jnp.stack([lat == 0, lat < 0, lat == tiles_lat - 1]).astype(jnp.int32)
    plan = rectangles(lat_cells, lon_cells)
    rest = sum(padded(tokens_of(plan[tile][number])) for tile, number in side_entries())
    weights = [
        first_gain.reshape(1, width),
        attn_weight,
        mix_weight,
        second_gain.reshape(1, width),
        up_weight,
        down_weight,
    ]
    smem = pl.BlockSpec(memory_space=pltpu.SMEM)
    vmem = pl.BlockSpec(memory_space=pltpu.VMEM)
    anywhere = pl.BlockSpec(memory_space=pl.ANY)
    params = pltpu.CompilerParams(vmem_limit_bytes=LIMIT)
    result = jax.ShapeDtypeStruct(background.shape, BF16)
    middle, rest = pl.pallas_call(
        functools.partial(middle_kernel, plan),
        out_shape=[result, jax.ShapeDtypeStruct((rest, PAD), F32)],
        in_specs=[smem] + [vmem] * (7 + len(weights)),
        out_specs=[anywhere, vmem],
        scratch_shapes=[
            pltpu.VMEM((lat_cells, lon_cells - WLON, LEV, width), BF16),
            pltpu.SemaphoreType.DMA((3,)),
        ],
        compiler_params=params,
        cost_estimate=pl.CostEstimate(
            flops=4 * 10**9, bytes_accessed=4 * 10**6, transcendentals=10**6
        ),
    )(
        scalars,
        received,
        north,
        south,
        background,
        input_weight,
        instrument_table,
        lift_weight,
        *weights,
    )
    rest, *got = lax.optimization_barrier((rest, *got))
    west, east = before_and_after(got, "lon")
    return pl.pallas_call(
        functools.partial(side_kernel, plan),
        out_shape=result,
        in_specs=[smem] + [vmem] * (6 + len(weights)) + [anywhere],
        out_specs=anywhere,
        scratch_shapes=[
            pltpu.VMEM((2, lat_cells, HLON, LEV, width), BF16),
            pltpu.SemaphoreType.DMA((2,)),
        ],
        input_output_aliases={7 + len(weights): 0},
        compiler_params=params,
        cost_estimate=pl.CostEstimate(
            flops=3 * 10**9, bytes_accessed=4 * 10**6, transcendentals=10**6
        ),
    )(scalars, rest, north, south, west, east, background, *weights, middle)


def solution(mesh):
    placed = (
        P("lon", "lat", None, None),
        P("lon", "lat", None),
        P("lon", "lat", None),
        P("lon", "lat"),
        P("lat", "lon", None, None),
        P(),
        P(),
        P(),
        P(),
        P(),
        P(),
        P(),
        P(),
        P(),
    )
    return jax.shard_map(
        local, mesh=mesh, in_specs=placed, out_specs=P("lat", "lon", None, None), check_vma=False
    )
```

```python
import functools

import jax
import jax.numpy as jnp
from jax import lax
from jax.experimental import pallas as pl
from jax.experimental.pallas import tpu as pltpu
from jax.sharding import PartitionSpec as P

HEADS = 6
INSTR = 8
LEV = 2
WLAT = 6
WLON = 12
HLAT = WLAT // 2
HLON = WLON // 2
LANES = 128
PAD = 256
CHUNK = 32
LIMIT = 40 * 2**20
BF16 = jnp.bfloat16
F32 = jnp.float32

AROUND = [(dy, dx) for dy in (-1, 0, 1) for dx in (-1, 0, 1)]
ROWS = INSTR * len(AROUND)
COLS = ROWS + len(AROUND)


def swapped(up, down, axis, wraps):
    count = lax.axis_size(axis)
    even = lax.axis_index(axis) % 2 == 0
    got = []
    for first, mine in ((0, jnp.where(even, down, up)), (1, jnp.where(even, up, down))):
        pairs = []
        for low in range(first, count, 2):
            high = (low + 1) % count
            if high > low or wraps:
                pairs += [(low, high), (high, low)]
        got.append(lax.ppermute(mine, axis, pairs))
    return got


def before_and_after(got, axis):
    even = lax.axis_index(axis) % 2 == 0
    return jnp.where(even, got[1], got[0]), jnp.where(even, got[0], got[1])


def rectangles(lat_cells, lon_cells):
    lat = {-1: [(lat_cells - HLAT, HLAT)], 1: [(0, HLAT)]}
    lat[0] = [(0, HLAT), (HLAT, lat_cells - WLAT), (lat_cells - HLAT, HLAT)]
    lon = {-1: [(lon_cells - HLON, HLON)], 1: [(0, HLON)]}
    lon[0] = [(0, HLON), (HLON, lon_cells - WLON), (lon_cells - HLON, HLON)]
    return [
        [(top, high, left, wide) for top, high in lat[dy] for left, wide in lon[dx]]
        for dy, dx in AROUND
    ]


def tokens_of(part):
    return part[1] * part[3] * LEV


def padded(count):
    return -(-count // 8) * 8


def gelu(x):
    half = 0.5 * x
    inner = x * (0.7978845608028654 + 0.035677408136300125 * (x * x))
    return half + half * jnp.tanh(inner)


def normalise(wide, gain):
    average = jnp.mean(wide, axis=-1, keepdims=True)
    centred = wide - average
    spread = jnp.mean(centred * centred, axis=-1, keepdims=True)
    return centred * lax.rsqrt(spread + 1e-05) * gain


def dot(a, b):
    return jnp.dot(a, b, preferred_element_type=F32)


def dot_nt(a, b):
    return lax.dot_general(a, b, (((1,), (1,)), ((), ())), preferred_element_type=F32)


def about_one_over(x):
    return pl.reciprocal(x, approx=True)


def with_ones(tensor):
    ones = jnp.ones((tensor.shape[0], PAD - tensor.shape[1]), F32)
    return jnp.concatenate([tensor, ones], axis=1).astype(BF16)


def below(*pieces):
    return jnp.concatenate(pieces, axis=0) if len(pieces) > 1 else pieces[0]


def pack_kernel(
    values_ref,
    cell_ref,
    tag_ref,
    count_ref,
    back_ref,
    *refs,
):
    out_ref, up_ref, down_ref, values, cells, tags, held, sem = refs
    tiles_lon, tiles_lat, capacity, _ = values_ref.shape
    lat_cells, lon_cells = back_ref.shape[:2]
    strips = [
        (back_ref.at[:HLAT], up_ref),
        (back_ref.at[lat_cells - HLAT :], down_ref),
    ]
    copies = [
        pltpu.make_async_copy(cell_ref, cells, sem.at[0]),
        pltpu.make_async_copy(tag_ref, tags, sem.at[1]),
        pltpu.make_async_copy(count_ref, held, sem.at[2]),
        pltpu.make_async_copy(values_ref, values, sem.at[3]),
    ]
    copies += [
        pltpu.make_async_copy(source, strip, sem.at[4 + n])
        for n, (source, strip) in enumerate(strips)
    ]
    for copy in copies:
        copy.start()
    for copy in copies[:3]:
        copy.wait()
    counts = below(*[held[tile : tile + 1, :] for tile in range(tiles_lat) for _ in range(capacity)])
    cell = cells[...]
    slot = lax.broadcasted_iota(jnp.int32, cell.shape, 0) % capacity
    row = cell // lon_cells
    fields = [jnp.where(slot < counts, row, 255), cell - row * lon_cells, tags[...]]
    rows, columns, kinds = (field.astype(F32) for field in fields)
    lane = lax.broadcasted_iota(jnp.int32, (cell.shape[0], LANES), 1)
    kind_of = (lane % INSTR).astype(F32)
    marks = [
        ((lane < ROWS) & (lane // INSTR == n)) | (lane == ROWS + n) | (lane == COLS + n)
        for n in range(len(AROUND))
    ]
    turned = []
    for lon in range(tiles_lon):
        meta = jnp.where(kind_of == kinds[:, lon : lon + 1], 1.0, 0.0)
        meta = jnp.where(lane >= ROWS, rows[:, lon : lon + 1], meta)
        meta = jnp.where(lane >= COLS, columns[:, lon : lon + 1], meta)
        turns = {0: meta}
        for dy in (-1, 1):
            by = dy * capacity % meta.shape[0]
            turns[dy] = below(meta[by:], meta[:by])
        turned.append(turns)
    for lon in range(tiles_lon):
        meta = jnp.zeros(lane.shape, F32)
        for mark, (dy, dx) in zip(marks, AROUND):
            meta = jnp.where(mark, turned[(lon + dx) % tiles_lon][dy], meta)
        out_ref[lon, :, len(AROUND)] = meta.astype(BF16).reshape(tiles_lat, capacity, LANES)
    copies[3].wait()
    for n, (dy, dx) in enumerate(AROUND):
        spans = {0: [(0, tiles_lat)], 1: [(0, tiles_lat - 1), (tiles_lat - 1, tiles_lat)]}
        spans[-1] = [(0, 1), (1, tiles_lat)]

        def copy_tiles(lon, n=n, dx=dx, dy=dy, spans=spans[dy]):
            source = lax.rem(lon + dx + tiles_lon, tiles_lon)
            for low, end in spans:
                first = (low + dy) % tiles_lat
                out_ref[lon, low:end, n] = values[source, first : first + end - low]

        if tiles_lon <= 8:
            for lon in range(tiles_lon):
                copy_tiles(lon)
        else:
            pl.loop(0, tiles_lon)(copy_tiles)
    for copy in copies[4:]:
        copy.wait()


def packed(record_values, record_cell, record_instrument, block_counts, background):
    tiles_lon, tiles_lat, capacity, wide = record_values.shape
    anywhere = pl.BlockSpec(memory_space=pltpu.HBM)
    ints = pltpu.VMEM((tiles_lat * capacity, tiles_lon), jnp.int32)
    shape = (tiles_lon, tiles_lat, len(AROUND) + 1, capacity, wide)
    lat_cells, lon_cells, levels, width = background.shape
    across = jax.ShapeDtypeStruct((HLAT, lon_cells, levels, width), BF16)
    out, *strips = pl.pallas_call(
        pack_kernel,
        out_shape=[jax.ShapeDtypeStruct(shape, BF16), across, across],
        in_specs=[anywhere] * 5,
        out_specs=[pl.BlockSpec(memory_space=pltpu.VMEM)] * 3,
        scratch_shapes=[
            pltpu.VMEM(record_values.shape, BF16),
            ints,
            ints,
            pltpu.VMEM((tiles_lat, tiles_lon), jnp.int32),
            pltpu.SemaphoreType.DMA((6,)),
        ],
        compiler_params=pltpu.CompilerParams(vmem_limit_bytes=56 * 2**20),
        cost_estimate=pl.CostEstimate(
            flops=20 * 10**9, bytes_accessed=10**6, transcendentals=0
        ),
    )(
        record_values,
        record_cell.transpose(1, 2, 0).reshape(-1, tiles_lon),
        record_instrument.transpose(1, 2, 0).reshape(-1, tiles_lon),
        block_counts.T,
        background,
    )
    return out.reshape((-1,) + shape[2:]), *strips


def token_codes(part, lon_cells):
    top, high, left, wide = part
    count = tokens_of(part)
    place = lax.broadcasted_iota(jnp.int32, (padded(count), LANES), 0)
    code = place + (top * lon_cells + left) * LEV
    for row in range(1, high):
        step = (lon_cells - wide) * LEV
        code = code + jnp.where(place >= row * wide * LEV, step, 0)
    return jnp.where(place < count, code, -8).astype(F32)


def entries_of(windows):
    entries = [(4, 3 * i + j) for i, j in windows]
    for i, j in windows:
        if i != 1:
            entries.append((3 * i + 1, j))
        if j != 1:
            entries.append((3 + j, i))
        if i != 1 and j != 1:
            entries.append((3 * i + j, 0))
    return entries


def scattered(recv_ref, first_ref, table_ref, lift_ref, plan, lon_cells):
    sources, _, capacity, _ = recv_ref.shape
    width = table_ref.shape[1]
    chunk = min(CHUNK, sources)
    slots = chunk * capacity
    first, lift = first_ref[...], lift_ref[...]
    table = below(*[table_ref[...].astype(F32)] * (LANES // INSTR)).astype(BF16)
    lane = lax.broadcasted_iota(jnp.int32, (16, LANES), 1)
    sub = lax.broadcasted_iota(jnp.int32, (16, LANES), 0)
    weigh = jnp.where(lane == ROWS + sub, float(lon_cells * LEV), 0.0)
    weigh = jnp.where(lane == COLS + sub, float(LEV), weigh).astype(BF16)
    codes = [below(*[token_codes(part, lon_cells) for part in parts]) for parts in plan]

    def scatter(begin):
        meta = recv_ref[pl.ds(begin, chunk), len(AROUND)].reshape(slots, LANES)
        records = below(
            *[
                recv_ref[pl.ds(begin, chunk), n].reshape(slots, LANES)
                for n in range(len(AROUND))
            ]
        )
        lane = lax.broadcasted_iota(jnp.int32, meta.shape, 1) // INSTR
        wide = meta.astype(F32)
        chosen = below(*[jnp.where(lane == n, wide, 0.0) for n in range(len(AROUND))]).astype(BF16)
        encoded = gelu(dot(records, first) + dot(chosen, table)).astype(BF16)
        lifted = gelu(dot(encoded, lift))
        tokens = dot_nt(weigh, meta)
        hots, parts = [], []
        for n in range(len(AROUND)):
            token = tokens[n : n + 1]
            token = jnp.concatenate([token + float(level) for level in range(LEV)], axis=1)
            if token.shape[1] == LANES:
                hot = codes[n] == token
            else:
                hot = codes[n][:, :1] == token
            hots.append(jnp.where(hot, 1.0, 0.0).astype(BF16))
        for n in range(len(AROUND)):
            part = lifted[n * slots : (n + 1) * slots]
            parts.append(
                with_ones(
                    below(*[part[:, level * width : (level + 1) * width] for level in range(LEV)])
                )
            )
        sums = [dot(hot, part) for hot, part in zip(hots, parts)]
        return tuple(sums)

    sums = scatter(0)
    if sources > chunk:
        sums = lax.fori_loop(
            1,
            sources // chunk,
            lambda step, total: tuple(a + b for a, b in zip(total, scatter(step * chunk))),
            sums,
        )
    return sums


def worked(plan, places, sum_of, borders, weights, scalars_ref, put):
    back_ref, north_ref, south_ref, west_ref, east_ref = borders
    gain_one_ref, attn_ref, mix_ref, gain_two_ref, up_ref, down_ref = weights
    lat_cells, width = back_ref.shape[0], back_ref.shape[3]
    pieces, spans, start = [], {}, 0
    for tile, number in entries_of(places):
        dy, dx = AROUND[tile]
        part = plan[tile][number]
        top, high, left, wide = part
        count = tokens_of(part)
        if dx:
            ref = west_ref if dx < 0 else east_ref
            top, left = {-1: 0, 0: top + HLAT, 1: lat_cells + HLAT}[dy], 0
        elif dy:
            ref, top = (north_ref, 0) if dy < 0 else (south_ref, 0)
        else:
            ref = back_ref
        piece = ref[top : top + high, left : left + wide].reshape(count, width).astype(F32)
        full = padded(count)
        if full > count:
            piece = below(piece, jnp.zeros((full - count, width), F32))
        pieces.append(piece)
        spans[tile, number] = (start, count)
        start += full
    sums = below(*[sum_of(*entry) for entry in entries_of(places)])
    tally = 1.0 + sums[:, width : width + 1]
    share = about_one_over(tally)
    share = share * (2.0 - tally * share)
    latent = ((below(*pieces) + sums[:, :width]) * share).astype(BF16).astype(F32)
    normed = normalise(latent, gain_one_ref[...].astype(F32))

    def piece_of(tile, number):
        start, count = spans[tile, number]
        return normed[start : start + count]

    groups = [padded(tokens_of(plan[4][3 * i + j])) for i, j in places]
    end = sum(groups)
    windows = []
    for i, j in places:
        window = [piece_of(4, 3 * i + j)]
        if i != 1:
            window.append(piece_of(3 * i + 1, j))
        if j != 1:
            window.append(piece_of(3 + j, i))
        if i != 1 and j != 1:
            window.append(piece_of(3 * i + j, 0))
        windows.append(window)
    tokens = below(*[piece for window in windows for piece in window]).astype(BF16)
    weight = attn_ref[...]
    head = width // HEADS
    keys = dot(tokens, weight[:, width : 2 * width])
    query = dot(normed[:end].astype(BF16), weight[:, :width]) * head ** (-0.5)
    query = jnp.concatenate([query, jnp.ones((end, PAD - width), F32)], axis=1)
    values = with_ones(dot(tokens, weight[:, 2 * width :]))

    lane = lax.broadcasted_iota(jnp.int32, (1, PAD), 1)
    many = WLAT * WLON * LEV
    corner = HLAT * HLON * LEV
    key = lax.broadcasted_iota(jnp.int32, (many, PAD - width), 0)
    spare = lax.broadcasted_iota(jnp.int32, (many, PAD - width), 1)
    unused = lax.broadcasted_iota(jnp.int32, (PAD - many, PAD), 1)
    unused = jnp.where(unused == width, -3e38, 0.0).astype(BF16)
    nothing = jnp.zeros((PAD - many, PAD), BF16)

    def keys_of(w, i, j):
        bias = jnp.zeros((many, PAD - width), F32)
        if i != 1:
            if j == 1:
                inside = key < 2 * corner
            else:
                inside = (key < corner) | ((key >= 2 * corner) & (key < 3 * corner))
            bias = jnp.where(inside | (spare > 0), 0.0, -3e38) * scalars_ref[i].astype(F32)
        here = jnp.concatenate([keys[w * many : (w + 1) * many], bias], axis=1)
        return below(here.astype(BF16), unused)

    begins = [sum(groups[:w]) for w in range(len(groups))]
    parts = [query[begin : begin + rows] for begin, rows in zip(begins, groups)]
    stacks = [
        below(
            *[jnp.where((lane // head == h) | (lane >= width), part, 0.0) for h in range(HEADS)]
        ).astype(BF16)
        for part in parts
    ]
    held = [keys_of(w, i, j) for w, (i, j) in enumerate(places)]
    scores = [dot_nt(stack, here) for stack, here in zip(stacks, held)]
    largest = [jnp.max(score, axis=-1, keepdims=True) for score in scores]
    raised = [jnp.exp((score - most).astype(BF16)) for score, most in zip(scores, largest)]
    held = [below(values[w * many : (w + 1) * many], nothing) for w in range(len(places))]
    products = [dot(one, here) for one, here in zip(raised, held)]
    shares = [about_one_over(product[:, width : width + 1]) for product in products]
    products = [product[:, :width] * share for product, share in zip(products, shares)]
    mixed = []
    for product, rows in zip(products, groups):
        total = product[:rows]
        for h in range(1, HEADS):
            own = lane[:, :width] // head == h
            total = jnp.where(own, product[h * rows : (h + 1) * rows], total)
        mixed.append(total)
    mixed = below(*mixed).astype(BF16)

    after = (latent[:end] + dot(mixed, mix_ref[...])).astype(BF16).astype(F32)
    normed_two = normalise(after, gain_two_ref[...].astype(F32)).astype(BF16)
    hidden = gelu(dot(normed_two, up_ref[...]).astype(BF16))
    result = after + dot(hidden, down_ref[...])
    for begin, (i, j) in zip(begins, places):
        part = plan[4][3 * i + j]
        piece = result[begin : begin + tokens_of(part)].astype(BF16)
        put(part, j, piece.reshape(part[1], part[3], LEV, width))


MIDDLE = [(0, 1), (1, 1), (2, 1)]
SIDES = [(0, 0), (0, 2), (2, 0), (2, 2), (1, 0), (1, 2)]


def side_entries():
    return entries_of(SIDES)


def middle_kernel(
    plan,
    scalars_ref,
    recv_ref,
    north_ref,
    south_ref,
    back_ref,
    first_ref,
    table_ref,
    lift_ref,
    *refs,
):
    *weights, out_ref, rest_ref = refs
    sums = scattered(recv_ref, first_ref, table_ref, lift_ref, plan, back_ref.shape[1])

    def sum_of(tile, number):
        start = sum(padded(tokens_of(part)) for part in plan[tile][:number])
        return sums[tile][start : start + padded(tokens_of(plan[tile][number]))]

    rest_ref[...] = below(*[sum_of(*entry) for entry in side_entries()])

    def put(part, _, piece):
        out_ref[part[0] : part[0] + part[1]] = piece

    borders = (back_ref, north_ref, south_ref, None, None)
    worked(plan, MIDDLE, sum_of, borders, weights, scalars_ref, put)


def side_kernel(
    plan,
    scalars_ref,
    rest_ref,
    north_ref,
    south_ref,
    west_ref,
    east_ref,
    back_ref,
    *refs,
):
    *weights, middle_ref, out_ref, held_ref, sem = refs
    left, wide = plan[4][4][2:]
    copies = [pltpu.make_async_copy(middle_ref, out_ref.at[:, left : left + wide], sem.at[2])]
    copies[0].start()
    spans, start = {}, 0
    for tile, number in side_entries():
        rows = padded(tokens_of(plan[tile][number]))
        spans[tile, number] = (start, start + rows)
        start += rows

    def sum_of(tile, number):
        start, end = spans[tile, number]
        return rest_ref[start:end, :]

    def put(part, j, piece):
        held_ref[j // 2, part[0] : part[0] + part[1]] = piece

    borders = (back_ref, north_ref, south_ref, west_ref, east_ref)
    worked(plan, SIDES, sum_of, borders, weights, scalars_ref, put)
    for n, number in enumerate((0, 2)):
        left, wide = plan[4][number][2:]
        copies.append(
            pltpu.make_async_copy(held_ref.at[n], out_ref.at[:, left : left + wide], sem.at[n])
        )
        copies[-1].start()
    for copy in copies:
        copy.wait()


def local(
    record_values,
    record_cell,
    record_instrument,
    block_counts,
    background,
    input_weight,
    instrument_table,
    lift_weight,
    first_gain,
    attn_weight,
    mix_weight,
    second_gain,
    up_weight,
    down_weight,
):
    lat_cells, lon_cells, _, width = background.shape
    tiles_lat = record_values.shape[1]

    sent, up, down = packed(
        record_values, record_cell, record_instrument, block_counts, background
    )
    received = lax.all_to_all(sent, ("lon", "lat"), split_axis=0, concat_axis=0, tiled=True)
    north, south = before_and_after(swapped(up, down, "lat", wraps=False), "lat")

    later, input_weight, down_weight, _ = lax.optimization_barrier(
        (background, input_weight, down_weight, up)
    )

    def columns(low, end):
        return jnp.concatenate([north[:, low:end], later[:, low:end], south[:, low:end]], axis=0)

    got = swapped(columns(0, HLON), columns(lon_cells - HLON, lon_cells), "lon", wraps=True)

    lat = lax.axis_index("lat")
    scalars = jnp.stack([lat == 0, lat < 0, lat == tiles_lat - 1]).astype(jnp.int32)
    plan = rectangles(lat_cells, lon_cells)
    rest = sum(padded(tokens_of(plan[tile][number])) for tile, number in side_entries())
    weights = [
        first_gain.reshape(1, width),
        attn_weight,
        mix_weight,
        second_gain.reshape(1, width),
        up_weight,
        down_weight,
    ]
    smem = pl.BlockSpec(memory_space=pltpu.SMEM)
    vmem = pl.BlockSpec(memory_space=pltpu.VMEM)
    anywhere = pl.BlockSpec(memory_space=pl.ANY)
    params = pltpu.CompilerParams(vmem_limit_bytes=LIMIT)
    result = jax.ShapeDtypeStruct(background.shape, BF16)
    middle, rest = pl.pallas_call(
        functools.partial(middle_kernel, plan),
        out_shape=[
            jax.ShapeDtypeStruct((lat_cells, lon_cells - WLON, LEV, width), BF16),
            jax.ShapeDtypeStruct((rest, PAD), F32),
        ],
        in_specs=[smem] + [vmem] * (7 + len(weights)),
        out_specs=[vmem, vmem],
        compiler_params=params,
        cost_estimate=pl.CostEstimate(
            flops=4 * 10**9, bytes_accessed=4 * 10**6, transcendentals=10**6
        ),
    )(
        scalars,
        received,
        north,
        south,
        background,
        input_weight,
        instrument_table,
        lift_weight,
        *weights,
    )
    rest, *got = lax.optimization_barrier((rest, *got))
    west, east = before_and_after(got, "lon")
    return pl.pallas_call(
        functools.partial(side_kernel, plan),
        out_shape=result,
        in_specs=[smem] + [vmem] * (7 + len(weights)),
        out_specs=anywhere,
        scratch_shapes=[
            pltpu.VMEM((2, lat_cells, HLON, LEV, width), BF16),
            pltpu.SemaphoreType.DMA((3,)),
        ],
        compiler_params=params,
        cost_estimate=pl.CostEstimate(
            flops=3 * 10**9, bytes_accessed=4 * 10**6, transcendentals=10**6
        ),
    )(scalars, rest, north, south, west, east, background, *weights, middle)


def solution(mesh):
    placed = (
        P("lon", "lat", None, None),
        P("lon", "lat", None),
        P("lon", "lat", None),
        P("lon", "lat"),
        P("lat", "lon", None, None),
        P(),
        P(),
        P(),
        P(),
        P(),
        P(),
        P(),
        P(),
        P(),
    )
    return jax.shard_map(
        local, mesh=mesh, in_specs=placed, out_specs=P("lat", "lon", None, None), check_vma=False
    )
```

```python
import functools

import jax
import jax.numpy as jnp
from jax import lax
from jax.experimental import pallas as pl
from jax.experimental.pallas import tpu as pltpu
from jax.sharding import PartitionSpec as P

HEADS = 6
INSTR = 8
LEV = 2
WLAT = 6
WLON = 12
HLAT = WLAT // 2
HLON = WLON // 2
LANES = 128
PAD = 256
CHUNK = 32
LIMIT = 40 * 2**20
BF16 = jnp.bfloat16
F32 = jnp.float32

AROUND = [(dy, dx) for dy in (-1, 0, 1) for dx in (-1, 0, 1)]
ROWS = INSTR * len(AROUND)
COLS = ROWS + len(AROUND)


def swapped(first, second, axis, wraps):
    count = lax.axis_size(axis)
    got = []
    for begin, mine in enumerate((first, second)):
        pairs = []
        for low in range(begin, count, 2):
            high = (low + 1) % count
            if high > low or wraps:
                pairs += [(low, high), (high, low)]
        got.append(lax.ppermute(mine, axis, pairs))
    return got


def in_order(got, axis):
    even = lax.axis_index(axis) % 2 == 0
    return jnp.where(even, got[1], got[0]), jnp.where(even, got[0], got[1])


def rectangles(lat_cells, lon_cells):
    lat = {-1: [(lat_cells - HLAT, HLAT)], 1: [(0, HLAT)]}
    lat[0] = [(0, HLAT), (HLAT, lat_cells - WLAT), (lat_cells - HLAT, HLAT)]
    lon = {-1: [(lon_cells - HLON, HLON)], 1: [(0, HLON)]}
    lon[0] = [(0, HLON), (HLON, lon_cells - WLON), (lon_cells - HLON, HLON)]
    return [
        [(top, high, left, wide) for top, high in lat[dy] for left, wide in lon[dx]]
        for dy, dx in AROUND
    ]


def tokens_of(part):
    return part[1] * part[3] * LEV


def padded(count):
    return -(-count // 8) * 8


def gelu(x):
    half = 0.5 * x
    inner = x * (0.7978845608028654 + 0.035677408136300125 * (x * x))
    return half + half * jnp.tanh(inner)


def normalise(wide, gain):
    average = jnp.mean(wide, axis=-1, keepdims=True)
    centred = wide - average
    spread = jnp.mean(centred * centred, axis=-1, keepdims=True)
    return centred * lax.rsqrt(spread + 1e-05) * gain


def dot(a, b):
    return jnp.dot(a, b, preferred_element_type=F32)


def dot_nt(a, b):
    return lax.dot_general(a, b, (((1,), (1,)), ((), ())), preferred_element_type=F32)


def about_one_over(x):
    return pl.reciprocal(x, approx=True)


def with_ones(tensor):
    ones = jnp.ones((tensor.shape[0], PAD - tensor.shape[1]), F32)
    return jnp.concatenate([tensor, ones], axis=1).astype(BF16)


def below(*pieces):
    return jnp.concatenate(pieces, axis=0) if len(pieces) > 1 else pieces[0]


def pack_kernel(
    values_ref,
    cell_ref,
    tag_ref,
    count_ref,
    back_ref,
    *refs,
):
    out_ref, up_ref, down_ref, values, cells, tags, held, sem = refs
    tiles_lon, tiles_lat, capacity, _ = values_ref.shape
    lat_cells, lon_cells = back_ref.shape[:2]
    strips = [
        (back_ref.at[:HLAT], up_ref),
        (back_ref.at[lat_cells - HLAT :], down_ref),
    ]
    copies = [
        pltpu.make_async_copy(cell_ref, cells, sem.at[0]),
        pltpu.make_async_copy(tag_ref, tags, sem.at[1]),
        pltpu.make_async_copy(count_ref, held, sem.at[2]),
        pltpu.make_async_copy(values_ref, values, sem.at[3]),
    ]
    copies += [
        pltpu.make_async_copy(source, strip, sem.at[4 + n])
        for n, (source, strip) in enumerate(strips)
    ]
    for copy in copies:
        copy.start()
    for copy in copies[:3]:
        copy.wait()
    counts = below(*[held[tile : tile + 1, :] for tile in range(tiles_lat) for _ in range(capacity)])
    cell = cells[...]
    slot = lax.broadcasted_iota(jnp.int32, cell.shape, 0) % capacity
    row = cell // lon_cells
    fields = [jnp.where(slot < counts, row, 255), cell - row * lon_cells, tags[...]]
    rows, columns, kinds = (field.astype(F32) for field in fields)
    lane = lax.broadcasted_iota(jnp.int32, (cell.shape[0], LANES), 1)
    kind_of = (lane % INSTR).astype(F32)
    marks = [
        ((lane < ROWS) & (lane // INSTR == n)) | (lane == ROWS + n) | (lane == COLS + n)
        for n in range(len(AROUND))
    ]
    turned = []
    for lon in range(tiles_lon):
        meta = jnp.where(kind_of == kinds[:, lon : lon + 1], 1.0, 0.0)
        meta = jnp.where(lane >= ROWS, rows[:, lon : lon + 1], meta)
        meta = jnp.where(lane >= COLS, columns[:, lon : lon + 1], meta)
        turns = {0: meta}
        for dy in (-1, 1):
            by = dy * capacity % meta.shape[0]
            turns[dy] = below(meta[by:], meta[:by])
        turned.append(turns)
    for lon in range(tiles_lon):
        meta = jnp.zeros(lane.shape, F32)
        for mark, (dy, dx) in zip(marks, AROUND):
            meta = jnp.where(mark, turned[(lon + dx) % tiles_lon][dy], meta)
        out_ref[lon, :, len(AROUND)] = meta.astype(BF16).reshape(tiles_lat, capacity, LANES)
    copies[3].wait()
    for n, (dy, dx) in enumerate(AROUND):
        spans = {0: [(0, tiles_lat)], 1: [(0, tiles_lat - 1), (tiles_lat - 1, tiles_lat)]}
        spans[-1] = [(0, 1), (1, tiles_lat)]

        def copy_tiles(lon, n=n, dx=dx, dy=dy, spans=spans[dy]):
            source = lax.rem(lon + dx + tiles_lon, tiles_lon)
            for low, end in spans:
                first = (low + dy) % tiles_lat
                out_ref[lon, low:end, n] = values[source, first : first + end - low]

        if tiles_lon <= 8:
            for lon in range(tiles_lon):
                copy_tiles(lon)
        else:
            pl.loop(0, tiles_lon)(copy_tiles)
    for copy in copies[4:]:
        copy.wait()


def packed(record_values, record_cell, record_instrument, block_counts, background):
    tiles_lon, tiles_lat, capacity, wide = record_values.shape
    anywhere = pl.BlockSpec(memory_space=pltpu.HBM)
    ints = pltpu.VMEM((tiles_lat * capacity, tiles_lon), jnp.int32)
    shape = (tiles_lon, tiles_lat, len(AROUND) + 1, capacity, wide)
    lat_cells, lon_cells, levels, width = background.shape
    across = jax.ShapeDtypeStruct((HLAT, lon_cells, levels, width), BF16)
    out, *strips = pl.pallas_call(
        pack_kernel,
        out_shape=[jax.ShapeDtypeStruct(shape, BF16), across, across],
        in_specs=[anywhere] * 5,
        out_specs=[pl.BlockSpec(memory_space=pltpu.VMEM)] * 3,
        scratch_shapes=[
            pltpu.VMEM(record_values.shape, BF16),
            ints,
            ints,
            pltpu.VMEM((tiles_lat, tiles_lon), jnp.int32),
            pltpu.SemaphoreType.DMA((6,)),
        ],
        compiler_params=pltpu.CompilerParams(vmem_limit_bytes=56 * 2**20),
        cost_estimate=pl.CostEstimate(
            flops=20 * 10**9, bytes_accessed=10**6, transcendentals=0
        ),
    )(
        record_values,
        record_cell.transpose(1, 2, 0).reshape(-1, tiles_lon),
        record_instrument.transpose(1, 2, 0).reshape(-1, tiles_lon),
        block_counts.T,
        background,
    )
    return out.reshape((-1,) + shape[2:]), *strips


def token_codes(part, lon_cells):
    top, high, left, wide = part
    count = tokens_of(part)
    place = lax.broadcasted_iota(jnp.int32, (padded(count), LANES), 0)
    code = place + (top * lon_cells + left) * LEV
    for row in range(1, high):
        step = (lon_cells - wide) * LEV
        code = code + jnp.where(place >= row * wide * LEV, step, 0)
    return jnp.where(place < count, code, -8).astype(F32)


def entries_of(windows):
    entries = [(4, 3 * i + j) for i, j in windows]
    for i, j in windows:
        if i != 1:
            entries.append((3 * i + 1, j))
        if j != 1:
            entries.append((3 + j, i))
        if i != 1 and j != 1:
            entries.append((3 * i + j, 0))
    return entries


def scattered(recv_ref, first_ref, table_ref, lift_ref, plan, lon_cells):
    sources, _, capacity, _ = recv_ref.shape
    width = table_ref.shape[1]
    chunk = min(CHUNK, sources)
    slots = chunk * capacity
    first, lift = first_ref[...], lift_ref[...]
    table = below(*[table_ref[...].astype(F32)] * (LANES // INSTR)).astype(BF16)
    lane = lax.broadcasted_iota(jnp.int32, (16, LANES), 1)
    sub = lax.broadcasted_iota(jnp.int32, (16, LANES), 0)
    weigh = jnp.where(lane == ROWS + sub, float(lon_cells * LEV), 0.0)
    weigh = jnp.where(lane == COLS + sub, float(LEV), weigh).astype(BF16)
    codes = [below(*[token_codes(part, lon_cells) for part in parts]) for parts in plan]

    def scatter(begin):
        meta = recv_ref[pl.ds(begin, chunk), len(AROUND)].reshape(slots, LANES)
        records = below(
            *[
                recv_ref[pl.ds(begin, chunk), n].reshape(slots, LANES)
                for n in range(len(AROUND))
            ]
        )
        lane = lax.broadcasted_iota(jnp.int32, meta.shape, 1) // INSTR
        wide = meta.astype(F32)
        chosen = below(*[jnp.where(lane == n, wide, 0.0) for n in range(len(AROUND))]).astype(BF16)
        encoded = gelu(dot(records, first) + dot(chosen, table)).astype(BF16)
        lifted = gelu(dot(encoded, lift))
        tokens = dot_nt(weigh, meta)
        hots, parts = [], []
        for n in range(len(AROUND)):
            token = tokens[n : n + 1]
            token = jnp.concatenate([token + float(level) for level in range(LEV)], axis=1)
            if token.shape[1] == LANES:
                hot = codes[n] == token
            else:
                hot = codes[n][:, :1] == token
            hots.append(jnp.where(hot, 1.0, 0.0).astype(BF16))
        for n in range(len(AROUND)):
            part = lifted[n * slots : (n + 1) * slots]
            parts.append(
                with_ones(
                    below(*[part[:, level * width : (level + 1) * width] for level in range(LEV)])
                )
            )
        sums = [dot(hot, part) for hot, part in zip(hots, parts)]
        return tuple(sums)

    sums = scatter(0)
    if sources > chunk:
        sums = lax.fori_loop(
            1,
            sources // chunk,
            lambda step, total: tuple(a + b for a, b in zip(total, scatter(step * chunk))),
            sums,
        )
    return sums


def worked(plan, places, sum_of, borders, weights, scalars_ref, put):
    back_ref, north_ref, south_ref, west_ref, east_ref = borders
    gain_one_ref, attn_ref, mix_ref, gain_two_ref, up_ref, down_ref = weights
    lat_cells, width = back_ref.shape[0], back_ref.shape[3]
    pieces, spans, start = [], {}, 0
    for tile, number in entries_of(places):
        dy, dx = AROUND[tile]
        part = plan[tile][number]
        top, high, left, wide = part
        count = tokens_of(part)
        if dx:
            ref = west_ref if dx < 0 else east_ref
            top, left = {-1: 0, 0: top + HLAT, 1: lat_cells + HLAT}[dy], 0
        elif dy:
            ref, top = (north_ref, 0) if dy < 0 else (south_ref, 0)
        else:
            ref = back_ref
        piece = ref[top : top + high, left : left + wide].reshape(count, width).astype(F32)
        full = padded(count)
        if full > count:
            piece = below(piece, jnp.zeros((full - count, width), F32))
        pieces.append(piece)
        spans[tile, number] = (start, count)
        start += full
    sums = below(*[sum_of(*entry) for entry in entries_of(places)])
    tally = 1.0 + sums[:, width : width + 1]
    share = about_one_over(tally)
    share = share * (2.0 - tally * share)
    latent = ((below(*pieces) + sums[:, :width]) * share).astype(BF16).astype(F32)
    normed = normalise(latent, gain_one_ref[...].astype(F32))

    def piece_of(tile, number):
        start, count = spans[tile, number]
        return normed[start : start + count]

    groups = [padded(tokens_of(plan[4][3 * i + j])) for i, j in places]
    end = sum(groups)
    windows = []
    for i, j in places:
        window = [piece_of(4, 3 * i + j)]
        if i != 1:
            window.append(piece_of(3 * i + 1, j))
        if j != 1:
            window.append(piece_of(3 + j, i))
        if i != 1 and j != 1:
            window.append(piece_of(3 * i + j, 0))
        windows.append(window)
    tokens = below(*[piece for window in windows for piece in window]).astype(BF16)
    weight = attn_ref[...]
    head = width // HEADS
    keys = dot(tokens, weight[:, width : 2 * width])
    query = dot(normed[:end].astype(BF16), weight[:, :width]) * head ** (-0.5)
    query = jnp.concatenate([query, jnp.ones((end, PAD - width), F32)], axis=1)
    values = with_ones(dot(tokens, weight[:, 2 * width :]))

    lane = lax.broadcasted_iota(jnp.int32, (1, PAD), 1)
    many = WLAT * WLON * LEV
    corner = HLAT * HLON * LEV
    key = lax.broadcasted_iota(jnp.int32, (many, PAD - width), 0)
    spare = lax.broadcasted_iota(jnp.int32, (many, PAD - width), 1)
    unused = lax.broadcasted_iota(jnp.int32, (PAD - many, PAD), 1)
    unused = jnp.where(unused == width, -3e38, 0.0).astype(BF16)
    nothing = jnp.zeros((PAD - many, PAD), BF16)

    def keys_of(w, i, j):
        bias = jnp.zeros((many, PAD - width), F32)
        if i != 1:
            if j == 1:
                inside = key < 2 * corner
            else:
                inside = (key < corner) | ((key >= 2 * corner) & (key < 3 * corner))
            bias = jnp.where(inside | (spare > 0), 0.0, -3e38) * scalars_ref[i].astype(F32)
        here = jnp.concatenate([keys[w * many : (w + 1) * many], bias], axis=1)
        return below(here.astype(BF16), unused)

    begins = [sum(groups[:w]) for w in range(len(groups))]
    parts = [query[begin : begin + rows] for begin, rows in zip(begins, groups)]
    stacks = [
        below(
            *[jnp.where((lane // head == h) | (lane >= width), part, 0.0) for h in range(HEADS)]
        ).astype(BF16)
        for part in parts
    ]
    held = [keys_of(w, i, j) for w, (i, j) in enumerate(places)]
    scores = [dot_nt(stack, here) for stack, here in zip(stacks, held)]
    largest = [jnp.max(score, axis=-1, keepdims=True) for score in scores]
    raised = [jnp.exp((score - most).astype(BF16)) for score, most in zip(scores, largest)]
    held = [below(values[w * many : (w + 1) * many], nothing) for w in range(len(places))]
    products = [dot(one, here) for one, here in zip(raised, held)]
    shares = [about_one_over(product[:, width : width + 1]) for product in products]
    products = [product[:, :width] * share for product, share in zip(products, shares)]
    mixed = []
    for product, rows in zip(products, groups):
        total = product[:rows]
        for h in range(1, HEADS):
            own = lane[:, :width] // head == h
            total = jnp.where(own, product[h * rows : (h + 1) * rows], total)
        mixed.append(total)
    mixed = below(*mixed).astype(BF16)

    after = (latent[:end] + dot(mixed, mix_ref[...])).astype(BF16).astype(F32)
    normed_two = normalise(after, gain_two_ref[...].astype(F32)).astype(BF16)
    hidden = gelu(dot(normed_two, up_ref[...]).astype(BF16))
    result = after + dot(hidden, down_ref[...])
    for begin, (i, j) in zip(begins, places):
        part = plan[4][3 * i + j]
        piece = result[begin : begin + tokens_of(part)].astype(BF16)
        put(part, j, piece.reshape(part[1], part[3], LEV, width))


MIDDLE = [(0, 1), (1, 1), (2, 1)]
SIDES = [(0, 0), (0, 2), (2, 0), (2, 2), (1, 0), (1, 2)]


def side_entries():
    return entries_of(SIDES)


def middle_kernel(
    plan,
    scalars_ref,
    recv_ref,
    north_ref,
    south_ref,
    back_ref,
    first_ref,
    table_ref,
    lift_ref,
    *refs,
):
    *weights, out_ref, rest_ref = refs
    sums = scattered(recv_ref, first_ref, table_ref, lift_ref, plan, back_ref.shape[1])

    def sum_of(tile, number):
        start = sum(padded(tokens_of(part)) for part in plan[tile][:number])
        return sums[tile][start : start + padded(tokens_of(plan[tile][number]))]

    rest_ref[...] = below(*[sum_of(*entry) for entry in side_entries()])

    def put(part, _, piece):
        out_ref[part[0] : part[0] + part[1]] = piece

    borders = (back_ref, north_ref, south_ref, None, None)
    worked(plan, MIDDLE, sum_of, borders, weights, scalars_ref, put)


def side_kernel(
    plan,
    scalars_ref,
    rest_ref,
    north_ref,
    south_ref,
    west_ref,
    east_ref,
    back_ref,
    *refs,
):
    *weights, middle_ref, out_ref, held_ref, sem = refs
    left, wide = plan[4][4][2:]
    copies = [pltpu.make_async_copy(middle_ref, out_ref.at[:, left : left + wide], sem.at[2])]
    copies[0].start()
    spans, start = {}, 0
    for tile, number in side_entries():
        rows = padded(tokens_of(plan[tile][number]))
        spans[tile, number] = (start, start + rows)
        start += rows

    def sum_of(tile, number):
        start, end = spans[tile, number]
        return rest_ref[start:end, :]

    def put(part, j, piece):
        held_ref[j // 2, part[0] : part[0] + part[1]] = piece

    borders = (back_ref, north_ref, south_ref, west_ref, east_ref)
    worked(plan, SIDES, sum_of, borders, weights, scalars_ref, put)
    for n, number in enumerate((0, 2)):
        left, wide = plan[4][number][2:]
        copies.append(
            pltpu.make_async_copy(held_ref.at[n], out_ref.at[:, left : left + wide], sem.at[n])
        )
        copies[-1].start()
    for copy in copies:
        copy.wait()


def join_kernel(even_ref, one_ref, two_ref, back_ref, north_ref, south_ref, first_ref, second_ref):
    lat_cells, lon_cells = back_ref.shape[:2]

    def strips(before, after):
        north_ref[...] = before[...]
        south_ref[...] = after[...]

    def sides(left, right):
        for ref, low in ((left, 0), (right, lon_cells - HLON)):
            ref[:HLAT] = north_ref[:, low : low + HLON]
            ref[HLAT : HLAT + lat_cells] = back_ref[:, low : low + HLON]
            ref[HLAT + lat_cells :] = south_ref[:, low : low + HLON]

    pl.when(even_ref[0] == 1)(lambda: strips(two_ref, one_ref))
    pl.when(even_ref[0] == 0)(lambda: strips(one_ref, two_ref))
    pl.when(even_ref[1] == 1)(lambda: sides(second_ref, first_ref))
    pl.when(even_ref[1] == 0)(lambda: sides(first_ref, second_ref))


def joined(even, got, background):
    lat_cells, lon_cells, levels, width = background.shape
    across = jax.ShapeDtypeStruct((HLAT, lon_cells, levels, width), BF16)
    along = jax.ShapeDtypeStruct((lat_cells + WLAT, HLON, levels, width), BF16)
    vmem = pl.BlockSpec(memory_space=pltpu.VMEM)
    return pl.pallas_call(
        join_kernel,
        out_shape=[across, across, along, along],
        in_specs=[pl.BlockSpec(memory_space=pltpu.SMEM), vmem, vmem, vmem],
        out_specs=[vmem] * 4,
        compiler_params=pltpu.CompilerParams(vmem_limit_bytes=LIMIT),
        cost_estimate=pl.CostEstimate(
            flops=10**12, bytes_accessed=10**6, transcendentals=0
        ),
    )(even, *got, background)


def local(
    record_values,
    record_cell,
    record_instrument,
    block_counts,
    background,
    input_weight,
    instrument_table,
    lift_weight,
    first_gain,
    attn_weight,
    mix_weight,
    second_gain,
    up_weight,
    down_weight,
):
    lat_cells, lon_cells, _, width = background.shape
    tiles_lat = record_values.shape[1]

    sent, up, down = packed(
        record_values, record_cell, record_instrument, block_counts, background
    )
    even = [lax.axis_index(axis) % 2 == 0 for axis in ("lat", "lon")]
    got = swapped(jnp.where(even[0], down, up), jnp.where(even[0], up, down), "lat", wraps=False)
    received = lax.all_to_all(sent, ("lon", "lat"), split_axis=0, concat_axis=0, tiled=True)
    later, input_weight, down_weight, _ = lax.optimization_barrier(
        (background, input_weight, down_weight, up)
    )
    north, south, *mine = joined(jnp.stack(even).astype(jnp.int32), got, later)
    got = swapped(*mine, "lon", wraps=True)

    lat = lax.axis_index("lat")
    scalars = jnp.stack([lat == 0, lat < 0, lat == tiles_lat - 1]).astype(jnp.int32)
    plan = rectangles(lat_cells, lon_cells)
    rest = sum(padded(tokens_of(plan[tile][number])) for tile, number in side_entries())
    weights = [
        first_gain.reshape(1, width),
        attn_weight,
        mix_weight,
        second_gain.reshape(1, width),
        up_weight,
        down_weight,
    ]
    smem = pl.BlockSpec(memory_space=pltpu.SMEM)
    vmem = pl.BlockSpec(memory_space=pltpu.VMEM)
    anywhere = pl.BlockSpec(memory_space=pl.ANY)
    params = pltpu.CompilerParams(vmem_limit_bytes=LIMIT)
    result = jax.ShapeDtypeStruct(background.shape, BF16)
    middle, rest = pl.pallas_call(
        functools.partial(middle_kernel, plan),
        out_shape=[
            jax.ShapeDtypeStruct((lat_cells, lon_cells - WLON, LEV, width), BF16),
            jax.ShapeDtypeStruct((rest, PAD), F32),
        ],
        in_specs=[smem] + [vmem] * (7 + len(weights)),
        out_specs=[vmem, vmem],
        compiler_params=params,
        cost_estimate=pl.CostEstimate(
            flops=4 * 10**9, bytes_accessed=4 * 10**6, transcendentals=10**6
        ),
    )(
        scalars,
        received,
        north,
        south,
        background,
        input_weight,
        instrument_table,
        lift_weight,
        *weights,
    )
    rest, *got = lax.optimization_barrier((rest, *got))
    west, east = in_order(got, "lon")
    return pl.pallas_call(
        functools.partial(side_kernel, plan),
        out_shape=result,
        in_specs=[smem] + [vmem] * (7 + len(weights)),
        out_specs=anywhere,
        scratch_shapes=[
            pltpu.VMEM((2, lat_cells, HLON, LEV, width), BF16),
            pltpu.SemaphoreType.DMA((3,)),
        ],
        compiler_params=params,
        cost_estimate=pl.CostEstimate(
            flops=3 * 10**9, bytes_accessed=4 * 10**6, transcendentals=10**6
        ),
    )(scalars, rest, north, south, west, east, background, *weights, middle)


def solution(mesh):
    placed = (
        P("lon", "lat", None, None),
        P("lon", "lat", None),
        P("lon", "lat", None),
        P("lon", "lat"),
        P("lat", "lon", None, None),
        P(),
        P(),
        P(),
        P(),
        P(),
        P(),
        P(),
        P(),
        P(),
    )
    return jax.shard_map(
        local, mesh=mesh, in_specs=placed, out_specs=P("lat", "lon", None, None), check_vma=False
    )
```

```python
import functools

import jax
import jax.numpy as jnp
from jax import lax
from jax.experimental import pallas as pl
from jax.experimental.pallas import tpu as pltpu
from jax.sharding import PartitionSpec as P

HEADS = 6
INSTR = 8
LEV = 2
WLAT = 6
WLON = 12
HLAT = WLAT // 2
HLON = WLON // 2
LANES = 128
PAD = 256
CHUNK = 32
LIMIT = 40 * 2**20
BF16 = jnp.bfloat16
F32 = jnp.float32

AROUND = [(dy, dx) for dy in (-1, 0, 1) for dx in (-1, 0, 1)]
ROWS = INSTR * len(AROUND)
COLS = ROWS + len(AROUND)


def swapped(up, down, axis, wraps):
    count = lax.axis_size(axis)
    even = lax.axis_index(axis) % 2 == 0
    got = []
    for first, mine in ((0, jnp.where(even, down, up)), (1, jnp.where(even, up, down))):
        pairs = []
        for low in range(first, count, 2):
            high = (low + 1) % count
            if high > low or wraps:
                pairs += [(low, high), (high, low)]
        got.append(lax.ppermute(mine, axis, pairs))
    return got


def before_and_after(got, axis):
    even = lax.axis_index(axis) % 2 == 0
    return jnp.where(even, got[1], got[0]), jnp.where(even, got[0], got[1])


def rectangles(lat_cells, lon_cells):
    lat = {-1: [(lat_cells - HLAT, HLAT)], 1: [(0, HLAT)]}
    lat[0] = [(0, HLAT), (HLAT, lat_cells - WLAT), (lat_cells - HLAT, HLAT)]
    lon = {-1: [(lon_cells - HLON, HLON)], 1: [(0, HLON)]}
    lon[0] = [(0, HLON), (HLON, lon_cells - WLON), (lon_cells - HLON, HLON)]
    return [
        [(top, high, left, wide) for top, high in lat[dy] for left, wide in lon[dx]]
        for dy, dx in AROUND
    ]


def tokens_of(part):
    return part[1] * part[3] * LEV


def padded(count):
    return -(-count // 8) * 8


def gelu(x):
    half = 0.5 * x
    inner = x * (0.7978845608028654 + 0.035677408136300125 * (x * x))
    return half + half * jnp.tanh(inner)


def normalise(wide, gain):
    average = jnp.mean(wide, axis=-1, keepdims=True)
    centred = wide - average
    spread = jnp.mean(centred * centred, axis=-1, keepdims=True)
    return centred * lax.rsqrt(spread + 1e-05) * gain


def dot(a, b):
    return jnp.dot(a, b, preferred_element_type=F32)


def dot_nt(a, b):
    return lax.dot_general(a, b, (((1,), (1,)), ((), ())), preferred_element_type=F32)


def about_one_over(x):
    return pl.reciprocal(x, approx=True)


def with_ones(tensor):
    ones = jnp.ones((tensor.shape[0], PAD - tensor.shape[1]), F32)
    return jnp.concatenate([tensor, ones], axis=1).astype(BF16)


def below(*pieces):
    return jnp.concatenate(pieces, axis=0) if len(pieces) > 1 else pieces[0]


def pack_kernel(
    values_ref,
    cell_ref,
    tag_ref,
    count_ref,
    back_ref,
    *refs,
):
    out_ref, up_ref, down_ref, values, cells, tags, held, sem = refs
    tiles_lon, tiles_lat, capacity, _ = values_ref.shape
    lat_cells, lon_cells = back_ref.shape[:2]
    strips = [
        (back_ref.at[:HLAT], up_ref),
        (back_ref.at[lat_cells - HLAT :], down_ref),
    ]
    copies = [
        pltpu.make_async_copy(cell_ref, cells, sem.at[0]),
        pltpu.make_async_copy(tag_ref, tags, sem.at[1]),
        pltpu.make_async_copy(count_ref, held, sem.at[2]),
        pltpu.make_async_copy(values_ref, values, sem.at[3]),
    ]
    copies += [
        pltpu.make_async_copy(source, strip, sem.at[4 + n])
        for n, (source, strip) in enumerate(strips)
    ]
    for copy in copies:
        copy.start()
    for copy in copies[:3]:
        copy.wait()
    counts = below(*[held[tile : tile + 1, :] for tile in range(tiles_lat) for _ in range(capacity)])
    cell = cells[...]
    slot = lax.broadcasted_iota(jnp.int32, cell.shape, 0) % capacity
    row = cell // lon_cells
    fields = [jnp.where(slot < counts, row, 255), cell - row * lon_cells, tags[...]]
    rows, columns, kinds = (field.astype(F32) for field in fields)
    lane = lax.broadcasted_iota(jnp.int32, (cell.shape[0], LANES), 1)
    kind_of = (lane % INSTR).astype(F32)
    marks = [
        ((lane < ROWS) & (lane // INSTR == n)) | (lane == ROWS + n) | (lane == COLS + n)
        for n in range(len(AROUND))
    ]
    turned = []
    for lon in range(tiles_lon):
        meta = jnp.where(kind_of == kinds[:, lon : lon + 1], 1.0, 0.0)
        meta = jnp.where(lane >= ROWS, rows[:, lon : lon + 1], meta)
        meta = jnp.where(lane >= COLS, columns[:, lon : lon + 1], meta)
        turns = {0: meta}
        for dy in (-1, 1):
            by = dy * capacity % meta.shape[0]
            turns[dy] = below(meta[by:], meta[:by])
        turned.append(turns)
    for lon in range(tiles_lon):
        meta = jnp.zeros(lane.shape, F32)
        for mark, (dy, dx) in zip(marks, AROUND):
            meta = jnp.where(mark, turned[(lon + dx) % tiles_lon][dy], meta)
        out_ref[lon, :, len(AROUND)] = meta.astype(BF16).reshape(tiles_lat, capacity, LANES)
    copies[3].wait()
    for n, (dy, dx) in enumerate(AROUND):
        spans = {0: [(0, tiles_lat)], 1: [(0, tiles_lat - 1), (tiles_lat - 1, tiles_lat)]}
        spans[-1] = [(0, 1), (1, tiles_lat)]

        def copy_tiles(lon, n=n, dx=dx, dy=dy, spans=spans[dy]):
            source = lax.rem(lon + dx + tiles_lon, tiles_lon)
            for low, end in spans:
                first = (low + dy) % tiles_lat
                out_ref[lon, low:end, n] = values[source, first : first + end - low]

        if tiles_lon <= 8:
            for lon in range(tiles_lon):
                copy_tiles(lon)
        else:
            pl.loop(0, tiles_lon)(copy_tiles)
    for copy in copies[4:]:
        copy.wait()


def packed(record_values, record_cell, record_instrument, block_counts, background):
    tiles_lon, tiles_lat, capacity, wide = record_values.shape
    anywhere = pl.BlockSpec(memory_space=pltpu.HBM)
    ints = pltpu.VMEM((tiles_lat * capacity, tiles_lon), jnp.int32)
    shape = (tiles_lon, tiles_lat, len(AROUND) + 1, capacity, wide)
    lat_cells, lon_cells, levels, width = background.shape
    across = jax.ShapeDtypeStruct((HLAT, lon_cells, levels, width), BF16)
    out, *strips = pl.pallas_call(
        pack_kernel,
        out_shape=[jax.ShapeDtypeStruct(shape, BF16), across, across],
        in_specs=[anywhere] * 5,
        out_specs=[pl.BlockSpec(memory_space=pltpu.VMEM)] * 3,
        scratch_shapes=[
            pltpu.VMEM(record_values.shape, BF16),
            ints,
            ints,
            pltpu.VMEM((tiles_lat, tiles_lon), jnp.int32),
            pltpu.SemaphoreType.DMA((6,)),
        ],
        compiler_params=pltpu.CompilerParams(vmem_limit_bytes=56 * 2**20),
        cost_estimate=pl.CostEstimate(
            flops=20 * 10**9, bytes_accessed=10**6, transcendentals=0
        ),
    )(
        record_values,
        record_cell.transpose(1, 2, 0).reshape(-1, tiles_lon),
        record_instrument.transpose(1, 2, 0).reshape(-1, tiles_lon),
        block_counts.T,
        background,
    )
    return out.reshape((-1,) + shape[2:]), *strips


def token_codes(part, lon_cells):
    top, high, left, wide = part
    count = tokens_of(part)
    place = lax.broadcasted_iota(jnp.int32, (padded(count), LANES), 0)
    code = place + (top * lon_cells + left) * LEV
    for row in range(1, high):
        step = (lon_cells - wide) * LEV
        code = code + jnp.where(place >= row * wide * LEV, step, 0)
    return jnp.where(place < count, code, -8).astype(F32)


def near_entries(windows):
    own = [(4, 3 * i + j) for i, j in windows]
    return own + [(3 * i + 1, j) for i, j in windows if i != 1]


def far_entries(windows):
    beside = [(3 + j, i) for i, j in windows if j != 1]
    return beside + [(3 * i + j, 0) for i, j in windows if i != 1 and j != 1]


def scattered(recv_ref, first_ref, lift_ref, plan, lon_cells):
    sources, _, capacity, _ = recv_ref.shape
    width = first_ref.shape[1]
    chunk = min(CHUNK, sources)
    slots = chunk * capacity
    first, lift = first_ref[...], lift_ref[...]
    lane = lax.broadcasted_iota(jnp.int32, (16, LANES), 1)
    sub = lax.broadcasted_iota(jnp.int32, (16, LANES), 0)
    weigh = jnp.where(lane == ROWS + sub, float(lon_cells * LEV), 0.0)
    weigh = jnp.where(lane == COLS + sub, float(LEV), weigh).astype(BF16)
    codes = [below(*[token_codes(part, lon_cells) for part in parts]) for parts in plan]

    def scatter(begin):
        meta = recv_ref[pl.ds(begin, chunk), len(AROUND)].reshape(slots, LANES)
        records = below(
            *[
                recv_ref[pl.ds(begin, chunk), n].reshape(slots, LANES)
                for n in range(len(AROUND))
            ]
        )
        lane = lax.broadcasted_iota(jnp.int32, meta.shape, 1) // INSTR
        wide = meta.astype(F32)
        chosen = below(*[jnp.where(lane == n, wide, 0.0) for n in range(len(AROUND))]).astype(BF16)
        both = jnp.concatenate([records, chosen], axis=1)
        encoded = gelu(dot(both, first)).astype(BF16)
        lifted = gelu(dot(encoded, lift))
        tokens = dot_nt(weigh, meta)
        hots, parts = [], []
        for n in range(len(AROUND)):
            token = tokens[n : n + 1]
            token = jnp.concatenate([token + float(level) for level in range(LEV)], axis=1)
            if token.shape[1] == LANES:
                hot = codes[n] == token
            else:
                hot = codes[n][:, :1] == token
            hots.append(jnp.where(hot, 1.0, 0.0).astype(BF16))
        for n in range(len(AROUND)):
            part = lifted[n * slots : (n + 1) * slots]
            parts.append(
                with_ones(
                    below(*[part[:, level * width : (level + 1) * width] for level in range(LEV)])
                )
            )
        sums = [dot(hot, part) for hot, part in zip(hots, parts)]
        return tuple(sums)

    sums = scatter(0)
    if sources > chunk:
        sums = lax.fori_loop(
            1,
            sources // chunk,
            lambda step, total: tuple(a + b for a, b in zip(total, scatter(step * chunk))),
            sums,
        )
    return sums


def prepare_kernel(plan, back_ref, first_ref, table_ref, attn_ref, rows_ref, both_ref, parts_ref):
    width = back_ref.shape[3]
    pieces = []
    for top, high, left, wide in plan[4]:
        count = high * wide * LEV
        piece = back_ref[top : top + high, left : left + wide].reshape(count, width).astype(F32)
        if padded(count) > count:
            piece = below(piece, jnp.zeros((padded(count) - count, width), F32))
        pieces.append(piece)
    rows_ref[...] = below(*pieces)
    table = below(*[table_ref[...].astype(F32)] * (LANES // INSTR)).astype(BF16)
    both_ref[:LANES, :] = first_ref[...]
    both_ref[LANES:, :] = table
    for n in range(3):
        parts_ref[n] = attn_ref[:, n * width : (n + 1) * width]


def prepared(plan, background, input_weight, instrument_table, attn_weight):
    width = background.shape[3]
    rows = sum(padded(tokens_of(part)) for part in plan[4])
    vmem = pl.BlockSpec(memory_space=pltpu.VMEM)
    return pl.pallas_call(
        functools.partial(prepare_kernel, plan),
        out_shape=[
            jax.ShapeDtypeStruct((rows, width), F32),
            jax.ShapeDtypeStruct((2 * LANES, width), BF16),
            jax.ShapeDtypeStruct((3, width, width), BF16),
        ],
        in_specs=[vmem] * 4,
        out_specs=[vmem] * 3,
        compiler_params=pltpu.CompilerParams(vmem_limit_bytes=LIMIT),
        cost_estimate=pl.CostEstimate(flops=10**9, bytes_accessed=10**6, transcendentals=0),
    )(background, input_weight, instrument_table, attn_weight)


def normed_of(plan, entries, sums, borders, gain):
    rows_ref, north_ref, south_ref, west_ref, east_ref, lat_cells = borders
    width = gain.shape[1]
    pieces, spans, start = [], {}, 0
    for tile, number in entries:
        dy, dx = AROUND[tile]
        top, high, left, wide = plan[tile][number]
        count = high * wide * LEV
        full = padded(count)
        if tile == 4:
            begin = sum(padded(tokens_of(part)) for part in plan[4][:number])
            piece = rows_ref[begin : begin + full, :]
        else:
            if dx:
                ref = west_ref if dx < 0 else east_ref
                top, left = {-1: 0, 0: top + HLAT, 1: lat_cells + HLAT}[dy], 0
            else:
                ref, top = (north_ref, 0) if dy < 0 else (south_ref, 0)
            piece = ref[top : top + high, left : left + wide].reshape(count, width).astype(F32)
            if full > count:
                piece = below(piece, jnp.zeros((full - count, width), F32))
        pieces.append(piece)
        spans[tile, number] = (start, count)
        start += full
    tally = 1.0 + sums[:, width : width + 1]
    share = about_one_over(tally)
    share = share * (2.0 - tally * share)
    latent = ((below(*pieces) + sums[:, :width]) * share).astype(BF16).astype(F32)
    return latent, normalise(latent, gain), spans


def worked(plan, places, piece_of, own_normed, latent, weights, scalars_ref, put):
    parts_ref, mix_ref, gain_ref, up_ref, down_ref = weights
    width = mix_ref.shape[0]
    groups = [padded(tokens_of(plan[4][3 * i + j])) for i, j in places]
    windows = []
    for i, j in places:
        window = [piece_of(4, 3 * i + j)]
        if i != 1:
            window.append(piece_of(3 * i + 1, j))
        if j != 1:
            window.append(piece_of(3 + j, i))
        if i != 1 and j != 1:
            window.append(piece_of(3 * i + j, 0))
        windows.append(window)
    tokens = below(*[piece for window in windows for piece in window]).astype(BF16)
    head = width // HEADS
    query = dot(own_normed.astype(BF16), parts_ref[0]) * head ** (-0.5)
    query = jnp.concatenate([query, jnp.ones((query.shape[0], PAD - width), F32)], axis=1)
    keys = dot(tokens, parts_ref[1])
    values = with_ones(dot(tokens, parts_ref[2]))

    lane = lax.broadcasted_iota(jnp.int32, (1, PAD), 1)
    many = WLAT * WLON * LEV
    corner = HLAT * HLON * LEV
    key = lax.broadcasted_iota(jnp.int32, (many, PAD - width), 0)
    spare = lax.broadcasted_iota(jnp.int32, (many, PAD - width), 1)
    unused = lax.broadcasted_iota(jnp.int32, (PAD - many, PAD), 1)
    unused = jnp.where(unused == width, -3e38, 0.0).astype(BF16)
    nothing = jnp.zeros((PAD - many, PAD), BF16)

    def keys_of(w, i, j):
        bias = jnp.zeros((many, PAD - width), F32)
        if i != 1:
            if j == 1:
                inside = key < 2 * corner
            else:
                inside = (key < corner) | ((key >= 2 * corner) & (key < 3 * corner))
            bias = jnp.where(inside | (spare > 0), 0.0, -3e38) * scalars_ref[i].astype(F32)
        here = jnp.concatenate([keys[w * many : (w + 1) * many], bias], axis=1)
        return below(here.astype(BF16), unused)

    begins = [sum(groups[:w]) for w in range(len(groups))]
    parts = [query[begin : begin + rows] for begin, rows in zip(begins, groups)]
    stacks = [
        below(
            *[jnp.where((lane // head == h) | (lane >= width), part, 0.0) for h in range(HEADS)]
        ).astype(BF16)
        for part in parts
    ]
    held = [keys_of(w, i, j) for w, (i, j) in enumerate(places)]
    scores = [dot_nt(stack, here) for stack, here in zip(stacks, held)]
    largest = [jnp.max(score, axis=-1, keepdims=True) for score in scores]
    raised = [jnp.exp((score - most).astype(BF16)) for score, most in zip(scores, largest)]
    held = [below(values[w * many : (w + 1) * many], nothing) for w in range(len(places))]
    products = [dot(one, here) for one, here in zip(raised, held)]
    shares = [about_one_over(product[:, width : width + 1]) for product in products]
    products = [product[:, :width] * share for product, share in zip(products, shares)]
    mixed = []
    for product, rows in zip(products, groups):
        total = product[:rows]
        for h in range(1, HEADS):
            own = lane[:, :width] // head == h
            total = jnp.where(own, product[h * rows : (h + 1) * rows], total)
        mixed.append(total)
    mixed = below(*mixed).astype(BF16)

    after = (latent + dot(mixed, mix_ref[...])).astype(BF16).astype(F32)
    normed_two = normalise(after, gain_ref[...].astype(F32)).astype(BF16)
    hidden = gelu(dot(normed_two, up_ref[...]).astype(BF16))
    result = after + dot(hidden, down_ref[...])
    for begin, (i, j) in zip(begins, places):
        part = plan[4][3 * i + j]
        piece = result[begin : begin + tokens_of(part)].astype(BF16)
        put(part, j, piece.reshape(part[1], part[3], LEV, width))


MIDDLE = [(0, 1), (1, 1), (2, 1)]
SIDES = [(0, 0), (0, 2), (2, 0), (2, 2), (1, 0), (1, 2)]


def own_rows(plan, places):
    return sum(padded(tokens_of(plan[4][3 * i + j])) for i, j in places)


def middle_kernel(
    plan,
    lat_cells,
    lon_cells,
    scalars_ref,
    recv_ref,
    north_ref,
    south_ref,
    rows_ref,
    both_ref,
    lift_ref,
    gain_one_ref,
    *refs,
):
    *weights, out_ref, rest_ref, latent_ref, normed_ref = refs
    sums = scattered(recv_ref, both_ref, lift_ref, plan, lon_cells)

    def sums_of(entries):
        pieces = []
        for tile, number in entries:
            start = sum(padded(tokens_of(part)) for part in plan[tile][:number])
            pieces.append(sums[tile][start : start + padded(tokens_of(plan[tile][number]))])
        return below(*pieces)

    borders = (rows_ref, north_ref, south_ref, None, None, lat_cells)
    gain = gain_one_ref[...].astype(F32)
    entries = near_entries(MIDDLE)
    latent, normed, spans = normed_of(plan, entries, sums_of(entries), borders, gain)

    def piece_of(tile, number):
        start, count = spans[tile, number]
        return normed[start : start + count]

    def put(part, _, piece):
        out_ref[part[0] : part[0] + part[1]] = piece

    end = own_rows(plan, MIDDLE)
    worked(plan, MIDDLE, piece_of, normed[:end], latent[:end], weights, scalars_ref, put)
    rest_ref[...] = sums_of(far_entries(SIDES))
    entries = near_entries(SIDES)
    latent, normed, _ = normed_of(plan, entries, sums_of(entries), borders, gain)
    latent_ref[...] = latent[: latent_ref.shape[0]]
    normed_ref[...] = normed


def side_kernel(
    plan,
    lat_cells,
    scalars_ref,
    rest_ref,
    latent_ref,
    normed_ref,
    west_ref,
    east_ref,
    gain_one_ref,
    *refs,
):
    *weights, middle_ref, out_ref, held_ref, sem = refs
    left, wide = plan[4][4][2:]
    copies = [pltpu.make_async_copy(middle_ref, out_ref.at[:, left : left + wide], sem.at[2])]
    copies[0].start()
    near, start = {}, 0
    for tile, number in near_entries(SIDES):
        near[tile, number] = start
        start += padded(tokens_of(plan[tile][number]))
    borders = (None, None, None, west_ref, east_ref, lat_cells)
    gain = gain_one_ref[...].astype(F32)
    _, far, spans = normed_of(plan, far_entries(SIDES), rest_ref[...], borders, gain)

    def piece_of(tile, number):
        if (tile, number) in spans:
            start, count = spans[tile, number]
            return far[start : start + count]
        start = near[tile, number]
        return normed_ref[start : start + tokens_of(plan[tile][number]), :]

    def put(part, j, piece):
        held_ref[j // 2, part[0] : part[0] + part[1]] = piece

    end = own_rows(plan, SIDES)
    worked(
        plan, SIDES, piece_of, normed_ref[:end, :], latent_ref[...], weights, scalars_ref, put
    )
    for n, number in enumerate((0, 2)):
        left, wide = plan[4][number][2:]
        copies.append(
            pltpu.make_async_copy(held_ref.at[n], out_ref.at[:, left : left + wide], sem.at[n])
        )
        copies[-1].start()
    for copy in copies:
        copy.wait()


def local(
    record_values,
    record_cell,
    record_instrument,
    block_counts,
    background,
    input_weight,
    instrument_table,
    lift_weight,
    first_gain,
    attn_weight,
    mix_weight,
    second_gain,
    up_weight,
    down_weight,
):
    lat_cells, lon_cells, _, width = background.shape
    tiles_lat = record_values.shape[1]

    sent, up, down = packed(
        record_values, record_cell, record_instrument, block_counts, background
    )
    received = lax.all_to_all(sent, ("lon", "lat"), split_axis=0, concat_axis=0, tiled=True)
    north, south = before_and_after(swapped(up, down, "lat", wraps=False), "lat")

    later, input_weight, instrument_table, attn_weight, down_weight, _ = lax.optimization_barrier(
        (background, input_weight, instrument_table, attn_weight, down_weight, up)
    )

    def columns(low, end):
        return jnp.concatenate([north[:, low:end], later[:, low:end], south[:, low:end]], axis=0)

    got = swapped(columns(0, HLON), columns(lon_cells - HLON, lon_cells), "lon", wraps=True)

    plan = rectangles(lat_cells, lon_cells)
    rows, both, parts = prepared(plan, later, input_weight, instrument_table, attn_weight)
    lat = lax.axis_index("lat")
    scalars = jnp.stack([lat == 0, lat < 0, lat == tiles_lat - 1]).astype(jnp.int32)

    def rows_in(entries):
        return sum(padded(tokens_of(plan[tile][number])) for tile, number in entries)

    gain_one = first_gain.reshape(1, width)
    weights = [parts, mix_weight, second_gain.reshape(1, width), up_weight, down_weight]
    smem = pl.BlockSpec(memory_space=pltpu.SMEM)
    vmem = pl.BlockSpec(memory_space=pltpu.VMEM)
    anywhere = pl.BlockSpec(memory_space=pl.ANY)
    params = pltpu.CompilerParams(vmem_limit_bytes=LIMIT)
    middle, rest, latent, normed = pl.pallas_call(
        functools.partial(middle_kernel, plan, lat_cells, lon_cells),
        out_shape=[
            jax.ShapeDtypeStruct((lat_cells, lon_cells - WLON, LEV, width), BF16),
            jax.ShapeDtypeStruct((rows_in(far_entries(SIDES)), PAD), F32),
            jax.ShapeDtypeStruct((own_rows(plan, SIDES), width), F32),
            jax.ShapeDtypeStruct((rows_in(near_entries(SIDES)), width), F32),
        ],
        in_specs=[smem] + [vmem] * (7 + len(weights)),
        out_specs=[vmem] * 4,
        compiler_params=params,
        cost_estimate=pl.CostEstimate(
            flops=4 * 10**9, bytes_accessed=4 * 10**6, transcendentals=10**6
        ),
    )(scalars, received, north, south, rows, both, lift_weight, gain_one, *weights)
    rest, *got = lax.optimization_barrier((rest, *got))
    west, east = before_and_after(got, "lon")
    return pl.pallas_call(
        functools.partial(side_kernel, plan, lat_cells),
        out_shape=jax.ShapeDtypeStruct(background.shape, BF16),
        in_specs=[smem] + [vmem] * (7 + len(weights)),
        out_specs=anywhere,
        scratch_shapes=[
            pltpu.VMEM((2, lat_cells, HLON, LEV, width), BF16),
            pltpu.SemaphoreType.DMA((3,)),
        ],
        compiler_params=params,
        cost_estimate=pl.CostEstimate(
            flops=3 * 10**9, bytes_accessed=4 * 10**6, transcendentals=10**6
        ),
    )(scalars, rest, latent, normed, west, east, gain_one, *weights, middle)


def solution(mesh):
    placed = (
        P("lon", "lat", None, None),
        P("lon", "lat", None),
        P("lon", "lat", None),
        P("lon", "lat"),
        P("lat", "lon", None, None),
        P(),
        P(),
        P(),
        P(),
        P(),
        P(),
        P(),
        P(),
        P(),
    )
    return jax.shard_map(
        local, mesh=mesh, in_specs=placed, out_specs=P("lat", "lon", None, None), check_vma=False
    )
```

```python
import functools

import jax
import jax.numpy as jnp
from jax import lax
from jax.experimental import pallas as pl
from jax.experimental.pallas import tpu as pltpu
from jax.sharding import PartitionSpec as P

HEADS = 6
INSTR = 8
LEV = 2
WLAT = 6
WLON = 12
HLAT = WLAT // 2
HLON = WLON // 2
LANES = 128
PAD = 256
CHUNK = 32
LIMIT = 40 * 2**20
BF16 = jnp.bfloat16
F32 = jnp.float32

AROUND = [(dy, dx) for dy in (-1, 0, 1) for dx in (-1, 0, 1)]
ROWS = INSTR * len(AROUND)
COLS = ROWS + len(AROUND)


def swapped(up, down, axis, wraps):
    count = lax.axis_size(axis)
    even = lax.axis_index(axis) % 2 == 0
    got = []
    for first, mine in ((0, jnp.where(even, down, up)), (1, jnp.where(even, up, down))):
        pairs = []
        for low in range(first, count, 2):
            high = (low + 1) % count
            if high > low or wraps:
                pairs += [(low, high), (high, low)]
        got.append(lax.ppermute(mine, axis, pairs))
    return got


def before_and_after(got, axis):
    even = lax.axis_index(axis) % 2 == 0
    return jnp.where(even, got[1], got[0]), jnp.where(even, got[0], got[1])


def rectangles(lat_cells, lon_cells):
    lat = {-1: [(lat_cells - HLAT, HLAT)], 1: [(0, HLAT)]}
    lat[0] = [(0, HLAT), (HLAT, lat_cells - WLAT), (lat_cells - HLAT, HLAT)]
    lon = {-1: [(lon_cells - HLON, HLON)], 1: [(0, HLON)]}
    lon[0] = [(0, HLON), (HLON, lon_cells - WLON), (lon_cells - HLON, HLON)]
    return [
        [(top, high, left, wide) for top, high in lat[dy] for left, wide in lon[dx]]
        for dy, dx in AROUND
    ]


def tokens_of(part):
    return part[1] * part[3] * LEV


def padded(count):
    return -(-count // 8) * 8


def gelu(x):
    half = 0.5 * x
    inner = x * (0.7978845608028654 + 0.035677408136300125 * (x * x))
    return half + half * jnp.tanh(inner)


def normalise(wide, gain):
    average = jnp.mean(wide, axis=-1, keepdims=True)
    centred = wide - average
    spread = jnp.mean(centred * centred, axis=-1, keepdims=True)
    return centred * lax.rsqrt(spread + 1e-05) * gain


def dot(a, b):
    return jnp.dot(a, b, preferred_element_type=F32)


def dot_nt(a, b):
    return lax.dot_general(a, b, (((1,), (1,)), ((), ())), preferred_element_type=F32)


def about_one_over(x):
    return pl.reciprocal(x, approx=True)


def with_ones(tensor):
    ones = jnp.ones((tensor.shape[0], PAD - tensor.shape[1]), F32)
    return jnp.concatenate([tensor, ones], axis=1).astype(BF16)


def below(*pieces):
    return jnp.concatenate(pieces, axis=0) if len(pieces) > 1 else pieces[0]


def pack_kernel(
    values_ref,
    cell_ref,
    tag_ref,
    count_ref,
    back_ref,
    *refs,
):
    out_ref, up_ref, down_ref, values, cells, tags, held, sem = refs
    tiles_lon, tiles_lat, capacity, _ = values_ref.shape
    lat_cells, lon_cells = back_ref.shape[:2]
    strips = [
        (back_ref.at[:HLAT], up_ref),
        (back_ref.at[lat_cells - HLAT :], down_ref),
    ]
    copies = [
        pltpu.make_async_copy(cell_ref, cells, sem.at[0]),
        pltpu.make_async_copy(tag_ref, tags, sem.at[1]),
        pltpu.make_async_copy(count_ref, held, sem.at[2]),
        pltpu.make_async_copy(values_ref, values, sem.at[3]),
    ]
    copies += [
        pltpu.make_async_copy(source, strip, sem.at[4 + n])
        for n, (source, strip) in enumerate(strips)
    ]
    for copy in copies:
        copy.start()
    for copy in copies[:3]:
        copy.wait()
    counts = below(*[held[tile : tile + 1, :] for tile in range(tiles_lat) for _ in range(capacity)])
    cell = cells[...]
    slot = lax.broadcasted_iota(jnp.int32, cell.shape, 0) % capacity
    row = cell // lon_cells
    fields = [jnp.where(slot < counts, row, 255), cell - row * lon_cells, tags[...]]
    rows, columns, kinds = (field.astype(F32) for field in fields)
    lane = lax.broadcasted_iota(jnp.int32, (cell.shape[0], LANES), 1)
    kind_of = (lane % INSTR).astype(F32)
    marks = [
        ((lane < ROWS) & (lane // INSTR == n)) | (lane == ROWS + n) | (lane == COLS + n)
        for n in range(len(AROUND))
    ]
    turned = []
    for lon in range(tiles_lon):
        meta = jnp.where(kind_of == kinds[:, lon : lon + 1], 1.0, 0.0)
        meta = jnp.where(lane >= ROWS, rows[:, lon : lon + 1], meta)
        meta = jnp.where(lane >= COLS, columns[:, lon : lon + 1], meta)
        turns = {0: meta}
        for dy in (-1, 1):
            by = dy * capacity % meta.shape[0]
            turns[dy] = below(meta[by:], meta[:by])
        turned.append(turns)
    for lon in range(tiles_lon):
        meta = jnp.zeros(lane.shape, F32)
        for mark, (dy, dx) in zip(marks, AROUND):
            meta = jnp.where(mark, turned[(lon + dx) % tiles_lon][dy], meta)
        out_ref[lon, :, len(AROUND)] = meta.astype(BF16).reshape(tiles_lat, capacity, LANES)
    copies[3].wait()
    for n, (dy, dx) in enumerate(AROUND):
        spans = {0: [(0, tiles_lat)], 1: [(0, tiles_lat - 1), (tiles_lat - 1, tiles_lat)]}
        spans[-1] = [(0, 1), (1, tiles_lat)]

        def copy_tiles(lon, n=n, dx=dx, dy=dy, spans=spans[dy]):
            source = lax.rem(lon + dx + tiles_lon, tiles_lon)
            for low, end in spans:
                first = (low + dy) % tiles_lat
                out_ref[lon, low:end, n] = values[source, first : first + end - low]

        if tiles_lon <= 8:
            for lon in range(tiles_lon):
                copy_tiles(lon)
        else:
            pl.loop(0, tiles_lon)(copy_tiles)
    for copy in copies[4:]:
        copy.wait()


def packed(record_values, record_cell, record_instrument, block_counts, background):
    tiles_lon, tiles_lat, capacity, wide = record_values.shape
    anywhere = pl.BlockSpec(memory_space=pltpu.HBM)
    ints = pltpu.VMEM((tiles_lat * capacity, tiles_lon), jnp.int32)
    shape = (tiles_lon, tiles_lat, len(AROUND) + 1, capacity, wide)
    lat_cells, lon_cells, levels, width = background.shape
    across = jax.ShapeDtypeStruct((HLAT, lon_cells, levels, width), BF16)
    out, *strips = pl.pallas_call(
        pack_kernel,
        out_shape=[jax.ShapeDtypeStruct(shape, BF16), across, across],
        in_specs=[anywhere] * 5,
        out_specs=[pl.BlockSpec(memory_space=pltpu.VMEM)] * 3,
        scratch_shapes=[
            pltpu.VMEM(record_values.shape, BF16),
            ints,
            ints,
            pltpu.VMEM((tiles_lat, tiles_lon), jnp.int32),
            pltpu.SemaphoreType.DMA((6,)),
        ],
        compiler_params=pltpu.CompilerParams(vmem_limit_bytes=56 * 2**20),
        cost_estimate=pl.CostEstimate(
            flops=20 * 10**9, bytes_accessed=10**6, transcendentals=0
        ),
    )(
        record_values,
        record_cell.transpose(1, 2, 0).reshape(-1, tiles_lon),
        record_instrument.transpose(1, 2, 0).reshape(-1, tiles_lon),
        block_counts.T,
        background,
    )
    return out.reshape((-1,) + shape[2:]), *strips


def token_codes(part, lon_cells):
    top, high, left, wide = part
    count = tokens_of(part)
    place = lax.broadcasted_iota(jnp.int32, (padded(count), LANES), 0)
    code = place + (top * lon_cells + left) * LEV
    for row in range(1, high):
        step = (lon_cells - wide) * LEV
        code = code + jnp.where(place >= row * wide * LEV, step, 0)
    return jnp.where(place < count, code, -8).astype(F32)


def near_entries(windows):
    own = [(4, 3 * i + j) for i, j in windows]
    return own + [(3 * i + 1, j) for i, j in windows if i != 1]


def far_entries(windows):
    beside = [(3 + j, i) for i, j in windows if j != 1]
    return beside + [(3 * i + j, 0) for i, j in windows if i != 1 and j != 1]


def scattered(recv_ref, first_ref, table_ref, lift_ref, plan, lon_cells):
    sources, _, capacity, _ = recv_ref.shape
    width = first_ref.shape[1]
    chunk = min(CHUNK, sources)
    slots = chunk * capacity
    table = below(*[table_ref[...].astype(F32)] * (LANES // INSTR)).astype(BF16)
    first, lift = below(first_ref[...], table), lift_ref[...]
    lane = lax.broadcasted_iota(jnp.int32, (16, LANES), 1)
    sub = lax.broadcasted_iota(jnp.int32, (16, LANES), 0)
    weigh = jnp.where(lane == ROWS + sub, float(lon_cells * LEV), 0.0)
    weigh = jnp.where(lane == COLS + sub, float(LEV), weigh).astype(BF16)
    codes = [below(*[token_codes(part, lon_cells) for part in parts]) for parts in plan]

    def scatter(begin):
        meta = recv_ref[pl.ds(begin, chunk), len(AROUND)].reshape(slots, LANES)
        records = below(
            *[
                recv_ref[pl.ds(begin, chunk), n].reshape(slots, LANES)
                for n in range(len(AROUND))
            ]
        )
        lane = lax.broadcasted_iota(jnp.int32, meta.shape, 1) // INSTR
        wide = meta.astype(F32)
        chosen = below(*[jnp.where(lane == n, wide, 0.0) for n in range(len(AROUND))]).astype(BF16)
        both = jnp.concatenate([records, chosen], axis=1)
        encoded = gelu(dot(both, first)).astype(BF16)
        lifted = gelu(dot(encoded, lift))
        tokens = dot_nt(weigh, meta)
        hots, parts = [], []
        for n in range(len(AROUND)):
            token = tokens[n : n + 1]
            token = jnp.concatenate([token + float(level) for level in range(LEV)], axis=1)
            if token.shape[1] == LANES:
                hot = codes[n] == token
            else:
                hot = codes[n][:, :1] == token
            hots.append(jnp.where(hot, 1.0, 0.0).astype(BF16))
        for n in range(len(AROUND)):
            part = lifted[n * slots : (n + 1) * slots]
            parts.append(
                with_ones(
                    below(*[part[:, level * width : (level + 1) * width] for level in range(LEV)])
                )
            )
        sums = [dot(hot, part) for hot, part in zip(hots, parts)]
        return tuple(sums)

    sums = scatter(0)
    if sources > chunk:
        sums = lax.fori_loop(
            1,
            sources // chunk,
            lambda step, total: tuple(a + b for a, b in zip(total, scatter(step * chunk))),
            sums,
        )
    return sums


def prepare_kernel(plan, back_ref, attn_ref, rows_ref, parts_ref):
    width = back_ref.shape[3]
    pieces = []
    for top, high, left, wide in plan[4]:
        count = high * wide * LEV
        piece = back_ref[top : top + high, left : left + wide].reshape(count, width).astype(F32)
        if padded(count) > count:
            piece = below(piece, jnp.zeros((padded(count) - count, width), F32))
        pieces.append(piece)
    rows_ref[...] = below(*pieces)
    for n in range(3):
        parts_ref[n] = attn_ref[:, n * width : (n + 1) * width]


def prepared(plan, background, attn_weight):
    width = background.shape[3]
    rows = sum(padded(tokens_of(part)) for part in plan[4])
    vmem = pl.BlockSpec(memory_space=pltpu.VMEM)
    return pl.pallas_call(
        functools.partial(prepare_kernel, plan),
        out_shape=[
            jax.ShapeDtypeStruct((rows, width), F32),
            jax.ShapeDtypeStruct((3, width, width), BF16),
        ],
        in_specs=[vmem] * 2,
        out_specs=[vmem] * 2,
        compiler_params=pltpu.CompilerParams(vmem_limit_bytes=LIMIT),
        cost_estimate=pl.CostEstimate(flops=10**9, bytes_accessed=10**6, transcendentals=0),
    )(background, attn_weight)


def normed_of(plan, entries, sums, borders, gain):
    rows_ref, north_ref, south_ref, west_ref, east_ref, lat_cells = borders
    width = gain.shape[1]
    pieces, spans, start = [], {}, 0
    for tile, number in entries:
        dy, dx = AROUND[tile]
        top, high, left, wide = plan[tile][number]
        count = high * wide * LEV
        full = padded(count)
        if tile == 4:
            begin = sum(padded(tokens_of(part)) for part in plan[4][:number])
            piece = rows_ref[begin : begin + full, :]
        else:
            if dx:
                ref = west_ref if dx < 0 else east_ref
                top, left = {-1: 0, 0: top + HLAT, 1: lat_cells + HLAT}[dy], 0
            else:
                ref, top = (north_ref, 0) if dy < 0 else (south_ref, 0)
            piece = ref[top : top + high, left : left + wide].reshape(count, width).astype(F32)
            if full > count:
                piece = below(piece, jnp.zeros((full - count, width), F32))
        pieces.append(piece)
        spans[tile, number] = (start, count)
        start += full
    tally = 1.0 + sums[:, width : width + 1]
    share = about_one_over(tally)
    share = share * (2.0 - tally * share)
    latent = ((below(*pieces) + sums[:, :width]) * share).astype(BF16).astype(F32)
    return latent, normalise(latent, gain), spans


def worked(plan, places, piece_of, own_normed, latent, weights, scalars_ref, put):
    parts_ref, mix_ref, gain_ref, up_ref, down_ref = weights
    width = mix_ref.shape[0]
    groups = [padded(tokens_of(plan[4][3 * i + j])) for i, j in places]
    windows = []
    for i, j in places:
        window = [piece_of(4, 3 * i + j)]
        if i != 1:
            window.append(piece_of(3 * i + 1, j))
        if j != 1:
            window.append(piece_of(3 + j, i))
        if i != 1 and j != 1:
            window.append(piece_of(3 * i + j, 0))
        windows.append(window)
    tokens = below(*[piece for window in windows for piece in window]).astype(BF16)
    head = width // HEADS
    query = dot(own_normed.astype(BF16), parts_ref[0]) * head ** (-0.5)
    query = jnp.concatenate([query, jnp.ones((query.shape[0], PAD - width), F32)], axis=1)
    keys = dot(tokens, parts_ref[1])
    values = with_ones(dot(tokens, parts_ref[2]))

    lane = lax.broadcasted_iota(jnp.int32, (1, PAD), 1)
    many = WLAT * WLON * LEV
    corner = HLAT * HLON * LEV
    key = lax.broadcasted_iota(jnp.int32, (many, PAD - width), 0)
    spare = lax.broadcasted_iota(jnp.int32, (many, PAD - width), 1)
    unused = lax.broadcasted_iota(jnp.int32, (PAD - many, PAD), 1)
    unused = jnp.where(unused == width, -3e38, 0.0).astype(BF16)
    nothing = jnp.zeros((PAD - many, PAD), BF16)

    def keys_of(w, i, j):
        bias = jnp.zeros((many, PAD - width), F32)
        if i != 1:
            if j == 1:
                inside = key < 2 * corner
            else:
                inside = (key < corner) | ((key >= 2 * corner) & (key < 3 * corner))
            bias = jnp.where(inside | (spare > 0), 0.0, -3e38) * scalars_ref[i].astype(F32)
        here = jnp.concatenate([keys[w * many : (w + 1) * many], bias], axis=1)
        return below(here.astype(BF16), unused)

    begins = [sum(groups[:w]) for w in range(len(groups))]
    parts = [query[begin : begin + rows] for begin, rows in zip(begins, groups)]
    stacks = [
        below(
            *[jnp.where((lane // head == h) | (lane >= width), part, 0.0) for h in range(HEADS)]
        ).astype(BF16)
        for part in parts
    ]
    held = [keys_of(w, i, j) for w, (i, j) in enumerate(places)]
    scores = [dot_nt(stack, here) for stack, here in zip(stacks, held)]
    largest = [jnp.max(score, axis=-1, keepdims=True) for score in scores]
    raised = [jnp.exp((score - most).astype(BF16)) for score, most in zip(scores, largest)]
    held = [below(values[w * many : (w + 1) * many], nothing) for w in range(len(places))]
    products = [dot(one, here) for one, here in zip(raised, held)]
    shares = [about_one_over(product[:, width : width + 1]) for product in products]
    products = [product[:, :width] * share for product, share in zip(products, shares)]
    mixed = []
    for product, rows in zip(products, groups):
        total = product[:rows]
        for h in range(1, HEADS):
            own = lane[:, :width] // head == h
            total = jnp.where(own, product[h * rows : (h + 1) * rows], total)
        mixed.append(total)
    mixed = below(*mixed).astype(BF16)

    after = (latent + dot(mixed, mix_ref[...])).astype(BF16).astype(F32)
    normed_two = normalise(after, gain_ref[...].astype(F32).reshape(1, -1)).astype(BF16)
    hidden = gelu(dot(normed_two, up_ref[...]).astype(BF16))
    result = after + dot(hidden, down_ref[...])
    for begin, (i, j) in zip(begins, places):
        part = plan[4][3 * i + j]
        piece = result[begin : begin + tokens_of(part)].astype(BF16)
        put(part, j, piece.reshape(part[1], part[3], LEV, width))


MIDDLE = [(0, 1), (1, 1), (2, 1)]
SIDES = [(0, 0), (0, 2), (2, 0), (2, 2), (1, 0), (1, 2)]


def own_rows(plan, places):
    return sum(padded(tokens_of(plan[4][3 * i + j])) for i, j in places)


def middle_kernel(
    plan,
    lat_cells,
    lon_cells,
    scalars_ref,
    recv_ref,
    north_ref,
    south_ref,
    rows_ref,
    first_ref,
    table_ref,
    lift_ref,
    gain_one_ref,
    *refs,
):
    *weights, out_ref, rest_ref, latent_ref, normed_ref = refs
    sums = scattered(recv_ref, first_ref, table_ref, lift_ref, plan, lon_cells)

    def sums_of(entries):
        pieces = []
        for tile, number in entries:
            start = sum(padded(tokens_of(part)) for part in plan[tile][:number])
            pieces.append(sums[tile][start : start + padded(tokens_of(plan[tile][number]))])
        return below(*pieces)

    borders = (rows_ref, north_ref, south_ref, None, None, lat_cells)
    gain = gain_one_ref[...].astype(F32).reshape(1, -1)
    entries = near_entries(MIDDLE)
    latent, normed, spans = normed_of(plan, entries, sums_of(entries), borders, gain)

    def piece_of(tile, number):
        start, count = spans[tile, number]
        return normed[start : start + count]

    def put(part, _, piece):
        out_ref[part[0] : part[0] + part[1]] = piece

    end = own_rows(plan, MIDDLE)
    worked(plan, MIDDLE, piece_of, normed[:end], latent[:end], weights, scalars_ref, put)
    rest_ref[...] = sums_of(far_entries(SIDES))
    entries = near_entries(SIDES)
    latent, normed, _ = normed_of(plan, entries, sums_of(entries), borders, gain)
    latent_ref[...] = latent[: latent_ref.shape[0]]
    normed_ref[...] = normed


def side_kernel(
    plan,
    lat_cells,
    scalars_ref,
    rest_ref,
    latent_ref,
    normed_ref,
    west_ref,
    east_ref,
    gain_one_ref,
    *refs,
):
    *weights, middle_ref, out_ref, held_ref, sem = refs
    left, wide = plan[4][4][2:]
    copies = [pltpu.make_async_copy(middle_ref, out_ref.at[:, left : left + wide], sem.at[2])]
    copies[0].start()
    near, start = {}, 0
    for tile, number in near_entries(SIDES):
        near[tile, number] = start
        start += padded(tokens_of(plan[tile][number]))
    borders = (None, None, None, west_ref, east_ref, lat_cells)
    gain = gain_one_ref[...].astype(F32).reshape(1, -1)
    _, far, spans = normed_of(plan, far_entries(SIDES), rest_ref[...], borders, gain)

    def piece_of(tile, number):
        if (tile, number) in spans:
            start, count = spans[tile, number]
            return far[start : start + count]
        start = near[tile, number]
        return normed_ref[start : start + tokens_of(plan[tile][number]), :]

    def put(part, j, piece):
        held_ref[j // 2, part[0] : part[0] + part[1]] = piece

    end = own_rows(plan, SIDES)
    worked(
        plan, SIDES, piece_of, normed_ref[:end, :], latent_ref[...], weights, scalars_ref, put
    )
    for n, number in enumerate((0, 2)):
        left, wide = plan[4][number][2:]
        copies.append(
            pltpu.make_async_copy(held_ref.at[n], out_ref.at[:, left : left + wide], sem.at[n])
        )
        copies[-1].start()
    for copy in copies:
        copy.wait()


def local(
    record_values,
    record_cell,
    record_instrument,
    block_counts,
    background,
    input_weight,
    instrument_table,
    lift_weight,
    first_gain,
    attn_weight,
    mix_weight,
    second_gain,
    up_weight,
    down_weight,
):
    lat_cells, lon_cells, _, width = background.shape
    tiles_lat = record_values.shape[1]

    sent, up, down = packed(
        record_values, record_cell, record_instrument, block_counts, background
    )
    received = lax.all_to_all(sent, ("lon", "lat"), split_axis=0, concat_axis=0, tiled=True)
    north, south = before_and_after(swapped(up, down, "lat", wraps=False), "lat")

    later, input_weight, attn_weight, down_weight, _ = lax.optimization_barrier(
        (background, input_weight, attn_weight, down_weight, up)
    )

    def columns(low, end):
        return jnp.concatenate([north[:, low:end], later[:, low:end], south[:, low:end]], axis=0)

    got = swapped(columns(0, HLON), columns(lon_cells - HLON, lon_cells), "lon", wraps=True)

    plan = rectangles(lat_cells, lon_cells)
    rows, parts = prepared(plan, later, attn_weight)
    lat = lax.axis_index("lat")
    scalars = jnp.stack([lat == 0, lat < 0, lat == tiles_lat - 1]).astype(jnp.int32)

    def rows_in(entries):
        return sum(padded(tokens_of(plan[tile][number])) for tile, number in entries)

    gain_one = first_gain
    weights = [parts, mix_weight, second_gain, up_weight, down_weight]
    smem = pl.BlockSpec(memory_space=pltpu.SMEM)
    vmem = pl.BlockSpec(memory_space=pltpu.VMEM)
    anywhere = pl.BlockSpec(memory_space=pl.ANY)
    params = pltpu.CompilerParams(vmem_limit_bytes=LIMIT)
    middle, rest, latent, normed = pl.pallas_call(
        functools.partial(middle_kernel, plan, lat_cells, lon_cells),
        out_shape=[
            jax.ShapeDtypeStruct((lat_cells, lon_cells - WLON, LEV, width), BF16),
            jax.ShapeDtypeStruct((rows_in(far_entries(SIDES)), PAD), F32),
            jax.ShapeDtypeStruct((own_rows(plan, SIDES), width), F32),
            jax.ShapeDtypeStruct((rows_in(near_entries(SIDES)), width), F32),
        ],
        in_specs=[smem] + [vmem] * (8 + len(weights)),
        out_specs=[vmem] * 4,
        compiler_params=params,
        cost_estimate=pl.CostEstimate(
            flops=4 * 10**9, bytes_accessed=4 * 10**6, transcendentals=10**6
        ),
    )(
        scalars,
        received,
        north,
        south,
        rows,
        input_weight,
        instrument_table,
        lift_weight,
        gain_one,
        *weights,
    )
    rest, *got = lax.optimization_barrier((rest, *got[::-1]))
    got = got[::-1]
    west, east = before_and_after(got, "lon")
    return pl.pallas_call(
        functools.partial(side_kernel, plan, lat_cells),
        out_shape=jax.ShapeDtypeStruct(background.shape, BF16),
        in_specs=[smem] + [vmem] * (7 + len(weights)),
        out_specs=anywhere,
        scratch_shapes=[
            pltpu.VMEM((2, lat_cells, HLON, LEV, width), BF16),
            pltpu.SemaphoreType.DMA((3,)),
        ],
        compiler_params=params,
        cost_estimate=pl.CostEstimate(
            flops=3 * 10**9, bytes_accessed=4 * 10**6, transcendentals=10**6
        ),
    )(scalars, rest, latent, normed, west, east, gain_one, *weights, middle)


def solution(mesh):
    placed = (
        P("lon", "lat", None, None),
        P("lon", "lat", None),
        P("lon", "lat", None),
        P("lon", "lat"),
        P("lat", "lon", None, None),
        P(),
        P(),
        P(),
        P(),
        P(),
        P(),
        P(),
        P(),
        P(),
    )
    return jax.shard_map(
        local, mesh=mesh, in_specs=placed, out_specs=P("lat", "lon", None, None), check_vma=False
    )
```

```python
import functools

import jax
import jax.numpy as jnp
from jax import lax
from jax.experimental import pallas as pl
from jax.experimental.pallas import tpu as pltpu
from jax.sharding import PartitionSpec as P

HEADS = 6
INSTR = 8
LEV = 2
WLAT = 6
WLON = 12
HLAT = WLAT // 2
HLON = WLON // 2
LANES = 128
PAD = 256
CHUNK = 32
LIMIT = 40 * 2**20
BF16 = jnp.bfloat16
F32 = jnp.float32

AROUND = [(dy, dx) for dy in (-1, 0, 1) for dx in (-1, 0, 1)]
ROWS = INSTR * len(AROUND)
COLS = ROWS + len(AROUND)


def swapped(up, down, axis, wraps):
    count = lax.axis_size(axis)
    even = lax.axis_index(axis) % 2 == 0
    got = []
    for first, mine in ((0, jnp.where(even, down, up)), (1, jnp.where(even, up, down))):
        pairs = []
        for low in range(first, count, 2):
            high = (low + 1) % count
            if high > low or wraps:
                pairs += [(low, high), (high, low)]
        got.append(lax.ppermute(mine, axis, pairs))
    return got


def before_and_after(got, axis):
    even = lax.axis_index(axis) % 2 == 0
    return jnp.where(even, got[1], got[0]), jnp.where(even, got[0], got[1])


def rectangles(lat_cells, lon_cells):
    lat = {-1: [(lat_cells - HLAT, HLAT)], 1: [(0, HLAT)]}
    lat[0] = [(0, HLAT), (HLAT, lat_cells - WLAT), (lat_cells - HLAT, HLAT)]
    lon = {-1: [(lon_cells - HLON, HLON)], 1: [(0, HLON)]}
    lon[0] = [(0, HLON), (HLON, lon_cells - WLON), (lon_cells - HLON, HLON)]
    return [
        [(top, high, left, wide) for top, high in lat[dy] for left, wide in lon[dx]]
        for dy, dx in AROUND
    ]


def tokens_of(part):
    return part[1] * part[3] * LEV


def padded(count):
    return -(-count // 8) * 8


def gelu(x):
    half = 0.5 * x
    inner = x * (0.7978845608028654 + 0.035677408136300125 * (x * x))
    return half + half * jnp.tanh(inner)


def normalise(wide, gain):
    average = jnp.mean(wide, axis=-1, keepdims=True)
    centred = wide - average
    spread = jnp.mean(centred * centred, axis=-1, keepdims=True)
    return centred * lax.rsqrt(spread + 1e-05) * gain


def dot(a, b):
    return jnp.dot(a, b, preferred_element_type=F32)


def dot_nt(a, b):
    return lax.dot_general(a, b, (((1,), (1,)), ((), ())), preferred_element_type=F32)


def about_one_over(x):
    return pl.reciprocal(x, approx=True)


def with_ones(tensor):
    ones = jnp.ones((tensor.shape[0], PAD - tensor.shape[1]), F32)
    return jnp.concatenate([tensor, ones], axis=1).astype(BF16)


def below(*pieces):
    return jnp.concatenate(pieces, axis=0) if len(pieces) > 1 else pieces[0]


def pack_kernel(
    values_ref,
    cell_ref,
    tag_ref,
    count_ref,
    back_ref,
    *refs,
):
    out_ref, up_ref, down_ref, values, cells, tags, held, sem = refs
    tiles_lon, tiles_lat, capacity, _ = values_ref.shape
    lat_cells, lon_cells = back_ref.shape[:2]
    strips = [
        (back_ref.at[:HLAT], up_ref),
        (back_ref.at[lat_cells - HLAT :], down_ref),
    ]
    copies = [
        pltpu.make_async_copy(cell_ref, cells, sem.at[0]),
        pltpu.make_async_copy(tag_ref, tags, sem.at[1]),
        pltpu.make_async_copy(count_ref, held, sem.at[2]),
        pltpu.make_async_copy(values_ref, values, sem.at[3]),
    ]
    copies += [
        pltpu.make_async_copy(source, strip, sem.at[4 + n])
        for n, (source, strip) in enumerate(strips)
    ]
    for copy in copies:
        copy.start()
    for copy in copies[:3]:
        copy.wait()
    counts = below(*[held[tile : tile + 1, :] for tile in range(tiles_lat) for _ in range(capacity)])
    cell = cells[...]
    slot = lax.broadcasted_iota(jnp.int32, cell.shape, 0) % capacity
    row = cell // lon_cells
    fields = [jnp.where(slot < counts, row, 255), cell - row * lon_cells, tags[...]]
    rows, columns, kinds = (field.astype(F32) for field in fields)
    lane = lax.broadcasted_iota(jnp.int32, (cell.shape[0], LANES), 1)
    kind_of = (lane % INSTR).astype(F32)
    marks = [
        ((lane < ROWS) & (lane // INSTR == n)) | (lane == ROWS + n) | (lane == COLS + n)
        for n in range(len(AROUND))
    ]
    turned = []
    for lon in range(tiles_lon):
        meta = jnp.where(kind_of == kinds[:, lon : lon + 1], 1.0, 0.0)
        meta = jnp.where(lane >= ROWS, rows[:, lon : lon + 1], meta)
        meta = jnp.where(lane >= COLS, columns[:, lon : lon + 1], meta)
        turns = {0: meta}
        for dy in (-1, 1):
            by = dy * capacity % meta.shape[0]
            turns[dy] = below(meta[by:], meta[:by])
        turned.append(turns)
    for lon in range(tiles_lon):
        meta = jnp.zeros(lane.shape, F32)
        for mark, (dy, dx) in zip(marks, AROUND):
            meta = jnp.where(mark, turned[(lon + dx) % tiles_lon][dy], meta)
        out_ref[lon, :, len(AROUND)] = meta.astype(BF16).reshape(tiles_lat, capacity, LANES)
    copies[3].wait()
    for n, (dy, dx) in enumerate(AROUND):
        spans = {0: [(0, tiles_lat)], 1: [(0, tiles_lat - 1), (tiles_lat - 1, tiles_lat)]}
        spans[-1] = [(0, 1), (1, tiles_lat)]

        def copy_tiles(lon, n=n, dx=dx, dy=dy, spans=spans[dy]):
            source = lax.rem(lon + dx + tiles_lon, tiles_lon)
            for low, end in spans:
                first = (low + dy) % tiles_lat
                out_ref[lon, low:end, n] = values[source, first : first + end - low]

        if tiles_lon <= 8:
            for lon in range(tiles_lon):
                copy_tiles(lon)
        else:
            pl.loop(0, tiles_lon)(copy_tiles)
    for copy in copies[4:]:
        copy.wait()


def packed(record_values, record_cell, record_instrument, block_counts, background):
    tiles_lon, tiles_lat, capacity, wide = record_values.shape
    anywhere = pl.BlockSpec(memory_space=pltpu.HBM)
    ints = pltpu.VMEM((tiles_lat * capacity, tiles_lon), jnp.int32)
    shape = (tiles_lon, tiles_lat, len(AROUND) + 1, capacity, wide)
    lat_cells, lon_cells, levels, width = background.shape
    across = jax.ShapeDtypeStruct((HLAT, lon_cells, levels, width), BF16)
    out, *strips = pl.pallas_call(
        pack_kernel,
        out_shape=[jax.ShapeDtypeStruct(shape, BF16), across, across],
        in_specs=[anywhere] * 5,
        out_specs=[pl.BlockSpec(memory_space=pltpu.VMEM), anywhere, anywhere],
        scratch_shapes=[
            pltpu.VMEM(record_values.shape, BF16),
            ints,
            ints,
            pltpu.VMEM((tiles_lat, tiles_lon), jnp.int32),
            pltpu.SemaphoreType.DMA((6,)),
        ],
        compiler_params=pltpu.CompilerParams(vmem_limit_bytes=56 * 2**20),
        cost_estimate=pl.CostEstimate(
            flops=20 * 10**9, bytes_accessed=10**6, transcendentals=0
        ),
    )(
        record_values,
        record_cell.transpose(1, 2, 0).reshape(-1, tiles_lon),
        record_instrument.transpose(1, 2, 0).reshape(-1, tiles_lon),
        block_counts.T,
        background,
    )
    return out.reshape((-1,) + shape[2:]), *strips


def token_codes(part, lon_cells):
    top, high, left, wide = part
    count = tokens_of(part)
    place = lax.broadcasted_iota(jnp.int32, (padded(count), LANES), 0)
    code = place + (top * lon_cells + left) * LEV
    for row in range(1, high):
        step = (lon_cells - wide) * LEV
        code = code + jnp.where(place >= row * wide * LEV, step, 0)
    return jnp.where(place < count, code, -8).astype(F32)


def near_entries(windows):
    own = [(4, 3 * i + j) for i, j in windows]
    return own + [(3 * i + 1, j) for i, j in windows if i != 1]


def far_entries(windows):
    beside = [(3 + j, i) for i, j in windows if j != 1]
    return beside + [(3 * i + j, 0) for i, j in windows if i != 1 and j != 1]


def scattered(recv_ref, first_ref, table_ref, lift_ref, plan, lon_cells):
    sources, _, capacity, _ = recv_ref.shape
    width = first_ref.shape[1]
    chunk = min(CHUNK, sources)
    slots = chunk * capacity
    table = below(*[table_ref[...].astype(F32)] * (LANES // INSTR)).astype(BF16)
    first, lift = below(first_ref[...], table), lift_ref[...]
    lane = lax.broadcasted_iota(jnp.int32, (16, LANES), 1)
    sub = lax.broadcasted_iota(jnp.int32, (16, LANES), 0)
    weigh = jnp.where(lane == ROWS + sub, float(lon_cells * LEV), 0.0)
    weigh = jnp.where(lane == COLS + sub, float(LEV), weigh).astype(BF16)
    codes = [below(*[token_codes(part, lon_cells) for part in parts]) for parts in plan]

    def scatter(begin):
        meta = recv_ref[pl.ds(begin, chunk), len(AROUND)].reshape(slots, LANES)
        records = below(
            *[
                recv_ref[pl.ds(begin, chunk), n].reshape(slots, LANES)
                for n in range(len(AROUND))
            ]
        )
        lane = lax.broadcasted_iota(jnp.int32, meta.shape, 1) // INSTR
        wide = meta.astype(F32)
        chosen = below(*[jnp.where(lane == n, wide, 0.0) for n in range(len(AROUND))]).astype(BF16)
        both = jnp.concatenate([records, chosen], axis=1)
        encoded = gelu(dot(both, first)).astype(BF16)
        lifted = gelu(dot(encoded, lift))
        tokens = dot_nt(weigh, meta)
        hots, parts = [], []
        for n in range(len(AROUND)):
            token = tokens[n : n + 1]
            token = jnp.concatenate([token + float(level) for level in range(LEV)], axis=1)
            if token.shape[1] == LANES:
                hot = codes[n] == token
            else:
                hot = codes[n][:, :1] == token
            hots.append(jnp.where(hot, 1.0, 0.0).astype(BF16))
        for n in range(len(AROUND)):
            part = lifted[n * slots : (n + 1) * slots]
            parts.append(
                with_ones(
                    below(*[part[:, level * width : (level + 1) * width] for level in range(LEV)])
                )
            )
        sums = [dot(hot, part) for hot, part in zip(hots, parts)]
        return tuple(sums)

    sums = scatter(0)
    if sources > chunk:
        sums = lax.fori_loop(
            1,
            sources // chunk,
            lambda step, total: tuple(a + b for a, b in zip(total, scatter(step * chunk))),
            sums,
        )
    return sums


def prepare_kernel(
    plan, back_ref, attn_ref, one_ref, two_ref, rows_ref, parts_ref, gain_one_ref, gain_two_ref
):
    width = back_ref.shape[3]
    pieces = []
    for top, high, left, wide in plan[4]:
        count = high * wide * LEV
        piece = back_ref[top : top + high, left : left + wide].reshape(count, width).astype(F32)
        if padded(count) > count:
            piece = below(piece, jnp.zeros((padded(count) - count, width), F32))
        pieces.append(piece)
    rows_ref[...] = below(*pieces)
    for gain, ref in ((one_ref, gain_one_ref), (two_ref, gain_two_ref)):
        ref[...] = jnp.broadcast_to(gain[...].astype(F32).reshape(1, width), ref.shape)
    for n in range(3):
        parts_ref[n] = attn_ref[:, n * width : (n + 1) * width]


def prepared(plan, background, attn_weight, first_gain, second_gain):
    width = background.shape[3]
    rows = sum(padded(tokens_of(part)) for part in plan[4])
    vmem = pl.BlockSpec(memory_space=pltpu.VMEM)
    return pl.pallas_call(
        functools.partial(prepare_kernel, plan),
        out_shape=[
            jax.ShapeDtypeStruct((rows, width), F32),
            jax.ShapeDtypeStruct((3, width, width), BF16),
            jax.ShapeDtypeStruct((8, width), F32),
            jax.ShapeDtypeStruct((8, width), F32),
        ],
        in_specs=[vmem] * 4,
        out_specs=[vmem] * 4,
        compiler_params=pltpu.CompilerParams(vmem_limit_bytes=LIMIT),
        cost_estimate=pl.CostEstimate(flops=10**9, bytes_accessed=10**6, transcendentals=0),
    )(background, attn_weight, first_gain, second_gain)


def normed_of(plan, entries, sums, borders, gain):
    rows_ref, north_ref, south_ref, west_ref, east_ref, lat_cells = borders
    width = gain.shape[1]
    pieces, spans, start = [], {}, 0
    for tile, number in entries:
        dy, dx = AROUND[tile]
        top, high, left, wide = plan[tile][number]
        count = high * wide * LEV
        full = padded(count)
        if tile == 4:
            begin = sum(padded(tokens_of(part)) for part in plan[4][:number])
            piece = rows_ref[begin : begin + full, :]
        else:
            if dx:
                ref = west_ref if dx < 0 else east_ref
                top, left = {-1: 0, 0: top + HLAT, 1: lat_cells + HLAT}[dy], 0
            else:
                ref, top = (north_ref, 0) if dy < 0 else (south_ref, 0)
            piece = ref[top : top + high, left : left + wide].reshape(count, width).astype(F32)
            if full > count:
                piece = below(piece, jnp.zeros((full - count, width), F32))
        pieces.append(piece)
        spans[tile, number] = (start, count)
        start += full
    tally = 1.0 + sums[:, width : width + 1]
    share = about_one_over(tally)
    share = share * (2.0 - tally * share)
    latent = ((below(*pieces) + sums[:, :width]) * share).astype(BF16).astype(F32)
    return latent, normalise(latent, gain), spans


def worked(plan, places, piece_of, own_normed, latent, weights, scalars_ref, put):
    parts_ref, mix_ref, gain_ref, up_ref, down_ref = weights
    width = mix_ref.shape[0]
    groups = [padded(tokens_of(plan[4][3 * i + j])) for i, j in places]
    windows = []
    for i, j in places:
        window = [piece_of(4, 3 * i + j)]
        if i != 1:
            window.append(piece_of(3 * i + 1, j))
        if j != 1:
            window.append(piece_of(3 + j, i))
        if i != 1 and j != 1:
            window.append(piece_of(3 * i + j, 0))
        windows.append(window)
    tokens = below(*[piece for window in windows for piece in window]).astype(BF16)
    head = width // HEADS
    query = dot(own_normed.astype(BF16), parts_ref[0]) * head ** (-0.5)
    query = jnp.concatenate([query, jnp.ones((query.shape[0], PAD - width), F32)], axis=1)
    keys = dot(tokens, parts_ref[1])
    values = with_ones(dot(tokens, parts_ref[2]))

    lane = lax.broadcasted_iota(jnp.int32, (1, PAD), 1)
    many = WLAT * WLON * LEV
    corner = HLAT * HLON * LEV
    key = lax.broadcasted_iota(jnp.int32, (many, PAD - width), 0)
    spare = lax.broadcasted_iota(jnp.int32, (many, PAD - width), 1)
    unused = lax.broadcasted_iota(jnp.int32, (PAD - many, PAD), 1)
    unused = jnp.where(unused == width, -3e38, 0.0).astype(BF16)
    nothing = jnp.zeros((PAD - many, PAD), BF16)

    def keys_of(w, i, j):
        bias = jnp.zeros((many, PAD - width), F32)
        if i != 1:
            if j == 1:
                inside = key < 2 * corner
            else:
                inside = (key < corner) | ((key >= 2 * corner) & (key < 3 * corner))
            bias = jnp.where(inside | (spare > 0), 0.0, -3e38) * scalars_ref[i].astype(F32)
        here = jnp.concatenate([keys[w * many : (w + 1) * many], bias], axis=1)
        return below(here.astype(BF16), unused)

    begins = [sum(groups[:w]) for w in range(len(groups))]
    parts = [query[begin : begin + rows] for begin, rows in zip(begins, groups)]
    stacks = [
        below(
            *[jnp.where((lane // head == h) | (lane >= width), part, 0.0) for h in range(HEADS)]
        ).astype(BF16)
        for part in parts
    ]
    held = [keys_of(w, i, j) for w, (i, j) in enumerate(places)]
    scores = [dot_nt(stack, here) for stack, here in zip(stacks, held)]
    largest = [jnp.max(score, axis=-1, keepdims=True) for score in scores]
    raised = [jnp.exp((score - most).astype(BF16)) for score, most in zip(scores, largest)]
    held = [below(values[w * many : (w + 1) * many], nothing) for w in range(len(places))]
    products = [dot(one, here) for one, here in zip(raised, held)]
    shares = [about_one_over(product[:, width : width + 1]) for product in products]
    products = [product[:, :width] * share for product, share in zip(products, shares)]
    mixed = []
    for product, rows in zip(products, groups):
        total = product[:rows]
        for h in range(1, HEADS):
            own = lane[:, :width] // head == h
            total = jnp.where(own, product[h * rows : (h + 1) * rows], total)
        mixed.append(total)
    mixed = below(*mixed).astype(BF16)

    after = (latent + dot(mixed, mix_ref[...])).astype(BF16).astype(F32)
    normed_two = normalise(after, gain_ref[:1, :]).astype(BF16)
    cuts = range(0, up_ref.shape[1], PAD)
    hidden = [dot(normed_two, up_ref[:, at : at + PAD]).astype(BF16) for at in cuts]
    result = after
    for at, chunk in zip(cuts, hidden):
        result = result + dot(gelu(chunk), down_ref[at : at + PAD, :])
    for begin, (i, j) in zip(begins, places):
        part = plan[4][3 * i + j]
        piece = result[begin : begin + tokens_of(part)].astype(BF16)
        put(part, j, piece.reshape(part[1], part[3], LEV, width))


MIDDLE = [(0, 1), (1, 1), (2, 1)]
SIDES = [(0, 0), (0, 2), (2, 0), (2, 2), (1, 0), (1, 2)]


def own_rows(plan, places):
    return sum(padded(tokens_of(plan[4][3 * i + j])) for i, j in places)


def middle_kernel(
    plan,
    lat_cells,
    lon_cells,
    scalars_ref,
    recv_ref,
    north_ref,
    south_ref,
    rows_ref,
    first_ref,
    table_ref,
    lift_ref,
    gain_one_ref,
    *refs,
):
    *weights, out_ref, rest_ref, latent_ref, normed_ref = refs
    sums = scattered(recv_ref, first_ref, table_ref, lift_ref, plan, lon_cells)

    def sums_of(entries):
        pieces = []
        for tile, number in entries:
            start = sum(padded(tokens_of(part)) for part in plan[tile][:number])
            pieces.append(sums[tile][start : start + padded(tokens_of(plan[tile][number]))])
        return below(*pieces)

    borders = (rows_ref, north_ref, south_ref, None, None, lat_cells)
    gain = gain_one_ref[:1, :]
    entries = near_entries(MIDDLE)
    latent, normed, spans = normed_of(plan, entries, sums_of(entries), borders, gain)

    def piece_of(tile, number):
        start, count = spans[tile, number]
        return normed[start : start + count]

    def put(part, _, piece):
        out_ref[part[0] : part[0] + part[1]] = piece

    end = own_rows(plan, MIDDLE)
    worked(plan, MIDDLE, piece_of, normed[:end], latent[:end], weights, scalars_ref, put)
    rest_ref[...] = sums_of(far_entries(SIDES))
    entries = near_entries(SIDES)
    latent, normed, _ = normed_of(plan, entries, sums_of(entries), borders, gain)
    latent_ref[...] = latent[: latent_ref.shape[0]]
    normed_ref[...] = normed


def side_kernel(
    plan,
    lat_cells,
    scalars_ref,
    rest_ref,
    latent_ref,
    normed_ref,
    west_ref,
    east_ref,
    gain_one_ref,
    *refs,
):
    *weights, middle_ref, out_ref, held_ref, sem = refs
    left, wide = plan[4][4][2:]
    copies = [pltpu.make_async_copy(middle_ref, out_ref.at[:, left : left + wide], sem.at[2])]
    copies[0].start()
    near, start = {}, 0
    for tile, number in near_entries(SIDES):
        near[tile, number] = start
        start += padded(tokens_of(plan[tile][number]))
    borders = (None, None, None, west_ref, east_ref, lat_cells)
    gain = gain_one_ref[:1, :]
    _, far, spans = normed_of(plan, far_entries(SIDES), rest_ref[...], borders, gain)

    def piece_of(tile, number):
        if (tile, number) in spans:
            start, count = spans[tile, number]
            return far[start : start + count]
        start = near[tile, number]
        return normed_ref[start : start + tokens_of(plan[tile][number]), :]

    def put(part, j, piece):
        held_ref[j // 2, part[0] : part[0] + part[1]] = piece

    end = own_rows(plan, SIDES)
    worked(
        plan, SIDES, piece_of, normed_ref[:end, :], latent_ref[...], weights, scalars_ref, put
    )
    for n, number in enumerate((0, 2)):
        left, wide = plan[4][number][2:]
        copies.append(
            pltpu.make_async_copy(held_ref.at[n], out_ref.at[:, left : left + wide], sem.at[n])
        )
        copies[-1].start()
    for copy in copies:
        copy.wait()


def local(
    record_values,
    record_cell,
    record_instrument,
    block_counts,
    background,
    input_weight,
    instrument_table,
    lift_weight,
    first_gain,
    attn_weight,
    mix_weight,
    second_gain,
    up_weight,
    down_weight,
):
    lat_cells, lon_cells, _, width = background.shape
    tiles_lat = record_values.shape[1]

    sent, up, down = packed(
        record_values, record_cell, record_instrument, block_counts, background
    )
    received = lax.all_to_all(sent, ("lon", "lat"), split_axis=0, concat_axis=0, tiled=True)
    north, south = before_and_after(swapped(up, down, "lat", wraps=False), "lat")

    later, input_weight, attn_weight, down_weight, first_gain, second_gain, _ = (
        lax.optimization_barrier(
            (background, input_weight, attn_weight, down_weight, first_gain, second_gain, up)
        )
    )

    def columns(low, end):
        return jnp.concatenate([north[:, low:end], later[:, low:end], south[:, low:end]], axis=0)

    got = swapped(columns(0, HLON), columns(lon_cells - HLON, lon_cells), "lon", wraps=True)

    plan = rectangles(lat_cells, lon_cells)
    rows, parts, gain_one, gain_two = prepared(
        plan, later, attn_weight, first_gain, second_gain
    )
    lat = lax.axis_index("lat")
    scalars = jnp.stack([lat == 0, lat < 0, lat == tiles_lat - 1]).astype(jnp.int32)

    def rows_in(entries):
        return sum(padded(tokens_of(plan[tile][number])) for tile, number in entries)

    weights = [parts, mix_weight, gain_two, up_weight, down_weight]
    smem = pl.BlockSpec(memory_space=pltpu.SMEM)
    vmem = pl.BlockSpec(memory_space=pltpu.VMEM)
    anywhere = pl.BlockSpec(memory_space=pl.ANY)
    params = pltpu.CompilerParams(vmem_limit_bytes=LIMIT)
    middle, rest, latent, normed = pl.pallas_call(
        functools.partial(middle_kernel, plan, lat_cells, lon_cells),
        out_shape=[
            jax.ShapeDtypeStruct((lat_cells, lon_cells - WLON, LEV, width), BF16),
            jax.ShapeDtypeStruct((rows_in(far_entries(SIDES)), PAD), F32),
            jax.ShapeDtypeStruct((own_rows(plan, SIDES), width), F32),
            jax.ShapeDtypeStruct((rows_in(near_entries(SIDES)), width), F32),
        ],
        in_specs=[smem] + [vmem] * (8 + len(weights)),
        out_specs=[vmem] * 4,
        compiler_params=params,
        cost_estimate=pl.CostEstimate(
            flops=4 * 10**9, bytes_accessed=4 * 10**6, transcendentals=10**6
        ),
    )(
        scalars,
        received,
        north,
        south,
        rows,
        input_weight,
        instrument_table,
        lift_weight,
        gain_one,
        *weights,
    )
    rest, *got = lax.optimization_barrier((rest, *got[::-1]))
    got = got[::-1]
    west, east = before_and_after(got, "lon")
    return pl.pallas_call(
        functools.partial(side_kernel, plan, lat_cells),
        out_shape=jax.ShapeDtypeStruct(background.shape, BF16),
        in_specs=[smem] + [vmem] * (7 + len(weights)),
        out_specs=anywhere,
        scratch_shapes=[
            pltpu.VMEM((2, lat_cells, HLON, LEV, width), BF16),
            pltpu.SemaphoreType.DMA((3,)),
        ],
        compiler_params=params,
        cost_estimate=pl.CostEstimate(
            flops=3 * 10**9, bytes_accessed=4 * 10**6, transcendentals=10**6
        ),
    )(scalars, rest, latent, normed, west, east, gain_one, *weights, middle)


def solution(mesh):
    placed = (
        P("lon", "lat", None, None),
        P("lon", "lat", None),
        P("lon", "lat", None),
        P("lon", "lat"),
        P("lat", "lon", None, None),
        P(),
        P(),
        P(),
        P(),
        P(),
        P(),
        P(),
        P(),
        P(),
    )
    return jax.shard_map(
        local, mesh=mesh, in_specs=placed, out_specs=P("lat", "lon", None, None), check_vma=False
    )
```

```python
import functools

import jax
import jax.numpy as jnp
from jax import lax
from jax.experimental import pallas as pl
from jax.experimental.pallas import tpu as pltpu
from jax.sharding import PartitionSpec as P

HEADS = 6
INSTR = 8
LEV = 2
WLAT = 6
WLON = 12
HLAT = WLAT // 2
HLON = WLON // 2
LANES = 128
PAD = 256
CHUNK = 32
LIMIT = 40 * 2**20
BF16 = jnp.bfloat16
F32 = jnp.float32

AROUND = [(dy, dx) for dy in (-1, 0, 1) for dx in (-1, 0, 1)]
ROWS = INSTR * len(AROUND)
COLS = ROWS + len(AROUND)


def swapped(up, down, axis, wraps):
    count = lax.axis_size(axis)
    even = lax.axis_index(axis) % 2 == 0
    got = []
    for first, mine in ((0, jnp.where(even, down, up)), (1, jnp.where(even, up, down))):
        pairs = []
        for low in range(first, count, 2):
            high = (low + 1) % count
            if high > low or wraps:
                pairs += [(low, high), (high, low)]
        got.append(lax.ppermute(mine, axis, pairs))
    return got


def before_and_after(got, axis):
    even = lax.axis_index(axis) % 2 == 0
    return jnp.where(even, got[1], got[0]), jnp.where(even, got[0], got[1])


def rectangles(lat_cells, lon_cells):
    lat = {-1: [(lat_cells - HLAT, HLAT)], 1: [(0, HLAT)]}
    lat[0] = [(0, HLAT), (HLAT, lat_cells - WLAT), (lat_cells - HLAT, HLAT)]
    lon = {-1: [(lon_cells - HLON, HLON)], 1: [(0, HLON)]}
    lon[0] = [(0, HLON), (HLON, lon_cells - WLON), (lon_cells - HLON, HLON)]
    return [
        [(top, high, left, wide) for top, high in lat[dy] for left, wide in lon[dx]]
        for dy, dx in AROUND
    ]


def tokens_of(part):
    return part[1] * part[3] * LEV


def padded(count):
    return -(-count // 8) * 8


def gelu(x):
    half = 0.5 * x
    inner = x * (0.7978845608028654 + 0.035677408136300125 * (x * x))
    return half + half * jnp.tanh(inner)


def normalise(wide, gain):
    average = jnp.mean(wide, axis=-1, keepdims=True)
    centred = wide - average
    spread = jnp.mean(centred * centred, axis=-1, keepdims=True)
    return centred * lax.rsqrt(spread + 1e-05) * gain


def dot(a, b):
    return jnp.dot(a, b, preferred_element_type=F32)


def dot_nt(a, b):
    return lax.dot_general(a, b, (((1,), (1,)), ((), ())), preferred_element_type=F32)


def about_one_over(x):
    return pl.reciprocal(x, approx=True)


def with_ones(tensor):
    ones = jnp.ones((tensor.shape[0], PAD - tensor.shape[1]), F32)
    return jnp.concatenate([tensor, ones], axis=1).astype(BF16)


def below(*pieces):
    return jnp.concatenate(pieces, axis=0) if len(pieces) > 1 else pieces[0]


def pack_kernel(
    values_ref,
    cell_ref,
    tag_ref,
    count_ref,
    back_ref,
    *refs,
):
    out_ref, up_ref, down_ref, values, cells, tags, held, sem = refs
    tiles_lon, tiles_lat, capacity, _ = values_ref.shape
    lat_cells, lon_cells = back_ref.shape[:2]
    strips = [
        (back_ref.at[:HLAT], up_ref),
        (back_ref.at[lat_cells - HLAT :], down_ref),
    ]
    copies = [
        pltpu.make_async_copy(cell_ref, cells, sem.at[0]),
        pltpu.make_async_copy(tag_ref, tags, sem.at[1]),
        pltpu.make_async_copy(count_ref, held, sem.at[2]),
        pltpu.make_async_copy(values_ref, values, sem.at[3]),
    ]
    copies += [
        pltpu.make_async_copy(source, strip, sem.at[4 + n])
        for n, (source, strip) in enumerate(strips)
    ]
    for copy in copies:
        copy.start()
    for copy in copies[:3]:
        copy.wait()
    counts = below(*[held[tile : tile + 1, :] for tile in range(tiles_lat) for _ in range(capacity)])
    cell = cells[...]
    slot = lax.broadcasted_iota(jnp.int32, cell.shape, 0) % capacity
    row = cell // lon_cells
    fields = [jnp.where(slot < counts, row, 255), cell - row * lon_cells, tags[...]]
    rows, columns, kinds = (field.astype(F32) for field in fields)
    lane = lax.broadcasted_iota(jnp.int32, (cell.shape[0], LANES), 1)
    kind_of = (lane % INSTR).astype(F32)
    marks = [
        ((lane < ROWS) & (lane // INSTR == n)) | (lane == ROWS + n) | (lane == COLS + n)
        for n in range(len(AROUND))
    ]
    turned = []
    for lon in range(tiles_lon):
        meta = jnp.where(kind_of == kinds[:, lon : lon + 1], 1.0, 0.0)
        meta = jnp.where(lane >= ROWS, rows[:, lon : lon + 1], meta)
        meta = jnp.where(lane >= COLS, columns[:, lon : lon + 1], meta)
        turns = {0: meta}
        for dy in (-1, 1):
            by = dy * capacity % meta.shape[0]
            turns[dy] = below(meta[by:], meta[:by])
        turned.append(turns)
    for lon in range(tiles_lon):
        meta = jnp.zeros(lane.shape, F32)
        for mark, (dy, dx) in zip(marks, AROUND):
            meta = jnp.where(mark, turned[(lon + dx) % tiles_lon][dy], meta)
        out_ref[lon, :, len(AROUND)] = meta.astype(BF16).reshape(tiles_lat, capacity, LANES)
    copies[3].wait()
    for n, (dy, dx) in enumerate(AROUND):
        spans = {0: [(0, tiles_lat)], 1: [(0, tiles_lat - 1), (tiles_lat - 1, tiles_lat)]}
        spans[-1] = [(0, 1), (1, tiles_lat)]

        def copy_tiles(lon, n=n, dx=dx, dy=dy, spans=spans[dy]):
            source = lax.rem(lon + dx + tiles_lon, tiles_lon)
            for low, end in spans:
                first = (low + dy) % tiles_lat
                out_ref[lon, low:end, n] = values[source, first : first + end - low]

        if tiles_lon <= 8:
            for lon in range(tiles_lon):
                copy_tiles(lon)
        else:
            pl.loop(0, tiles_lon)(copy_tiles)
    for copy in copies[4:]:
        copy.wait()


def packed(record_values, record_cell, record_instrument, block_counts, background):
    tiles_lon, tiles_lat, capacity, wide = record_values.shape
    anywhere = pl.BlockSpec(memory_space=pltpu.HBM)
    ints = pltpu.VMEM((tiles_lat * capacity, tiles_lon), jnp.int32)
    shape = (tiles_lon, tiles_lat, len(AROUND) + 1, capacity, wide)
    lat_cells, lon_cells, levels, width = background.shape
    across = jax.ShapeDtypeStruct((HLAT, lon_cells, levels, width), BF16)
    out, *strips = pl.pallas_call(
        pack_kernel,
        out_shape=[jax.ShapeDtypeStruct(shape, BF16), across, across],
        in_specs=[anywhere] * 5,
        out_specs=[pl.BlockSpec(memory_space=pltpu.VMEM)] * 3,
        scratch_shapes=[
            pltpu.VMEM(record_values.shape, BF16),
            ints,
            ints,
            pltpu.VMEM((tiles_lat, tiles_lon), jnp.int32),
            pltpu.SemaphoreType.DMA((6,)),
        ],
        compiler_params=pltpu.CompilerParams(vmem_limit_bytes=56 * 2**20),
        cost_estimate=pl.CostEstimate(
            flops=20 * 10**9, bytes_accessed=10**6, transcendentals=0
        ),
    )(
        record_values,
        record_cell.transpose(1, 2, 0).reshape(-1, tiles_lon),
        record_instrument.transpose(1, 2, 0).reshape(-1, tiles_lon),
        block_counts.T,
        background,
    )
    return out.reshape((-1,) + shape[2:]), *strips


def token_codes(part, lon_cells):
    top, high, left, wide = part
    count = tokens_of(part)
    place = lax.broadcasted_iota(jnp.int32, (padded(count), LANES), 0)
    code = place + (top * lon_cells + left) * LEV
    for row in range(1, high):
        step = (lon_cells - wide) * LEV
        code = code + jnp.where(place >= row * wide * LEV, step, 0)
    return jnp.where(place < count, code, -8).astype(F32)


def near_entries(windows):
    own = [(4, 3 * i + j) for i, j in windows]
    return own + [(3 * i + 1, j) for i, j in windows if i != 1]


def far_entries(windows):
    beside = [(3 + j, i) for i, j in windows if j != 1]
    return beside + [(3 * i + j, 0) for i, j in windows if i != 1 and j != 1]


def scattered(recv_ref, first_ref, table_ref, lift_ref, plan, lon_cells):
    sources, _, capacity, _ = recv_ref.shape
    width = first_ref.shape[1]
    chunk = min(CHUNK, sources)
    slots = chunk * capacity
    table = below(*[table_ref[...].astype(F32)] * (LANES // INSTR)).astype(BF16)
    first, lift = below(first_ref[...], table), lift_ref[...]
    lane = lax.broadcasted_iota(jnp.int32, (16, LANES), 1)
    sub = lax.broadcasted_iota(jnp.int32, (16, LANES), 0)
    weigh = jnp.where(lane == ROWS + sub, float(lon_cells * LEV), 0.0)
    weigh = jnp.where(lane == COLS + sub, float(LEV), weigh).astype(BF16)
    codes = [below(*[token_codes(part, lon_cells) for part in parts]) for parts in plan]

    def scatter(begin):
        meta = recv_ref[pl.ds(begin, chunk), len(AROUND)].reshape(slots, LANES)
        records = below(
            *[
                recv_ref[pl.ds(begin, chunk), n].reshape(slots, LANES)
                for n in range(len(AROUND))
            ]
        )
        lane = lax.broadcasted_iota(jnp.int32, meta.shape, 1) // INSTR
        wide = meta.astype(F32)
        chosen = below(*[jnp.where(lane == n, wide, 0.0) for n in range(len(AROUND))]).astype(BF16)
        both = jnp.concatenate([records, chosen], axis=1)
        encoded = gelu(dot(both, first)).astype(BF16)
        lifted = gelu(dot(encoded, lift))
        tokens = dot_nt(weigh, meta)
        hots, parts = [], []
        for n in range(len(AROUND)):
            token = tokens[n : n + 1]
            token = jnp.concatenate([token + float(level) for level in range(LEV)], axis=1)
            if token.shape[1] == LANES:
                hot = codes[n] == token
            else:
                hot = codes[n][:, :1] == token
            hots.append(jnp.where(hot, 1.0, 0.0).astype(BF16))
        for n in range(len(AROUND)):
            part = lifted[n * slots : (n + 1) * slots]
            parts.append(
                with_ones(
                    below(*[part[:, level * width : (level + 1) * width] for level in range(LEV)])
                )
            )
        sums = [dot(hot, part) for hot, part in zip(hots, parts)]
        return tuple(sums)

    sums = scatter(0)
    if sources > chunk:
        sums = lax.fori_loop(
            1,
            sources // chunk,
            lambda step, total: tuple(a + b for a, b in zip(total, scatter(step * chunk))),
            sums,
        )
    return sums


def prepare_kernel(
    plan, back_ref, attn_ref, one_ref, two_ref, rows_ref, parts_ref, gain_one_ref, gain_two_ref
):
    width = back_ref.shape[3]
    pieces = []
    for top, high, left, wide in plan[4]:
        count = high * wide * LEV
        piece = back_ref[top : top + high, left : left + wide].reshape(count, width).astype(F32)
        if padded(count) > count:
            piece = below(piece, jnp.zeros((padded(count) - count, width), F32))
        pieces.append(piece)
    rows_ref[...] = below(*pieces).astype(BF16)
    for gain, ref in ((one_ref, gain_one_ref), (two_ref, gain_two_ref)):
        ref[...] = jnp.broadcast_to(gain[...].astype(F32).reshape(1, width), ref.shape)
    for n in range(3):
        parts_ref[n] = attn_ref[:, n * width : (n + 1) * width]


def prepared(plan, background, attn_weight, first_gain, second_gain):
    width = background.shape[3]
    rows = sum(padded(tokens_of(part)) for part in plan[4])
    vmem = pl.BlockSpec(memory_space=pltpu.VMEM)
    return pl.pallas_call(
        functools.partial(prepare_kernel, plan),
        out_shape=[
            jax.ShapeDtypeStruct((rows, width), BF16),
            jax.ShapeDtypeStruct((3, width, width), BF16),
            jax.ShapeDtypeStruct((8, width), F32),
            jax.ShapeDtypeStruct((8, width), F32),
        ],
        in_specs=[vmem] * 4,
        out_specs=[vmem] * 4,
        compiler_params=pltpu.CompilerParams(vmem_limit_bytes=LIMIT),
        cost_estimate=pl.CostEstimate(flops=10**9, bytes_accessed=10**6, transcendentals=0),
    )(background, attn_weight, first_gain, second_gain)


def normed_of(plan, entries, sums, borders, gain):
    rows, north_ref, south_ref, west_ref, east_ref, lat_cells = borders
    width = gain.shape[1]
    pieces, spans, start = [], {}, 0
    for tile, number in entries:
        dy, dx = AROUND[tile]
        top, high, left, wide = plan[tile][number]
        count = high * wide * LEV
        full = padded(count)
        if tile == 4:
            begin = sum(padded(tokens_of(part)) for part in plan[4][:number])
            piece = rows[begin : begin + full]
        else:
            if dx:
                ref = west_ref if dx < 0 else east_ref
                top, left = {-1: 0, 0: top + HLAT, 1: lat_cells + HLAT}[dy], 0
            else:
                ref, top = (north_ref, 0) if dy < 0 else (south_ref, 0)
            piece = ref[top : top + high, left : left + wide].reshape(count, width).astype(F32)
            if full > count:
                piece = below(piece, jnp.zeros((full - count, width), F32))
        pieces.append(piece)
        spans[tile, number] = (start, count)
        start += full
    tally = 1.0 + sums[:, width : width + 1]
    share = about_one_over(tally)
    share = share * (2.0 - tally * share)
    latent = ((below(*pieces) + sums[:, :width]) * share).astype(BF16).astype(F32)
    return latent, normalise(latent, gain), spans


def worked(plan, places, piece_of, own_normed, latent, weights, scalars_ref, put):
    parts_ref, mix_ref, gain_ref, up_ref, down_ref = weights
    width = mix_ref.shape[0]
    groups = [padded(tokens_of(plan[4][3 * i + j])) for i, j in places]
    windows = []
    for i, j in places:
        window = [piece_of(4, 3 * i + j)]
        if i != 1:
            window.append(piece_of(3 * i + 1, j))
        if j != 1:
            window.append(piece_of(3 + j, i))
        if i != 1 and j != 1:
            window.append(piece_of(3 * i + j, 0))
        windows.append(window)
    tokens = below(*[piece for window in windows for piece in window]).astype(BF16)
    head = width // HEADS
    query = dot(own_normed.astype(BF16), parts_ref[0]) * head ** (-0.5)
    query = jnp.concatenate([query, jnp.ones((query.shape[0], PAD - width), F32)], axis=1)
    keys = dot(tokens, parts_ref[1])
    values = with_ones(dot(tokens, parts_ref[2]))

    lane = lax.broadcasted_iota(jnp.int32, (1, PAD), 1)
    many = WLAT * WLON * LEV
    corner = HLAT * HLON * LEV
    key = lax.broadcasted_iota(jnp.int32, (many, PAD - width), 0)
    spare = lax.broadcasted_iota(jnp.int32, (many, PAD - width), 1)
    unused = lax.broadcasted_iota(jnp.int32, (PAD - many, PAD), 1)
    unused = jnp.where(unused == width, -3e38, 0.0).astype(BF16)
    nothing = jnp.zeros((PAD - many, PAD), BF16)

    def keys_of(w, i, j):
        bias = jnp.zeros((many, PAD - width), F32)
        if i != 1:
            if j == 1:
                inside = key < 2 * corner
            else:
                inside = (key < corner) | ((key >= 2 * corner) & (key < 3 * corner))
            bias = jnp.where(inside | (spare > 0), 0.0, -3e38) * scalars_ref[i].astype(F32)
        here = jnp.concatenate([keys[w * many : (w + 1) * many], bias], axis=1)
        return below(here.astype(BF16), unused)

    begins = [sum(groups[:w]) for w in range(len(groups))]
    parts = [query[begin : begin + rows] for begin, rows in zip(begins, groups)]
    stacks = [
        below(
            *[jnp.where((lane // head == h) | (lane >= width), part, 0.0) for h in range(HEADS)]
        ).astype(BF16)
        for part in parts
    ]
    held = [keys_of(w, i, j) for w, (i, j) in enumerate(places)]
    scores = [dot_nt(stack, here) for stack, here in zip(stacks, held)]
    largest = [jnp.max(score, axis=-1, keepdims=True) for score in scores]
    raised = [jnp.exp((score - most).astype(BF16)) for score, most in zip(scores, largest)]
    held = [below(values[w * many : (w + 1) * many], nothing) for w in range(len(places))]
    products = [dot(one, here) for one, here in zip(raised, held)]
    shares = [about_one_over(product[:, width : width + 1]) for product in products]
    products = [product[:, :width] * share for product, share in zip(products, shares)]
    mixed = []
    for product, rows in zip(products, groups):
        total = product[:rows]
        for h in range(1, HEADS):
            own = lane[:, :width] // head == h
            total = jnp.where(own, product[h * rows : (h + 1) * rows], total)
        mixed.append(total)
    mixed = below(*mixed).astype(BF16)

    after = (latent + dot(mixed, mix_ref[...])).astype(BF16).astype(F32)
    normed_two = normalise(after, gain_ref[:1, :]).astype(BF16)
    hidden = gelu(dot(normed_two, up_ref[...]).astype(BF16))
    result = after + dot(hidden, down_ref[...])
    for begin, (i, j) in zip(begins, places):
        part = plan[4][3 * i + j]
        piece = result[begin : begin + tokens_of(part)].astype(BF16)
        put(part, j, piece.reshape(part[1], part[3], LEV, width))


MIDDLE = [(0, 1), (1, 1), (2, 1)]
SIDES = [(0, 0), (0, 2), (2, 0), (2, 2), (1, 0), (1, 2)]


def own_rows(plan, places):
    return sum(padded(tokens_of(plan[4][3 * i + j])) for i, j in places)


def middle_kernel(
    plan,
    lat_cells,
    lon_cells,
    scalars_ref,
    recv_ref,
    north_ref,
    south_ref,
    rows_ref,
    first_ref,
    table_ref,
    lift_ref,
    gain_one_ref,
    *refs,
):
    *weights, out_ref, rest_ref, latent_ref, normed_ref = refs
    sums = scattered(recv_ref, first_ref, table_ref, lift_ref, plan, lon_cells)

    def sums_of(entries):
        pieces = []
        for tile, number in entries:
            start = sum(padded(tokens_of(part)) for part in plan[tile][:number])
            pieces.append(sums[tile][start : start + padded(tokens_of(plan[tile][number]))])
        return below(*pieces)

    borders = (rows_ref[...].astype(F32), north_ref, south_ref, None, None, lat_cells)
    gain = gain_one_ref[:1, :]
    entries = near_entries(MIDDLE)
    latent, normed, spans = normed_of(plan, entries, sums_of(entries), borders, gain)

    def piece_of(tile, number):
        start, count = spans[tile, number]
        return normed[start : start + count]

    def put(part, _, piece):
        out_ref[part[0] : part[0] + part[1]] = piece

    end = own_rows(plan, MIDDLE)
    worked(plan, MIDDLE, piece_of, normed[:end], latent[:end], weights, scalars_ref, put)
    rest_ref[...] = sums_of(far_entries(SIDES))
    entries = near_entries(SIDES)
    latent, normed, _ = normed_of(plan, entries, sums_of(entries), borders, gain)
    latent_ref[...] = latent[: latent_ref.shape[0]]
    normed_ref[...] = normed


def side_kernel(
    plan,
    lat_cells,
    scalars_ref,
    rest_ref,
    latent_ref,
    normed_ref,
    west_ref,
    east_ref,
    gain_one_ref,
    *refs,
):
    *weights, middle_ref, out_ref, held_ref, sem = refs
    left, wide = plan[4][4][2:]
    copies = [pltpu.make_async_copy(middle_ref, out_ref.at[:, left : left + wide], sem.at[2])]
    copies[0].start()
    near, start = {}, 0
    for tile, number in near_entries(SIDES):
        near[tile, number] = start
        start += padded(tokens_of(plan[tile][number]))
    borders = (None, None, None, west_ref, east_ref, lat_cells)
    gain = gain_one_ref[:1, :]
    _, far, spans = normed_of(plan, far_entries(SIDES), rest_ref[...], borders, gain)

    def piece_of(tile, number):
        if (tile, number) in spans:
            start, count = spans[tile, number]
            return far[start : start + count]
        start = near[tile, number]
        return normed_ref[start : start + tokens_of(plan[tile][number]), :]

    def put(part, j, piece):
        held_ref[j // 2, part[0] : part[0] + part[1]] = piece

    end = own_rows(plan, SIDES)
    worked(
        plan, SIDES, piece_of, normed_ref[:end, :], latent_ref[...], weights, scalars_ref, put
    )
    for n, number in enumerate((0, 2)):
        left, wide = plan[4][number][2:]
        copies.append(
            pltpu.make_async_copy(held_ref.at[n], out_ref.at[:, left : left + wide], sem.at[n])
        )
        copies[-1].start()
    for copy in copies:
        copy.wait()


def local(
    record_values,
    record_cell,
    record_instrument,
    block_counts,
    background,
    input_weight,
    instrument_table,
    lift_weight,
    first_gain,
    attn_weight,
    mix_weight,
    second_gain,
    up_weight,
    down_weight,
):
    lat_cells, lon_cells, _, width = background.shape
    tiles_lat = record_values.shape[1]

    sent, up, down = packed(
        record_values, record_cell, record_instrument, block_counts, background
    )
    received = lax.all_to_all(sent, ("lon", "lat"), split_axis=0, concat_axis=0, tiled=True)
    north, south = before_and_after(swapped(up, down, "lat", wraps=False), "lat")

    later, input_weight, attn_weight, down_weight, first_gain, second_gain, _ = (
        lax.optimization_barrier(
            (background, input_weight, attn_weight, down_weight, first_gain, second_gain, up)
        )
    )

    def columns(low, end):
        return jnp.concatenate([north[:, low:end], later[:, low:end], south[:, low:end]], axis=0)

    got = swapped(columns(0, HLON), columns(lon_cells - HLON, lon_cells), "lon", wraps=True)

    plan = rectangles(lat_cells, lon_cells)
    rows, parts, gain_one, gain_two = prepared(
        plan, later, attn_weight, first_gain, second_gain
    )
    lat = lax.axis_index("lat")
    scalars = jnp.stack([lat == 0, lat < 0, lat == tiles_lat - 1]).astype(jnp.int32)

    def rows_in(entries):
        return sum(padded(tokens_of(plan[tile][number])) for tile, number in entries)

    weights = [parts, mix_weight, gain_two, up_weight, down_weight]
    smem = pl.BlockSpec(memory_space=pltpu.SMEM)
    vmem = pl.BlockSpec(memory_space=pltpu.VMEM)
    anywhere = pl.BlockSpec(memory_space=pl.ANY)
    params = pltpu.CompilerParams(vmem_limit_bytes=LIMIT)
    middle, rest, latent, normed = pl.pallas_call(
        functools.partial(middle_kernel, plan, lat_cells, lon_cells),
        out_shape=[
            jax.ShapeDtypeStruct((lat_cells, lon_cells - WLON, LEV, width), BF16),
            jax.ShapeDtypeStruct((rows_in(far_entries(SIDES)), PAD), F32),
            jax.ShapeDtypeStruct((own_rows(plan, SIDES), width), F32),
            jax.ShapeDtypeStruct((rows_in(near_entries(SIDES)), width), F32),
        ],
        in_specs=[smem] + [vmem] * (8 + len(weights)),
        out_specs=[vmem] * 4,
        compiler_params=params,
        cost_estimate=pl.CostEstimate(
            flops=4 * 10**9, bytes_accessed=4 * 10**6, transcendentals=10**6
        ),
    )(
        scalars,
        received,
        north,
        south,
        rows,
        input_weight,
        instrument_table,
        lift_weight,
        gain_one,
        *weights,
    )
    rest, *got = lax.optimization_barrier((rest, *got[::-1]))
    got = got[::-1]
    west, east = before_and_after(got, "lon")
    return pl.pallas_call(
        functools.partial(side_kernel, plan, lat_cells),
        out_shape=jax.ShapeDtypeStruct(background.shape, BF16),
        in_specs=[smem] + [vmem] * (7 + len(weights)),
        out_specs=anywhere,
        scratch_shapes=[
            pltpu.VMEM((2, lat_cells, HLON, LEV, width), BF16),
            pltpu.SemaphoreType.DMA((3,)),
        ],
        compiler_params=params,
        cost_estimate=pl.CostEstimate(
            flops=3 * 10**9, bytes_accessed=4 * 10**6, transcendentals=10**6
        ),
    )(scalars, rest, latent, normed, west, east, gain_one, *weights, middle)


def solution(mesh):
    placed = (
        P("lon", "lat", None, None),
        P("lon", "lat", None),
        P("lon", "lat", None),
        P("lon", "lat"),
        P("lat", "lon", None, None),
        P(),
        P(),
        P(),
        P(),
        P(),
        P(),
        P(),
        P(),
        P(),
    )
    return jax.shard_map(
        local, mesh=mesh, in_specs=placed, out_specs=P("lat", "lon", None, None), check_vma=False
    )
```

```python
import functools

import jax
import jax.numpy as jnp
from jax import lax
from jax.experimental import pallas as pl
from jax.experimental.pallas import tpu as pltpu
from jax.sharding import PartitionSpec as P

HEADS = 6
INSTR = 8
LEV = 2
WLAT = 6
WLON = 12
HLAT = WLAT // 2
HLON = WLON // 2
LANES = 128
PAD = 256
CHUNK = 32
LIMIT = 40 * 2**20
BF16 = jnp.bfloat16
F32 = jnp.float32

AROUND = [(dy, dx) for dy in (-1, 0, 1) for dx in (-1, 0, 1)]
ROWS = INSTR * len(AROUND)
COLS = ROWS + len(AROUND)


def swapped(up, down, axis, wraps):
    count = lax.axis_size(axis)
    even = lax.axis_index(axis) % 2 == 0
    got = []
    for first, mine in ((0, jnp.where(even, down, up)), (1, jnp.where(even, up, down))):
        pairs = []
        for low in range(first, count, 2):
            high = (low + 1) % count
            if high > low or wraps:
                pairs += [(low, high), (high, low)]
        got.append(lax.ppermute(mine, axis, pairs))
    return got


def before_and_after(got, axis):
    even = lax.axis_index(axis) % 2 == 0
    return jnp.where(even, got[1], got[0]), jnp.where(even, got[0], got[1])


def rectangles(lat_cells, lon_cells):
    lat = {-1: [(lat_cells - HLAT, HLAT)], 1: [(0, HLAT)]}
    lat[0] = [(0, HLAT), (HLAT, lat_cells - WLAT), (lat_cells - HLAT, HLAT)]
    lon = {-1: [(lon_cells - HLON, HLON)], 1: [(0, HLON)]}
    lon[0] = [(0, HLON), (HLON, lon_cells - WLON), (lon_cells - HLON, HLON)]
    return [
        [(top, high, left, wide) for top, high in lat[dy] for left, wide in lon[dx]]
        for dy, dx in AROUND
    ]


def tokens_of(part):
    return part[1] * part[3] * LEV


def padded(count):
    return -(-count // 8) * 8


def gelu(x):
    half = 0.5 * x
    inner = x * (0.7978845608028654 + 0.035677408136300125 * (x * x))
    return half + half * jnp.tanh(inner)


def normalise(wide, gain):
    average = jnp.mean(wide, axis=-1, keepdims=True)
    centred = wide - average
    spread = jnp.mean(centred * centred, axis=-1, keepdims=True)
    return centred * lax.rsqrt(spread + 1e-05) * gain


def dot(a, b):
    return jnp.dot(a, b, preferred_element_type=F32)


def dot_nt(a, b):
    return lax.dot_general(a, b, (((1,), (1,)), ((), ())), preferred_element_type=F32)


def about_one_over(x):
    return pl.reciprocal(x, approx=True)


def with_ones(tensor):
    ones = jnp.ones((tensor.shape[0], PAD - tensor.shape[1]), tensor.dtype)
    return jnp.concatenate([tensor, ones], axis=1).astype(BF16)


def below(*pieces):
    return jnp.concatenate(pieces, axis=0) if len(pieces) > 1 else pieces[0]


def pack_kernel(
    values_ref,
    cell_ref,
    tag_ref,
    count_ref,
    back_ref,
    *refs,
):
    out_ref, up_ref, down_ref, values, cells, tags, held, sem = refs
    tiles_lon, tiles_lat, capacity, _ = values_ref.shape
    lat_cells, lon_cells = back_ref.shape[:2]
    strips = [
        (back_ref.at[:HLAT], up_ref),
        (back_ref.at[lat_cells - HLAT :], down_ref),
    ]
    copies = [
        pltpu.make_async_copy(cell_ref, cells, sem.at[0]),
        pltpu.make_async_copy(tag_ref, tags, sem.at[1]),
        pltpu.make_async_copy(count_ref, held, sem.at[2]),
        pltpu.make_async_copy(values_ref, values, sem.at[3]),
    ]
    copies += [
        pltpu.make_async_copy(source, strip, sem.at[4 + n])
        for n, (source, strip) in enumerate(strips)
    ]
    for copy in copies:
        copy.start()
    for copy in copies[:3]:
        copy.wait()
    counts = below(*[held[tile : tile + 1, :] for tile in range(tiles_lat) for _ in range(capacity)])
    cell = cells[...]
    slot = lax.broadcasted_iota(jnp.int32, cell.shape, 0) % capacity
    row = cell // lon_cells
    fields = [jnp.where(slot < counts, row, 255), cell - row * lon_cells, tags[...]]
    rows, columns, kinds = (field.astype(F32) for field in fields)
    lane = lax.broadcasted_iota(jnp.int32, (cell.shape[0], LANES), 1)
    kind_of = (lane % INSTR).astype(F32)
    marks = [
        ((lane < ROWS) & (lane // INSTR == n)) | (lane == ROWS + n) | (lane == COLS + n)
        for n in range(len(AROUND))
    ]
    turned = []
    for lon in range(tiles_lon):
        meta = jnp.where(kind_of == kinds[:, lon : lon + 1], 1.0, 0.0)
        meta = jnp.where(lane >= ROWS, rows[:, lon : lon + 1], meta)
        meta = jnp.where(lane >= COLS, columns[:, lon : lon + 1], meta)
        turns = {0: meta}
        for dy in (-1, 1):
            by = dy * capacity % meta.shape[0]
            turns[dy] = below(meta[by:], meta[:by])
        turned.append(turns)
    for lon in range(tiles_lon):
        meta = jnp.zeros(lane.shape, F32)
        for mark, (dy, dx) in zip(marks, AROUND):
            meta = jnp.where(mark, turned[(lon + dx) % tiles_lon][dy], meta)
        out_ref[lon, :, len(AROUND)] = meta.astype(BF16).reshape(tiles_lat, capacity, LANES)
    copies[3].wait()
    for n, (dy, dx) in enumerate(AROUND):
        spans = {0: [(0, tiles_lat)], 1: [(0, tiles_lat - 1), (tiles_lat - 1, tiles_lat)]}
        spans[-1] = [(0, 1), (1, tiles_lat)]

        def copy_tiles(lon, n=n, dx=dx, dy=dy, spans=spans[dy]):
            source = lax.rem(lon + dx + tiles_lon, tiles_lon)
            for low, end in spans:
                first = (low + dy) % tiles_lat
                out_ref[lon, low:end, n] = values[source, first : first + end - low]

        if tiles_lon <= 8:
            for lon in range(tiles_lon):
                copy_tiles(lon)
        else:
            pl.loop(0, tiles_lon)(copy_tiles)
    for copy in copies[4:]:
        copy.wait()


def packed(record_values, record_cell, record_instrument, block_counts, background):
    tiles_lon, tiles_lat, capacity, wide = record_values.shape
    anywhere = pl.BlockSpec(memory_space=pltpu.HBM)
    ints = pltpu.VMEM((tiles_lat * capacity, tiles_lon), jnp.int32)
    shape = (tiles_lon, tiles_lat, len(AROUND) + 1, capacity, wide)
    lat_cells, lon_cells, levels, width = background.shape
    across = jax.ShapeDtypeStruct((HLAT, lon_cells, levels, width), BF16)
    out, *strips = pl.pallas_call(
        pack_kernel,
        out_shape=[jax.ShapeDtypeStruct(shape, BF16), across, across],
        in_specs=[anywhere] * 5,
        out_specs=[pl.BlockSpec(memory_space=pltpu.VMEM)] * 3,
        scratch_shapes=[
            pltpu.VMEM(record_values.shape, BF16),
            ints,
            ints,
            pltpu.VMEM((tiles_lat, tiles_lon), jnp.int32),
            pltpu.SemaphoreType.DMA((6,)),
        ],
        compiler_params=pltpu.CompilerParams(vmem_limit_bytes=56 * 2**20),
        cost_estimate=pl.CostEstimate(
            flops=20 * 10**9, bytes_accessed=10**6, transcendentals=0
        ),
    )(
        record_values,
        record_cell.transpose(1, 2, 0).reshape(-1, tiles_lon),
        record_instrument.transpose(1, 2, 0).reshape(-1, tiles_lon),
        block_counts.T,
        background,
    )
    return out.reshape((-1,) + shape[2:]), *strips


def token_codes(part, lon_cells):
    top, high, left, wide = part
    count = tokens_of(part)
    place = lax.broadcasted_iota(jnp.int32, (padded(count), LANES), 0)
    code = place + (top * lon_cells + left) * LEV
    for row in range(1, high):
        step = (lon_cells - wide) * LEV
        code = code + jnp.where(place >= row * wide * LEV, step, 0)
    return jnp.where(place < count, code, -8).astype(F32)


def near_entries(windows):
    own = [(4, 3 * i + j) for i, j in windows]
    return own + [(3 * i + 1, j) for i, j in windows if i != 1]


def far_entries(windows):
    beside = [(3 + j, i) for i, j in windows if j != 1]
    return beside + [(3 * i + j, 0) for i, j in windows if i != 1 and j != 1]


def scattered(recv_ref, first_ref, table_ref, lift_ref, plan, lon_cells):
    sources, _, capacity, _ = recv_ref.shape
    width = first_ref.shape[1]
    chunk = min(CHUNK, sources)
    slots = chunk * capacity
    first, lift = below(first_ref[...], table_ref[...]), lift_ref[...]
    lane = lax.broadcasted_iota(jnp.int32, (16, LANES), 1)
    sub = lax.broadcasted_iota(jnp.int32, (16, LANES), 0)
    weigh = jnp.where(lane == ROWS + sub, float(lon_cells * LEV), 0.0)
    weigh = jnp.where(lane == COLS + sub, float(LEV), weigh).astype(BF16)
    codes = [below(*[token_codes(part, lon_cells) for part in parts]) for parts in plan]

    def scatter(begin):
        meta = recv_ref[pl.ds(begin, chunk), len(AROUND)].reshape(slots, LANES)
        records = below(
            *[
                recv_ref[pl.ds(begin, chunk), n].reshape(slots, LANES)
                for n in range(len(AROUND))
            ]
        )
        lane = lax.broadcasted_iota(jnp.int32, meta.shape, 1) // INSTR
        wide = meta.astype(F32)
        chosen = below(*[jnp.where(lane == n, wide, 0.0) for n in range(len(AROUND))]).astype(BF16)
        both = jnp.concatenate([records, chosen], axis=1)
        encoded = gelu(dot(both, first).astype(BF16))
        lifted = gelu(dot(encoded, lift).astype(BF16))
        tokens = dot_nt(weigh, meta)
        hots, parts = [], []
        for n in range(len(AROUND)):
            token = tokens[n : n + 1]
            token = jnp.concatenate([token + float(level) for level in range(LEV)], axis=1)
            if token.shape[1] == LANES:
                hot = codes[n] == token
            else:
                hot = codes[n][:, :1] == token
            hots.append(jnp.where(hot, 1.0, 0.0).astype(BF16))
        for n in range(len(AROUND)):
            part = lifted[n * slots : (n + 1) * slots]
            parts.append(
                with_ones(
                    below(*[part[:, level * width : (level + 1) * width] for level in range(LEV)])
                )
            )
        sums = [dot(hot, part) for hot, part in zip(hots, parts)]
        return tuple(sums)

    sums = scatter(0)
    if sources > chunk:
        sums = lax.fori_loop(
            1,
            sources // chunk,
            lambda step, total: tuple(a + b for a, b in zip(total, scatter(step * chunk))),
            sums,
        )
    return sums


def prepare_kernel(
    plan,
    back_ref,
    attn_ref,
    table_ref,
    one_ref,
    two_ref,
    rows_ref,
    parts_ref,
    tables_ref,
    gain_one_ref,
    gain_two_ref,
):
    width = back_ref.shape[3]
    pieces = []
    for top, high, left, wide in plan[4]:
        count = high * wide * LEV
        piece = back_ref[top : top + high, left : left + wide].reshape(count, width).astype(F32)
        if padded(count) > count:
            piece = below(piece, jnp.zeros((padded(count) - count, width), F32))
        pieces.append(piece)
    rows_ref[...] = below(*pieces).astype(BF16)
    tables_ref[...] = below(*[table_ref[...].astype(F32)] * (LANES // INSTR)).astype(BF16)
    for gain, ref in ((one_ref, gain_one_ref), (two_ref, gain_two_ref)):
        ref[...] = jnp.broadcast_to(gain[...].astype(F32).reshape(1, width), ref.shape)
    for n in range(3):
        parts_ref[n] = attn_ref[:, n * width : (n + 1) * width]


def prepared(plan, background, attn_weight, instrument_table, first_gain, second_gain):
    width = background.shape[3]
    rows = sum(padded(tokens_of(part)) for part in plan[4])
    vmem = pl.BlockSpec(memory_space=pltpu.VMEM)
    return pl.pallas_call(
        functools.partial(prepare_kernel, plan),
        out_shape=[
            jax.ShapeDtypeStruct((rows, width), BF16),
            jax.ShapeDtypeStruct((3, width, width), BF16),
            jax.ShapeDtypeStruct((LANES, width), BF16),
            jax.ShapeDtypeStruct((8, width), F32),
            jax.ShapeDtypeStruct((8, width), F32),
        ],
        in_specs=[vmem] * 5,
        out_specs=[vmem] * 5,
        compiler_params=pltpu.CompilerParams(vmem_limit_bytes=LIMIT),
        cost_estimate=pl.CostEstimate(flops=10**9, bytes_accessed=10**6, transcendentals=0),
    )(background, attn_weight, instrument_table, first_gain, second_gain)


def normed_of(plan, entries, sums, borders, gain):
    rows, north_ref, south_ref, west_ref, east_ref, lat_cells = borders
    width = gain.shape[1]
    pieces, spans, start = [], {}, 0
    for tile, number in entries:
        dy, dx = AROUND[tile]
        top, high, left, wide = plan[tile][number]
        count = high * wide * LEV
        full = padded(count)
        if tile == 4:
            begin = sum(padded(tokens_of(part)) for part in plan[4][:number])
            piece = rows[begin : begin + full]
        else:
            if dx:
                ref = west_ref if dx < 0 else east_ref
                top, left = {-1: 0, 0: top + HLAT, 1: lat_cells + HLAT}[dy], 0
            else:
                ref, top = (north_ref, 0) if dy < 0 else (south_ref, 0)
            piece = ref[top : top + high, left : left + wide].reshape(count, width).astype(F32)
            if full > count:
                piece = below(piece, jnp.zeros((full - count, width), F32))
        pieces.append(piece)
        spans[tile, number] = (start, count)
        start += full
    tally = 1.0 + sums[:, width : width + 1]
    share = about_one_over(tally)
    share = share * (2.0 - tally * share)
    latent = ((below(*pieces) + sums[:, :width]) * share).astype(BF16).astype(F32)
    return latent, normalise(latent, gain), spans


def worked(plan, places, piece_of, own_normed, latent, weights, scalars_ref, put):
    parts_ref, mix_ref, gain_ref, up_ref, down_ref = weights
    width = mix_ref.shape[0]
    groups = [padded(tokens_of(plan[4][3 * i + j])) for i, j in places]
    windows = []
    for i, j in places:
        window = [piece_of(4, 3 * i + j)]
        if i != 1:
            window.append(piece_of(3 * i + 1, j))
        if j != 1:
            window.append(piece_of(3 + j, i))
        if i != 1 and j != 1:
            window.append(piece_of(3 * i + j, 0))
        windows.append(window)
    tokens = below(*[piece for window in windows for piece in window]).astype(BF16)
    head = width // HEADS
    query = dot(own_normed.astype(BF16), parts_ref[0]) * head ** (-0.5)
    query = jnp.concatenate([query, jnp.ones((query.shape[0], PAD - width), F32)], axis=1)
    keys = dot(tokens, parts_ref[1])
    values = with_ones(dot(tokens, parts_ref[2]))

    lane = lax.broadcasted_iota(jnp.int32, (1, PAD), 1)
    many = WLAT * WLON * LEV
    corner = HLAT * HLON * LEV
    key = lax.broadcasted_iota(jnp.int32, (many, PAD - width), 0)
    spare = lax.broadcasted_iota(jnp.int32, (many, PAD - width), 1)
    unused = lax.broadcasted_iota(jnp.int32, (PAD - many, PAD), 1)
    unused = jnp.where(unused == width, -3e38, 0.0).astype(BF16)
    nothing = jnp.zeros((PAD - many, PAD), BF16)

    def keys_of(w, i, j):
        bias = jnp.zeros((many, PAD - width), F32)
        if i != 1:
            if j == 1:
                inside = key < 2 * corner
            else:
                inside = (key < corner) | ((key >= 2 * corner) & (key < 3 * corner))
            bias = jnp.where(inside | (spare > 0), 0.0, -3e38) * scalars_ref[i].astype(F32)
        here = jnp.concatenate([keys[w * many : (w + 1) * many], bias], axis=1)
        return below(here.astype(BF16), unused)

    begins = [sum(groups[:w]) for w in range(len(groups))]
    parts = [query[begin : begin + rows] for begin, rows in zip(begins, groups)]
    stacks = [
        below(
            *[jnp.where((lane // head == h) | (lane >= width), part, 0.0) for h in range(HEADS)]
        ).astype(BF16)
        for part in parts
    ]
    held = [keys_of(w, i, j) for w, (i, j) in enumerate(places)]
    scores = [dot_nt(stack, here) for stack, here in zip(stacks, held)]
    largest = [jnp.max(score, axis=-1, keepdims=True) for score in scores]
    raised = [jnp.exp((score - most).astype(BF16)) for score, most in zip(scores, largest)]
    held = [below(values[w * many : (w + 1) * many], nothing) for w in range(len(places))]
    products = [dot(one, here) for one, here in zip(raised, held)]
    shares = [about_one_over(product[:, width : width + 1]) for product in products]
    products = [product[:, :width] * share for product, share in zip(products, shares)]
    mixed = []
    for product, rows in zip(products, groups):
        total = product[:rows]
        for h in range(1, HEADS):
            own = lane[:, :width] // head == h
            total = jnp.where(own, product[h * rows : (h + 1) * rows], total)
        mixed.append(total)
    mixed = below(*mixed).astype(BF16)

    after = (latent + dot(mixed, mix_ref[...])).astype(BF16).astype(F32)
    normed_two = normalise(after, gain_ref[:1, :]).astype(BF16)
    hidden = gelu(dot(normed_two, up_ref[...]).astype(BF16))
    result = after + dot(hidden, down_ref[...])
    for begin, (i, j) in zip(begins, places):
        part = plan[4][3 * i + j]
        piece = result[begin : begin + tokens_of(part)].astype(BF16)
        put(part, j, piece.reshape(part[1], part[3], LEV, width))


MIDDLE = [(0, 1), (1, 1), (2, 1)]
SIDES = [(0, 0), (0, 2), (2, 0), (2, 2), (1, 0), (1, 2)]


def own_rows(plan, places):
    return sum(padded(tokens_of(plan[4][3 * i + j])) for i, j in places)


def middle_kernel(
    plan,
    lat_cells,
    lon_cells,
    scalars_ref,
    recv_ref,
    north_ref,
    south_ref,
    rows_ref,
    first_ref,
    table_ref,
    lift_ref,
    gain_one_ref,
    *refs,
):
    *weights, out_ref, rest_ref, latent_ref, normed_ref = refs
    sums = scattered(recv_ref, first_ref, table_ref, lift_ref, plan, lon_cells)

    def sums_of(entries):
        pieces = []
        for tile, number in entries:
            start = sum(padded(tokens_of(part)) for part in plan[tile][:number])
            pieces.append(sums[tile][start : start + padded(tokens_of(plan[tile][number]))])
        return below(*pieces)

    borders = (rows_ref[...].astype(F32), north_ref, south_ref, None, None, lat_cells)
    gain = gain_one_ref[:1, :]
    entries = near_entries(MIDDLE)
    latent, normed, spans = normed_of(plan, entries, sums_of(entries), borders, gain)

    def piece_of(tile, number):
        start, count = spans[tile, number]
        return normed[start : start + count]

    def put(part, _, piece):
        out_ref[part[0] : part[0] + part[1]] = piece

    end = own_rows(plan, MIDDLE)
    worked(plan, MIDDLE, piece_of, normed[:end], latent[:end], weights, scalars_ref, put)
    rest_ref[...] = sums_of(far_entries(SIDES))
    entries = near_entries(SIDES)
    latent, normed, _ = normed_of(plan, entries, sums_of(entries), borders, gain)
    latent_ref[...] = latent[: latent_ref.shape[0]]
    normed_ref[...] = normed


def side_kernel(
    plan,
    lat_cells,
    scalars_ref,
    rest_ref,
    latent_ref,
    normed_ref,
    west_ref,
    east_ref,
    gain_one_ref,
    *refs,
):
    *weights, middle_ref, out_ref, held_ref, sem = refs
    left, wide = plan[4][4][2:]
    copies = [pltpu.make_async_copy(middle_ref, out_ref.at[:, left : left + wide], sem.at[2])]
    copies[0].start()
    near, start = {}, 0
    for tile, number in near_entries(SIDES):
        near[tile, number] = start
        start += padded(tokens_of(plan[tile][number]))
    borders = (None, None, None, west_ref, east_ref, lat_cells)
    gain = gain_one_ref[:1, :]
    _, far, spans = normed_of(plan, far_entries(SIDES), rest_ref[...], borders, gain)

    def piece_of(tile, number):
        if (tile, number) in spans:
            start, count = spans[tile, number]
            return far[start : start + count]
        start = near[tile, number]
        return normed_ref[start : start + tokens_of(plan[tile][number]), :]

    def put(part, j, piece):
        held_ref[j // 2, part[0] : part[0] + part[1]] = piece

    end = own_rows(plan, SIDES)
    worked(
        plan, SIDES, piece_of, normed_ref[:end, :], latent_ref[...], weights, scalars_ref, put
    )
    for n, number in enumerate((0, 2)):
        left, wide = plan[4][number][2:]
        copies.append(
            pltpu.make_async_copy(held_ref.at[n], out_ref.at[:, left : left + wide], sem.at[n])
        )
        copies[-1].start()
    for copy in copies:
        copy.wait()


def local(
    record_values,
    record_cell,
    record_instrument,
    block_counts,
    background,
    input_weight,
    instrument_table,
    lift_weight,
    first_gain,
    attn_weight,
    mix_weight,
    second_gain,
    up_weight,
    down_weight,
):
    lat_cells, lon_cells, _, width = background.shape
    tiles_lat = record_values.shape[1]

    sent, up, down = packed(
        record_values, record_cell, record_instrument, block_counts, background
    )
    received = lax.all_to_all(sent, ("lon", "lat"), split_axis=0, concat_axis=0, tiled=True)
    north, south = before_and_after(swapped(up, down, "lat", wraps=False), "lat")

    held = (background, input_weight, instrument_table, attn_weight, down_weight)
    held = lax.optimization_barrier((*held, first_gain, second_gain, up))
    later, input_weight, instrument_table, attn_weight, down_weight = held[:5]
    first_gain, second_gain = held[5:7]

    def columns(low, end):
        return jnp.concatenate([north[:, low:end], later[:, low:end], south[:, low:end]], axis=0)

    got = swapped(columns(0, HLON), columns(lon_cells - HLON, lon_cells), "lon", wraps=True)

    plan = rectangles(lat_cells, lon_cells)
    rows, parts, tables, gain_one, gain_two = prepared(
        plan, later, attn_weight, instrument_table, first_gain, second_gain
    )
    lat = lax.axis_index("lat")
    scalars = jnp.stack([lat == 0, lat < 0, lat == tiles_lat - 1]).astype(jnp.int32)

    def rows_in(entries):
        return sum(padded(tokens_of(plan[tile][number])) for tile, number in entries)

    weights = [parts, mix_weight, gain_two, up_weight, down_weight]
    smem = pl.BlockSpec(memory_space=pltpu.SMEM)
    vmem = pl.BlockSpec(memory_space=pltpu.VMEM)
    anywhere = pl.BlockSpec(memory_space=pl.ANY)
    params = pltpu.CompilerParams(vmem_limit_bytes=LIMIT)
    middle, rest, latent, normed = pl.pallas_call(
        functools.partial(middle_kernel, plan, lat_cells, lon_cells),
        out_shape=[
            jax.ShapeDtypeStruct((lat_cells, lon_cells - WLON, LEV, width), BF16),
            jax.ShapeDtypeStruct((rows_in(far_entries(SIDES)), PAD), F32),
            jax.ShapeDtypeStruct((own_rows(plan, SIDES), width), F32),
            jax.ShapeDtypeStruct((rows_in(near_entries(SIDES)), width), F32),
        ],
        in_specs=[smem] + [vmem] * (8 + len(weights)),
        out_specs=[vmem] * 4,
        compiler_params=params,
        cost_estimate=pl.CostEstimate(
            flops=4 * 10**9, bytes_accessed=4 * 10**6, transcendentals=10**6
        ),
    )(
        scalars,
        received,
        north,
        south,
        rows,
        input_weight,
        tables,
        lift_weight,
        gain_one,
        *weights,
    )
    rest, *got = lax.optimization_barrier((rest, *got[::-1]))
    got = got[::-1]
    west, east = before_and_after(got, "lon")
    return pl.pallas_call(
        functools.partial(side_kernel, plan, lat_cells),
        out_shape=jax.ShapeDtypeStruct(background.shape, BF16),
        in_specs=[smem] + [vmem] * (7 + len(weights)),
        out_specs=anywhere,
        scratch_shapes=[
            pltpu.VMEM((2, lat_cells, HLON, LEV, width), BF16),
            pltpu.SemaphoreType.DMA((3,)),
        ],
        compiler_params=params,
        cost_estimate=pl.CostEstimate(
            flops=3 * 10**9, bytes_accessed=4 * 10**6, transcendentals=10**6
        ),
    )(scalars, rest, latent, normed, west, east, gain_one, *weights, middle)


def solution(mesh):
    placed = (
        P("lon", "lat", None, None),
        P("lon", "lat", None),
        P("lon", "lat", None),
        P("lon", "lat"),
        P("lat", "lon", None, None),
        P(),
        P(),
        P(),
        P(),
        P(),
        P(),
        P(),
        P(),
        P(),
    )
    return jax.shard_map(
        local, mesh=mesh, in_specs=placed, out_specs=P("lat", "lon", None, None), check_vma=False
    )
```

```python
import functools

import jax
import jax.numpy as jnp
from jax import lax
from jax.experimental import pallas as pl
from jax.experimental.pallas import tpu as pltpu
from jax.sharding import PartitionSpec as P

HEADS = 6
INSTR = 8
LEV = 2
WLAT = 6
WLON = 12
HLAT = WLAT // 2
HLON = WLON // 2
LANES = 128
PAD = 256
CHUNK = 32
LIMIT = 40 * 2**20
BF16 = jnp.bfloat16
F32 = jnp.float32

AROUND = [(dy, dx) for dy in (-1, 0, 1) for dx in (-1, 0, 1)]
ROWS = INSTR * len(AROUND)
COLS = ROWS + len(AROUND)


def swapped(up, down, axis, wraps):
    count = lax.axis_size(axis)
    even = lax.axis_index(axis) % 2 == 0
    got = []
    for first, mine in ((0, jnp.where(even, down, up)), (1, jnp.where(even, up, down))):
        pairs = []
        for low in range(first, count, 2):
            high = (low + 1) % count
            if high > low or wraps:
                pairs += [(low, high), (high, low)]
        got.append(lax.ppermute(mine, axis, pairs))
    return got


def before_and_after(got, axis):
    even = lax.axis_index(axis) % 2 == 0
    return jnp.where(even, got[1], got[0]), jnp.where(even, got[0], got[1])


def rectangles(lat_cells, lon_cells):
    lat = {-1: [(lat_cells - HLAT, HLAT)], 1: [(0, HLAT)]}
    lat[0] = [(0, HLAT), (HLAT, lat_cells - WLAT), (lat_cells - HLAT, HLAT)]
    lon = {-1: [(lon_cells - HLON, HLON)], 1: [(0, HLON)]}
    lon[0] = [(0, HLON), (HLON, lon_cells - WLON), (lon_cells - HLON, HLON)]
    return [
        [(top, high, left, wide) for top, high in lat[dy] for left, wide in lon[dx]]
        for dy, dx in AROUND
    ]


def tokens_of(part):
    return part[1] * part[3] * LEV


def padded(count):
    return -(-count // 8) * 8


def gelu(x):
    half = 0.5 * x
    inner = x * (0.7978845608028654 + 0.035677408136300125 * (x * x))
    return half + half * jnp.tanh(inner)


def normalise(wide, gain):
    average = jnp.mean(wide, axis=-1, keepdims=True)
    centred = wide - average
    spread = jnp.mean(centred * centred, axis=-1, keepdims=True)
    return centred * lax.rsqrt(spread + 1e-05) * gain


def dot(a, b):
    return jnp.dot(a, b, preferred_element_type=F32)


def dot_nt(a, b):
    return lax.dot_general(a, b, (((1,), (1,)), ((), ())), preferred_element_type=F32)


def about_one_over(x):
    return pl.reciprocal(x, approx=True)


def with_ones(tensor):
    ones = jnp.ones((tensor.shape[0], PAD - tensor.shape[1]), tensor.dtype)
    return jnp.concatenate([tensor, ones], axis=1).astype(BF16)


def below(*pieces):
    return jnp.concatenate(pieces, axis=0) if len(pieces) > 1 else pieces[0]


def pack_kernel(
    values_ref,
    cell_ref,
    tag_ref,
    count_ref,
    back_ref,
    *refs,
):
    out_ref, up_ref, down_ref, values, cells, tags, held, sem = refs
    tiles_lon, tiles_lat, capacity, _ = values_ref.shape
    lat_cells, lon_cells = back_ref.shape[:2]
    strips = [
        (back_ref.at[:HLAT], up_ref),
        (back_ref.at[lat_cells - HLAT :], down_ref),
    ]
    copies = [
        pltpu.make_async_copy(cell_ref, cells, sem.at[0]),
        pltpu.make_async_copy(tag_ref, tags, sem.at[1]),
        pltpu.make_async_copy(count_ref, held, sem.at[2]),
        pltpu.make_async_copy(values_ref, values, sem.at[3]),
    ]
    copies += [
        pltpu.make_async_copy(source, strip, sem.at[4 + n])
        for n, (source, strip) in enumerate(strips)
    ]
    for copy in copies:
        copy.start()
    for copy in copies[:3]:
        copy.wait()
    counts = below(*[held[tile : tile + 1, :] for tile in range(tiles_lat) for _ in range(capacity)])
    cell = cells[...]
    slot = lax.broadcasted_iota(jnp.int32, cell.shape, 0) % capacity
    row = cell // lon_cells
    fields = [jnp.where(slot < counts, row, 255), cell - row * lon_cells, tags[...]]
    rows, columns, kinds = (field.astype(F32) for field in fields)
    lane = lax.broadcasted_iota(jnp.int32, (cell.shape[0], LANES), 1)
    kind_of = (lane % INSTR).astype(F32)
    marks = [
        ((lane < ROWS) & (lane // INSTR == n)) | (lane == ROWS + n) | (lane == COLS + n)
        for n in range(len(AROUND))
    ]
    turned = []
    for lon in range(tiles_lon):
        meta = jnp.where(kind_of == kinds[:, lon : lon + 1], 1.0, 0.0)
        meta = jnp.where(lane >= ROWS, rows[:, lon : lon + 1], meta)
        meta = jnp.where(lane >= COLS, columns[:, lon : lon + 1], meta)
        turns = {0: meta}
        for dy in (-1, 1):
            by = dy * capacity % meta.shape[0]
            turns[dy] = below(meta[by:], meta[:by])
        turned.append(turns)
    for lon in range(tiles_lon):
        meta = jnp.zeros(lane.shape, F32)
        for mark, (dy, dx) in zip(marks, AROUND):
            meta = jnp.where(mark, turned[(lon + dx) % tiles_lon][dy], meta)
        out_ref[lon, :, len(AROUND)] = meta.astype(BF16).reshape(tiles_lat, capacity, LANES)
    copies[3].wait()
    for n, (dy, dx) in enumerate(AROUND):
        spans = {0: [(0, tiles_lat)], 1: [(0, tiles_lat - 1), (tiles_lat - 1, tiles_lat)]}
        spans[-1] = [(0, 1), (1, tiles_lat)]

        def copy_tiles(lon, n=n, dx=dx, dy=dy, spans=spans[dy]):
            source = lax.rem(lon + dx + tiles_lon, tiles_lon)
            for low, end in spans:
                first = (low + dy) % tiles_lat
                out_ref[lon, low:end, n] = values[source, first : first + end - low]

        if tiles_lon <= 8:
            for lon in range(tiles_lon):
                copy_tiles(lon)
        else:
            pl.loop(0, tiles_lon)(copy_tiles)
    for copy in copies[4:]:
        copy.wait()


def packed(record_values, record_cell, record_instrument, block_counts, background):
    tiles_lon, tiles_lat, capacity, wide = record_values.shape
    anywhere = pl.BlockSpec(memory_space=pltpu.HBM)
    ints = pltpu.VMEM((tiles_lat * capacity, tiles_lon), jnp.int32)
    shape = (tiles_lon, tiles_lat, len(AROUND) + 1, capacity, wide)
    lat_cells, lon_cells, levels, width = background.shape
    across = jax.ShapeDtypeStruct((HLAT, lon_cells, levels, width), BF16)
    out, *strips = pl.pallas_call(
        pack_kernel,
        out_shape=[jax.ShapeDtypeStruct(shape, BF16), across, across],
        in_specs=[anywhere] * 5,
        out_specs=[pl.BlockSpec(memory_space=pltpu.VMEM)] * 3,
        scratch_shapes=[
            pltpu.VMEM(record_values.shape, BF16),
            ints,
            ints,
            pltpu.VMEM((tiles_lat, tiles_lon), jnp.int32),
            pltpu.SemaphoreType.DMA((6,)),
        ],
        compiler_params=pltpu.CompilerParams(vmem_limit_bytes=56 * 2**20),
        cost_estimate=pl.CostEstimate(
            flops=20 * 10**9, bytes_accessed=10**6, transcendentals=0
        ),
    )(
        record_values,
        record_cell.transpose(1, 2, 0).reshape(-1, tiles_lon),
        record_instrument.transpose(1, 2, 0).reshape(-1, tiles_lon),
        block_counts.T,
        background,
    )
    return out.reshape((-1,) + shape[2:]), *strips


def token_codes(part, lon_cells):
    top, high, left, wide = part
    count = tokens_of(part)
    place = lax.broadcasted_iota(jnp.int32, (padded(count), LANES), 0)
    code = place + (top * lon_cells + left) * LEV
    for row in range(1, high):
        step = (lon_cells - wide) * LEV
        code = code + jnp.where(place >= row * wide * LEV, step, 0)
    return jnp.where(place < count, code, -8).astype(F32)


def near_entries(windows):
    own = [(4, 3 * i + j) for i, j in windows]
    return own + [(3 * i + 1, j) for i, j in windows if i != 1]


def far_entries(windows):
    beside = [(3 + j, i) for i, j in windows if j != 1]
    return beside + [(3 * i + j, 0) for i, j in windows if i != 1 and j != 1]


def scattered(recv_ref, first_ref, table_ref, lift_ref, plan, lon_cells):
    sources, _, capacity, _ = recv_ref.shape
    width = first_ref.shape[1]
    chunk = min(CHUNK, sources)
    slots = chunk * capacity
    first, lift = below(first_ref[...], table_ref[...]), lift_ref[...]
    lane = lax.broadcasted_iota(jnp.int32, (16, LANES), 1)
    sub = lax.broadcasted_iota(jnp.int32, (16, LANES), 0)
    weigh = jnp.where(lane == ROWS + sub, float(lon_cells * LEV), 0.0)
    weigh = jnp.where(lane == COLS + sub, float(LEV), weigh).astype(BF16)
    codes = [below(*[token_codes(part, lon_cells) for part in parts]) for parts in plan]

    def scatter(begin):
        meta = recv_ref[pl.ds(begin, chunk), len(AROUND)].reshape(slots, LANES)
        records = below(
            *[
                recv_ref[pl.ds(begin, chunk), n].reshape(slots, LANES)
                for n in range(len(AROUND))
            ]
        )
        lane = lax.broadcasted_iota(jnp.int32, meta.shape, 1) // INSTR
        wide = meta.astype(F32)
        chosen = below(*[jnp.where(lane == n, wide, 0.0) for n in range(len(AROUND))]).astype(BF16)
        both = jnp.concatenate([records, chosen], axis=1)
        encoded = gelu(dot(both, first).astype(BF16))
        lifted = gelu(dot(encoded, lift).astype(BF16))
        tokens = dot_nt(weigh, meta)
        hots, parts = [], []
        for n in range(len(AROUND)):
            token = tokens[n : n + 1]
            token = jnp.concatenate([token + float(level) for level in range(LEV)], axis=1)
            if token.shape[1] == LANES:
                hot = codes[n] == token
            else:
                hot = codes[n][:, :1] == token
            hots.append(jnp.where(hot, 1.0, 0.0).astype(BF16))
        for n in range(len(AROUND)):
            part = lifted[n * slots : (n + 1) * slots]
            parts.append(
                with_ones(
                    below(*[part[:, level * width : (level + 1) * width] for level in range(LEV)])
                )
            )
        sums = [dot(hot, part) for hot, part in zip(hots, parts)]
        return tuple(sums)

    sums = scatter(0)
    if sources > chunk:
        sums = lax.fori_loop(
            1,
            sources // chunk,
            lambda step, total: tuple(a + b for a, b in zip(total, scatter(step * chunk))),
            sums,
        )
    return sums


def prepare_kernel(
    plan,
    back_ref,
    attn_ref,
    table_ref,
    one_ref,
    two_ref,
    rows_ref,
    parts_ref,
    tables_ref,
    gain_one_ref,
    gain_two_ref,
):
    width = back_ref.shape[3]
    pieces = []
    for top, high, left, wide in plan[4]:
        count = high * wide * LEV
        piece = back_ref[top : top + high, left : left + wide].reshape(count, width).astype(F32)
        if padded(count) > count:
            piece = below(piece, jnp.zeros((padded(count) - count, width), F32))
        pieces.append(piece)
    rows_ref[...] = below(*pieces).astype(BF16)
    tables_ref[...] = below(*[table_ref[...].astype(F32)] * (LANES // INSTR)).astype(BF16)
    for gain, ref in ((one_ref, gain_one_ref), (two_ref, gain_two_ref)):
        ref[...] = jnp.broadcast_to(gain[...].astype(F32).reshape(1, width), ref.shape)
    for n in range(3):
        parts_ref[n] = attn_ref[:, n * width : (n + 1) * width]


def prepared(plan, background, attn_weight, instrument_table, first_gain, second_gain):
    width = background.shape[3]
    rows = sum(padded(tokens_of(part)) for part in plan[4])
    vmem = pl.BlockSpec(memory_space=pltpu.VMEM)
    return pl.pallas_call(
        functools.partial(prepare_kernel, plan),
        out_shape=[
            jax.ShapeDtypeStruct((rows, width), BF16),
            jax.ShapeDtypeStruct((3, width, width), BF16),
            jax.ShapeDtypeStruct((LANES, width), BF16),
            jax.ShapeDtypeStruct((8, width), F32),
            jax.ShapeDtypeStruct((8, width), F32),
        ],
        in_specs=[vmem] * 5,
        out_specs=[vmem] * 5,
        compiler_params=pltpu.CompilerParams(vmem_limit_bytes=LIMIT),
        cost_estimate=pl.CostEstimate(flops=10**9, bytes_accessed=10**6, transcendentals=0),
    )(background, attn_weight, instrument_table, first_gain, second_gain)


def normed_of(plan, entries, sums, borders, gain):
    rows, north_ref, south_ref, west_ref, east_ref, lat_cells = borders
    width = gain.shape[1]
    pieces, spans, start = [], {}, 0
    for tile, number in entries:
        dy, dx = AROUND[tile]
        top, high, left, wide = plan[tile][number]
        count = high * wide * LEV
        full = padded(count)
        if tile == 4:
            begin = sum(padded(tokens_of(part)) for part in plan[4][:number])
            piece = rows[begin : begin + full]
        else:
            if dx:
                ref = west_ref if dx < 0 else east_ref
                top, left = {-1: 0, 0: top + HLAT, 1: lat_cells + HLAT}[dy], 0
            else:
                ref, top = (north_ref, 0) if dy < 0 else (south_ref, 0)
            piece = ref[top : top + high, left : left + wide].reshape(count, width).astype(F32)
            if full > count:
                piece = below(piece, jnp.zeros((full - count, width), F32))
        pieces.append(piece)
        spans[tile, number] = (start, count)
        start += full
    tally = 1.0 + sums[:, width : width + 1]
    share = about_one_over(tally)
    share = share * (2.0 - tally * share)
    latent = ((below(*pieces) + sums[:, :width]) * share).astype(BF16).astype(F32)
    return latent, normalise(latent, gain), spans


def stacks_of(plan, places, own_normed, weight):
    width = weight.shape[0]
    head = width // HEADS
    query = dot(own_normed.astype(BF16), weight) * head ** (-0.5)
    query = jnp.concatenate([query, jnp.ones((query.shape[0], PAD - width), F32)], axis=1)
    lane = lax.broadcasted_iota(jnp.int32, (1, PAD), 1)
    stacks, begin = [], 0
    for i, j in places:
        rows = padded(tokens_of(plan[4][3 * i + j]))
        part = query[begin : begin + rows]
        begin += rows
        stacks.append(
            below(
                *[jnp.where((lane // head == h) | (lane >= width), part, 0.0) for h in range(HEADS)]
            ).astype(BF16)
        )
    return stacks


def worked(plan, places, stacks, keys, values, latent, weights, scalars_ref, put):
    mix_ref, gain_ref, up_ref, down_ref = weights
    width = mix_ref.shape[0]
    head = width // HEADS
    groups = [padded(tokens_of(plan[4][3 * i + j])) for i, j in places]
    lane = lax.broadcasted_iota(jnp.int32, (1, PAD), 1)
    many = WLAT * WLON * LEV
    corner = HLAT * HLON * LEV
    key = lax.broadcasted_iota(jnp.int32, (many, PAD - width), 0)
    spare = lax.broadcasted_iota(jnp.int32, (many, PAD - width), 1)
    unused = lax.broadcasted_iota(jnp.int32, (PAD - many, PAD), 1)
    unused = jnp.where(unused == width, -3e38, 0.0).astype(BF16)
    nothing = jnp.zeros((PAD - many, PAD), BF16)

    def keys_of(w, i, j):
        bias = jnp.zeros((many, PAD - width), F32)
        if i != 1:
            if j == 1:
                inside = key < 2 * corner
            else:
                inside = (key < corner) | ((key >= 2 * corner) & (key < 3 * corner))
            bias = jnp.where(inside | (spare > 0), 0.0, -3e38) * scalars_ref[i].astype(F32)
        here = jnp.concatenate([keys[w], bias], axis=1)
        return below(here.astype(BF16), unused)

    begins = [sum(groups[:w]) for w in range(len(groups))]
    held = [keys_of(w, i, j) for w, (i, j) in enumerate(places)]
    scores = [dot_nt(stack, here) for stack, here in zip(stacks, held)]
    largest = [jnp.max(score, axis=-1, keepdims=True) for score in scores]
    raised = [jnp.exp((score - most).astype(BF16)) for score, most in zip(scores, largest)]
    held = [below(with_ones(value).astype(BF16), nothing) for value in values]
    products = [dot(one, here) for one, here in zip(raised, held)]
    shares = [about_one_over(product[:, width : width + 1]) for product in products]
    products = [product[:, :width] * share for product, share in zip(products, shares)]
    mixed = []
    for product, rows in zip(products, groups):
        total = product[:rows]
        for h in range(1, HEADS):
            own = lane[:, :width] // head == h
            total = jnp.where(own, product[h * rows : (h + 1) * rows], total)
        mixed.append(total)
    mixed = below(*mixed).astype(BF16)

    after = (latent + dot(mixed, mix_ref[...])).astype(BF16).astype(F32)
    normed_two = normalise(after, gain_ref[:1, :]).astype(BF16)
    hidden = gelu(dot(normed_two, up_ref[...]).astype(BF16))
    result = after + dot(hidden, down_ref[...])
    for begin, (i, j) in zip(begins, places):
        part = plan[4][3 * i + j]
        piece = result[begin : begin + tokens_of(part)].astype(BF16)
        put(part, j, piece.reshape(part[1], part[3], LEV, width))


MIDDLE = [(0, 1), (1, 1), (2, 1)]
SIDES = [(0, 0), (0, 2), (2, 0), (2, 2), (1, 0), (1, 2)]


def own_rows(plan, places):
    return sum(padded(tokens_of(plan[4][3 * i + j])) for i, j in places)


def middle_kernel(
    plan,
    lat_cells,
    lon_cells,
    scalars_ref,
    recv_ref,
    north_ref,
    south_ref,
    rows_ref,
    first_ref,
    table_ref,
    lift_ref,
    gain_one_ref,
    *refs,
):
    parts_ref, *weights, out_ref, rest_ref, latent_ref, keys_ref, values_ref, stacks_ref = refs
    sums = scattered(recv_ref, first_ref, table_ref, lift_ref, plan, lon_cells)

    def sums_of(entries):
        pieces = []
        for tile, number in entries:
            start = sum(padded(tokens_of(part)) for part in plan[tile][:number])
            pieces.append(sums[tile][start : start + padded(tokens_of(plan[tile][number]))])
        return below(*pieces)

    borders = (rows_ref[...].astype(F32), north_ref, south_ref, None, None, lat_cells)
    gain = gain_one_ref[:1, :]
    entries = near_entries(MIDDLE)
    latent, normed, spans = normed_of(plan, entries, sums_of(entries), borders, gain)

    def piece_of(tile, number):
        start, count = spans[tile, number]
        return normed[start : start + count]

    def put(part, _, piece):
        out_ref[part[0] : part[0] + part[1]] = piece

    end = own_rows(plan, MIDDLE)
    many = WLAT * WLON * LEV
    tokens = []
    for i, j in MIDDLE:
        tokens.append(piece_of(4, 3 * i + j))
        if i != 1:
            tokens.append(piece_of(3 * i + 1, j))
    tokens = below(*tokens).astype(BF16)
    keys, values = dot(tokens, parts_ref[1]), dot(tokens, parts_ref[2])
    spots = [slice(w * many, (w + 1) * many) for w in range(len(MIDDLE))]
    worked(
        plan,
        MIDDLE,
        stacks_of(plan, MIDDLE, normed[:end], parts_ref[0]),
        [keys[spot] for spot in spots],
        [values[spot] for spot in spots],
        latent[:end],
        weights,
        scalars_ref,
        put,
    )
    rest_ref[...] = sums_of(far_entries(SIDES))
    entries = near_entries(SIDES)
    latent, normed, spans = normed_of(plan, entries, sums_of(entries), borders, gain)
    end = latent_ref.shape[0]
    latent_ref[...] = latent[:end]
    tokens = []
    for i, j in SIDES:
        start, count = spans[4, 3 * i + j]
        tokens.append(normed[start : start + count])
        if i != 1:
            start, count = spans[3 * i + 1, j]
            tokens.append(normed[start : start + count])
    tokens = below(*tokens).astype(BF16)
    keys_ref[...] = dot(tokens, parts_ref[1])
    values_ref[...] = dot(tokens, parts_ref[2])
    stacks_ref[...] = below(*stacks_of(plan, SIDES, normed[:end], parts_ref[0]))


def side_kernel(
    plan,
    lat_cells,
    scalars_ref,
    rest_ref,
    latent_ref,
    keys_ref,
    values_ref,
    stacks_ref,
    west_ref,
    east_ref,
    gain_one_ref,
    *refs,
):
    parts_ref, *weights, middle_ref, out_ref, held_ref, sem = refs
    left, wide = plan[4][4][2:]
    copies = [pltpu.make_async_copy(middle_ref, out_ref.at[:, left : left + wide], sem.at[2])]
    copies[0].start()
    borders = (None, None, None, west_ref, east_ref, lat_cells)
    gain = gain_one_ref[:1, :]
    _, far, spans = normed_of(plan, far_entries(SIDES), rest_ref[...], borders, gain)

    tokens = []
    for i, j in SIDES:
        for entry in [(3 + j, i)] + ([(3 * i + j, 0)] if i != 1 else []):
            start, count = spans[entry]
            tokens.append(far[start : start + count])
    tokens = below(*tokens).astype(BF16)
    keys, values = dot(tokens, parts_ref[1]), dot(tokens, parts_ref[2])
    half = WLAT * HLON * LEV
    spots = [slice(w * half, (w + 1) * half) for w in range(len(SIDES))]
    stacks, start = [], 0
    for i, j in SIDES:
        rows = HEADS * padded(tokens_of(plan[4][3 * i + j]))
        stacks.append(stacks_ref[start : start + rows, :])
        start += rows

    def put(part, j, piece):
        held_ref[j // 2, part[0] : part[0] + part[1]] = piece

    worked(
        plan,
        SIDES,
        stacks,
        [below(keys_ref[spot, :], keys[spot]) for spot in spots],
        [below(values_ref[spot, :], values[spot]) for spot in spots],
        latent_ref[...],
        weights,
        scalars_ref,
        put,
    )
    for n, number in enumerate((0, 2)):
        left, wide = plan[4][number][2:]
        copies.append(
            pltpu.make_async_copy(held_ref.at[n], out_ref.at[:, left : left + wide], sem.at[n])
        )
        copies[-1].start()
    for copy in copies:
        copy.wait()


def local(
    record_values,
    record_cell,
    record_instrument,
    block_counts,
    background,
    input_weight,
    instrument_table,
    lift_weight,
    first_gain,
    attn_weight,
    mix_weight,
    second_gain,
    up_weight,
    down_weight,
):
    lat_cells, lon_cells, _, width = background.shape
    tiles_lat = record_values.shape[1]

    sent, up, down = packed(
        record_values, record_cell, record_instrument, block_counts, background
    )
    received = lax.all_to_all(sent, ("lon", "lat"), split_axis=0, concat_axis=0, tiled=True)
    north, south = before_and_after(swapped(up, down, "lat", wraps=False), "lat")

    held = (background, input_weight, instrument_table, attn_weight, down_weight)
    held = lax.optimization_barrier((*held, first_gain, second_gain, up))
    later, input_weight, instrument_table, attn_weight, down_weight = held[:5]
    first_gain, second_gain = held[5:7]

    def columns(low, end):
        return jnp.concatenate([north[:, low:end], later[:, low:end], south[:, low:end]], axis=0)

    got = swapped(columns(0, HLON), columns(lon_cells - HLON, lon_cells), "lon", wraps=True)

    plan = rectangles(lat_cells, lon_cells)
    rows, parts, tables, gain_one, gain_two = prepared(
        plan, later, attn_weight, instrument_table, first_gain, second_gain
    )
    lat = lax.axis_index("lat")
    scalars = jnp.stack([lat == 0, lat < 0, lat == tiles_lat - 1]).astype(jnp.int32)

    def rows_in(entries):
        return sum(padded(tokens_of(plan[tile][number])) for tile, number in entries)

    weights = [parts, mix_weight, gain_two, up_weight, down_weight]
    smem = pl.BlockSpec(memory_space=pltpu.SMEM)
    vmem = pl.BlockSpec(memory_space=pltpu.VMEM)
    anywhere = pl.BlockSpec(memory_space=pl.ANY)
    params = pltpu.CompilerParams(vmem_limit_bytes=LIMIT)
    half = WLAT * HLON * LEV * len(SIDES)
    middle, rest, latent, *near = pl.pallas_call(
        functools.partial(middle_kernel, plan, lat_cells, lon_cells),
        out_shape=[
            jax.ShapeDtypeStruct((lat_cells, lon_cells - WLON, LEV, width), BF16),
            jax.ShapeDtypeStruct((rows_in(far_entries(SIDES)), PAD), F32),
            jax.ShapeDtypeStruct((own_rows(plan, SIDES), width), F32),
            jax.ShapeDtypeStruct((half, width), F32),
            jax.ShapeDtypeStruct((half, width), F32),
            jax.ShapeDtypeStruct((HEADS * own_rows(plan, SIDES), PAD), BF16),
        ],
        in_specs=[smem] + [vmem] * (8 + len(weights)),
        out_specs=[vmem] * 6,
        compiler_params=params,
        cost_estimate=pl.CostEstimate(
            flops=4 * 10**9, bytes_accessed=4 * 10**6, transcendentals=10**6
        ),
    )(
        scalars,
        received,
        north,
        south,
        rows,
        input_weight,
        tables,
        lift_weight,
        gain_one,
        *weights,
    )
    rest, *got = lax.optimization_barrier((rest, *got[::-1]))
    got = got[::-1]
    west, east = before_and_after(got, "lon")
    return pl.pallas_call(
        functools.partial(side_kernel, plan, lat_cells),
        out_shape=jax.ShapeDtypeStruct(background.shape, BF16),
        in_specs=[smem] + [vmem] * (9 + len(weights)),
        out_specs=anywhere,
        scratch_shapes=[
            pltpu.VMEM((2, lat_cells, HLON, LEV, width), BF16),
            pltpu.SemaphoreType.DMA((3,)),
        ],
        compiler_params=params,
        cost_estimate=pl.CostEstimate(
            flops=3 * 10**9, bytes_accessed=4 * 10**6, transcendentals=10**6
        ),
    )(scalars, rest, latent, *near, west, east, gain_one, *weights, middle)


def solution(mesh):
    placed = (
        P("lon", "lat", None, None),
        P("lon", "lat", None),
        P("lon", "lat", None),
        P("lon", "lat"),
        P("lat", "lon", None, None),
        P(),
        P(),
        P(),
        P(),
        P(),
        P(),
        P(),
        P(),
        P(),
    )
    return jax.shard_map(
        local, mesh=mesh, in_specs=placed, out_specs=P("lat", "lon", None, None), check_vma=False
    )
```

```python
import functools

import jax
import jax.numpy as jnp
from jax import lax
from jax.experimental import pallas as pl
from jax.experimental.pallas import tpu as pltpu
from jax.sharding import PartitionSpec as P

HEADS = 6
INSTR = 8
LEV = 2
WLAT = 6
WLON = 12
HLAT = WLAT // 2
HLON = WLON // 2
LANES = 128
PAD = 256
CHUNK = 32
LIMIT = 40 * 2**20
BF16 = jnp.bfloat16
F32 = jnp.float32

AROUND = [(dy, dx) for dy in (-1, 0, 1) for dx in (-1, 0, 1)]
ROWS = INSTR * len(AROUND)
COLS = ROWS + len(AROUND)


def swapped(up, down, axis, wraps):
    count = lax.axis_size(axis)
    even = lax.axis_index(axis) % 2 == 0
    got = []
    for first, mine in ((0, jnp.where(even, down, up)), (1, jnp.where(even, up, down))):
        pairs = []
        for low in range(first, count, 2):
            high = (low + 1) % count
            if high > low or wraps:
                pairs += [(low, high), (high, low)]
        got.append(lax.ppermute(mine, axis, pairs))
    return got


def before_and_after(got, axis):
    even = lax.axis_index(axis) % 2 == 0
    return jnp.where(even, got[1], got[0]), jnp.where(even, got[0], got[1])


def rectangles(lat_cells, lon_cells):
    lat = {-1: [(lat_cells - HLAT, HLAT)], 1: [(0, HLAT)]}
    lat[0] = [(0, HLAT), (HLAT, lat_cells - WLAT), (lat_cells - HLAT, HLAT)]
    lon = {-1: [(lon_cells - HLON, HLON)], 1: [(0, HLON)]}
    lon[0] = [(0, HLON), (HLON, lon_cells - WLON), (lon_cells - HLON, HLON)]
    return [
        [(top, high, left, wide) for top, high in lat[dy] for left, wide in lon[dx]]
        for dy, dx in AROUND
    ]


def tokens_of(part):
    return part[1] * part[3] * LEV


def padded(count):
    return -(-count // 8) * 8


def gelu(x):
    half = 0.5 * x
    inner = x * (0.7978845608028654 + 0.035677408136300125 * (x * x))
    return half + half * jnp.tanh(inner)


def normalise(wide, gain):
    average = jnp.mean(wide, axis=-1, keepdims=True)
    centred = wide - average
    spread = jnp.mean(centred * centred, axis=-1, keepdims=True)
    return centred * lax.rsqrt(spread + 1e-05) * gain


def dot(a, b):
    return jnp.dot(a, b, preferred_element_type=F32)


def dot_nt(a, b):
    return lax.dot_general(a, b, (((1,), (1,)), ((), ())), preferred_element_type=F32)


def about_one_over(x):
    return pl.reciprocal(x, approx=True)


def with_ones(tensor):
    ones = jnp.ones((tensor.shape[0], PAD - tensor.shape[1]), tensor.dtype)
    return jnp.concatenate([tensor, ones], axis=1).astype(BF16)


def below(*pieces):
    return jnp.concatenate(pieces, axis=0) if len(pieces) > 1 else pieces[0]


def pack_kernel(
    values_ref,
    cell_ref,
    tag_ref,
    count_ref,
    back_ref,
    *refs,
):
    out_ref, up_ref, down_ref, values, cells, tags, held, sem = refs
    tiles_lon, tiles_lat, capacity, _ = values_ref.shape
    lat_cells, lon_cells = back_ref.shape[:2]
    strips = [
        (back_ref.at[:HLAT], up_ref),
        (back_ref.at[lat_cells - HLAT :], down_ref),
    ]
    copies = [
        pltpu.make_async_copy(cell_ref, cells, sem.at[0]),
        pltpu.make_async_copy(tag_ref, tags, sem.at[1]),
        pltpu.make_async_copy(count_ref, held, sem.at[2]),
        pltpu.make_async_copy(values_ref, values, sem.at[3]),
    ]
    copies += [
        pltpu.make_async_copy(source, strip, sem.at[4 + n])
        for n, (source, strip) in enumerate(strips)
    ]
    for copy in copies:
        copy.start()
    for copy in copies[:3]:
        copy.wait()
    counts = below(*[held[tile : tile + 1, :] for tile in range(tiles_lat) for _ in range(capacity)])
    cell = cells[...]
    slot = lax.broadcasted_iota(jnp.int32, cell.shape, 0) % capacity
    row = cell // lon_cells
    fields = [jnp.where(slot < counts, row, 255), cell - row * lon_cells, tags[...]]
    rows, columns, kinds = (field.astype(F32) for field in fields)
    lane = lax.broadcasted_iota(jnp.int32, (cell.shape[0], LANES), 1)
    kind_of = (lane % INSTR).astype(F32)
    marks = [
        ((lane < ROWS) & (lane // INSTR == n)) | (lane == ROWS + n) | (lane == COLS + n)
        for n in range(len(AROUND))
    ]
    turned = []
    for lon in range(tiles_lon):
        meta = jnp.where(kind_of == kinds[:, lon : lon + 1], 1.0, 0.0)
        meta = jnp.where(lane >= ROWS, rows[:, lon : lon + 1], meta)
        meta = jnp.where(lane >= COLS, columns[:, lon : lon + 1], meta)
        turns = {0: meta}
        for dy in (-1, 1):
            by = dy * capacity % meta.shape[0]
            turns[dy] = below(meta[by:], meta[:by])
        turned.append(turns)
    for lon in range(tiles_lon):
        meta = jnp.zeros(lane.shape, F32)
        for mark, (dy, dx) in zip(marks, AROUND):
            meta = jnp.where(mark, turned[(lon + dx) % tiles_lon][dy], meta)
        out_ref[lon, :, len(AROUND)] = meta.astype(BF16).reshape(tiles_lat, capacity, LANES)
    copies[3].wait()
    for n, (dy, dx) in enumerate(AROUND):
        spans = {0: [(0, tiles_lat)], 1: [(0, tiles_lat - 1), (tiles_lat - 1, tiles_lat)]}
        spans[-1] = [(0, 1), (1, tiles_lat)]

        def copy_tiles(lon, n=n, dx=dx, dy=dy, spans=spans[dy]):
            source = lax.rem(lon + dx + tiles_lon, tiles_lon)
            for low, end in spans:
                first = (low + dy) % tiles_lat
                out_ref[lon, low:end, n] = values[source, first : first + end - low]

        if tiles_lon <= 8:
            for lon in range(tiles_lon):
                copy_tiles(lon)
        else:
            pl.loop(0, tiles_lon)(copy_tiles)
    for copy in copies[4:]:
        copy.wait()


def packed(record_values, record_cell, record_instrument, block_counts, background):
    tiles_lon, tiles_lat, capacity, wide = record_values.shape
    anywhere = pl.BlockSpec(memory_space=pltpu.HBM)
    ints = pltpu.VMEM((tiles_lat * capacity, tiles_lon), jnp.int32)
    shape = (tiles_lon, tiles_lat, len(AROUND) + 1, capacity, wide)
    lat_cells, lon_cells, levels, width = background.shape
    across = jax.ShapeDtypeStruct((HLAT, lon_cells, levels, width), BF16)
    out, *strips = pl.pallas_call(
        pack_kernel,
        out_shape=[jax.ShapeDtypeStruct(shape, BF16), across, across],
        in_specs=[anywhere] * 5,
        out_specs=[pl.BlockSpec(memory_space=pltpu.VMEM)] * 3,
        scratch_shapes=[
            pltpu.VMEM(record_values.shape, BF16),
            ints,
            ints,
            pltpu.VMEM((tiles_lat, tiles_lon), jnp.int32),
            pltpu.SemaphoreType.DMA((6,)),
        ],
        compiler_params=pltpu.CompilerParams(vmem_limit_bytes=56 * 2**20),
        cost_estimate=pl.CostEstimate(
            flops=20 * 10**9, bytes_accessed=10**6, transcendentals=0
        ),
    )(
        record_values,
        record_cell.transpose(1, 2, 0).reshape(-1, tiles_lon),
        record_instrument.transpose(1, 2, 0).reshape(-1, tiles_lon),
        block_counts.T,
        background,
    )
    return out.reshape((-1,) + shape[2:]), *strips


def token_codes(part, lon_cells):
    top, high, left, wide = part
    count = tokens_of(part)
    place = lax.broadcasted_iota(jnp.int32, (padded(count), LANES), 0)
    code = place + (top * lon_cells + left) * LEV
    for row in range(1, high):
        step = (lon_cells - wide) * LEV
        code = code + jnp.where(place >= row * wide * LEV, step, 0)
    return jnp.where(place < count, code, -8).astype(F32)


def near_entries(windows):
    own = [(4, 3 * i + j) for i, j in windows]
    return own + [(3 * i + 1, j) for i, j in windows if i != 1]


def far_entries(windows):
    beside = [(3 + j, i) for i, j in windows if j != 1]
    return beside + [(3 * i + j, 0) for i, j in windows if i != 1 and j != 1]


def scattered(recv_ref, first_ref, table_ref, lift_ref, plan, lon_cells):
    sources, _, capacity, _ = recv_ref.shape
    width = first_ref.shape[1]
    chunk = min(CHUNK, sources)
    slots = chunk * capacity
    first, lift = below(first_ref[...], table_ref[...]), lift_ref[...]
    lane = lax.broadcasted_iota(jnp.int32, (16, LANES), 1)
    sub = lax.broadcasted_iota(jnp.int32, (16, LANES), 0)
    weigh = jnp.where(lane == ROWS + sub, float(lon_cells * LEV), 0.0)
    weigh = jnp.where(lane == COLS + sub, float(LEV), weigh).astype(BF16)
    codes = [below(*[token_codes(part, lon_cells) for part in parts]) for parts in plan]

    def scatter(begin):
        meta = recv_ref[pl.ds(begin, chunk), len(AROUND)].reshape(slots, LANES)
        records = below(
            *[
                recv_ref[pl.ds(begin, chunk), n].reshape(slots, LANES)
                for n in range(len(AROUND))
            ]
        )
        lane = lax.broadcasted_iota(jnp.int32, meta.shape, 1) // INSTR
        wide = meta.astype(F32)
        chosen = below(*[jnp.where(lane == n, wide, 0.0) for n in range(len(AROUND))]).astype(BF16)
        both = jnp.concatenate([records, chosen], axis=1)
        encoded = gelu(dot(both, first).astype(BF16))
        lifted = gelu(dot(encoded, lift).astype(BF16))
        tokens = dot_nt(weigh, meta)
        hots, parts = [], []
        for n in range(len(AROUND)):
            token = tokens[n : n + 1]
            token = jnp.concatenate([token + float(level) for level in range(LEV)], axis=1)
            if token.shape[1] == LANES:
                hot = codes[n] == token
            else:
                hot = codes[n][:, :1] == token
            hots.append(jnp.where(hot, 1.0, 0.0).astype(BF16))
        for n in range(len(AROUND)):
            part = lifted[n * slots : (n + 1) * slots]
            parts.append(
                with_ones(
                    below(*[part[:, level * width : (level + 1) * width] for level in range(LEV)])
                )
            )
        sums = [dot(hot, part) for hot, part in zip(hots, parts)]
        return tuple(sums)

    sums = scatter(0)
    if sources > chunk:
        sums = lax.fori_loop(
            1,
            sources // chunk,
            lambda step, total: tuple(a + b for a, b in zip(total, scatter(step * chunk))),
            sums,
        )
    return sums


def prepare_kernel(
    plan,
    back_ref,
    attn_ref,
    table_ref,
    one_ref,
    two_ref,
    rows_ref,
    parts_ref,
    tables_ref,
    gain_one_ref,
    gain_two_ref,
):
    width = back_ref.shape[3]
    pieces = []
    for top, high, left, wide in plan[4]:
        count = high * wide * LEV
        piece = back_ref[top : top + high, left : left + wide].reshape(count, width).astype(F32)
        if padded(count) > count:
            piece = below(piece, jnp.zeros((padded(count) - count, width), F32))
        pieces.append(piece)
    rows_ref[...] = below(*pieces).astype(BF16)
    tables_ref[...] = below(*[table_ref[...].astype(F32)] * (LANES // INSTR)).astype(BF16)
    for gain, ref in ((one_ref, gain_one_ref), (two_ref, gain_two_ref)):
        ref[...] = jnp.broadcast_to(gain[...].astype(F32).reshape(1, width), ref.shape)
    for n in range(3):
        parts_ref[n] = attn_ref[:, n * width : (n + 1) * width]


def prepared(plan, background, attn_weight, instrument_table, first_gain, second_gain):
    width = background.shape[3]
    rows = sum(padded(tokens_of(part)) for part in plan[4])
    vmem = pl.BlockSpec(memory_space=pltpu.VMEM)
    return pl.pallas_call(
        functools.partial(prepare_kernel, plan),
        out_shape=[
            jax.ShapeDtypeStruct((rows, width), BF16),
            jax.ShapeDtypeStruct((3, width, width), BF16),
            jax.ShapeDtypeStruct((LANES, width), BF16),
            jax.ShapeDtypeStruct((8, width), F32),
            jax.ShapeDtypeStruct((8, width), F32),
        ],
        in_specs=[vmem] * 5,
        out_specs=[vmem] * 5,
        compiler_params=pltpu.CompilerParams(vmem_limit_bytes=LIMIT),
        cost_estimate=pl.CostEstimate(flops=10**9, bytes_accessed=10**6, transcendentals=0),
    )(background, attn_weight, instrument_table, first_gain, second_gain)


def normed_of(plan, entries, sums, borders, gain):
    rows, north_ref, south_ref, west_ref, east_ref, lat_cells = borders
    width = gain.shape[1]
    pieces, spans, start = [], {}, 0
    for tile, number in entries:
        dy, dx = AROUND[tile]
        top, high, left, wide = plan[tile][number]
        count = high * wide * LEV
        full = padded(count)
        if tile == 4:
            begin = sum(padded(tokens_of(part)) for part in plan[4][:number])
            piece = rows[begin : begin + full]
        else:
            if dx:
                ref = west_ref if dx < 0 else east_ref
                top, left = {-1: 0, 0: top + HLAT, 1: lat_cells + HLAT}[dy], 0
            else:
                ref, top = (north_ref, 0) if dy < 0 else (south_ref, 0)
            block = ref(top, high) if dx else ref[top : top + high, left : left + wide]
            piece = block.reshape(count, width).astype(F32)
            if full > count:
                piece = below(piece, jnp.zeros((full - count, width), F32))
        pieces.append(piece)
        spans[tile, number] = (start, count)
        start += full
    tally = 1.0 + sums[:, width : width + 1]
    share = about_one_over(tally)
    share = share * (2.0 - tally * share)
    latent = ((below(*pieces) + sums[:, :width]) * share).astype(BF16).astype(F32)
    return latent, normalise(latent, gain), spans


def stacks_of(plan, places, own_normed, weight):
    width = weight.shape[0]
    head = width // HEADS
    query = dot(own_normed.astype(BF16), weight) * head ** (-0.5)
    query = jnp.concatenate([query, jnp.ones((query.shape[0], PAD - width), F32)], axis=1)
    lane = lax.broadcasted_iota(jnp.int32, (1, PAD), 1)
    stacks, begin = [], 0
    for i, j in places:
        rows = padded(tokens_of(plan[4][3 * i + j]))
        part = query[begin : begin + rows]
        begin += rows
        stacks.append(
            below(
                *[jnp.where((lane // head == h) | (lane >= width), part, 0.0) for h in range(HEADS)]
            ).astype(BF16)
        )
    return stacks


def worked(plan, places, stacks, keys, values, latent, weights, scalars_ref, put):
    mix_ref, gain_ref, up_ref, down_ref = weights
    width = mix_ref.shape[0]
    head = width // HEADS
    groups = [padded(tokens_of(plan[4][3 * i + j])) for i, j in places]
    lane = lax.broadcasted_iota(jnp.int32, (1, PAD), 1)
    many = WLAT * WLON * LEV
    corner = HLAT * HLON * LEV
    key = lax.broadcasted_iota(jnp.int32, (many, PAD - width), 0)
    spare = lax.broadcasted_iota(jnp.int32, (many, PAD - width), 1)
    unused = lax.broadcasted_iota(jnp.int32, (PAD - many, PAD), 1)
    unused = jnp.where(unused == width, -3e38, 0.0).astype(BF16)
    nothing = jnp.zeros((PAD - many, PAD), BF16)

    def keys_of(w, i, j):
        bias = jnp.zeros((many, PAD - width), F32)
        if i != 1:
            if j == 1:
                inside = key < 2 * corner
            else:
                inside = (key < corner) | ((key >= 2 * corner) & (key < 3 * corner))
            bias = jnp.where(inside | (spare > 0), 0.0, -3e38) * scalars_ref[i].astype(F32)
        here = jnp.concatenate([keys[w], bias], axis=1)
        return below(here.astype(BF16), unused)

    begins = [sum(groups[:w]) for w in range(len(groups))]
    held = [keys_of(w, i, j) for w, (i, j) in enumerate(places)]
    scores = [dot_nt(stack, here) for stack, here in zip(stacks, held)]
    largest = [jnp.max(score, axis=-1, keepdims=True) for score in scores]
    raised = [jnp.exp((score - most).astype(BF16)) for score, most in zip(scores, largest)]
    held = [below(with_ones(value).astype(BF16), nothing) for value in values]
    products = [dot(one, here) for one, here in zip(raised, held)]
    shares = [about_one_over(product[:, width : width + 1]) for product in products]
    products = [product[:, :width] * share for product, share in zip(products, shares)]
    mixed = []
    for product, rows in zip(products, groups):
        total = product[:rows]
        for h in range(1, HEADS):
            own = lane[:, :width] // head == h
            total = jnp.where(own, product[h * rows : (h + 1) * rows], total)
        mixed.append(total)
    mixed = below(*mixed).astype(BF16)

    after = (latent + dot(mixed, mix_ref[...])).astype(BF16).astype(F32)
    normed_two = normalise(after, gain_ref[:1, :]).astype(BF16)
    hidden = gelu(dot(normed_two, up_ref[...]).astype(BF16))
    result = after + dot(hidden, down_ref[...])
    for begin, (i, j) in zip(begins, places):
        part = plan[4][3 * i + j]
        piece = result[begin : begin + tokens_of(part)].astype(BF16)
        put(part, j, piece.reshape(part[1], part[3], LEV, width))


MIDDLE = [(0, 1), (1, 1), (2, 1)]
SIDES = [(0, 0), (0, 2), (2, 0), (2, 2), (1, 0), (1, 2)]


def own_rows(plan, places):
    return sum(padded(tokens_of(plan[4][3 * i + j])) for i, j in places)


def middle_kernel(
    plan,
    lat_cells,
    lon_cells,
    scalars_ref,
    recv_ref,
    north_ref,
    south_ref,
    rows_ref,
    first_ref,
    table_ref,
    lift_ref,
    gain_one_ref,
    *refs,
):
    parts_ref, *weights, out_ref, rest_ref, latent_ref, keys_ref, values_ref, stacks_ref = refs
    sums = scattered(recv_ref, first_ref, table_ref, lift_ref, plan, lon_cells)

    def sums_of(entries):
        pieces = []
        for tile, number in entries:
            start = sum(padded(tokens_of(part)) for part in plan[tile][:number])
            pieces.append(sums[tile][start : start + padded(tokens_of(plan[tile][number]))])
        return below(*pieces)

    borders = (rows_ref[...].astype(F32), north_ref, south_ref, None, None, lat_cells)
    gain = gain_one_ref[:1, :]
    entries = near_entries(MIDDLE)
    latent, normed, spans = normed_of(plan, entries, sums_of(entries), borders, gain)

    def piece_of(tile, number):
        start, count = spans[tile, number]
        return normed[start : start + count]

    def put(part, _, piece):
        out_ref[part[0] : part[0] + part[1]] = piece

    end = own_rows(plan, MIDDLE)
    many = WLAT * WLON * LEV
    tokens = []
    for i, j in MIDDLE:
        tokens.append(piece_of(4, 3 * i + j))
        if i != 1:
            tokens.append(piece_of(3 * i + 1, j))
    tokens = below(*tokens).astype(BF16)
    keys, values = dot(tokens, parts_ref[1]), dot(tokens, parts_ref[2])
    spots = [slice(w * many, (w + 1) * many) for w in range(len(MIDDLE))]
    worked(
        plan,
        MIDDLE,
        stacks_of(plan, MIDDLE, normed[:end], parts_ref[0]),
        [keys[spot] for spot in spots],
        [values[spot] for spot in spots],
        latent[:end],
        weights,
        scalars_ref,
        put,
    )
    rest_ref[...] = sums_of(far_entries(SIDES))
    entries = near_entries(SIDES)
    latent, normed, spans = normed_of(plan, entries, sums_of(entries), borders, gain)
    end = latent_ref.shape[0]
    latent_ref[...] = latent[:end]
    tokens = []
    for i, j in SIDES:
        start, count = spans[4, 3 * i + j]
        tokens.append(normed[start : start + count])
        if i != 1:
            start, count = spans[3 * i + 1, j]
            tokens.append(normed[start : start + count])
    tokens = below(*tokens).astype(BF16)
    keys_ref[...] = dot(tokens, parts_ref[1])
    values_ref[...] = dot(tokens, parts_ref[2])
    stacks_ref[...] = below(*stacks_of(plan, SIDES, normed[:end], parts_ref[0]))


def side_kernel(
    plan,
    lat_cells,
    scalars_ref,
    rest_ref,
    latent_ref,
    keys_ref,
    values_ref,
    stacks_ref,
    one_ref,
    two_ref,
    gain_one_ref,
    *refs,
):
    parts_ref, *weights, middle_ref, out_ref, held_ref, sem = refs
    left, wide = plan[4][4][2:]
    copies = [pltpu.make_async_copy(middle_ref, out_ref.at[:, left : left + wide], sem.at[2])]
    copies[0].start()
    even = scalars_ref[3] == 1

    def west(top, high):
        return jnp.where(even, two_ref[top : top + high], one_ref[top : top + high])

    def east(top, high):
        return jnp.where(even, one_ref[top : top + high], two_ref[top : top + high])

    borders = (None, None, None, west, east, lat_cells)
    gain = gain_one_ref[:1, :]
    _, far, spans = normed_of(plan, far_entries(SIDES), rest_ref[...], borders, gain)

    tokens = []
    for i, j in SIDES:
        for entry in [(3 + j, i)] + ([(3 * i + j, 0)] if i != 1 else []):
            start, count = spans[entry]
            tokens.append(far[start : start + count])
    tokens = below(*tokens).astype(BF16)
    keys, values = dot(tokens, parts_ref[1]), dot(tokens, parts_ref[2])
    half = WLAT * HLON * LEV
    spots = [slice(w * half, (w + 1) * half) for w in range(len(SIDES))]
    stacks, start = [], 0
    for i, j in SIDES:
        rows = HEADS * padded(tokens_of(plan[4][3 * i + j]))
        stacks.append(stacks_ref[start : start + rows, :])
        start += rows

    def put(part, j, piece):
        held_ref[j // 2, part[0] : part[0] + part[1]] = piece

    worked(
        plan,
        SIDES,
        stacks,
        [below(keys_ref[spot, :], keys[spot]) for spot in spots],
        [below(values_ref[spot, :], values[spot]) for spot in spots],
        latent_ref[...],
        weights,
        scalars_ref,
        put,
    )
    for n, number in enumerate((0, 2)):
        left, wide = plan[4][number][2:]
        copies.append(
            pltpu.make_async_copy(held_ref.at[n], out_ref.at[:, left : left + wide], sem.at[n])
        )
        copies[-1].start()
    for copy in copies:
        copy.wait()


def local(
    record_values,
    record_cell,
    record_instrument,
    block_counts,
    background,
    input_weight,
    instrument_table,
    lift_weight,
    first_gain,
    attn_weight,
    mix_weight,
    second_gain,
    up_weight,
    down_weight,
):
    lat_cells, lon_cells, _, width = background.shape
    tiles_lat = record_values.shape[1]

    sent, up, down = packed(
        record_values, record_cell, record_instrument, block_counts, background
    )
    received = lax.all_to_all(sent, ("lon", "lat"), split_axis=0, concat_axis=0, tiled=True)
    north, south = before_and_after(swapped(up, down, "lat", wraps=False), "lat")

    held = (background, input_weight, instrument_table, attn_weight, down_weight)
    held = lax.optimization_barrier((*held, first_gain, second_gain, up))
    later, input_weight, instrument_table, attn_weight, down_weight = held[:5]
    first_gain, second_gain = held[5:7]

    def columns(low, end):
        return jnp.concatenate([north[:, low:end], later[:, low:end], south[:, low:end]], axis=0)

    got = swapped(columns(0, HLON), columns(lon_cells - HLON, lon_cells), "lon", wraps=True)

    plan = rectangles(lat_cells, lon_cells)
    rows, parts, tables, gain_one, gain_two = prepared(
        plan, later, attn_weight, instrument_table, first_gain, second_gain
    )
    lat = lax.axis_index("lat")
    even = lax.axis_index("lon") % 2 == 0
    scalars = jnp.stack([lat == 0, lat < 0, lat == tiles_lat - 1, even]).astype(jnp.int32)

    def rows_in(entries):
        return sum(padded(tokens_of(plan[tile][number])) for tile, number in entries)

    weights = [parts, mix_weight, gain_two, up_weight, down_weight]
    smem = pl.BlockSpec(memory_space=pltpu.SMEM)
    vmem = pl.BlockSpec(memory_space=pltpu.VMEM)
    anywhere = pl.BlockSpec(memory_space=pl.ANY)
    params = pltpu.CompilerParams(vmem_limit_bytes=LIMIT)
    half = WLAT * HLON * LEV * len(SIDES)
    middle, rest, latent, *near = pl.pallas_call(
        functools.partial(middle_kernel, plan, lat_cells, lon_cells),
        out_shape=[
            jax.ShapeDtypeStruct((lat_cells, lon_cells - WLON, LEV, width), BF16),
            jax.ShapeDtypeStruct((rows_in(far_entries(SIDES)), PAD), F32),
            jax.ShapeDtypeStruct((own_rows(plan, SIDES), width), F32),
            jax.ShapeDtypeStruct((half, width), F32),
            jax.ShapeDtypeStruct((half, width), F32),
            jax.ShapeDtypeStruct((HEADS * own_rows(plan, SIDES), PAD), BF16),
        ],
        in_specs=[smem] + [vmem] * (8 + len(weights)),
        out_specs=[vmem] * 6,
        compiler_params=params,
        cost_estimate=pl.CostEstimate(
            flops=4 * 10**9, bytes_accessed=4 * 10**6, transcendentals=10**6
        ),
    )(
        scalars,
        received,
        north,
        south,
        rows,
        input_weight,
        tables,
        lift_weight,
        gain_one,
        *weights,
    )
    rest, *got = lax.optimization_barrier((rest, *got[::-1]))
    got = got[::-1]
    return pl.pallas_call(
        functools.partial(side_kernel, plan, lat_cells),
        out_shape=jax.ShapeDtypeStruct(background.shape, BF16),
        in_specs=[smem] + [vmem] * (9 + len(weights)),
        out_specs=anywhere,
        scratch_shapes=[
            pltpu.VMEM((2, lat_cells, HLON, LEV, width), BF16),
            pltpu.SemaphoreType.DMA((3,)),
        ],
        compiler_params=params,
        cost_estimate=pl.CostEstimate(
            flops=3 * 10**9, bytes_accessed=4 * 10**6, transcendentals=10**6
        ),
    )(scalars, rest, latent, *near, *got, gain_one, *weights, middle)


def solution(mesh):
    placed = (
        P("lon", "lat", None, None),
        P("lon", "lat", None),
        P("lon", "lat", None),
        P("lon", "lat"),
        P("lat", "lon", None, None),
        P(),
        P(),
        P(),
        P(),
        P(),
        P(),
        P(),
        P(),
        P(),
    )
    return jax.shard_map(
        local, mesh=mesh, in_specs=placed, out_specs=P("lat", "lon", None, None), check_vma=False
    )
```

```python
import functools

import jax
import jax.numpy as jnp
from jax import lax
from jax.experimental import pallas as pl
from jax.experimental.pallas import tpu as pltpu
from jax.sharding import PartitionSpec as P

HEADS = 6
INSTR = 8
LEV = 2
WLAT = 6
WLON = 12
HLAT = WLAT // 2
HLON = WLON // 2
LANES = 128
PAD = 256
CHUNK = 32
LIMIT = 40 * 2**20
BF16 = jnp.bfloat16
F32 = jnp.float32

AROUND = [(dy, dx) for dy in (-1, 0, 1) for dx in (-1, 0, 1)]
ROWS = INSTR * len(AROUND)
COLS = ROWS + len(AROUND)


def swapped_as(mine, axis, wraps):
    count = lax.axis_size(axis)
    got = []
    for first, one in enumerate(mine):
        pairs = []
        for low in range(first, count, 2):
            high = (low + 1) % count
            if high > low or wraps:
                pairs += [(low, high), (high, low)]
        got.append(lax.ppermute(one, axis, pairs))
    return got


def swapped(up, down, axis, wraps):
    even = lax.axis_index(axis) % 2 == 0
    return swapped_as((jnp.where(even, down, up), jnp.where(even, up, down)), axis, wraps)


def rectangles(lat_cells, lon_cells):
    lat = {-1: [(lat_cells - HLAT, HLAT)], 1: [(0, HLAT)]}
    lat[0] = [(0, HLAT), (HLAT, lat_cells - WLAT), (lat_cells - HLAT, HLAT)]
    lon = {-1: [(lon_cells - HLON, HLON)], 1: [(0, HLON)]}
    lon[0] = [(0, HLON), (HLON, lon_cells - WLON), (lon_cells - HLON, HLON)]
    return [
        [(top, high, left, wide) for top, high in lat[dy] for left, wide in lon[dx]]
        for dy, dx in AROUND
    ]


def tokens_of(part):
    return part[1] * part[3] * LEV


def padded(count):
    return -(-count // 8) * 8


def gelu(x):
    half = 0.5 * x
    inner = x * (0.7978845608028654 + 0.035677408136300125 * (x * x))
    return half + half * jnp.tanh(inner)


def normalise(wide, gain):
    average = jnp.mean(wide, axis=-1, keepdims=True)
    centred = wide - average
    spread = jnp.mean(centred * centred, axis=-1, keepdims=True)
    return centred * lax.rsqrt(spread + 1e-05) * gain


def dot(a, b):
    return jnp.dot(a, b, preferred_element_type=F32)


def dot_nt(a, b):
    return lax.dot_general(a, b, (((1,), (1,)), ((), ())), preferred_element_type=F32)


def about_one_over(x):
    return pl.reciprocal(x, approx=True)


def with_ones(tensor):
    ones = jnp.ones((tensor.shape[0], PAD - tensor.shape[1]), tensor.dtype)
    return jnp.concatenate([tensor, ones], axis=1).astype(BF16)


def below(*pieces):
    return jnp.concatenate(pieces, axis=0) if len(pieces) > 1 else pieces[0]


def pack_kernel(
    values_ref,
    cell_ref,
    tag_ref,
    count_ref,
    back_ref,
    *refs,
):
    out_ref, up_ref, down_ref, values, cells, tags, held, sem = refs
    tiles_lon, tiles_lat, capacity, _ = values_ref.shape
    lat_cells, lon_cells = back_ref.shape[:2]
    strips = [
        (back_ref.at[:HLAT], up_ref),
        (back_ref.at[lat_cells - HLAT :], down_ref),
    ]
    copies = [
        pltpu.make_async_copy(cell_ref, cells, sem.at[0]),
        pltpu.make_async_copy(tag_ref, tags, sem.at[1]),
        pltpu.make_async_copy(count_ref, held, sem.at[2]),
        pltpu.make_async_copy(values_ref, values, sem.at[3]),
    ]
    copies += [
        pltpu.make_async_copy(source, strip, sem.at[4 + n])
        for n, (source, strip) in enumerate(strips)
    ]
    for copy in copies:
        copy.start()
    for copy in copies[:3]:
        copy.wait()
    counts = below(*[held[tile : tile + 1, :] for tile in range(tiles_lat) for _ in range(capacity)])
    cell = cells[...]
    slot = lax.broadcasted_iota(jnp.int32, cell.shape, 0) % capacity
    row = cell // lon_cells
    fields = [jnp.where(slot < counts, row, 255), cell - row * lon_cells, tags[...]]
    rows, columns, kinds = (field.astype(F32) for field in fields)
    lane = lax.broadcasted_iota(jnp.int32, (cell.shape[0], LANES), 1)
    kind_of = (lane % INSTR).astype(F32)
    marks = [
        ((lane < ROWS) & (lane // INSTR == n)) | (lane == ROWS + n) | (lane == COLS + n)
        for n in range(len(AROUND))
    ]
    turned = []
    for lon in range(tiles_lon):
        meta = jnp.where(kind_of == kinds[:, lon : lon + 1], 1.0, 0.0)
        meta = jnp.where(lane >= ROWS, rows[:, lon : lon + 1], meta)
        meta = jnp.where(lane >= COLS, columns[:, lon : lon + 1], meta)
        turns = {0: meta}
        for dy in (-1, 1):
            by = dy * capacity % meta.shape[0]
            turns[dy] = below(meta[by:], meta[:by])
        turned.append(turns)
    for lon in range(tiles_lon):
        meta = jnp.zeros(lane.shape, F32)
        for mark, (dy, dx) in zip(marks, AROUND):
            meta = jnp.where(mark, turned[(lon + dx) % tiles_lon][dy], meta)
        out_ref[lon, :, len(AROUND)] = meta.astype(BF16).reshape(tiles_lat, capacity, LANES)
    copies[3].wait()
    for n, (dy, dx) in enumerate(AROUND):
        spans = {0: [(0, tiles_lat)], 1: [(0, tiles_lat - 1), (tiles_lat - 1, tiles_lat)]}
        spans[-1] = [(0, 1), (1, tiles_lat)]

        def copy_tiles(lon, n=n, dx=dx, dy=dy, spans=spans[dy]):
            source = lax.rem(lon + dx + tiles_lon, tiles_lon)
            for low, end in spans:
                first = (low + dy) % tiles_lat
                out_ref[lon, low:end, n] = values[source, first : first + end - low]

        if tiles_lon <= 8:
            for lon in range(tiles_lon):
                copy_tiles(lon)
        else:
            pl.loop(0, tiles_lon)(copy_tiles)
    for copy in copies[4:]:
        copy.wait()


def packed(record_values, record_cell, record_instrument, block_counts, background):
    tiles_lon, tiles_lat, capacity, wide = record_values.shape
    anywhere = pl.BlockSpec(memory_space=pltpu.HBM)
    ints = pltpu.VMEM((tiles_lat * capacity, tiles_lon), jnp.int32)
    shape = (tiles_lon, tiles_lat, len(AROUND) + 1, capacity, wide)
    lat_cells, lon_cells, levels, width = background.shape
    across = jax.ShapeDtypeStruct((HLAT, lon_cells, levels, width), BF16)
    out, *strips = pl.pallas_call(
        pack_kernel,
        out_shape=[jax.ShapeDtypeStruct(shape, BF16), across, across],
        in_specs=[anywhere] * 5,
        out_specs=[pl.BlockSpec(memory_space=pltpu.VMEM)] * 3,
        scratch_shapes=[
            pltpu.VMEM(record_values.shape, BF16),
            ints,
            ints,
            pltpu.VMEM((tiles_lat, tiles_lon), jnp.int32),
            pltpu.SemaphoreType.DMA((6,)),
        ],
        compiler_params=pltpu.CompilerParams(vmem_limit_bytes=56 * 2**20),
        cost_estimate=pl.CostEstimate(
            flops=20 * 10**9, bytes_accessed=10**6, transcendentals=0
        ),
    )(
        record_values,
        record_cell.transpose(1, 2, 0).reshape(-1, tiles_lon),
        record_instrument.transpose(1, 2, 0).reshape(-1, tiles_lon),
        block_counts.T,
        background,
    )
    return out.reshape((-1,) + shape[2:]), *strips


def token_codes(part, lon_cells):
    top, high, left, wide = part
    count = tokens_of(part)
    place = lax.broadcasted_iota(jnp.int32, (padded(count), LANES), 0)
    code = place + (top * lon_cells + left) * LEV
    for row in range(1, high):
        step = (lon_cells - wide) * LEV
        code = code + jnp.where(place >= row * wide * LEV, step, 0)
    return jnp.where(place < count, code, -8).astype(F32)


def near_entries(windows):
    own = [(4, 3 * i + j) for i, j in windows]
    return own + [(3 * i + 1, j) for i, j in windows if i != 1]


def far_entries(windows):
    beside = [(3 + j, i) for i, j in windows if j != 1]
    return beside + [(3 * i + j, 0) for i, j in windows if i != 1 and j != 1]


def scattered(recv_ref, first_ref, table_ref, lift_ref, plan, lon_cells):
    sources, _, capacity, _ = recv_ref.shape
    width = first_ref.shape[1]
    chunk = min(CHUNK, sources)
    slots = chunk * capacity
    first, lift = below(first_ref[...], table_ref[...]), lift_ref[...]
    lane = lax.broadcasted_iota(jnp.int32, (16, LANES), 1)
    sub = lax.broadcasted_iota(jnp.int32, (16, LANES), 0)
    weigh = jnp.where(lane == ROWS + sub, float(lon_cells * LEV), 0.0)
    weigh = jnp.where(lane == COLS + sub, float(LEV), weigh).astype(BF16)
    codes = [below(*[token_codes(part, lon_cells) for part in parts]) for parts in plan]

    def scatter(begin):
        meta = recv_ref[pl.ds(begin, chunk), len(AROUND)].reshape(slots, LANES)
        records = below(
            *[
                recv_ref[pl.ds(begin, chunk), n].reshape(slots, LANES)
                for n in range(len(AROUND))
            ]
        )
        lane = lax.broadcasted_iota(jnp.int32, meta.shape, 1) // INSTR
        wide = meta.astype(F32)
        chosen = below(*[jnp.where(lane == n, wide, 0.0) for n in range(len(AROUND))]).astype(BF16)
        both = jnp.concatenate([records, chosen], axis=1)
        encoded = gelu(dot(both, first).astype(BF16))
        lifted = gelu(dot(encoded, lift).astype(BF16))
        tokens = dot_nt(weigh, meta)
        hots, parts = [], []
        for n in range(len(AROUND)):
            token = tokens[n : n + 1]
            token = jnp.concatenate([token + float(level) for level in range(LEV)], axis=1)
            if token.shape[1] == LANES:
                hot = codes[n] == token
            else:
                hot = codes[n][:, :1] == token
            hots.append(jnp.where(hot, 1.0, 0.0).astype(BF16))
        for n in range(len(AROUND)):
            part = lifted[n * slots : (n + 1) * slots]
            parts.append(
                with_ones(
                    below(*[part[:, level * width : (level + 1) * width] for level in range(LEV)])
                )
            )
        sums = [dot(hot, part) for hot, part in zip(hots, parts)]
        return tuple(sums)

    sums = scatter(0)
    if sources > chunk:
        sums = lax.fori_loop(
            1,
            sources // chunk,
            lambda step, total: tuple(a + b for a, b in zip(total, scatter(step * chunk))),
            sums,
        )
    return sums


def prepare_kernel(
    plan,
    even_ref,
    back_ref,
    attn_ref,
    table_ref,
    one_ref,
    two_ref,
    rows_ref,
    parts_ref,
    tables_ref,
    gain_one_ref,
    gain_two_ref,
    mine_ref,
    other_ref,
):
    lon_cells, _, width = back_ref.shape[1:]
    even = even_ref[1] == 1
    left, right = back_ref[:, :HLON], back_ref[:, lon_cells - HLON :]
    mine_ref[...] = jnp.where(even, right, left)
    other_ref[...] = jnp.where(even, left, right)
    pieces = []
    for top, high, left, wide in plan[4]:
        count = high * wide * LEV
        piece = back_ref[top : top + high, left : left + wide].reshape(count, width).astype(F32)
        if padded(count) > count:
            piece = below(piece, jnp.zeros((padded(count) - count, width), F32))
        pieces.append(piece)
    rows_ref[...] = below(*pieces).astype(BF16)
    tables_ref[...] = below(*[table_ref[...].astype(F32)] * (LANES // INSTR)).astype(BF16)
    for gain, ref in ((one_ref, gain_one_ref), (two_ref, gain_two_ref)):
        ref[...] = jnp.broadcast_to(gain[...].astype(F32).reshape(1, width), ref.shape)
    for n in range(3):
        parts_ref[n] = attn_ref[:, n * width : (n + 1) * width]


def prepared(plan, even, background, attn_weight, instrument_table, first_gain, second_gain):
    lat_cells, _, levels, width = background.shape
    rows = sum(padded(tokens_of(part)) for part in plan[4])
    vmem = pl.BlockSpec(memory_space=pltpu.VMEM)
    return pl.pallas_call(
        functools.partial(prepare_kernel, plan),
        out_shape=[
            jax.ShapeDtypeStruct((rows, width), BF16),
            jax.ShapeDtypeStruct((3, width, width), BF16),
            jax.ShapeDtypeStruct((LANES, width), BF16),
            jax.ShapeDtypeStruct((8, width), F32),
            jax.ShapeDtypeStruct((8, width), F32),
            *[jax.ShapeDtypeStruct((lat_cells, HLON, levels, width), BF16)] * 2,
        ],
        in_specs=[pl.BlockSpec(memory_space=pltpu.SMEM)] + [vmem] * 5,
        out_specs=[vmem] * 7,
        compiler_params=pltpu.CompilerParams(vmem_limit_bytes=LIMIT),
        cost_estimate=pl.CostEstimate(flops=10**9, bytes_accessed=10**6, transcendentals=0),
    )(even, background, attn_weight, instrument_table, first_gain, second_gain)


def join_kernel(even_ref, one_ref, two_ref, mine_ref, other_ref, first_ref, second_ref):
    lon_cells, lat_cells = one_ref.shape[1], mine_ref.shape[0]
    lat_even, lon_even = even_ref[0] == 1, even_ref[1] == 1
    for ref, strip, same in ((first_ref, mine_ref, True), (second_ref, other_ref, False)):
        ref[HLAT : HLAT + lat_cells] = strip[...]
        low, high = slice(0, HLON), slice(lon_cells - HLON, lon_cells)
        spots = (high, low) if same else (low, high)
        ends = [jnp.where(lon_even, got[:, spots[0]], got[:, spots[1]]) for got in (one_ref, two_ref)]
        ref[:HLAT] = jnp.where(lat_even, ends[1], ends[0])
        ref[HLAT + lat_cells :] = jnp.where(lat_even, ends[0], ends[1])


def joined(even, got, mine):
    lat_cells, _, levels, width = mine[0].shape
    vmem = pl.BlockSpec(memory_space=pltpu.VMEM)
    return pl.pallas_call(
        join_kernel,
        out_shape=[jax.ShapeDtypeStruct((lat_cells + WLAT, HLON, levels, width), BF16)] * 2,
        in_specs=[pl.BlockSpec(memory_space=pltpu.SMEM)] + [vmem] * 4,
        out_specs=[vmem] * 2,
        compiler_params=pltpu.CompilerParams(vmem_limit_bytes=LIMIT),
    )(even, *got, *mine)


def normed_of(plan, entries, sums, borders, gain):
    rows, north_ref, south_ref, west_ref, east_ref, lat_cells = borders
    width = gain.shape[1]
    pieces, spans, start = [], {}, 0
    for tile, number in entries:
        dy, dx = AROUND[tile]
        top, high, left, wide = plan[tile][number]
        count = high * wide * LEV
        full = padded(count)
        if tile == 4:
            begin = sum(padded(tokens_of(part)) for part in plan[4][:number])
            piece = rows[begin : begin + full]
        else:
            if dx:
                ref = west_ref if dx < 0 else east_ref
                top, left = {-1: 0, 0: top + HLAT, 1: lat_cells + HLAT}[dy], 0
            else:
                ref = north_ref if dy < 0 else south_ref
            block = ref(top, high) if dx else ref(left, wide)
            piece = block.reshape(count, width).astype(F32)
            if full > count:
                piece = below(piece, jnp.zeros((full - count, width), F32))
        pieces.append(piece)
        spans[tile, number] = (start, count)
        start += full
    tally = 1.0 + sums[:, width : width + 1]
    share = about_one_over(tally)
    share = share * (2.0 - tally * share)
    latent = ((below(*pieces) + sums[:, :width]) * share).astype(BF16).astype(F32)
    return latent, normalise(latent, gain), spans


def stacks_of(plan, places, own_normed, weight):
    width = weight.shape[0]
    head = width // HEADS
    query = dot(own_normed.astype(BF16), weight) * head ** (-0.5)
    query = jnp.concatenate([query, jnp.ones((query.shape[0], PAD - width), F32)], axis=1)
    lane = lax.broadcasted_iota(jnp.int32, (1, PAD), 1)
    stacks, begin = [], 0
    for i, j in places:
        rows = padded(tokens_of(plan[4][3 * i + j]))
        part = query[begin : begin + rows]
        begin += rows
        stacks.append(
            below(
                *[jnp.where((lane // head == h) | (lane >= width), part, 0.0) for h in range(HEADS)]
            ).astype(BF16)
        )
    return stacks


def worked(plan, places, stacks, keys, values, latent, weights, scalars_ref, put):
    mix_ref, gain_ref, up_ref, down_ref = weights
    width = mix_ref.shape[0]
    head = width // HEADS
    groups = [padded(tokens_of(plan[4][3 * i + j])) for i, j in places]
    lane = lax.broadcasted_iota(jnp.int32, (1, PAD), 1)
    many = WLAT * WLON * LEV
    corner = HLAT * HLON * LEV
    key = lax.broadcasted_iota(jnp.int32, (many, PAD - width), 0)
    spare = lax.broadcasted_iota(jnp.int32, (many, PAD - width), 1)
    unused = lax.broadcasted_iota(jnp.int32, (PAD - many, PAD), 1)
    unused = jnp.where(unused == width, -3e38, 0.0).astype(BF16)
    nothing = jnp.zeros((PAD - many, PAD), BF16)

    def keys_of(w, i, j):
        bias = jnp.zeros((many, PAD - width), F32)
        if i != 1:
            if j == 1:
                inside = key < 2 * corner
            else:
                inside = (key < corner) | ((key >= 2 * corner) & (key < 3 * corner))
            bias = jnp.where(inside | (spare > 0), 0.0, -3e38) * scalars_ref[i].astype(F32)
        here = jnp.concatenate([keys[w], bias], axis=1)
        return below(here.astype(BF16), unused)

    begins = [sum(groups[:w]) for w in range(len(groups))]
    held = [keys_of(w, i, j) for w, (i, j) in enumerate(places)]
    scores = [dot_nt(stack, here) for stack, here in zip(stacks, held)]
    largest = [jnp.max(score, axis=-1, keepdims=True) for score in scores]
    raised = [jnp.exp((score - most).astype(BF16)) for score, most in zip(scores, largest)]
    held = [below(with_ones(value).astype(BF16), nothing) for value in values]
    products = [dot(one, here) for one, here in zip(raised, held)]
    shares = [about_one_over(product[:, width : width + 1]) for product in products]
    products = [product[:, :width] * share for product, share in zip(products, shares)]
    mixed = []
    for product, rows in zip(products, groups):
        total = product[:rows]
        for h in range(1, HEADS):
            own = lane[:, :width] // head == h
            total = jnp.where(own, product[h * rows : (h + 1) * rows], total)
        mixed.append(total)
    mixed = below(*mixed).astype(BF16)

    after = (latent + dot(mixed, mix_ref[...])).astype(BF16).astype(F32)
    normed_two = normalise(after, gain_ref[:1, :]).astype(BF16)
    hidden = gelu(dot(normed_two, up_ref[...]).astype(BF16))
    result = after + dot(hidden, down_ref[...])
    for begin, (i, j) in zip(begins, places):
        part = plan[4][3 * i + j]
        piece = result[begin : begin + tokens_of(part)].astype(BF16)
        put(part, j, piece.reshape(part[1], part[3], LEV, width))


MIDDLE = [(0, 1), (1, 1), (2, 1)]
SIDES = [(0, 0), (0, 2), (2, 0), (2, 2), (1, 0), (1, 2)]


def own_rows(plan, places):
    return sum(padded(tokens_of(plan[4][3 * i + j])) for i, j in places)


def middle_kernel(
    plan,
    lat_cells,
    lon_cells,
    scalars_ref,
    recv_ref,
    one_ref,
    two_ref,
    rows_ref,
    first_ref,
    table_ref,
    lift_ref,
    gain_one_ref,
    *refs,
):
    parts_ref, *weights, out_ref, rest_ref, latent_ref, keys_ref, values_ref, stacks_ref = refs
    sums = scattered(recv_ref, first_ref, table_ref, lift_ref, plan, lon_cells)

    def sums_of(entries):
        pieces = []
        for tile, number in entries:
            start = sum(padded(tokens_of(part)) for part in plan[tile][:number])
            pieces.append(sums[tile][start : start + padded(tokens_of(plan[tile][number]))])
        return below(*pieces)

    even = scalars_ref[4] == 1

    def north(left, wide):
        return jnp.where(even, two_ref[:, left : left + wide], one_ref[:, left : left + wide])

    def south(left, wide):
        return jnp.where(even, one_ref[:, left : left + wide], two_ref[:, left : left + wide])

    borders = (rows_ref[...].astype(F32), north, south, None, None, lat_cells)
    gain = gain_one_ref[:1, :]
    entries = near_entries(MIDDLE)
    latent, normed, spans = normed_of(plan, entries, sums_of(entries), borders, gain)

    def piece_of(tile, number):
        start, count = spans[tile, number]
        return normed[start : start + count]

    def put(part, _, piece):
        out_ref[part[0] : part[0] + part[1]] = piece

    end = own_rows(plan, MIDDLE)
    many = WLAT * WLON * LEV
    tokens = []
    for i, j in MIDDLE:
        tokens.append(piece_of(4, 3 * i + j))
        if i != 1:
            tokens.append(piece_of(3 * i + 1, j))
    tokens = below(*tokens).astype(BF16)
    keys, values = dot(tokens, parts_ref[1]), dot(tokens, parts_ref[2])
    spots = [slice(w * many, (w + 1) * many) for w in range(len(MIDDLE))]
    worked(
        plan,
        MIDDLE,
        stacks_of(plan, MIDDLE, normed[:end], parts_ref[0]),
        [keys[spot] for spot in spots],
        [values[spot] for spot in spots],
        latent[:end],
        weights,
        scalars_ref,
        put,
    )
    rest_ref[...] = sums_of(far_entries(SIDES))
    entries = near_entries(SIDES)
    latent, normed, spans = normed_of(plan, entries, sums_of(entries), borders, gain)
    end = latent_ref.shape[0]
    latent_ref[...] = latent[:end]
    tokens = []
    for i, j in SIDES:
        start, count = spans[4, 3 * i + j]
        tokens.append(normed[start : start + count])
        if i != 1:
            start, count = spans[3 * i + 1, j]
            tokens.append(normed[start : start + count])
    tokens = below(*tokens).astype(BF16)
    keys_ref[...] = dot(tokens, parts_ref[1])
    values_ref[...] = dot(tokens, parts_ref[2])
    stacks_ref[...] = below(*stacks_of(plan, SIDES, normed[:end], parts_ref[0]))


def side_kernel(
    plan,
    lat_cells,
    scalars_ref,
    rest_ref,
    latent_ref,
    keys_ref,
    values_ref,
    stacks_ref,
    one_ref,
    two_ref,
    gain_one_ref,
    *refs,
):
    parts_ref, *weights, middle_ref, out_ref, held_ref, sem = refs
    left, wide = plan[4][4][2:]
    copies = [pltpu.make_async_copy(middle_ref, out_ref.at[:, left : left + wide], sem.at[2])]
    copies[0].start()
    even = scalars_ref[3] == 1

    def west(top, high):
        return jnp.where(even, two_ref[top : top + high], one_ref[top : top + high])

    def east(top, high):
        return jnp.where(even, one_ref[top : top + high], two_ref[top : top + high])

    borders = (None, None, None, west, east, lat_cells)
    gain = gain_one_ref[:1, :]
    _, far, spans = normed_of(plan, far_entries(SIDES), rest_ref[...], borders, gain)

    tokens = []
    for i, j in SIDES:
        for entry in [(3 + j, i)] + ([(3 * i + j, 0)] if i != 1 else []):
            start, count = spans[entry]
            tokens.append(far[start : start + count])
    tokens = below(*tokens).astype(BF16)
    keys, values = dot(tokens, parts_ref[1]), dot(tokens, parts_ref[2])
    half = WLAT * HLON * LEV
    spots = [slice(w * half, (w + 1) * half) for w in range(len(SIDES))]
    stacks, start = [], 0
    for i, j in SIDES:
        rows = HEADS * padded(tokens_of(plan[4][3 * i + j]))
        stacks.append(stacks_ref[start : start + rows, :])
        start += rows

    def put(part, j, piece):
        held_ref[j // 2, part[0] : part[0] + part[1]] = piece

    worked(
        plan,
        SIDES,
        stacks,
        [below(keys_ref[spot, :], keys[spot]) for spot in spots],
        [below(values_ref[spot, :], values[spot]) for spot in spots],
        latent_ref[...],
        weights,
        scalars_ref,
        put,
    )
    for n, number in enumerate((0, 2)):
        left, wide = plan[4][number][2:]
        copies.append(
            pltpu.make_async_copy(held_ref.at[n], out_ref.at[:, left : left + wide], sem.at[n])
        )
        copies[-1].start()
    for copy in copies:
        copy.wait()


def local(
    record_values,
    record_cell,
    record_instrument,
    block_counts,
    background,
    input_weight,
    instrument_table,
    lift_weight,
    first_gain,
    attn_weight,
    mix_weight,
    second_gain,
    up_weight,
    down_weight,
):
    lat_cells, lon_cells, _, width = background.shape
    tiles_lat = record_values.shape[1]

    sent, up, down = packed(
        record_values, record_cell, record_instrument, block_counts, background
    )
    received = lax.all_to_all(sent, ("lon", "lat"), split_axis=0, concat_axis=0, tiled=True)
    borders = swapped(up, down, "lat", wraps=False)

    held = (background, input_weight, instrument_table, attn_weight, down_weight)
    held = lax.optimization_barrier((*held, first_gain, second_gain, up))
    later, input_weight, instrument_table, attn_weight, down_weight = held[:5]
    first_gain, second_gain = held[5:7]

    plan = rectangles(lat_cells, lon_cells)
    even = [lax.axis_index(axis) % 2 == 0 for axis in ("lat", "lon")]
    evens = jnp.stack(even).astype(jnp.int32)
    rows, parts, tables, gain_one, gain_two, *mine = prepared(
        plan, evens, later, attn_weight, instrument_table, first_gain, second_gain
    )
    got = swapped_as(joined(evens, borders, mine), "lon", wraps=True)
    lat = lax.axis_index("lat")
    scalars = jnp.stack([lat == 0, lat < 0, lat == tiles_lat - 1, even[1], even[0]]).astype(jnp.int32)

    def rows_in(entries):
        return sum(padded(tokens_of(plan[tile][number])) for tile, number in entries)

    weights = [parts, mix_weight, gain_two, up_weight, down_weight]
    smem = pl.BlockSpec(memory_space=pltpu.SMEM)
    vmem = pl.BlockSpec(memory_space=pltpu.VMEM)
    anywhere = pl.BlockSpec(memory_space=pl.ANY)
    params = pltpu.CompilerParams(vmem_limit_bytes=LIMIT)
    half = WLAT * HLON * LEV * len(SIDES)
    middle, rest, latent, *near = pl.pallas_call(
        functools.partial(middle_kernel, plan, lat_cells, lon_cells),
        out_shape=[
            jax.ShapeDtypeStruct((lat_cells, lon_cells - WLON, LEV, width), BF16),
            jax.ShapeDtypeStruct((rows_in(far_entries(SIDES)), PAD), F32),
            jax.ShapeDtypeStruct((own_rows(plan, SIDES), width), F32),
            jax.ShapeDtypeStruct((half, width), F32),
            jax.ShapeDtypeStruct((half, width), F32),
            jax.ShapeDtypeStruct((HEADS * own_rows(plan, SIDES), PAD), BF16),
        ],
        in_specs=[smem] + [vmem] * (8 + len(weights)),
        out_specs=[vmem] * 6,
        compiler_params=params,
        cost_estimate=pl.CostEstimate(
            flops=4 * 10**9, bytes_accessed=4 * 10**6, transcendentals=10**6
        ),
    )(
        scalars,
        received,
        *borders,
        rows,
        input_weight,
        tables,
        lift_weight,
        gain_one,
        *weights,
    )
    rest, *got = lax.optimization_barrier((rest, *got[::-1]))
    got = got[::-1]
    return pl.pallas_call(
        functools.partial(side_kernel, plan, lat_cells),
        out_shape=jax.ShapeDtypeStruct(background.shape, BF16),
        in_specs=[smem] + [vmem] * (9 + len(weights)),
        out_specs=anywhere,
        scratch_shapes=[
            pltpu.VMEM((2, lat_cells, HLON, LEV, width), BF16),
            pltpu.SemaphoreType.DMA((3,)),
        ],
        compiler_params=params,
        cost_estimate=pl.CostEstimate(
            flops=3 * 10**9, bytes_accessed=4 * 10**6, transcendentals=10**6
        ),
    )(scalars, rest, latent, *near, *got, gain_one, *weights, middle)


def solution(mesh):
    placed = (
        P("lon", "lat", None, None),
        P("lon", "lat", None),
        P("lon", "lat", None),
        P("lon", "lat"),
        P("lat", "lon", None, None),
        P(),
        P(),
        P(),
        P(),
        P(),
        P(),
        P(),
        P(),
        P(),
    )
    return jax.shard_map(
        local, mesh=mesh, in_specs=placed, out_specs=P("lat", "lon", None, None), check_vma=False
    )
```

```python
import functools

import jax
import jax.numpy as jnp
from jax import lax
from jax.experimental import pallas as pl
from jax.experimental.pallas import tpu as pltpu
from jax.sharding import PartitionSpec as P

HEADS = 6
INSTR = 8
LEV = 2
WLAT = 6
WLON = 12
HLAT = WLAT // 2
HLON = WLON // 2
LANES = 128
PAD = 256
CHUNK = 32
LIMIT = 40 * 2**20
BF16 = jnp.bfloat16
F32 = jnp.float32

AROUND = [(dy, dx) for dy in (-1, 0, 1) for dx in (-1, 0, 1)]
ROWS = INSTR * len(AROUND)
COLS = ROWS + len(AROUND)


def swapped_as(mine, axis, wraps):
    count = lax.axis_size(axis)
    got = []
    for first, one in enumerate(mine):
        pairs = []
        for low in range(first, count, 2):
            high = (low + 1) % count
            if high > low or wraps:
                pairs += [(low, high), (high, low)]
        got.append(lax.ppermute(one, axis, pairs))
    return got


def swapped(up, down, axis, wraps):
    even = lax.axis_index(axis) % 2 == 0
    return swapped_as((jnp.where(even, down, up), jnp.where(even, up, down)), axis, wraps)


def rectangles(lat_cells, lon_cells):
    lat = {-1: [(lat_cells - HLAT, HLAT)], 1: [(0, HLAT)]}
    lat[0] = [(0, HLAT), (HLAT, lat_cells - WLAT), (lat_cells - HLAT, HLAT)]
    lon = {-1: [(lon_cells - HLON, HLON)], 1: [(0, HLON)]}
    lon[0] = [(0, HLON), (HLON, lon_cells - WLON), (lon_cells - HLON, HLON)]
    return [
        [(top, high, left, wide) for top, high in lat[dy] for left, wide in lon[dx]]
        for dy, dx in AROUND
    ]


def tokens_of(part):
    return part[1] * part[3] * LEV


def padded(count):
    return -(-count // 8) * 8


def gelu(x):
    half = 0.5 * x
    inner = x * (0.7978845608028654 + 0.035677408136300125 * (x * x))
    return half + half * jnp.tanh(inner)


def normalise(wide, gain):
    average = jnp.mean(wide, axis=-1, keepdims=True)
    centred = wide - average
    spread = jnp.mean(centred * centred, axis=-1, keepdims=True)
    return centred * lax.rsqrt(spread + 1e-05) * gain


def dot(a, b):
    return jnp.dot(a, b, preferred_element_type=F32)


def dot_nt(a, b):
    return lax.dot_general(a, b, (((1,), (1,)), ((), ())), preferred_element_type=F32)


def about_one_over(x):
    return pl.reciprocal(x, approx=True)


def with_ones(tensor):
    ones = jnp.ones((tensor.shape[0], PAD - tensor.shape[1]), tensor.dtype)
    return jnp.concatenate([tensor, ones], axis=1).astype(BF16)


def below(*pieces):
    return jnp.concatenate(pieces, axis=0) if len(pieces) > 1 else pieces[0]


def pack_kernel(
    values_ref,
    cell_ref,
    tag_ref,
    count_ref,
    back_ref,
    *refs,
):
    out_ref, up_ref, down_ref, values, cells, tags, held, sem = refs
    tiles_lon, tiles_lat, capacity, _ = values_ref.shape
    lat_cells, lon_cells = back_ref.shape[:2]
    strips = [
        (back_ref.at[:HLAT], up_ref),
        (back_ref.at[lat_cells - HLAT :], down_ref),
    ]
    copies = [
        pltpu.make_async_copy(cell_ref, cells, sem.at[0]),
        pltpu.make_async_copy(tag_ref, tags, sem.at[1]),
        pltpu.make_async_copy(count_ref, held, sem.at[2]),
        pltpu.make_async_copy(values_ref, values, sem.at[3]),
    ]
    copies += [
        pltpu.make_async_copy(source, strip, sem.at[4 + n])
        for n, (source, strip) in enumerate(strips)
    ]
    for copy in copies:
        copy.start()
    for copy in copies[:3]:
        copy.wait()
    counts = below(*[held[tile : tile + 1, :] for tile in range(tiles_lat) for _ in range(capacity)])
    cell = cells[...]
    slot = lax.broadcasted_iota(jnp.int32, cell.shape, 0) % capacity
    row = cell // lon_cells
    fields = [jnp.where(slot < counts, row, 255), cell - row * lon_cells, tags[...]]
    rows, columns, kinds = (field.astype(F32) for field in fields)
    lane = lax.broadcasted_iota(jnp.int32, (cell.shape[0], LANES), 1)
    kind_of = (lane % INSTR).astype(F32)
    marks = [
        ((lane < ROWS) & (lane // INSTR == n)) | (lane == ROWS + n) | (lane == COLS + n)
        for n in range(len(AROUND))
    ]
    turned = []
    for lon in range(tiles_lon):
        meta = jnp.where(kind_of == kinds[:, lon : lon + 1], 1.0, 0.0)
        meta = jnp.where(lane >= ROWS, rows[:, lon : lon + 1], meta)
        meta = jnp.where(lane >= COLS, columns[:, lon : lon + 1], meta)
        turns = {0: meta}
        for dy in (-1, 1):
            by = dy * capacity % meta.shape[0]
            turns[dy] = below(meta[by:], meta[:by])
        turned.append(turns)
    for lon in range(tiles_lon):
        meta = jnp.zeros(lane.shape, F32)
        for mark, (dy, dx) in zip(marks, AROUND):
            meta = jnp.where(mark, turned[(lon + dx) % tiles_lon][dy], meta)
        out_ref[lon, :, len(AROUND)] = meta.astype(BF16).reshape(tiles_lat, capacity, LANES)
    copies[3].wait()
    for n, (dy, dx) in enumerate(AROUND):
        spans = {0: [(0, tiles_lat)], 1: [(0, tiles_lat - 1), (tiles_lat - 1, tiles_lat)]}
        spans[-1] = [(0, 1), (1, tiles_lat)]

        def copy_tiles(lon, n=n, dx=dx, dy=dy, spans=spans[dy]):
            source = lax.rem(lon + dx + tiles_lon, tiles_lon)
            for low, end in spans:
                first = (low + dy) % tiles_lat
                out_ref[lon, low:end, n] = values[source, first : first + end - low]

        if tiles_lon <= 8:
            for lon in range(tiles_lon):
                copy_tiles(lon)
        else:
            pl.loop(0, tiles_lon)(copy_tiles)
    for copy in copies[4:]:
        copy.wait()


def packed(record_values, record_cell, record_instrument, block_counts, background):
    tiles_lon, tiles_lat, capacity, wide = record_values.shape
    anywhere = pl.BlockSpec(memory_space=pltpu.HBM)
    ints = pltpu.VMEM((tiles_lat * capacity, tiles_lon), jnp.int32)
    shape = (tiles_lon, tiles_lat, len(AROUND) + 1, capacity, wide)
    lat_cells, lon_cells, levels, width = background.shape
    across = jax.ShapeDtypeStruct((HLAT, lon_cells, levels, width), BF16)
    out, *strips = pl.pallas_call(
        pack_kernel,
        out_shape=[jax.ShapeDtypeStruct(shape, BF16), across, across],
        in_specs=[anywhere] * 5,
        out_specs=[pl.BlockSpec(memory_space=pltpu.VMEM)] * 3,
        scratch_shapes=[
            pltpu.VMEM(record_values.shape, BF16),
            ints,
            ints,
            pltpu.VMEM((tiles_lat, tiles_lon), jnp.int32),
            pltpu.SemaphoreType.DMA((6,)),
        ],
        compiler_params=pltpu.CompilerParams(vmem_limit_bytes=56 * 2**20),
        cost_estimate=pl.CostEstimate(
            flops=20 * 10**9, bytes_accessed=10**6, transcendentals=0
        ),
    )(
        record_values,
        record_cell.transpose(1, 2, 0).reshape(-1, tiles_lon),
        record_instrument.transpose(1, 2, 0).reshape(-1, tiles_lon),
        block_counts.T,
        background,
    )
    return out.reshape((-1,) + shape[2:]), *strips


def token_codes(part, lon_cells):
    top, high, left, wide = part
    count = tokens_of(part)
    place = lax.broadcasted_iota(jnp.int32, (padded(count), LANES), 0)
    code = place + (top * lon_cells + left) * LEV
    for row in range(1, high):
        step = (lon_cells - wide) * LEV
        code = code + jnp.where(place >= row * wide * LEV, step, 0)
    return jnp.where(place < count, code, -8).astype(F32)


def near_entries(windows):
    own = [(4, 3 * i + j) for i, j in windows]
    return own + [(3 * i + 1, j) for i, j in windows if i != 1]


def far_entries(windows):
    beside = [(3 + j, i) for i, j in windows if j != 1]
    return beside + [(3 * i + j, 0) for i, j in windows if i != 1 and j != 1]


def scattered(recv_ref, first_ref, table_ref, lift_ref, plan, lon_cells):
    sources, _, capacity, _ = recv_ref.shape
    width = first_ref.shape[1]
    chunk = min(CHUNK, sources)
    slots = chunk * capacity
    first, lift = below(first_ref[...], table_ref[...]), lift_ref[...]
    lane = lax.broadcasted_iota(jnp.int32, (16, LANES), 1)
    sub = lax.broadcasted_iota(jnp.int32, (16, LANES), 0)
    weigh = jnp.where(lane == ROWS + sub, float(lon_cells * LEV), 0.0)
    weigh = jnp.where(lane == COLS + sub, float(LEV), weigh).astype(BF16)
    codes = [below(*[token_codes(part, lon_cells) for part in parts]) for parts in plan]

    def scatter(begin):
        meta = recv_ref[pl.ds(begin, chunk), len(AROUND)].reshape(slots, LANES)
        records = below(
            *[
                recv_ref[pl.ds(begin, chunk), n].reshape(slots, LANES)
                for n in range(len(AROUND))
            ]
        )
        lane = lax.broadcasted_iota(jnp.int32, meta.shape, 1) // INSTR
        wide = meta.astype(F32)
        chosen = below(*[jnp.where(lane == n, wide, 0.0) for n in range(len(AROUND))]).astype(BF16)
        both = jnp.concatenate([records, chosen], axis=1)
        encoded = gelu(dot(both, first).astype(BF16))
        lifted = gelu(dot(encoded, lift).astype(BF16))
        tokens = dot_nt(weigh, meta)
        hots, parts = [], []
        for n in range(len(AROUND)):
            token = tokens[n : n + 1]
            token = jnp.concatenate([token + float(level) for level in range(LEV)], axis=1)
            if token.shape[1] == LANES:
                hot = codes[n] == token
            else:
                hot = codes[n][:, :1] == token
            hots.append(jnp.where(hot, 1.0, 0.0).astype(BF16))
        for n in range(len(AROUND)):
            part = lifted[n * slots : (n + 1) * slots]
            parts.append(
                with_ones(
                    below(*[part[:, level * width : (level + 1) * width] for level in range(LEV)])
                )
            )
        sums = [dot(hot, part) for hot, part in zip(hots, parts)]
        return tuple(sums)

    sums = scatter(0)
    if sources > chunk:
        sums = lax.fori_loop(
            1,
            sources // chunk,
            lambda step, total: tuple(a + b for a, b in zip(total, scatter(step * chunk))),
            sums,
        )
    return sums


def prepare_kernel(
    plan,
    even_ref,
    back_ref,
    attn_ref,
    table_ref,
    one_ref,
    two_ref,
    rows_ref,
    parts_ref,
    tables_ref,
    gain_one_ref,
    gain_two_ref,
    mine_ref,
    other_ref,
):
    lon_cells, _, width = back_ref.shape[1:]
    even = even_ref[1] == 1
    left, right = back_ref[:, :HLON], back_ref[:, lon_cells - HLON :]
    mine_ref[...] = jnp.where(even, right, left)
    other_ref[...] = jnp.where(even, left, right)
    pieces = []
    for top, high, left, wide in plan[4]:
        count = high * wide * LEV
        piece = back_ref[top : top + high, left : left + wide].reshape(count, width).astype(F32)
        if padded(count) > count:
            piece = below(piece, jnp.zeros((padded(count) - count, width), F32))
        pieces.append(piece)
    rows_ref[...] = below(*pieces).astype(BF16)
    tables_ref[...] = below(*[table_ref[...].astype(F32)] * (LANES // INSTR)).astype(BF16)
    for gain, ref in ((one_ref, gain_one_ref), (two_ref, gain_two_ref)):
        ref[...] = jnp.broadcast_to(gain[...].astype(F32).reshape(1, width), ref.shape)
    for n in range(3):
        parts_ref[n] = attn_ref[:, n * width : (n + 1) * width]


def prepared(plan, even, background, attn_weight, instrument_table, first_gain, second_gain):
    lat_cells, _, levels, width = background.shape
    rows = sum(padded(tokens_of(part)) for part in plan[4])
    vmem = pl.BlockSpec(memory_space=pltpu.VMEM)
    return pl.pallas_call(
        functools.partial(prepare_kernel, plan),
        out_shape=[
            jax.ShapeDtypeStruct((rows, width), BF16),
            jax.ShapeDtypeStruct((3, width, width), BF16),
            jax.ShapeDtypeStruct((LANES, width), BF16),
            jax.ShapeDtypeStruct((8, width), F32),
            jax.ShapeDtypeStruct((8, width), F32),
            *[jax.ShapeDtypeStruct((lat_cells, HLON, levels, width), BF16)] * 2,
        ],
        in_specs=[pl.BlockSpec(memory_space=pltpu.SMEM)] + [vmem] * 5,
        out_specs=[vmem] * 7,
        compiler_params=pltpu.CompilerParams(vmem_limit_bytes=LIMIT),
        cost_estimate=pl.CostEstimate(flops=10**9, bytes_accessed=10**6, transcendentals=0),
    )(even, background, attn_weight, instrument_table, first_gain, second_gain)


def joined(even, got, mine):
    lon_cells = got[0].shape[1]
    low, high = slice(0, HLON), slice(lon_cells - HLON, lon_cells)
    strips = []
    for own, spots in zip(mine, ((high, low), (low, high))):
        ends = [jnp.where(even[1], one[:, spots[0]], one[:, spots[1]]) for one in got]
        north = jnp.where(even[0], ends[1], ends[0])
        south = jnp.where(even[0], ends[0], ends[1])
        strips.append(jnp.concatenate([north, own, south], axis=0))
    return strips


def normed_of(plan, entries, sums, borders, gain):
    rows, north_ref, south_ref, west_ref, east_ref, lat_cells = borders
    width = gain.shape[1]
    pieces, spans, start = [], {}, 0
    for tile, number in entries:
        dy, dx = AROUND[tile]
        top, high, left, wide = plan[tile][number]
        count = high * wide * LEV
        full = padded(count)
        if tile == 4:
            begin = sum(padded(tokens_of(part)) for part in plan[4][:number])
            piece = rows[begin : begin + full]
        else:
            if dx:
                ref = west_ref if dx < 0 else east_ref
                top, left = {-1: 0, 0: top + HLAT, 1: lat_cells + HLAT}[dy], 0
            else:
                ref = north_ref if dy < 0 else south_ref
            block = ref(top, high) if dx else ref(left, wide)
            piece = block.reshape(count, width).astype(F32)
            if full > count:
                piece = below(piece, jnp.zeros((full - count, width), F32))
        pieces.append(piece)
        spans[tile, number] = (start, count)
        start += full
    tally = 1.0 + sums[:, width : width + 1]
    share = about_one_over(tally)
    share = share * (2.0 - tally * share)
    latent = ((below(*pieces) + sums[:, :width]) * share).astype(BF16).astype(F32)
    return latent, normalise(latent, gain), spans


def stacks_of(plan, places, own_normed, weight):
    width = weight.shape[0]
    head = width // HEADS
    query = dot(own_normed.astype(BF16), weight) * head ** (-0.5)
    query = jnp.concatenate([query, jnp.ones((query.shape[0], PAD - width), F32)], axis=1)
    lane = lax.broadcasted_iota(jnp.int32, (1, PAD), 1)
    stacks, begin = [], 0
    for i, j in places:
        rows = padded(tokens_of(plan[4][3 * i + j]))
        part = query[begin : begin + rows]
        begin += rows
        stacks.append(
            below(
                *[jnp.where((lane // head == h) | (lane >= width), part, 0.0) for h in range(HEADS)]
            ).astype(BF16)
        )
    return stacks


def worked(plan, places, stacks, keys, values, latent, weights, scalars_ref, put):
    mix_ref, gain_ref, up_ref, down_ref = weights
    width = mix_ref.shape[0]
    head = width // HEADS
    groups = [padded(tokens_of(plan[4][3 * i + j])) for i, j in places]
    lane = lax.broadcasted_iota(jnp.int32, (1, PAD), 1)
    many = WLAT * WLON * LEV
    corner = HLAT * HLON * LEV
    key = lax.broadcasted_iota(jnp.int32, (many, PAD - width), 0)
    spare = lax.broadcasted_iota(jnp.int32, (many, PAD - width), 1)
    unused = lax.broadcasted_iota(jnp.int32, (PAD - many, PAD), 1)
    unused = jnp.where(unused == width, -3e38, 0.0).astype(BF16)
    nothing = jnp.zeros((PAD - many, PAD), BF16)

    def keys_of(w, i, j):
        bias = jnp.zeros((many, PAD - width), F32)
        if i != 1:
            if j == 1:
                inside = key < 2 * corner
            else:
                inside = (key < corner) | ((key >= 2 * corner) & (key < 3 * corner))
            bias = jnp.where(inside | (spare > 0), 0.0, -3e38) * scalars_ref[i].astype(F32)
        here = jnp.concatenate([keys[w], bias], axis=1)
        return below(here.astype(BF16), unused)

    begins = [sum(groups[:w]) for w in range(len(groups))]
    held = [keys_of(w, i, j) for w, (i, j) in enumerate(places)]
    scores = [dot_nt(stack, here) for stack, here in zip(stacks, held)]
    largest = [jnp.max(score, axis=-1, keepdims=True) for score in scores]
    raised = [jnp.exp((score - most).astype(BF16)) for score, most in zip(scores, largest)]
    held = [below(with_ones(value).astype(BF16), nothing) for value in values]
    products = [dot(one, here) for one, here in zip(raised, held)]
    shares = [about_one_over(product[:, width : width + 1]) for product in products]
    products = [product[:, :width] * share for product, share in zip(products, shares)]
    mixed = []
    for product, rows in zip(products, groups):
        total = product[:rows]
        for h in range(1, HEADS):
            own = lane[:, :width] // head == h
            total = jnp.where(own, product[h * rows : (h + 1) * rows], total)
        mixed.append(total)
    mixed = below(*mixed).astype(BF16)

    after = (latent + dot(mixed, mix_ref[...])).astype(BF16).astype(F32)
    normed_two = normalise(after, gain_ref[:1, :]).astype(BF16)
    hidden = gelu(dot(normed_two, up_ref[...]).astype(BF16))
    result = after + dot(hidden, down_ref[...])
    for begin, (i, j) in zip(begins, places):
        part = plan[4][3 * i + j]
        piece = result[begin : begin + tokens_of(part)].astype(BF16)
        put(part, j, piece.reshape(part[1], part[3], LEV, width))


MIDDLE = [(0, 1), (1, 1), (2, 1)]
SIDES = [(0, 0), (0, 2), (2, 0), (2, 2), (1, 0), (1, 2)]


def own_rows(plan, places):
    return sum(padded(tokens_of(plan[4][3 * i + j])) for i, j in places)


def middle_kernel(
    plan,
    lat_cells,
    lon_cells,
    scalars_ref,
    recv_ref,
    one_ref,
    two_ref,
    rows_ref,
    first_ref,
    table_ref,
    lift_ref,
    gain_one_ref,
    *refs,
):
    parts_ref, *weights, out_ref, rest_ref, latent_ref, keys_ref, values_ref, stacks_ref = refs
    sums = scattered(recv_ref, first_ref, table_ref, lift_ref, plan, lon_cells)

    def sums_of(entries):
        pieces = []
        for tile, number in entries:
            start = sum(padded(tokens_of(part)) for part in plan[tile][:number])
            pieces.append(sums[tile][start : start + padded(tokens_of(plan[tile][number]))])
        return below(*pieces)

    even = scalars_ref[4] == 1

    def north(left, wide):
        return jnp.where(even, two_ref[:, left : left + wide], one_ref[:, left : left + wide])

    def south(left, wide):
        return jnp.where(even, one_ref[:, left : left + wide], two_ref[:, left : left + wide])

    borders = (rows_ref[...].astype(F32), north, south, None, None, lat_cells)
    gain = gain_one_ref[:1, :]
    entries = near_entries(MIDDLE)
    latent, normed, spans = normed_of(plan, entries, sums_of(entries), borders, gain)

    def piece_of(tile, number):
        start, count = spans[tile, number]
        return normed[start : start + count]

    def put(part, _, piece):
        out_ref[part[0] : part[0] + part[1]] = piece

    end = own_rows(plan, MIDDLE)
    many = WLAT * WLON * LEV
    tokens = []
    for i, j in MIDDLE:
        tokens.append(piece_of(4, 3 * i + j))
        if i != 1:
            tokens.append(piece_of(3 * i + 1, j))
    tokens = below(*tokens).astype(BF16)
    keys, values = dot(tokens, parts_ref[1]), dot(tokens, parts_ref[2])
    spots = [slice(w * many, (w + 1) * many) for w in range(len(MIDDLE))]
    worked(
        plan,
        MIDDLE,
        stacks_of(plan, MIDDLE, normed[:end], parts_ref[0]),
        [keys[spot] for spot in spots],
        [values[spot] for spot in spots],
        latent[:end],
        weights,
        scalars_ref,
        put,
    )
    rest_ref[...] = sums_of(far_entries(SIDES))
    entries = near_entries(SIDES)
    latent, normed, spans = normed_of(plan, entries, sums_of(entries), borders, gain)
    end = latent_ref.shape[0]
    latent_ref[...] = latent[:end]
    tokens = []
    for i, j in SIDES:
        start, count = spans[4, 3 * i + j]
        tokens.append(normed[start : start + count])
        if i != 1:
            start, count = spans[3 * i + 1, j]
            tokens.append(normed[start : start + count])
    tokens = below(*tokens).astype(BF16)
    keys_ref[...] = dot(tokens, parts_ref[1])
    values_ref[...] = dot(tokens, parts_ref[2])
    stacks_ref[...] = below(*stacks_of(plan, SIDES, normed[:end], parts_ref[0]))


def side_kernel(
    plan,
    lat_cells,
    scalars_ref,
    rest_ref,
    latent_ref,
    keys_ref,
    values_ref,
    stacks_ref,
    one_ref,
    two_ref,
    gain_one_ref,
    *refs,
):
    parts_ref, *weights, middle_ref, out_ref, held_ref, sem = refs
    left, wide = plan[4][4][2:]
    copies = [pltpu.make_async_copy(middle_ref, out_ref.at[:, left : left + wide], sem.at[2])]
    copies[0].start()
    even = scalars_ref[3] == 1

    def west(top, high):
        return jnp.where(even, two_ref[top : top + high], one_ref[top : top + high])

    def east(top, high):
        return jnp.where(even, one_ref[top : top + high], two_ref[top : top + high])

    borders = (None, None, None, west, east, lat_cells)
    gain = gain_one_ref[:1, :]
    _, far, spans = normed_of(plan, far_entries(SIDES), rest_ref[...], borders, gain)

    tokens = []
    for i, j in SIDES:
        for entry in [(3 + j, i)] + ([(3 * i + j, 0)] if i != 1 else []):
            start, count = spans[entry]
            tokens.append(far[start : start + count])
    tokens = below(*tokens).astype(BF16)
    keys, values = dot(tokens, parts_ref[1]), dot(tokens, parts_ref[2])
    half = WLAT * HLON * LEV
    spots = [slice(w * half, (w + 1) * half) for w in range(len(SIDES))]
    stacks, start = [], 0
    for i, j in SIDES:
        rows = HEADS * padded(tokens_of(plan[4][3 * i + j]))
        stacks.append(stacks_ref[start : start + rows, :])
        start += rows

    def put(part, j, piece):
        held_ref[j // 2, part[0] : part[0] + part[1]] = piece

    worked(
        plan,
        SIDES,
        stacks,
        [below(keys_ref[spot, :], keys[spot]) for spot in spots],
        [below(values_ref[spot, :], values[spot]) for spot in spots],
        latent_ref[...],
        weights,
        scalars_ref,
        put,
    )
    for n, number in enumerate((0, 2)):
        left, wide = plan[4][number][2:]
        copies.append(
            pltpu.make_async_copy(held_ref.at[n], out_ref.at[:, left : left + wide], sem.at[n])
        )
        copies[-1].start()
    for copy in copies:
        copy.wait()


def local(
    record_values,
    record_cell,
    record_instrument,
    block_counts,
    background,
    input_weight,
    instrument_table,
    lift_weight,
    first_gain,
    attn_weight,
    mix_weight,
    second_gain,
    up_weight,
    down_weight,
):
    lat_cells, lon_cells, _, width = background.shape
    tiles_lat = record_values.shape[1]

    sent, up, down = packed(
        record_values, record_cell, record_instrument, block_counts, background
    )
    received = lax.all_to_all(sent, ("lon", "lat"), split_axis=0, concat_axis=0, tiled=True)
    borders = swapped(up, down, "lat", wraps=False)

    held = (background, input_weight, instrument_table, attn_weight, down_weight)
    held = lax.optimization_barrier((*held, first_gain, second_gain, up))
    later, input_weight, instrument_table, attn_weight, down_weight = held[:5]
    first_gain, second_gain = held[5:7]

    plan = rectangles(lat_cells, lon_cells)
    even = [lax.axis_index(axis) % 2 == 0 for axis in ("lat", "lon")]
    evens = jnp.stack(even).astype(jnp.int32)
    rows, parts, tables, gain_one, gain_two, *mine = prepared(
        plan, evens, later, attn_weight, instrument_table, first_gain, second_gain
    )
    got = swapped_as(joined(even, borders, mine), "lon", wraps=True)
    lat = lax.axis_index("lat")
    scalars = jnp.stack([lat == 0, lat < 0, lat == tiles_lat - 1, even[1], even[0]]).astype(jnp.int32)

    def rows_in(entries):
        return sum(padded(tokens_of(plan[tile][number])) for tile, number in entries)

    weights = [parts, mix_weight, gain_two, up_weight, down_weight]
    smem = pl.BlockSpec(memory_space=pltpu.SMEM)
    vmem = pl.BlockSpec(memory_space=pltpu.VMEM)
    anywhere = pl.BlockSpec(memory_space=pl.ANY)
    params = pltpu.CompilerParams(vmem_limit_bytes=LIMIT)
    half = WLAT * HLON * LEV * len(SIDES)
    middle, rest, latent, *near = pl.pallas_call(
        functools.partial(middle_kernel, plan, lat_cells, lon_cells),
        out_shape=[
            jax.ShapeDtypeStruct((lat_cells, lon_cells - WLON, LEV, width), BF16),
            jax.ShapeDtypeStruct((rows_in(far_entries(SIDES)), PAD), F32),
            jax.ShapeDtypeStruct((own_rows(plan, SIDES), width), F32),
            jax.ShapeDtypeStruct((half, width), F32),
            jax.ShapeDtypeStruct((half, width), F32),
            jax.ShapeDtypeStruct((HEADS * own_rows(plan, SIDES), PAD), BF16),
        ],
        in_specs=[smem] + [vmem] * (8 + len(weights)),
        out_specs=[vmem] * 6,
        compiler_params=params,
        cost_estimate=pl.CostEstimate(
            flops=4 * 10**9, bytes_accessed=4 * 10**6, transcendentals=10**6
        ),
    )(
        scalars,
        received,
        *borders,
        rows,
        input_weight,
        tables,
        lift_weight,
        gain_one,
        *weights,
    )
    rest, *got = lax.optimization_barrier((rest, *got[::-1]))
    got = got[::-1]
    return pl.pallas_call(
        functools.partial(side_kernel, plan, lat_cells),
        out_shape=jax.ShapeDtypeStruct(background.shape, BF16),
        in_specs=[smem] + [vmem] * (9 + len(weights)),
        out_specs=anywhere,
        scratch_shapes=[
            pltpu.VMEM((2, lat_cells, HLON, LEV, width), BF16),
            pltpu.SemaphoreType.DMA((3,)),
        ],
        compiler_params=params,
        cost_estimate=pl.CostEstimate(
            flops=3 * 10**9, bytes_accessed=4 * 10**6, transcendentals=10**6
        ),
    )(scalars, rest, latent, *near, *got, gain_one, *weights, middle)


def solution(mesh):
    placed = (
        P("lon", "lat", None, None),
        P("lon", "lat", None),
        P("lon", "lat", None),
        P("lon", "lat"),
        P("lat", "lon", None, None),
        P(),
        P(),
        P(),
        P(),
        P(),
        P(),
        P(),
        P(),
        P(),
    )
    return jax.shard_map(
        local, mesh=mesh, in_specs=placed, out_specs=P("lat", "lon", None, None), check_vma=False
    )
```

```python
import functools

import jax
import jax.numpy as jnp
from jax import lax
from jax.experimental import pallas as pl
from jax.experimental.pallas import tpu as pltpu
from jax.sharding import PartitionSpec as P

HEADS = 6
INSTR = 8
LEV = 2
WLAT = 6
WLON = 12
HLAT = WLAT // 2
HLON = WLON // 2
LANES = 128
PAD = 256
CHUNK = 32
LIMIT = 40 * 2**20
BF16 = jnp.bfloat16
F32 = jnp.float32

AROUND = [(dy, dx) for dy in (-1, 0, 1) for dx in (-1, 0, 1)]
ROWS = INSTR * len(AROUND)
COLS = ROWS + len(AROUND)


def swapped(up, down, axis, wraps):
    count = lax.axis_size(axis)
    even = lax.axis_index(axis) % 2 == 0
    got = []
    for first, mine in ((0, jnp.where(even, down, up)), (1, jnp.where(even, up, down))):
        pairs = []
        for low in range(first, count, 2):
            high = (low + 1) % count
            if high > low or wraps:
                pairs += [(low, high), (high, low)]
        got.append(lax.ppermute(mine, axis, pairs))
    return got


def before_and_after(got, axis):
    even = lax.axis_index(axis) % 2 == 0
    return jnp.where(even, got[1], got[0]), jnp.where(even, got[0], got[1])


def rectangles(lat_cells, lon_cells):
    lat = {-1: [(lat_cells - HLAT, HLAT)], 1: [(0, HLAT)]}
    lat[0] = [(0, HLAT), (HLAT, lat_cells - WLAT), (lat_cells - HLAT, HLAT)]
    lon = {-1: [(lon_cells - HLON, HLON)], 1: [(0, HLON)]}
    lon[0] = [(0, HLON), (HLON, lon_cells - WLON), (lon_cells - HLON, HLON)]
    return [
        [(top, high, left, wide) for top, high in lat[dy] for left, wide in lon[dx]]
        for dy, dx in AROUND
    ]


def tokens_of(part):
    return part[1] * part[3] * LEV


def padded(count):
    return -(-count // 8) * 8


def gelu(x):
    half = 0.5 * x
    inner = x * (0.7978845608028654 + 0.035677408136300125 * (x * x))
    return half + half * jnp.tanh(inner)


def normalise(wide, gain):
    average = jnp.mean(wide, axis=-1, keepdims=True)
    centred = wide - average
    spread = jnp.mean(centred * centred, axis=-1, keepdims=True)
    return centred * lax.rsqrt(spread + 1e-05) * gain


def dot(a, b):
    return jnp.dot(a, b, preferred_element_type=F32)


def dot_nt(a, b):
    return lax.dot_general(a, b, (((1,), (1,)), ((), ())), preferred_element_type=F32)


def about_one_over(x):
    return pl.reciprocal(x, approx=True)


def with_ones(tensor):
    ones = jnp.ones((tensor.shape[0], PAD - tensor.shape[1]), tensor.dtype)
    return jnp.concatenate([tensor, ones], axis=1).astype(BF16)


def below(*pieces):
    return jnp.concatenate(pieces, axis=0) if len(pieces) > 1 else pieces[0]


def pack_kernel(
    values_ref,
    cell_ref,
    tag_ref,
    count_ref,
    back_ref,
    *refs,
):
    out_ref, up_ref, down_ref, values, cells, tags, held, sem = refs
    tiles_lon, tiles_lat, capacity, _ = values_ref.shape
    lat_cells, lon_cells = back_ref.shape[:2]
    strips = [
        (back_ref.at[:HLAT], up_ref),
        (back_ref.at[lat_cells - HLAT :], down_ref),
    ]
    copies = [
        pltpu.make_async_copy(cell_ref, cells, sem.at[0]),
        pltpu.make_async_copy(tag_ref, tags, sem.at[1]),
        pltpu.make_async_copy(count_ref, held, sem.at[2]),
        pltpu.make_async_copy(values_ref, values, sem.at[3]),
    ]
    copies += [
        pltpu.make_async_copy(source, strip, sem.at[4 + n])
        for n, (source, strip) in enumerate(strips)
    ]
    for copy in copies:
        copy.start()
    for copy in copies[:3]:
        copy.wait()
    counts = below(*[held[tile : tile + 1, :] for tile in range(tiles_lat) for _ in range(capacity)])
    cell = cells[...]
    slot = lax.broadcasted_iota(jnp.int32, cell.shape, 0) % capacity
    row = cell // lon_cells
    fields = [jnp.where(slot < counts, row, 255), cell - row * lon_cells, tags[...]]
    rows, columns, kinds = (field.astype(F32) for field in fields)
    lane = lax.broadcasted_iota(jnp.int32, (cell.shape[0], LANES), 1)
    kind_of = (lane % INSTR).astype(F32)
    marks = [
        ((lane < ROWS) & (lane // INSTR == n)) | (lane == ROWS + n) | (lane == COLS + n)
        for n in range(len(AROUND))
    ]
    turned = []
    for lon in range(tiles_lon):
        meta = jnp.where(kind_of == kinds[:, lon : lon + 1], 1.0, 0.0)
        meta = jnp.where(lane >= ROWS, rows[:, lon : lon + 1], meta)
        meta = jnp.where(lane >= COLS, columns[:, lon : lon + 1], meta)
        turns = {0: meta}
        for dy in (-1, 1):
            by = dy * capacity % meta.shape[0]
            turns[dy] = below(meta[by:], meta[:by])
        turned.append(turns)
    for lon in range(tiles_lon):
        meta = jnp.zeros(lane.shape, F32)
        for mark, (dy, dx) in zip(marks, AROUND):
            meta = jnp.where(mark, turned[(lon + dx) % tiles_lon][dy], meta)
        out_ref[lon, :, len(AROUND)] = meta.astype(BF16).reshape(tiles_lat, capacity, LANES)
    copies[3].wait()
    for n, (dy, dx) in enumerate(AROUND):
        spans = {0: [(0, tiles_lat)], 1: [(0, tiles_lat - 1), (tiles_lat - 1, tiles_lat)]}
        spans[-1] = [(0, 1), (1, tiles_lat)]

        def copy_tiles(lon, n=n, dx=dx, dy=dy, spans=spans[dy]):
            source = lax.rem(lon + dx + tiles_lon, tiles_lon)
            for low, end in spans:
                first = (low + dy) % tiles_lat
                out_ref[lon, low:end, n] = values[source, first : first + end - low]

        if tiles_lon <= 8:
            for lon in range(tiles_lon):
                copy_tiles(lon)
        else:
            pl.loop(0, tiles_lon)(copy_tiles)
    for copy in copies[4:]:
        copy.wait()


def packed(record_values, record_cell, record_instrument, block_counts, background):
    tiles_lon, tiles_lat, capacity, wide = record_values.shape
    anywhere = pl.BlockSpec(memory_space=pltpu.HBM)
    ints = pltpu.VMEM((tiles_lat * capacity, tiles_lon), jnp.int32)
    shape = (tiles_lon, tiles_lat, len(AROUND) + 1, capacity, wide)
    lat_cells, lon_cells, levels, width = background.shape
    across = jax.ShapeDtypeStruct((HLAT, lon_cells, levels, width), BF16)
    out, *strips = pl.pallas_call(
        pack_kernel,
        out_shape=[jax.ShapeDtypeStruct(shape, BF16), across, across],
        in_specs=[anywhere] * 5,
        out_specs=[pl.BlockSpec(memory_space=pltpu.VMEM)] * 3,
        scratch_shapes=[
            pltpu.VMEM(record_values.shape, BF16),
            ints,
            ints,
            pltpu.VMEM((tiles_lat, tiles_lon), jnp.int32),
            pltpu.SemaphoreType.DMA((6,)),
        ],
        compiler_params=pltpu.CompilerParams(vmem_limit_bytes=56 * 2**20),
        cost_estimate=pl.CostEstimate(
            flops=20 * 10**9, bytes_accessed=10**6, transcendentals=0
        ),
    )(
        record_values,
        record_cell.transpose(1, 2, 0).reshape(-1, tiles_lon),
        record_instrument.transpose(1, 2, 0).reshape(-1, tiles_lon),
        block_counts.T,
        background,
    )
    return out.reshape((-1,) + shape[2:]), *strips


def token_codes(part, lon_cells):
    top, high, left, wide = part
    count = tokens_of(part)
    place = lax.broadcasted_iota(jnp.int32, (padded(count), LANES), 0)
    code = place + (top * lon_cells + left) * LEV
    for row in range(1, high):
        step = (lon_cells - wide) * LEV
        code = code + jnp.where(place >= row * wide * LEV, step, 0)
    return jnp.where(place < count, code, -8).astype(F32)


def near_entries(windows):
    own = [(4, 3 * i + j) for i, j in windows]
    return own + [(3 * i + 1, j) for i, j in windows if i != 1]


def far_entries(windows):
    beside = [(3 + j, i) for i, j in windows if j != 1]
    return beside + [(3 * i + j, 0) for i, j in windows if i != 1 and j != 1]


def scattered(recv_ref, first_ref, table_ref, lift_ref, plan, lon_cells):
    sources, _, capacity, _ = recv_ref.shape
    width = first_ref.shape[1]
    chunk = min(CHUNK, sources)
    slots = chunk * capacity
    first, lift = below(first_ref[...], table_ref[...]), lift_ref[...]
    lane = lax.broadcasted_iota(jnp.int32, (16, LANES), 1)
    sub = lax.broadcasted_iota(jnp.int32, (16, LANES), 0)
    weigh = jnp.where(lane == ROWS + sub, float(lon_cells * LEV), 0.0)
    weigh = jnp.where(lane == COLS + sub, float(LEV), weigh).astype(BF16)
    codes = [below(*[token_codes(part, lon_cells) for part in parts]) for parts in plan]

    def scatter(begin):
        meta = recv_ref[pl.ds(begin, chunk), len(AROUND)].reshape(slots, LANES)
        records = below(
            *[
                recv_ref[pl.ds(begin, chunk), n].reshape(slots, LANES)
                for n in range(len(AROUND))
            ]
        )
        lane = lax.broadcasted_iota(jnp.int32, meta.shape, 1) // INSTR
        wide = meta.astype(F32)
        chosen = below(*[jnp.where(lane == n, wide, 0.0) for n in range(len(AROUND))]).astype(BF16)
        both = jnp.concatenate([records, chosen], axis=1)
        encoded = gelu(dot(both, first).astype(BF16))
        lifted = gelu(dot(encoded, lift).astype(BF16))
        tokens = dot_nt(weigh, meta)
        hots, parts = [], []
        for n in range(len(AROUND)):
            token = tokens[n : n + 1]
            token = jnp.concatenate([token + float(level) for level in range(LEV)], axis=1)
            if token.shape[1] == LANES:
                hot = codes[n] == token
            else:
                hot = codes[n][:, :1] == token
            hots.append(jnp.where(hot, 1.0, 0.0).astype(BF16))
        for n in range(len(AROUND)):
            part = lifted[n * slots : (n + 1) * slots]
            parts.append(
                with_ones(
                    below(*[part[:, level * width : (level + 1) * width] for level in range(LEV)])
                )
            )
        sums = [dot(hot, part) for hot, part in zip(hots, parts)]
        return tuple(sums)

    sums = scatter(0)
    if sources > chunk:
        sums = lax.fori_loop(
            1,
            sources // chunk,
            lambda step, total: tuple(a + b for a, b in zip(total, scatter(step * chunk))),
            sums,
        )
    return sums


def prepare_kernel(
    plan,
    back_ref,
    attn_ref,
    table_ref,
    one_ref,
    two_ref,
    rows_ref,
    parts_ref,
    tables_ref,
    gain_one_ref,
    gain_two_ref,
):
    width = back_ref.shape[3]
    pieces = []
    for top, high, left, wide in plan[4]:
        count = high * wide * LEV
        piece = back_ref[top : top + high, left : left + wide].reshape(count, width).astype(F32)
        if padded(count) > count:
            piece = below(piece, jnp.zeros((padded(count) - count, width), F32))
        pieces.append(piece)
    rows_ref[...] = below(*pieces).astype(BF16)
    tables_ref[...] = below(*[table_ref[...].astype(F32)] * (LANES // INSTR)).astype(BF16)
    for gain, ref in ((one_ref, gain_one_ref), (two_ref, gain_two_ref)):
        ref[...] = jnp.broadcast_to(gain[...].astype(F32).reshape(1, width), ref.shape)
    for n in range(3):
        parts_ref[n] = attn_ref[:, n * width : (n + 1) * width]


def prepared(plan, background, attn_weight, instrument_table, first_gain, second_gain):
    width = background.shape[3]
    rows = sum(padded(tokens_of(part)) for part in plan[4])
    vmem = pl.BlockSpec(memory_space=pltpu.VMEM)
    return pl.pallas_call(
        functools.partial(prepare_kernel, plan),
        out_shape=[
            jax.ShapeDtypeStruct((rows, width), BF16),
            jax.ShapeDtypeStruct((3, width, width), BF16),
            jax.ShapeDtypeStruct((LANES, width), BF16),
            jax.ShapeDtypeStruct((8, width), F32),
            jax.ShapeDtypeStruct((8, width), F32),
        ],
        in_specs=[vmem] * 5,
        out_specs=[vmem] * 5,
        compiler_params=pltpu.CompilerParams(vmem_limit_bytes=LIMIT),
        cost_estimate=pl.CostEstimate(flops=10**9, bytes_accessed=10**6, transcendentals=0),
    )(background, attn_weight, instrument_table, first_gain, second_gain)


def normed_of(plan, entries, sums, borders, gain):
    rows, north_ref, south_ref, west_ref, east_ref, lat_cells = borders
    width = gain.shape[1]
    pieces, spans, start = [], {}, 0
    for tile, number in entries:
        dy, dx = AROUND[tile]
        top, high, left, wide = plan[tile][number]
        count = high * wide * LEV
        full = padded(count)
        if tile == 4:
            begin = sum(padded(tokens_of(part)) for part in plan[4][:number])
            piece = rows[begin : begin + full]
        else:
            if dx:
                ref = west_ref if dx < 0 else east_ref
                top, left = {-1: 0, 0: top + HLAT, 1: lat_cells + HLAT}[dy], 0
            else:
                ref, top = (north_ref, 0) if dy < 0 else (south_ref, 0)
            block = ref(top, high) if dx else ref[top : top + high, left : left + wide]
            piece = block.reshape(count, width).astype(F32)
            if full > count:
                piece = below(piece, jnp.zeros((full - count, width), F32))
        pieces.append(piece)
        spans[tile, number] = (start, count)
        start += full
    tally = 1.0 + sums[:, width : width + 1]
    share = about_one_over(tally)
    share = share * (2.0 - tally * share)
    latent = ((below(*pieces) + sums[:, :width]) * share).astype(BF16).astype(F32)
    return latent, normalise(latent, gain), spans


def stacks_of(plan, places, own_normed, weight):
    width = weight.shape[0]
    head = width // HEADS
    query = dot(own_normed.astype(BF16), weight) * head ** (-0.5)
    query = jnp.concatenate([query, jnp.ones((query.shape[0], PAD - width), F32)], axis=1)
    lane = lax.broadcasted_iota(jnp.int32, (1, PAD), 1)
    stacks, begin = [], 0
    for i, j in places:
        rows = padded(tokens_of(plan[4][3 * i + j]))
        part = query[begin : begin + rows]
        begin += rows
        stacks.append(
            below(
                *[jnp.where((lane // head == h) | (lane >= width), part, 0.0) for h in range(HEADS)]
            ).astype(BF16)
        )
    return stacks


def worked(plan, places, stacks, keys, values, latent, weights, scalars_ref, put):
    mix_ref, gain_ref, up_ref, down_ref = weights
    width = mix_ref.shape[0]
    head = width // HEADS
    groups = [padded(tokens_of(plan[4][3 * i + j])) for i, j in places]
    lane = lax.broadcasted_iota(jnp.int32, (1, PAD), 1)
    many = WLAT * WLON * LEV
    corner = HLAT * HLON * LEV
    key = lax.broadcasted_iota(jnp.int32, (many, PAD - width), 0)
    spare = lax.broadcasted_iota(jnp.int32, (many, PAD - width), 1)
    unused = lax.broadcasted_iota(jnp.int32, (PAD - many, PAD), 1)
    unused = jnp.where(unused == width, -3e38, 0.0).astype(BF16)
    nothing = jnp.zeros((PAD - many, PAD), BF16)

    def keys_of(w, i, j):
        bias = jnp.zeros((many, PAD - width), F32)
        if i != 1:
            if j == 1:
                inside = key < 2 * corner
            else:
                inside = (key < corner) | ((key >= 2 * corner) & (key < 3 * corner))
            bias = jnp.where(inside | (spare > 0), 0.0, -3e38) * scalars_ref[i].astype(F32)
        here = jnp.concatenate([keys[w], bias], axis=1)
        return below(here.astype(BF16), unused)

    begins = [sum(groups[:w]) for w in range(len(groups))]
    held = [keys_of(w, i, j) for w, (i, j) in enumerate(places)]
    scores = [dot_nt(stack, here) for stack, here in zip(stacks, held)]
    largest = [jnp.max(score, axis=-1, keepdims=True) for score in scores]
    raised = [jnp.exp((score - most).astype(BF16)) for score, most in zip(scores, largest)]
    held = [below(with_ones(value).astype(BF16), nothing) for value in values]
    products = [dot(one, here) for one, here in zip(raised, held)]
    shares = [about_one_over(product[:, width : width + 1]) for product in products]
    products = [product[:, :width] * share for product, share in zip(products, shares)]
    mixed = []
    for product, rows in zip(products, groups):
        total = product[:rows]
        for h in range(1, HEADS):
            own = lane[:, :width] // head == h
            total = jnp.where(own, product[h * rows : (h + 1) * rows], total)
        mixed.append(total)
    mixed = below(*mixed).astype(BF16)

    after = (latent + dot(mixed, mix_ref[...])).astype(BF16).astype(F32)
    normed_two = normalise(after, gain_ref[:1, :]).astype(BF16)
    hidden = gelu(dot(normed_two, up_ref[...]).astype(BF16))
    result = after + dot(hidden, down_ref[...])
    for begin, (i, j) in zip(begins, places):
        part = plan[4][3 * i + j]
        piece = result[begin : begin + tokens_of(part)].astype(BF16)
        put(part, j, piece.reshape(part[1], part[3], LEV, width))


MIDDLE = [(0, 1), (1, 1), (2, 1)]
SIDES = [(1, 0), (1, 2), (0, 0), (0, 2), (2, 0), (2, 2)]


def own_rows(plan, places):
    return sum(padded(tokens_of(plan[4][3 * i + j])) for i, j in places)


def middle_kernel(
    plan,
    lat_cells,
    lon_cells,
    scalars_ref,
    recv_ref,
    north_ref,
    south_ref,
    rows_ref,
    first_ref,
    table_ref,
    lift_ref,
    gain_one_ref,
    *refs,
):
    parts_ref, *weights, out_ref, rest_ref, latent_ref, keys_ref, values_ref, stacks_ref = refs
    sums = scattered(recv_ref, first_ref, table_ref, lift_ref, plan, lon_cells)

    def sums_of(entries):
        pieces = []
        for tile, number in entries:
            start = sum(padded(tokens_of(part)) for part in plan[tile][:number])
            pieces.append(sums[tile][start : start + padded(tokens_of(plan[tile][number]))])
        return below(*pieces)

    borders = (rows_ref[...].astype(F32), north_ref, south_ref, None, None, lat_cells)
    gain = gain_one_ref[:1, :]
    entries = near_entries(MIDDLE)
    latent, normed, spans = normed_of(plan, entries, sums_of(entries), borders, gain)

    def piece_of(tile, number):
        start, count = spans[tile, number]
        return normed[start : start + count]

    def put(part, _, piece):
        out_ref[part[0] : part[0] + part[1]] = piece

    end = own_rows(plan, MIDDLE)
    many = WLAT * WLON * LEV
    tokens = []
    for i, j in MIDDLE:
        tokens.append(piece_of(4, 3 * i + j))
        if i != 1:
            tokens.append(piece_of(3 * i + 1, j))
    tokens = below(*tokens).astype(BF16)
    keys, values = dot(tokens, parts_ref[1]), dot(tokens, parts_ref[2])
    spots = [slice(w * many, (w + 1) * many) for w in range(len(MIDDLE))]
    worked(
        plan,
        MIDDLE,
        stacks_of(plan, MIDDLE, normed[:end], parts_ref[0]),
        [keys[spot] for spot in spots],
        [values[spot] for spot in spots],
        latent[:end],
        weights,
        scalars_ref,
        put,
    )
    rest_ref[...] = sums_of(far_entries(SIDES))
    entries = near_entries(SIDES)
    latent, normed, spans = normed_of(plan, entries, sums_of(entries), borders, gain)
    end = latent_ref.shape[0]
    latent_ref[...] = latent[:end]
    tokens = []
    for i, j in SIDES:
        start, count = spans[4, 3 * i + j]
        tokens.append(normed[start : start + count])
        if i != 1:
            start, count = spans[3 * i + 1, j]
            tokens.append(normed[start : start + count])
    tokens = below(*tokens).astype(BF16)
    keys_ref[...] = dot(tokens, parts_ref[1])
    values_ref[...] = dot(tokens, parts_ref[2])
    stacks_ref[...] = below(*stacks_of(plan, SIDES, normed[:end], parts_ref[0]))


def side_kernel(
    plan,
    lat_cells,
    scalars_ref,
    rest_ref,
    latent_ref,
    keys_ref,
    values_ref,
    stacks_ref,
    one_ref,
    two_ref,
    gain_one_ref,
    *refs,
):
    parts_ref, *weights, middle_ref, out_ref, held_ref, sem = refs
    left, wide = plan[4][4][2:]
    copies = [pltpu.make_async_copy(middle_ref, out_ref.at[:, left : left + wide], sem.at[2])]
    copies[0].start()
    even = scalars_ref[3] == 1

    def west(top, high):
        return jnp.where(even, two_ref[top : top + high], one_ref[top : top + high])

    def east(top, high):
        return jnp.where(even, one_ref[top : top + high], two_ref[top : top + high])

    borders = (None, None, None, west, east, lat_cells)
    gain = gain_one_ref[:1, :]
    _, far, spans = normed_of(plan, far_entries(SIDES), rest_ref[...], borders, gain)

    tokens = []
    for i, j in SIDES:
        for entry in [(3 + j, i)] + ([(3 * i + j, 0)] if i != 1 else []):
            start, count = spans[entry]
            tokens.append(far[start : start + count])
    tokens = below(*tokens).astype(BF16)
    keys, values = dot(tokens, parts_ref[1]), dot(tokens, parts_ref[2])
    half = WLAT * HLON * LEV
    spots = [slice(w * half, (w + 1) * half) for w in range(len(SIDES))]
    stacks, start = [], 0
    for i, j in SIDES:
        rows = HEADS * padded(tokens_of(plan[4][3 * i + j]))
        stacks.append(stacks_ref[start : start + rows, :])
        start += rows

    def put(part, j, piece):
        held_ref[j // 2, part[0] : part[0] + part[1]] = piece

    worked(
        plan,
        SIDES,
        stacks,
        [below(keys_ref[spot, :], keys[spot]) for spot in spots],
        [below(values_ref[spot, :], values[spot]) for spot in spots],
        latent_ref[...],
        weights,
        scalars_ref,
        put,
    )
    for n, number in enumerate((0, 2)):
        left, wide = plan[4][number][2:]
        copies.append(
            pltpu.make_async_copy(held_ref.at[n], out_ref.at[:, left : left + wide], sem.at[n])
        )
        copies[-1].start()
    for copy in copies:
        copy.wait()


def local(
    record_values,
    record_cell,
    record_instrument,
    block_counts,
    background,
    input_weight,
    instrument_table,
    lift_weight,
    first_gain,
    attn_weight,
    mix_weight,
    second_gain,
    up_weight,
    down_weight,
):
    lat_cells, lon_cells, _, width = background.shape
    tiles_lat = record_values.shape[1]

    sent, up, down = packed(
        record_values, record_cell, record_instrument, block_counts, background
    )
    received = lax.all_to_all(sent, ("lon", "lat"), split_axis=0, concat_axis=0, tiled=True)
    north, south = before_and_after(swapped(up, down, "lat", wraps=False), "lat")

    held = (background, input_weight, instrument_table, attn_weight, down_weight)
    held = lax.optimization_barrier((*held, first_gain, second_gain, up))
    later, input_weight, instrument_table, attn_weight, down_weight = held[:5]
    first_gain, second_gain = held[5:7]

    def columns(low, end):
        return jnp.concatenate([north[:, low:end], later[:, low:end], south[:, low:end]], axis=0)

    got = swapped(columns(0, HLON), columns(lon_cells - HLON, lon_cells), "lon", wraps=True)

    plan = rectangles(lat_cells, lon_cells)
    rows, parts, tables, gain_one, gain_two = prepared(
        plan, later, attn_weight, instrument_table, first_gain, second_gain
    )
    lat = lax.axis_index("lat")
    even = lax.axis_index("lon") % 2 == 0
    scalars = jnp.stack([lat == 0, lat < 0, lat == tiles_lat - 1, even]).astype(jnp.int32)

    def rows_in(entries):
        return sum(padded(tokens_of(plan[tile][number])) for tile, number in entries)

    weights = [parts, mix_weight, gain_two, up_weight, down_weight]
    smem = pl.BlockSpec(memory_space=pltpu.SMEM)
    vmem = pl.BlockSpec(memory_space=pltpu.VMEM)
    anywhere = pl.BlockSpec(memory_space=pl.ANY)
    params = pltpu.CompilerParams(vmem_limit_bytes=LIMIT)
    half = WLAT * HLON * LEV * len(SIDES)
    middle, rest, latent, *near = pl.pallas_call(
        functools.partial(middle_kernel, plan, lat_cells, lon_cells),
        out_shape=[
            jax.ShapeDtypeStruct((lat_cells, lon_cells - WLON, LEV, width), BF16),
            jax.ShapeDtypeStruct((rows_in(far_entries(SIDES)), PAD), F32),
            jax.ShapeDtypeStruct((own_rows(plan, SIDES), width), F32),
            jax.ShapeDtypeStruct((half, width), F32),
            jax.ShapeDtypeStruct((half, width), F32),
            jax.ShapeDtypeStruct((HEADS * own_rows(plan, SIDES), PAD), BF16),
        ],
        in_specs=[smem] + [vmem] * (8 + len(weights)),
        out_specs=[vmem] * 6,
        compiler_params=params,
        cost_estimate=pl.CostEstimate(
            flops=4 * 10**9, bytes_accessed=4 * 10**6, transcendentals=10**6
        ),
    )(
        scalars,
        received,
        north,
        south,
        rows,
        input_weight,
        tables,
        lift_weight,
        gain_one,
        *weights,
    )
    rest, *got = lax.optimization_barrier((rest, *got[::-1]))
    got = got[::-1]
    return pl.pallas_call(
        functools.partial(side_kernel, plan, lat_cells),
        out_shape=jax.ShapeDtypeStruct(background.shape, BF16),
        in_specs=[smem] + [vmem] * (9 + len(weights)),
        out_specs=anywhere,
        scratch_shapes=[
            pltpu.VMEM((2, lat_cells, HLON, LEV, width), BF16),
            pltpu.SemaphoreType.DMA((3,)),
        ],
        compiler_params=params,
        cost_estimate=pl.CostEstimate(
            flops=3 * 10**9, bytes_accessed=4 * 10**6, transcendentals=10**6
        ),
    )(scalars, rest, latent, *near, *got, gain_one, *weights, middle)


def solution(mesh):
    placed = (
        P("lon", "lat", None, None),
        P("lon", "lat", None),
        P("lon", "lat", None),
        P("lon", "lat"),
        P("lat", "lon", None, None),
        P(),
        P(),
        P(),
        P(),
        P(),
        P(),
        P(),
        P(),
        P(),
    )
    return jax.shard_map(
        local, mesh=mesh, in_specs=placed, out_specs=P("lat", "lon", None, None), check_vma=False
    )
```
